32 devices in a mesh: wide: 16 (over z, y, core), narrow: 2 (over x).
Axes of the slice: x: 2, y: 2, z: 4, core: 2. Of those that a mesh axis runs over, the one named last changes fastest.
Arguments:
- embedded_patches: bfloat16 [4096, 1280], P(('wide', 'narrow')), may hold values from -6 to 6
- sequence_number: int32 [4096], P(('wide', 'narrow')), may hold values from 0 to 1023, never falling along the last dimension, each value on 1 to 16 neighbouring positions
- filler_flag: int32 [4096], P(('wide', 'narrow')), may hold values 0 or 1
- triple_projection_matrix: bfloat16 [2, 1280, 3840], P(None, ('wide', 'narrow')), may hold values from -0.15625 to 0.15625
- mixing_exit_matrix: bfloat16 [2, 1280, 1280], P(None, ('wide', 'narrow')), may hold values from -0.3125 to 0.3125
- perceptron_expand_matrix: bfloat16 [2, 1280, 5120], P(None, ('wide', 'narrow')), may hold values from -0.15625 to 0.15625
- perceptron_shrink_matrix: bfloat16 [2, 5120, 1280], P(None, ('wide', 'narrow')), may hold values from -0.078125 to 0.078125
- premix_scale_vector: bfloat16 [2, 1280], P(None, ('wide', 'narrow')), may hold values from 0.5 to 1.5
- preperceptron_scale_vector: bfloat16 [2, 1280], P(None, ('wide', 'narrow')), may hold values from 0.5 to 1.5
- readout_first_matrix: bfloat16 [1280, 1280], replicated, may hold values from -0.15625 to 0.15625
- readout_first_offset: bfloat16 [1280], replicated, may hold values from -3 to 3
- readout_final_matrix: bfloat16 [1280, 1280], P(None, 'narrow'), may hold values from -0.15625 to 0.15625
- prediction_offset: bfloat16 [1280], P('narrow'), may hold values from -3 to 3
- readout_shortcut_matrix: bfloat16 [1280, 1280], P(None, 'narrow'), may hold values from -0.15625 to 0.15625
- prediction_adjoint: bfloat16 [4096, 1280], P('wide', 'narrow'), may hold values from -6 to 6
Outputs:
- predictions: bfloat16 [4096, 1280], P('wide', 'narrow')
- input_grad: float32 [4096, 1280], P(('wide', 'narrow'))
- qkv_grad: float32 [2, 1280, 3840], P(None, ('wide', 'narrow'))
- out_grad: float32 [2, 1280, 1280], P(None, ('wide', 'narrow'))
- in_grad: float32 [2, 1280, 5120], P(None, ('wide', 'narrow'))
- down_grad: float32 [2, 5120, 1280], P(None, ('wide', 'narrow'))
- attn_gain_grad: float32 [2, 1280], P(None, ('wide', 'narrow'))
- mlp_gain_grad: float32 [2, 1280], P(None, ('wide', 'narrow'))
- head_in_grad: float32 [1280, 1280], P(('wide', 'narrow'))
- head_in_bias_grad: float32 [1280], P(('wide', 'narrow'))
- head_out_grad: float32 [1280, 1280], P('wide', 'narrow')
- head_out_bias_grad: float32 [1280], P('narrow')
- head_skip_grad: float32 [1280, 1280], P('wide', 'narrow')
The draws below stay inside these ranges and needn't reach their ends.
Inputs may be any that keep to these rules, and one draw needn't show every extreme that they name: `sequence_number`: segment numbers never fall along the tokens, and one segment spans 1 to 16 tokens.
All inputs are finite; a program needn't handle non-finite values. No bound on the sum of `filler_flag` on one device may be relied on, other than what follows from the above.
Results may differ from the reference program's by a relative error of at most 0.019.
Values may be sent and summed in bfloat16 or wider, within the bound.
A program may use at most 640 MiB of HBM per device.

```python
import math
import jax
import jax.numpy as jnp
import numpy as np
from jax import lax

EMBED_WIDTH = 1280
HDIM = 80
FF = 5120
PREDICTION_SPAN = 1280
LAYERS = 2
ROW_LEN = 16
PATCH_AMOUNT = 4096


def with_ends(entries, rng, smallest, largest):
    place = [jax.random.randint(jax.random.fold_in(rng, axis), (), 0, length) for axis, length in enumerate(entries.shape)]
    main_axis = entries.shape.index(max(entries.shape))
    beside = place[:main_axis] + [(place[main_axis] + 1) % entries.shape[main_axis]] + place[main_axis + 1:]
    return entries.at[tuple(place)].set(smallest).at[tuple(beside)].set(largest)


def block_scale(own_key, extent, cuts, low, largest):
    loudness = 1.0
    for dim, blocks in cuts:
        steps = jax.random.uniform(jax.random.fold_in(jax.random.fold_in(own_key, 6), dim), (blocks,), jnp.float32, low / len(cuts), largest / len(cuts))
        loudness = loudness * jnp.repeat(jnp.exp(steps), extent[dim] // blocks).reshape((-1,) + (1,) * (len(extent) - 1 - dim))
    return loudness


def length_profile(count, total, bound, skew):
    loads = [(1 << 20) // math.isqrt(rank ** skew) + 1 for rank in range(2, count + 1)]
    surplus, holding = total - bound - (count - 1), [1] * (count - 1)
    while surplus > 0:
        movable = [i for i in range(count - 1) if holding[i] < bound]
        mass, budget = sum([loads[i] for i in movable]), surplus
        for i in movable:
            addition = min(bound - holding[i], max(1, budget * loads[i] // mass), surplus)
            holding[i] = holding[i] + addition
            surplus = surplus - addition
    return np.array([bound] + holding)


def uneven(stream_key, amount, total, bound, skew):
    if amount == 2:
        one = jax.random.randint(stream_key, (), max(1, total - bound), min(bound, total - 1) + 1)
        return jnp.stack([one, total - one])
    lengths = jnp.asarray(length_profile(amount, total, bound, skew), jnp.int32)
    pairs = (amount - 1) // 2
    donor, taker = lengths[1:1 + 2 * pairs:2], lengths[2:2 + 2 * pairs:2]
    margin = jnp.minimum(donor - 1, bound - taker)
    passed = jax.random.randint(jax.random.fold_in(stream_key, 1), (pairs,), 0, 1 << 20) % (margin + 1)
    lengths = lengths.at[1:1 + 2 * pairs:2].set(donor - passed).at[2:2 + 2 * pairs:2].set(taker + passed)
    return lengths[jax.random.permutation(jax.random.fold_in(stream_key, 2), amount)]


def normal_values(stream_key, dims, width, limit, split=(), held_as=jnp.bfloat16):
    entries = jax.random.normal(stream_key, dims, jnp.float32) * width
    if len(split) > 0:
        entries = block_scale(stream_key, dims, split, -0.22, 0.18) * entries
    return jnp.clip(entries, min=-limit, max=limit).astype(held_as)


def setup_inputs(seed: int = 0) -> dict:
    key_of = jax.random.split(jax.random.key(seed), 16)
    embedded_patches = normal_values(key_of[0], (PATCH_AMOUNT, EMBED_WIDTH), 1.0, 6.0, ((0, 32),))
    sequence_number = jnp.searchsorted(jnp.cumsum(uneven(key_of[1], PATCH_AMOUNT // 4, PATCH_AMOUNT, 16, 2)), jnp.arange(PATCH_AMOUNT), side="right").astype(jnp.int32)
    filler_flag = with_ends((jax.random.randint(key_of[2], (PATCH_AMOUNT,), 0, 8) < 1).astype(jnp.int32), jax.random.fold_in(key_of[2], 1), 0, 1)
    triple_projection_matrix = normal_values(key_of[3], (LAYERS, EMBED_WIDTH, 3 * EMBED_WIDTH), EMBED_WIDTH ** -0.5, 0.15625, ((1, 32),))
    mixing_exit_matrix = normal_values(key_of[4], (LAYERS, EMBED_WIDTH, EMBED_WIDTH), (EMBED_WIDTH // 4) ** -0.5, 0.3125, ((1, 32),))
    perceptron_expand_matrix = normal_values(key_of[5], (LAYERS, EMBED_WIDTH, FF), EMBED_WIDTH ** -0.5, 0.15625, ((1, 32),))
    perceptron_shrink_matrix = normal_values(key_of[6], (LAYERS, FF, EMBED_WIDTH), FF ** -0.5, 0.078125, ((1, 32),))
    premix_scale_vector = jnp.clip(1.0 + 0.1 * jax.random.normal(key_of[7], (LAYERS, EMBED_WIDTH), jnp.float32), 0.5, 1.5).astype(jnp.bfloat16)
    preperceptron_scale_vector = jnp.clip(1.0 + 0.1 * jax.random.normal(key_of[8], (LAYERS, EMBED_WIDTH), jnp.float32), 0.5, 1.5).astype(jnp.bfloat16)
    readout_first_matrix = normal_values(key_of[9], (EMBED_WIDTH, EMBED_WIDTH), EMBED_WIDTH ** -0.5, 0.15625)
    readout_first_offset = normal_values(key_of[10], (EMBED_WIDTH,), 0.5, 3.0)
    readout_final_matrix = normal_values(key_of[11], (EMBED_WIDTH, PREDICTION_SPAN), EMBED_WIDTH ** -0.5, 0.15625, ((1, 2),))
    prediction_offset = normal_values(key_of[12], (PREDICTION_SPAN,), 0.5, 3.0, ((0, 2),))
    readout_shortcut_matrix = normal_values(key_of[13], (EMBED_WIDTH, PREDICTION_SPAN), EMBED_WIDTH ** -0.5, 0.15625, ((1, 2),))
    prediction_adjoint = normal_values(key_of[14], (PATCH_AMOUNT, PREDICTION_SPAN), 1.0, 6.0, ((0, 16), (1, 2)))
    return dict(embedded_patches=embedded_patches, sequence_number=sequence_number, filler_flag=filler_flag, triple_projection_matrix=triple_projection_matrix, mixing_exit_matrix=mixing_exit_matrix, perceptron_expand_matrix=perceptron_expand_matrix, perceptron_shrink_matrix=perceptron_shrink_matrix, premix_scale_vector=premix_scale_vector, preperceptron_scale_vector=preperceptron_scale_vector, readout_first_matrix=readout_first_matrix, readout_first_offset=readout_first_offset, readout_final_matrix=readout_final_matrix, prediction_offset=prediction_offset, readout_shortcut_matrix=readout_shortcut_matrix, prediction_adjoint=prediction_adjoint)


epsilon = 1e-06
rotary_base = 10000.0

@jax.custom_vjp
def low(v):
    return lax.optimization_barrier(v.astype(jnp.bfloat16)).astype(jnp.float32)

@jax.custom_vjp
def low_back(v):
    return v

def low_keep(v):
    return (low(v), None)

def low_pass(kept, grad):
    return (grad,)

def back_keep(v):
    return (v, None)

def back_low(kept, grad):
    return (low(grad),)
low.defvjp(low_keep, low_pass)
low_back.defvjp(back_keep, back_low)

def matrix_product(left, right):
    return jnp.dot(left, right, precision=lax.Precision.HIGHEST, preferred_element_type=jnp.float32)

def rms_gain(values, gain_row):
    return values * lax.rsqrt(lax.optimization_barrier(jnp.mean(values * values, axis=-1, keepdims=True)) + epsilon) * gain_row

def rotary_tables(token_count):
    halfway = HDIM // 2
    position = (jnp.arange(token_count) % ROW_LEN).astype(jnp.float32)
    inverse = rotary_base ** (-jnp.arange(halfway).astype(jnp.float32) / halfway)
    angles = position[:, None] * inverse[None, :]
    return (jnp.cos(angles)[:, None, :], jnp.sin(angles)[:, None, :])

def rotate(values, cosine_table, sine_table):
    halfway = values.shape[-1] // 2
    first_half = values[..., :halfway]
    second_half = values[..., halfway:]
    return jnp.concatenate([first_half * cosine_table - second_half * sine_table, second_half * cosine_table + first_half * sine_table], axis=-1)

def block_mask(segments, padded):
    within = jnp.arange(128)
    row_of = within // ROW_LEN
    query_side = within[:, None]
    key_side = within[None, :]
    static = (row_of[:, None] == row_of[None, :]) & (key_side <= query_side)
    same_segment = segments[:, :, None] == segments[:, None, :]
    open_key = (padded[:, None, :] == 0) | (query_side == key_side)[None]
    return static[None] & same_segment & open_key

def attend_piece(pieces):
    queries, keys_in, values_in, segments, padded = pieces
    piece_rows, head_count, head_dim = queries.shape
    groups = piece_rows // 128
    query_blocks = queries.reshape(groups, 128, head_count, head_dim)
    key_blocks = keys_in.reshape(groups, 128, head_count, head_dim)
    value_blocks = values_in.reshape(groups, 128, head_count, head_dim)
    scores = jnp.einsum('gqhd,gkhd->ghqk', query_blocks, key_blocks, precision=lax.Precision.HIGHEST) / jnp.sqrt(jnp.float32(head_dim))
    scores = low_back(scores)
    allowed = block_mask(segments.reshape(groups, 128), padded.reshape(groups, 128))
    scores = jnp.where(allowed[:, None], scores, jnp.float32(-1e+30))
    attn_probs = low(jax.nn.softmax(scores, axis=-1))
    output = jnp.einsum('ghqk,gkhd->gqhd', attn_probs, value_blocks, precision=lax.Precision.HIGHEST)
    return output.reshape(piece_rows, head_count, head_dim)

def layer_forward(residual, w_qkv, w_out, w_in, w_down, gain_attn, gain_mlp, sequence_number, filler_flag, cosine_table, sine_table):
    token_count, model_width = residual.shape
    head_count = model_width // HDIM
    normed = low(rms_gain(residual, gain_attn))
    projected = low_back(matrix_product(normed, w_qkv))
    queries = low(rotate(projected[:, :model_width].reshape(token_count, head_count, HDIM), cosine_table, sine_table))
    keys_in = low(rotate(projected[:, model_width:2 * model_width].reshape(token_count, head_count, HDIM), cosine_table, sine_table))
    values_in = low(projected[:, 2 * model_width:].reshape(token_count, head_count, HDIM))
    piece_rows = min(4096, token_count)
    pieces = token_count // piece_rows

    def to_pieces(numeric_tensor):
        return numeric_tensor.reshape((pieces, piece_rows) + numeric_tensor.shape[1:])
    attended = lax.map(jax.checkpoint(attend_piece), (to_pieces(queries), to_pieces(keys_in), to_pieces(values_in), to_pieces(sequence_number), to_pieces(filler_flag)))
    attended = low_back(low(attended.reshape(token_count, model_width)))
    middle = residual + low_back(matrix_product(attended, w_out))
    normed_mlp = low(rms_gain(middle, gain_mlp))
    lifted = low_back(matrix_product(normed_mlp, w_in))
    activated = low(jax.nn.gelu(lifted))
    return middle + low_back(matrix_product(activated, w_down))

def causal_network(embedded_patches, triple_projection_matrix, mixing_exit_matrix, perceptron_expand_matrix, perceptron_shrink_matrix, premix_scale_vector, preperceptron_scale_vector, readout_first_matrix, readout_first_offset, readout_final_matrix, prediction_offset, readout_shortcut_matrix, sequence_number, filler_flag):
    cosine_table, sine_table = rotary_tables(embedded_patches.shape[0])
    residual = embedded_patches
    for layer_index in range(LAYERS):
        residual = layer_forward(residual, triple_projection_matrix[layer_index], mixing_exit_matrix[layer_index], perceptron_expand_matrix[layer_index], perceptron_shrink_matrix[layer_index], premix_scale_vector[layer_index], preperceptron_scale_vector[layer_index], sequence_number, filler_flag, cosine_table, sine_table)
    patch_lines = low(residual)
    pre = low_back(matrix_product(patch_lines, readout_first_matrix) + readout_first_offset)
    readout_latent_activation = low(jax.nn.silu(pre))
    return matrix_product(readout_latent_activation, readout_final_matrix) + prediction_offset + matrix_product(patch_lines, readout_shortcut_matrix)

def reference(embedded_patches, sequence_number, filler_flag, triple_projection_matrix, mixing_exit_matrix, perceptron_expand_matrix, perceptron_shrink_matrix, premix_scale_vector, preperceptron_scale_vector, readout_first_matrix, readout_first_offset, readout_final_matrix, prediction_offset, readout_shortcut_matrix, prediction_adjoint):
    real_numbers_cast = tuple((numeric_tensor.astype(jnp.float32) for numeric_tensor in (embedded_patches, triple_projection_matrix, mixing_exit_matrix, perceptron_expand_matrix, perceptron_shrink_matrix, premix_scale_vector, preperceptron_scale_vector, readout_first_matrix, readout_first_offset, readout_final_matrix, prediction_offset, readout_shortcut_matrix)))
    prediction_lines, reverse_pass_rule = jax.vjp(lambda *learnable_nest: causal_network(*learnable_nest, sequence_number, filler_flag), *real_numbers_cast)
    learnable_slopes = reverse_pass_rule(prediction_adjoint.astype(jnp.float32))
    return (prediction_lines.astype(jnp.bfloat16), learnable_slopes[0], learnable_slopes[1], learnable_slopes[2], learnable_slopes[3], learnable_slopes[4], learnable_slopes[5], learnable_slopes[6], learnable_slopes[7], learnable_slopes[8], learnable_slopes[9], learnable_slopes[10], learnable_slopes[11])
```

```python
import math

import jax
import jax.numpy as jnp
import numpy as np
from jax import lax
from jax.experimental import pallas as pl
from jax.experimental.pallas import tpu as pltpu
from jax.sharding import PartitionSpec as P

HDIM = 80
HALF = HDIM // 2
LAYERS = 2
ROW_LEN = 16
BLOCK = 128
PLANE = 8
PHASES = 2 * LAYERS
MESH = pl.DeviceIdType.MESH
BF = jnp.bfloat16
F32 = jnp.float32
EPS = 1e-06
ROTARY_BASE = 10000.0
MIB = 1024 * 1024
VMEM = pl.BlockSpec(memory_space=pltpu.VMEM)
ANY = pl.BlockSpec(memory_space=pl.ANY)


def up16(rows):
    return -(-rows // 16) * 16


def rows_at(start, count, step=16):
    return pl.ds(pl.multiple_of(start, step), count)


def dot(a, b, ca=1, cb=0):
    return lax.dot_general(a, b, (((ca,), (cb,)), ((), ())), preferred_element_type=F32)


class Place:
    def __init__(self):
        wide = lax.axis_index("wide")
        self.x = lax.axis_index("narrow")
        self.core = wide % 2
        self.y = (wide // 2) % 2
        self.z = wide // 4

    def device(self, z, y, core, x):
        return (z * 4 + y * 2 + core, x)

    def sibling(self):
        return self.device(self.z, self.y, 1 - self.core, self.x)

    def peer(self, k):
        return self.device(self.z, (self.y + k // 2) % 2, self.core, (self.x + k % 2) % 2)

    def pair(self, k):
        return 2 * ((self.y + k // 2) % 2) + (self.x + k % 2) % 2

    def level(self, z):
        return self.device(z, self.y, self.core, self.x)


def greet(place, levels):
    barrier = pltpu.get_barrier_semaphore()
    others = [place.sibling()] + [place.peer(k) for k in (1, 2, 3)]
    others += [place.level((place.z + d) % levels) for d in range(1, levels)]
    for other in others:
        pl.semaphore_signal(barrier, inc=1, device_id=other, device_id_type=MESH)
    pl.semaphore_wait(barrier, len(others))


def remote(src, dst, send, recv, device):
    return pltpu.make_async_remote_copy(
        src_ref=src, dst_ref=dst, send_sem=send, recv_sem=recv, device_id=device,
        device_id_type=MESH,
    )


class Exchange:
    def __init__(self, place, phase, buf, scratch):
        (self.part, self.recv_s, self.recv_c, self.send_c, self.sems) = scratch
        self.place, self.phase, self.buf = place, phase, buf

    def sem(self, kind, k):
        return self.sems.at[self.phase, kind, k]

    def rows(self, k, core):
        return rows_at(2 * BLOCK * self.place.pair(k) + BLOCK * core, BLOCK, BLOCK)

    def to_peer(self, k):
        own = self.buf.at[self.rows(0, self.place.core)]
        return remote(own, own, self.sem(0, k), self.sem(1, k), self.place.peer(k))

    def from_peer(self, k):
        there = self.buf.at[self.rows(k, self.place.core)]
        return remote(there, there, self.sem(0, k), self.sem(1, k), self.place.peer(k))

    def to_sibling(self, k):
        rows = self.buf.at[self.rows(k, self.place.core)]
        return remote(rows, rows, self.sem(2, k), self.sem(3, k), self.place.sibling())

    def from_sibling(self, k):
        rows = self.buf.at[self.rows(k, 1 - self.place.core)]
        return remote(rows, rows, self.sem(2, k), self.sem(3, k), self.place.sibling())

    def sum_sibling(self, k):
        src = self.part.at[k, rows_at(BLOCK * (1 - self.place.core), BLOCK, BLOCK)]
        return remote(src, self.recv_s.at[k], self.sem(4, k), self.sem(5, k), self.place.sibling())

    def sum_peer(self, k):
        return remote(
            self.send_c.at[k], self.recv_c.at[k], self.sem(6, k), self.sem(7, k), self.place.peer(k)
        )

    def chip_sum(self, k):
        own = self.part[k, rows_at(BLOCK * self.place.core, BLOCK, BLOCK), :]
        return own.astype(F32) + self.recv_s[k].astype(F32)

    def start(self):
        self.to_sibling(0).start()
        for k in (1, 2, 3):
            self.to_peer(k).start()

    def finish_chip(self, k):
        self.sum_sibling(k).wait_recv()
        self.send_c[k] = self.chip_sum(k).astype(BF)
        self.sum_peer(k).start()

    def run(self, compute):
        def body(k, carry):
            @pl.when(k > 0)
            def _():
                self.from_peer(k).wait_recv()
                self.to_sibling(k).start()

            self.from_sibling(k).wait_recv()
            compute(2 * BLOCK * self.place.pair(k), k)
            self.sum_sibling(k).start()

            @pl.when(k > 1)
            def _():
                self.finish_chip(k - 1)

            return carry

        lax.fori_loop(0, 4, body, 0)
        self.finish_chip(3)

    def total(self):
        self.sum_sibling(0).wait_recv()
        total = self.chip_sum(0)
        for k in (1, 2, 3):
            self.sum_peer(k).wait_recv()
            total = total + self.recv_c[k].astype(F32)
        for k in range(4):
            self.to_sibling(k).wait_send()
            self.sum_sibling(k).wait_send()
            if k:
                self.to_peer(k).wait_send()
                self.sum_peer(k).wait_send()
        return total


def exchange_scratch(width):
    return [
        pltpu.VMEM((4, 2 * BLOCK, width), BF),
        pltpu.VMEM((4, BLOCK, width), BF),
        pltpu.VMEM((4, BLOCK, width), BF),
        pltpu.VMEM((4, BLOCK, width), BF),
        pltpu.SemaphoreType.DMA((PHASES, 8, 4)),
    ]


def root(values):
    return lax.rsqrt(jnp.mean(values * values, axis=-1, keepdims=True) + EPS)


def forward_kernel(levels, *refs):
    (x_in, mask, gains, rope, sel_q, sel_o, *pieces) = refs[:10]
    (rows_out, nrm, nml, qkv, prb, att, dgl, act, xs, mid, *slabs) = refs[10:24]
    (part, recv_s, recv_c, send_c, sems, wide_q, z_sems, own_sems) = refs[24:]
    place = Place()
    z = place.z
    scratch = (part, recv_s, recv_c, send_c, sems)
    heads = (sel_q.shape[0] // HDIM) // 3
    lanes = heads * BLOCK

    def spread(layer, m, delta):
        count = pieces[m].shape[1]
        return remote(
            pieces[m].at[layer],
            slabs[m].at[layer, rows_at(z * count, count)],
            z_sems.at[0, layer, m, delta - 1],
            z_sems.at[1, layer, m, delta - 1],
            place.level((z + delta) % levels),
        )

    def arriving(layer, m, delta):
        count = pieces[m].shape[1]
        return remote(
            pieces[m].at[layer],
            slabs[m].at[layer, rows_at((z + levels - delta) % levels * count, count)],
            z_sems.at[0, layer, m, delta - 1],
            z_sems.at[1, layer, m, delta - 1],
            place.level((z + delta) % levels),
        )

    def keep(layer, m):
        count = pieces[m].shape[1]
        return pltpu.make_async_copy(
            pieces[m].at[layer], slabs[m].at[layer, rows_at(z * count, count)],
            own_sems.at[layer, m],
        )

    def send_weights(layer, m):
        for delta in range(1, levels):
            spread(layer, m, delta).start()

    def wait_weights(layer, m):
        for delta in range(1, levels):
            arriving(layer, m, delta).wait_recv()
        for delta in range(1, levels):
            spread(layer, m, delta).wait_send()
        keep(layer, m).wait()

    order = [(layer, m) for layer in range(LAYERS) for m in range(4)]
    for layer, m in order:
        keep(layer, m).start()
    greet(place, levels)
    for layer, m in order[:3]:
        send_weights(layer, m)

    def weights_here(index):
        wait_weights(*order[index])
        if index + 3 < len(order):
            send_weights(*order[index + 3])

    xs[0] = x_in[...].astype(F32)
    for layer in range(LAYERS):
        wq, wo, wi, wd = [slab.at[layer] for slab in slabs]

        own = rows_at(2 * BLOCK * place.pair(0) + BLOCK * place.core, BLOCK, BLOCK)
        residual = xs[layer]
        normed = residual * root(residual) * gains[layer : layer + 1]
        nrm[layer, own, :] = normed.astype(BF)
        phase = Exchange(place, 2 * layer, nrm.at[layer], scratch)
        phase.start()
        weights_here(4 * layer)
        for n in range(0, wide_q.shape[1], 256):
            wide_q[:, n : n + 256] = dot(wq[...], sel_q[:, n : n + 256]).astype(BF)
        weights_here(4 * layer + 1)

        def attend(start, k, layer=layer, wo=wo):
            projected = dot(nrm[layer, rows_at(start, 2 * BLOCK, BLOCK), :], wide_q[...])
            cosine, sine = rope[:, :BLOCK], rope[:, BLOCK:]
            for half in range(2):
                rows = rows_at(start + half * BLOCK, BLOCK, BLOCK)
                allowed = mask[rows, :] > 0
                here = projected[half * BLOCK : (half + 1) * BLOCK]
                outs = []
                for h in range(heads):
                    def part_of(kind, h=h, here=here):
                        return here[:, kind * lanes + h * BLOCK : kind * lanes + (h + 1) * BLOCK]

                    turned = []
                    for kind in range(2):
                        value = part_of(kind)
                        value = value * cosine + pltpu.roll(value, BLOCK // 2, 1) * sine
                        turned.append(value.astype(BF))
                    query, key = turned
                    value = part_of(2).astype(BF)
                    qkv[layer, rows, h * BLOCK : (h + 1) * BLOCK] = query
                    qkv[layer, rows, lanes + h * BLOCK : lanes + (h + 1) * BLOCK] = key
                    qkv[layer, rows, 2 * lanes + h * BLOCK : 2 * lanes + (h + 1) * BLOCK] = value
                    scores = dot(query, key, 1, 1) * (1.0 / math.sqrt(HDIM))
                    scores = jnp.where(allowed, scores, -1e30)
                    scores = jnp.exp(scores - jnp.max(scores, axis=-1, keepdims=True))
                    probs = (scores / jnp.sum(scores, axis=-1, keepdims=True)).astype(BF)
                    prb[layer, rows, h * BLOCK : (h + 1) * BLOCK] = probs
                    outs.append(dot(probs, value).astype(BF))
                att[layer, rows, :] = dot(jnp.concatenate(outs, axis=1), sel_o[...], 1, 1).astype(BF)
            both = att[layer, rows_at(start, 2 * BLOCK, BLOCK), :]
            part[k] = dot(both, wo[...]).astype(BF)

        phase.run(attend)
        middle = residual + phase.total()
        mid[layer] = middle

        normed = middle * root(middle) * gains[LAYERS + layer : LAYERS + layer + 1]
        nml[layer, own, :] = normed.astype(BF)
        phase = Exchange(place, 2 * layer + 1, nml.at[layer], scratch)
        phase.start()
        weights_here(4 * layer + 2)
        weights_here(4 * layer + 3)

        def perceptron(start, k, layer=layer, wi=wi, wd=wd):
            rows = rows_at(start, 2 * BLOCK, BLOCK)
            for n in range(0, wi.shape[1], BLOCK):
                width = slice(n, n + BLOCK)
                lifted = dot(nml[layer, rows, :], wi[:, width])
                root_two = math.sqrt(2.0 / math.pi)
                square = lifted * lifted
                tanh = jnp.tanh(root_two * lifted * (1.0 + 0.044715 * square))
                act[layer, rows, width] = (0.5 * lifted * (1.0 + tanh)).astype(BF)
                slope = 0.5 * (1.0 + tanh) + 0.5 * lifted * (1.0 - tanh * tanh) * root_two * (
                    1.0 + 3.0 * 0.044715 * square
                )
                dgl[layer, rows, width] = slope.astype(BF)
            part[k] = dot(act[layer, rows, :], wd[...]).astype(BF)

        phase.run(perceptron)
        output = middle + phase.total()
        if layer + 1 < LAYERS:
            xs[layer + 1] = output
        else:
            rows_out[...] = output.astype(BF)


def norm_back(values, gain, grad_normed):
    scale = root(values)
    n = values * scale
    q = grad_normed * gain
    grad = scale * (q - n * jnp.mean(q * n, axis=-1, keepdims=True))
    return grad, jnp.sum(grad_normed * n, axis=0, keepdims=True)


def backward_kernel(levels, *refs):
    (dy_in, gains, rope, sel_q, sel_o, xs, mid, *stored) = refs[:18]
    (dx_out, gain_out, *reduced) = refs[18:24]
    (part, recv_s, recv_c, send_c, sems, ag) = refs[24:30]
    loaded = refs[30:41]
    gp = refs[41]
    stages = refs[42:46]
    arrivals = refs[46:50]
    z_sems, load_sems = refs[50:]
    (nml, act, gl, wi, wd, nrm, qkv, prb, att, wq, wo) = loaded
    place = Place()
    z = place.z
    scratch = (part, recv_s, recv_c, send_c, sems)
    heads = (sel_q.shape[0] // HDIM) // 3
    lanes = heads * BLOCK

    def load(layer, i):
        return pltpu.make_async_copy(stored[i].at[layer], loaded[i], load_sems.at[i])

    mlp_part, attn_part = range(5), range(5, 11)
    for i in range(11):
        load(LAYERS - 1, i).start()
    greet(place, levels)

    def count_of(m):
        return stages[m].shape[1] // levels

    def send(layer, m, delta):
        there = (z + delta) % levels
        return remote(
            stages[m].at[layer, rows_at(there * count_of(m), count_of(m))],
            arrivals[m].at[layer, delta - 1],
            z_sems.at[0, layer, m, delta - 1],
            z_sems.at[1, layer, m, delta - 1],
            place.level(there),
        )

    def send_all(layer, m):
        for delta in range(1, levels):
            send(layer, m, delta).start()

    def weight_grad(layer, m, left, right, tile):
        width = left.shape[1]
        if width % tile:
            stages[m][layer] = dot(left[...], right[...], 0, 0).astype(BF)
        else:
            def body(i, carry):
                here = rows_at(i * tile, tile, tile)
                stages[m][layer, here, :] = dot(left[:, here], right[...], 0, 0).astype(BF)
                return carry

            lax.fori_loop(0, width // tile, body, 0)
        send_all(layer, m)

    own = rows_at(2 * BLOCK * place.pair(0) + BLOCK * place.core, BLOCK, BLOCK)
    grad = dy_in[...]
    for step, layer in enumerate(reversed(range(LAYERS))):
        buf = ag.at[0]
        buf[own, :] = grad.astype(BF)
        phase = Exchange(place, 2 * step, buf, scratch)
        phase.start()
        for i in mlp_part:
            load(layer, i).wait()

        def perceptron(start, k, buf=buf):
            rows = rows_at(start, 2 * BLOCK, BLOCK)
            for n in range(0, gl.shape[1], BLOCK):
                width = slice(n, n + BLOCK)
                grad_act = dot(buf[rows, :], wd[width, :], 1, 1)
                gl[rows, width] = (grad_act * gl[rows, width].astype(F32)).astype(BF)
            part[k] = dot(gl[rows, :], wi[...], 1, 1).astype(BF)

        phase.run(perceptron)
        weight_grad(layer, 3, act, buf, BLOCK)
        grad_part, gain_grad = norm_back(
            mid[layer], gains[LAYERS + layer : LAYERS + layer + 1], phase.total()
        )
        gain_out[LAYERS + layer : LAYERS + layer + 1] = gain_grad
        grad = grad + grad_part

        buf = ag.at[1]
        buf[own, :] = grad.astype(BF)
        phase = Exchange(place, 2 * step + 1, buf, scratch)
        phase.start()
        weight_grad(layer, 2, nml, gl, 2 * BLOCK)
        if layer > 0:
            for i in mlp_part:
                load(layer - 1, i).start()
        for i in attn_part:
            load(layer, i).wait()

        def attend(start, k, buf=buf):
            cosine, sine = rope[:, :BLOCK], rope[:, BLOCK:]
            both = rows_at(start, 2 * BLOCK, BLOCK)
            grad_heads = dot(buf[both, :], wo[...], 1, 1).astype(BF)
            grad_heads = dot(grad_heads, sel_o[...]).astype(BF)
            for half in range(2):
                rows = rows_at(start + half * BLOCK, BLOCK, BLOCK)
                outs = [[], [], []]
                for h in range(heads):
                    def part_of(kind, h=h, rows=rows):
                        low = kind * lanes + h * BLOCK
                        return qkv[rows, low : low + BLOCK]

                    query, key, value = part_of(0), part_of(1), part_of(2)
                    probs = prb[rows, h * BLOCK : (h + 1) * BLOCK]
                    grad_head = grad_heads[
                        half * BLOCK : (half + 1) * BLOCK, h * BLOCK : (h + 1) * BLOCK
                    ]
                    outs[2].append(dot(probs, grad_head, 0, 0).astype(BF))
                    grad_probs = dot(grad_head, value, 1, 1)
                    probs = probs.astype(F32)
                    inner = jnp.sum(probs * grad_probs, axis=-1, keepdims=True)
                    grad_scores = (probs * (grad_probs - inner)).astype(BF)
                    for kind, turned in (
                        (0, dot(grad_scores, key)),
                        (1, dot(grad_scores, query, 0, 0)),
                    ):
                        turned = turned * (1.0 / math.sqrt(HDIM))
                        turned = turned * cosine - pltpu.roll(turned, BLOCK // 2, 1) * sine
                        outs[kind].append(turned.astype(BF))
                packed = jnp.concatenate(outs[0] + outs[1] + outs[2], axis=1)
                gp[rows, :] = dot(packed, sel_q[...], 1, 1).astype(BF)
            part[k] = dot(gp[both, :], wq[...], 1, 1).astype(BF)

        phase.run(attend)
        weight_grad(layer, 1, att, buf, 2 * BLOCK)
        weight_grad(layer, 0, nrm, gp, 2 * BLOCK)
        if layer > 0:
            for i in attn_part:
                load(layer - 1, i).start()
        grad_part, gain_grad = norm_back(xs[layer], gains[layer : layer + 1], phase.total())
        gain_out[layer : layer + 1] = gain_grad
        grad = grad + grad_part
    dx_out[...] = grad

    for layer in reversed(range(LAYERS)):
        for m in (3, 2, 1, 0):
            count = count_of(m)
            total = stages[m][layer, rows_at(z * count, count), :].astype(F32)
            for delta in range(1, levels):
                send(layer, m, delta).wait_recv()
                total = total + arrivals[m][layer, delta - 1].astype(F32)
            reduced[m][layer] = total.astype(reduced[m].dtype)
            for delta in range(1, levels):
                send(layer, m, delta).wait_send()


def shape(*dims, dtype=BF):
    return jax.ShapeDtypeStruct(dims, dtype)


def rope_table():
    position = np.arange(BLOCK) % ROW_LEN
    inverse = ROTARY_BASE ** (-np.arange(HALF) / HALF)
    angles = (position[:, None] * inverse[None, :]).astype(np.float32)
    table = np.zeros((BLOCK, 2, 2, BLOCK // 2), np.float32)
    table[:, 0, :, :HALF] = np.cos(angles)[:, None]
    table[:, 1, 0, :HALF] = -np.sin(angles)
    table[:, 1, 1, :HALF] = np.sin(angles)
    return table.reshape(BLOCK, 2 * BLOCK)


def lane_of(index):
    head, inside = divmod(index, HDIM)
    half, place = divmod(inside, HALF)
    return head * BLOCK + half * (BLOCK // 2) + place


def token_mask(starts, padded):
    within = jnp.arange(BLOCK)
    same_row = within[:, None] // ROW_LEN == within[None, :] // ROW_LEN
    causal = within[None, :] <= within[:, None]
    begun = (within % ROW_LEN)[None, None, :] >= starts[:, :, None]
    open_key = (padded[:, None, :] == 0) | (within[:, None] == within[None, :])[None]
    return ((same_row & causal)[None] & begun & open_key).astype(BF)


def per_device(devices, x, segments, padded, w_qkv, w_out, w_in, w_down, gain_attn, gain_mlp,
               head_first, head_first_bias, head_final, head_bias, head_skip, adjoint):
    levels = devices // PLANE
    width = x.shape[1]
    ff = w_in.shape[2]
    everywhere = ("wide", "narrow")
    groups = [[PLANE * z + r for r in range(PLANE)] for z in range(levels)]
    tokens = PLANE * BLOCK
    heads = width // HDIM // PLANE
    span = heads * HDIM
    rows = width // devices
    out_rows = up16(rows)
    ff_rows = ff // devices
    down_rows = up16(ff_rows)
    q_cols, o_rows, f_cols = 3 * span, levels * out_rows, levels * down_rows
    lanes = heads * BLOCK

    sel_q = np.zeros((q_cols, 3 * lanes), np.float32)
    sel_o = np.zeros((o_rows, lanes), np.float32)
    for e in range(span):
        for kind in range(3):
            sel_q[kind * span + e, kind * lanes + lane_of(e)] = 1
        sel_o[e // rows * out_rows + e % rows, lane_of(e)] = 1
    sel_q, sel_o = jnp.asarray(sel_q, BF), jnp.asarray(sel_o, BF)
    rope = jnp.asarray(rope_table())

    seg_rows = segments.reshape(-1, ROW_LEN)
    earlier = jnp.arange(ROW_LEN)[None, :] < jnp.arange(ROW_LEN)[:, None]
    starts = jnp.sum((seg_rows[:, None, :] != seg_rows[:, :, None]) & earlier[None], axis=-1)
    code = (starts.reshape(-1) + ROW_LEN * padded).astype(BF)
    small = jnp.concatenate([gain_attn.reshape(-1), gain_mlp.reshape(-1), code])
    small = lax.all_gather(small, everywhere, axis=0)
    gains = small[:, : 2 * LAYERS * rows].reshape(devices, 2 * LAYERS, rows)
    gains = jnp.swapaxes(gains, 0, 1).reshape(2 * LAYERS, width).astype(F32)
    z = lax.axis_index("wide") // 4
    code = lax.dynamic_slice_in_dim(small[:, 2 * LAYERS * rows :], z * PLANE, PLANE, 0)
    code = jnp.swapaxes(code.reshape(2, 2, 2, BLOCK), 1, 2).reshape(PLANE, BLOCK).astype(jnp.int32)
    mask = token_mask(code % ROW_LEN, code // ROW_LEN).reshape(tokens, BLOCK)

    q_part = w_qkv.reshape(LAYERS, rows, 3, PLANE, span).transpose(3, 0, 1, 2, 4)
    q_part = q_part.reshape(PLANE, LAYERS, rows, q_cols)
    i_part = w_in.reshape(LAYERS, rows, levels, PLANE, ff_rows).transpose(3, 0, 1, 2, 4)
    i_part = jnp.pad(i_part, [(0, 0)] * 4 + [(0, down_rows - ff_rows)])
    i_part = i_part.reshape(PLANE, LAYERS, rows, f_cols)
    both = jnp.concatenate([q_part, i_part], axis=-1)
    both = lax.all_to_all(both, everywhere, 0, 0, axis_index_groups=groups)
    both = jnp.swapaxes(both, 0, 1).reshape(LAYERS, PLANE * rows, q_cols + f_cols)
    q_piece, i_piece = both[..., :q_cols], both[..., q_cols:]
    trade = [(levels * t + zz, PLANE * zz + t) for t in range(PLANE) for zz in range(levels)]
    o_piece = lax.ppermute(w_out, everywhere, trade)
    o_piece = jnp.pad(o_piece, [(0, 0), (0, out_rows - rows), (0, 0)])
    d_piece = jnp.pad(w_down, [(0, 0), (0, down_rows - ff_rows), (0, 0)])

    pieces = (q_piece, o_piece, i_piece, d_piece)
    kept = [
        shape(LAYERS, tokens, width), shape(LAYERS, tokens, width), shape(LAYERS, tokens, 3 * lanes),
        shape(LAYERS, tokens, lanes), shape(LAYERS, tokens, o_rows), shape(LAYERS, tokens, f_cols),
        shape(LAYERS, tokens, f_cols), shape(LAYERS, BLOCK, width, dtype=F32),
        shape(LAYERS, BLOCK, width, dtype=F32),
    ]
    slab_shapes = [
        shape(LAYERS, width, q_cols), shape(LAYERS, o_rows, width), shape(LAYERS, width, f_cols),
        shape(LAYERS, f_cols, width),
    ]
    outs = [shape(BLOCK, width)] + kept + slab_shapes
    (final, nrm, nml, qkv, prb, att, dgl, act, xs, mid, wq, wo, wi, wd) = pl.pallas_call(
        lambda *refs: forward_kernel(levels, *refs),
        out_shape=outs,
        in_specs=[VMEM] * 6 + [ANY] * 4,
        out_specs=[VMEM] * len(outs),
        scratch_shapes=exchange_scratch(width) + [
            pltpu.VMEM((width, 3 * lanes), BF),
            pltpu.SemaphoreType.DMA((2, LAYERS, 4, levels - 1)),
            pltpu.SemaphoreType.DMA((LAYERS, 4)),
        ],
        compiler_params=pltpu.CompilerParams(
            collective_id=1, has_side_effects=True, vmem_limit_bytes=60 * MIB
        ),
        name="decoder_forward",
    )(x, mask, gains, rope, sel_q, sel_o, *pieces)

    lines = lax.all_gather(final, "narrow", axis=0, tiled=True)
    pre = jnp.dot(lines, head_first, preferred_element_type=F32) + head_first_bias.astype(F32)
    gate = jax.nn.sigmoid(pre)
    hidden = (pre * gate).astype(BF)
    predictions = (
        jnp.dot(hidden, head_final, preferred_element_type=F32)
        + head_bias.astype(F32)
        + jnp.dot(lines, head_skip, preferred_element_type=F32)
    ).astype(BF)
    grad_hidden = jnp.einsum("dx,ix->di", adjoint, head_final, preferred_element_type=F32)
    grad_pre = (grad_hidden * (gate * (1.0 + pre * (1.0 - gate)))).astype(BF)
    grad_rows = jnp.einsum("te,de->td", grad_pre, head_first, preferred_element_type=F32)
    grad_rows = grad_rows + jnp.einsum("dx,ix->di", adjoint, head_skip, preferred_element_type=F32)
    grad_final = lax.psum_scatter(
        grad_rows.astype(BF), "narrow", scatter_dimension=0, tiled=True
    ).astype(F32)
    g_first = jnp.einsum("td,te->de", lines, grad_pre, preferred_element_type=F32).astype(BF)
    g_out = jnp.einsum("sq,sm->qm", hidden, adjoint, preferred_element_type=F32).astype(BF)
    g_skip = jnp.einsum("sq,sm->qm", lines, adjoint, preferred_element_type=F32).astype(BF)
    g_first = lax.psum_scatter(g_first, everywhere, scatter_dimension=0, tiled=True).astype(F32)
    g_out = lax.psum_scatter(g_out, "wide", scatter_dimension=0, tiled=True).astype(F32)
    g_skip = lax.psum_scatter(g_skip, "wide", scatter_dimension=0, tiled=True).astype(F32)
    g_first_bias = jnp.sum(grad_pre.astype(F32), axis=0)
    g_bias = lax.psum(jnp.sum(adjoint.astype(F32), axis=0), "wide")

    chunk = [PLANE * rows, out_rows, PLANE * rows, down_rows]
    cols = [q_cols, width, f_cols, width]
    stage_rows = [levels * n for n in chunk]
    kept_shapes = [
        (tokens, width), (tokens, f_cols), (tokens, f_cols), (width, f_cols), (f_cols, width),
        (tokens, width), (tokens, 3 * lanes), (tokens, lanes), (tokens, o_rows), (width, q_cols),
        (o_rows, width),
    ]
    outs = [shape(BLOCK, width, dtype=F32), shape(2 * LAYERS, width, dtype=F32)]
    outs += [shape(LAYERS, chunk[m], cols[m], dtype=F32 if m == 3 else BF) for m in range(4)]
    (input_grad, gain_grads, q_grad, o_grad, i_grad, d_grad) = pl.pallas_call(
        lambda *refs: backward_kernel(levels, *refs),
        out_shape=outs,
        in_specs=[VMEM] * 7 + [ANY] * 11,
        out_specs=[VMEM] * len(outs),
        scratch_shapes=exchange_scratch(width)
        + [pltpu.VMEM((2, tokens, width), BF)]
        + [pltpu.VMEM(dims, BF) for dims in kept_shapes]
        + [pltpu.VMEM((tokens, q_cols), BF)]
        + [pltpu.VMEM((LAYERS, stage_rows[m], cols[m]), BF) for m in range(4)]
        + [pltpu.VMEM((LAYERS, levels - 1, chunk[m], cols[m]), BF) for m in range(4)]
        + [
            pltpu.SemaphoreType.DMA((2, LAYERS, 4, levels - 1)),
            pltpu.SemaphoreType.DMA((11,)),
        ],
        compiler_params=pltpu.CompilerParams(
            collective_id=2, has_side_effects=True, vmem_limit_bytes=60 * MIB
        ),
        name="decoder_backward",
    )(grad_final, gains, rope, sel_q, sel_o, xs, mid, nml, act, dgl, wi, wd, nrm, qkv, prb, att, wq, wo)

    both = jnp.concatenate([q_grad, i_grad], axis=-1)
    both = jnp.swapaxes(both.reshape(LAYERS, PLANE, rows, q_cols + f_cols), 0, 1)
    both = lax.all_to_all(both, everywhere, 0, 0, axis_index_groups=groups)
    q_grad = both[..., :q_cols].reshape(PLANE, LAYERS, rows, 3, span)
    q_grad = q_grad.transpose(1, 2, 3, 0, 4).reshape(LAYERS, rows, 3 * width).astype(F32)
    i_grad = both[..., q_cols:].reshape(PLANE, LAYERS, rows, levels, down_rows)[..., :ff_rows]
    i_grad = i_grad.transpose(1, 2, 3, 0, 4).reshape(LAYERS, rows, ff).astype(F32)
    o_grad = lax.ppermute(o_grad[:, :rows], everywhere, [(b, a) for a, b in trade]).astype(F32)
    d_grad = d_grad[:, :ff_rows]
    sums = jnp.concatenate([gain_grads, g_first_bias[None]])
    sums = lax.psum_scatter(sums, everywhere, scatter_dimension=1, tiled=True)
    return (
        predictions, input_grad, q_grad, o_grad, i_grad, d_grad, sums[:LAYERS],
        sums[LAYERS : 2 * LAYERS], g_first, sums[2 * LAYERS], g_out, g_bias, g_skip,
    )


def solution(mesh):
    devices = mesh.shape["wide"] * mesh.shape["narrow"]
    both = ("wide", "narrow")
    weight, gain = P(None, both, None), P(None, both)
    return jax.shard_map(
        lambda *arrays: per_device(devices, *arrays),
        mesh=mesh,
        in_specs=(
            P(both, None), P(both), P(both), weight, weight, weight, weight, gain, gain, P(), P(),
            P(None, "narrow"), P("narrow"), P(None, "narrow"), P("wide", "narrow"),
        ),
        out_specs=(
            P("wide", "narrow"), P(both, None), weight, weight, weight, weight, gain, gain,
            P(both, None), P(both), P("wide", "narrow"), P("narrow"), P("wide", "narrow"),
        ),
        check_vma=False,
    )
```

```python
import math

import jax
import jax.numpy as jnp
import numpy as np
from jax import lax
from jax.experimental import pallas as pl
from jax.experimental.pallas import tpu as pltpu
from jax.sharding import PartitionSpec as P

HDIM = 80
HALF = HDIM // 2
LAYERS = 2
ROW_LEN = 16
BLOCK = 128
PLANE = 8
PHASES = 2 * LAYERS
MESH = pl.DeviceIdType.MESH
BF = jnp.bfloat16
F32 = jnp.float32
EPS = 1e-06
ROTARY_BASE = 10000.0
MIB = 1024 * 1024
VMEM = pl.BlockSpec(memory_space=pltpu.VMEM)
ANY = pl.BlockSpec(memory_space=pl.ANY)


def up16(rows):
    return -(-rows // 16) * 16


def rows_at(start, count, step=16):
    return pl.ds(pl.multiple_of(start, step), count)


def dot(a, b, ca=1, cb=0):
    return lax.dot_general(a, b, (((ca,), (cb,)), ((), ())), preferred_element_type=F32)


class Place:
    def __init__(self):
        wide = lax.axis_index("wide")
        self.x = lax.axis_index("narrow")
        self.core = wide % 2
        self.y = (wide // 2) % 2
        self.z = wide // 4

    def device(self, z, y, core, x):
        return (z * 4 + y * 2 + core, x)

    def sibling(self):
        return self.device(self.z, self.y, 1 - self.core, self.x)

    def peer(self, k):
        return self.device(self.z, (self.y + k // 2) % 2, self.core, (self.x + k % 2) % 2)

    def pair(self, k):
        return 2 * ((self.y + k // 2) % 2) + (self.x + k % 2) % 2

    def level(self, z):
        return self.device(z, self.y, self.core, self.x)


def greet(place, levels):
    barrier = pltpu.get_barrier_semaphore()
    others = [place.sibling()] + [place.peer(k) for k in (1, 2, 3)]
    others += [place.level((place.z + d) % levels) for d in range(1, levels)]
    for other in others:
        pl.semaphore_signal(barrier, inc=1, device_id=other, device_id_type=MESH)
    pl.semaphore_wait(barrier, len(others))


def remote(src, dst, send, recv, device):
    return pltpu.make_async_remote_copy(
        src_ref=src, dst_ref=dst, send_sem=send, recv_sem=recv, device_id=device,
        device_id_type=MESH,
    )


class Exchange:
    def __init__(self, place, phase, buf, scratch):
        (self.part, self.recv_s, self.recv_c, self.send_c, self.sems) = scratch
        self.place, self.phase, self.buf = place, phase, buf

    def sem(self, kind, k):
        return self.sems.at[self.phase, kind, k]

    def rows(self, k, core):
        return rows_at(2 * BLOCK * self.place.pair(k) + BLOCK * core, BLOCK, BLOCK)

    def to_peer(self, k):
        own = self.buf.at[self.rows(0, self.place.core)]
        return remote(own, own, self.sem(0, k), self.sem(1, k), self.place.peer(k))

    def from_peer(self, k):
        there = self.buf.at[self.rows(k, self.place.core)]
        return remote(there, there, self.sem(0, k), self.sem(1, k), self.place.peer(k))

    def to_sibling(self, k):
        rows = self.buf.at[self.rows(k, self.place.core)]
        return remote(rows, rows, self.sem(2, k), self.sem(3, k), self.place.sibling())

    def from_sibling(self, k):
        rows = self.buf.at[self.rows(k, 1 - self.place.core)]
        return remote(rows, rows, self.sem(2, k), self.sem(3, k), self.place.sibling())

    def sum_sibling(self, k):
        src = self.part.at[k, rows_at(BLOCK * (1 - self.place.core), BLOCK, BLOCK)]
        return remote(src, self.recv_s.at[k], self.sem(4, k), self.sem(5, k), self.place.sibling())

    def sum_peer(self, k):
        return remote(
            self.send_c.at[k], self.recv_c.at[k], self.sem(6, k), self.sem(7, k), self.place.peer(k)
        )

    def chip_sum(self, k):
        own = self.part[k, rows_at(BLOCK * self.place.core, BLOCK, BLOCK), :]
        return own.astype(F32) + self.recv_s[k].astype(F32)

    def start(self):
        self.to_sibling(0).start()
        for k in (1, 2, 3):
            self.to_peer(k).start()

    def finish_chip(self, k):
        self.sum_sibling(k).wait_recv()
        self.send_c[k] = self.chip_sum(k).astype(BF)
        self.sum_peer(k).start()

    def run(self, compute):
        def body(k, carry):
            @pl.when(k > 0)
            def _():
                self.from_peer(k).wait_recv()
                self.to_sibling(k).start()

            self.from_sibling(k).wait_recv()
            compute(2 * BLOCK * self.place.pair(k), k)
            self.sum_sibling(k).start()

            @pl.when(k > 1)
            def _():
                self.finish_chip(k - 1)

            return carry

        lax.fori_loop(0, 4, body, 0)
        self.finish_chip(3)

    def total(self):
        self.sum_sibling(0).wait_recv()
        total = self.chip_sum(0)
        for k in (1, 2, 3):
            self.sum_peer(k).wait_recv()
            total = total + self.recv_c[k].astype(F32)
        for k in range(4):
            self.to_sibling(k).wait_send()
            self.sum_sibling(k).wait_send()
            if k:
                self.to_peer(k).wait_send()
                self.sum_peer(k).wait_send()
        return total


def exchange_scratch(width, phases):
    return [
        pltpu.VMEM((4, 2 * BLOCK, width), BF),
        pltpu.VMEM((4, BLOCK, width), BF),
        pltpu.VMEM((4, BLOCK, width), BF),
        pltpu.VMEM((4, BLOCK, width), BF),
        pltpu.SemaphoreType.DMA((phases, 8, 4)),
    ]


def root(values):
    return lax.rsqrt(jnp.mean(values * values, axis=-1, keepdims=True) + EPS)


def forward_kernel(levels, *refs):
    (x_in, mask, rope, sel_q, sel_o, head_lanes, adjoint, bias_first, bias_last) = refs[:9]
    pieces, head_weights = refs[9:13], refs[13:16]
    (predictions, grad_out, xs, mid) = refs[16:20]
    kept, (slab_q, slab_o, slab_i, slab_d) = refs[20:32], refs[32:36]
    exchange = refs[36:41]
    (nrm, nml, qkv, prb, att, gl, act) = refs[41:48]
    slabs = refs[48:52]
    (wide_q, first, final, pick, first_q, final_q, g, hidden, gpre, picked, hidden_all) = refs[52:63]
    (z_sems, own_sems, keep_sems, load_sems, g_sems) = refs[63:]
    slab_outs = (slab_q, slab_o, slab_i, slab_d)
    place = Place()
    z = place.z
    heads = sel_o.shape[1] // BLOCK
    lanes = heads * BLOCK
    kept_here, waited = [], []

    def keep(src, dst):
        copy = pltpu.make_async_copy(src, dst, keep_sems.at[len(kept_here)])
        copy.start()
        kept_here.append(copy)
        return copy

    def forget(copy):
        copy.wait()
        waited.append(copy)

    relayed = levels == 4

    def far(delta):
        there = (z + delta) % levels
        return (z + there == 3) & (z * there == 0)

    def rows_of(m, level):
        count = pieces[m].shape[1]
        return rows_at(level * count, count)

    def spread(layer, m, delta):
        return remote(
            pieces[m].at[layer], slabs[m].at[layer, rows_of(m, z)],
            z_sems.at[0, layer, m, delta - 1], z_sems.at[1, layer, m, delta - 1],
            place.level((z + delta) % levels),
        )

    def arriving(layer, m, delta):
        rows = slabs[m].at[layer, rows_of(m, (z + levels - delta) % levels)]
        return remote(
            rows, rows, z_sems.at[0, layer, m, delta - 1], z_sems.at[1, layer, m, delta - 1],
            place.level((z + delta) % levels),
        )

    def relay(layer, m):
        rows = slabs[m].at[layer, rows_of(m, (z + 2) % levels)]
        return remote(
            rows, rows, z_sems.at[2, layer, m, 0], z_sems.at[1, layer, m, 2 * (z - 1)],
            place.level(3 * (z - 1)),
        )

    def for_spread(layer, m, act_on):
        for delta in range(1, levels):
            if relayed and delta != 2:
                @pl.when(jnp.logical_not(far(delta)))
                def _(delta=delta):
                    act_on(spread(layer, m, delta))
            else:
                act_on(spread(layer, m, delta))

    def own_piece(layer, m):
        return pltpu.make_async_copy(
            pieces[m].at[layer], slabs[m].at[layer, rows_of(m, z)], own_sems.at[layer, m]
        )

    order = [(layer, m) for layer in range(LAYERS) for m in range(4)]

    def weights_here(index):
        layer, m = order[index]
        if relayed:
            middle = (z == 1) | (z == 2)
            arriving(layer, m, 2).wait_recv()

            @pl.when(middle)
            def _():
                relay(layer, m).start()

        if index + 3 < len(order):
            for_spread(*order[index + 3], lambda copy: copy.start())
        for delta in range(1, levels):
            if not (relayed and delta == 2):
                arriving(layer, m, delta).wait_recv()
        for_spread(layer, m, lambda copy: copy.wait_send())
        own_piece(layer, m).wait()
        if relayed:
            @pl.when(middle)
            def _():
                relay(layer, m).wait_send()

        return keep(slabs[m].at[layer], slab_outs[m].at[layer])

    for layer, m in order:
        own_piece(layer, m).start()
    skip = slabs[2].at[0, :, : adjoint.shape[2]]
    loads = [
        pltpu.make_async_copy(src, dst, load_sems.at[i])
        for i, (src, dst) in enumerate(zip(head_weights, (first, final, skip)))
    ]
    loads[0].start()
    loads[1].start()
    greet(place, levels)

    g_own = g.at[pl.ds(2 * place.y, 2), place.core]
    g_far = g.at[pl.ds(2 * (1 - place.y), 2), place.core]
    g_local = pltpu.make_async_copy(adjoint, g_own, g_sems.at[0, 0])
    g_peer = remote(adjoint, g_own, g_sems.at[0, 1], g_sems.at[1, 1], place.peer(2))
    g_sibling = remote(adjoint, g_own, g_sems.at[0, 2], g_sems.at[1, 2], place.sibling())
    g_pass = remote(g_far, g_far, g_sems.at[0, 3], g_sems.at[1, 3], place.sibling())
    for index in range(3):
        for_spread(*order[index], lambda copy: copy.start())

    own = rows_at(2 * BLOCK * place.pair(0) + BLOCK * place.core, BLOCK, BLOCK)
    xs[0] = x_in[...].astype(F32)
    pending = []
    slab_keeps = []
    for layer in range(LAYERS):
        wq, wo, wi, wd = [slab.at[layer] for slab in slabs]

        residual = xs[layer]
        nrm[layer, own, :] = (residual * root(residual)).astype(BF)
        phase = Exchange(place, 2 * layer, nrm.at[layer], exchange)
        phase.start()
        if layer == 0:
            for copy in (g_local, g_peer, g_sibling):
                copy.start()
        slab_keeps.append(weights_here(4 * layer))
        for n in range(0, wide_q.shape[1], 256):
            wide_q[:, n : n + 256] = dot(wq[...], sel_q[:, n : n + 256]).astype(BF)
        slab_keeps.append(weights_here(4 * layer + 1))
        for copy in pending[:3]:
            forget(copy)

        def attend(start, k, layer=layer, wo=wo):
            projected = dot(nrm[layer, rows_at(start, 2 * BLOCK, BLOCK), :], wide_q[...])
            cosine, sine = rope[:, :BLOCK], rope[:, BLOCK:]
            for half in range(2):
                rows = rows_at(start + half * BLOCK, BLOCK, BLOCK)
                allowed = mask[rows, :] > 0
                here = projected[half * BLOCK : (half + 1) * BLOCK]
                outs = []
                for h in range(heads):
                    def part_of(kind, h=h, here=here):
                        return here[:, kind * lanes + h * BLOCK : kind * lanes + (h + 1) * BLOCK]

                    turned = []
                    for kind in range(2):
                        value = part_of(kind)
                        value = value * cosine + pltpu.roll(value, BLOCK // 2, 1) * sine
                        turned.append(value.astype(BF))
                    query, key = turned
                    value = part_of(2).astype(BF)
                    qkv[rows, h * BLOCK : (h + 1) * BLOCK] = query
                    qkv[rows, lanes + h * BLOCK : lanes + (h + 1) * BLOCK] = key
                    qkv[rows, 2 * lanes + h * BLOCK : 2 * lanes + (h + 1) * BLOCK] = value
                    scores = dot(query, key, 1, 1) * (1.0 / math.sqrt(HDIM))
                    scores = jnp.where(allowed, scores, -1e30)
                    scores = jnp.exp(scores - jnp.max(scores, axis=-1, keepdims=True))
                    probs = (scores / jnp.sum(scores, axis=-1, keepdims=True)).astype(BF)
                    prb[rows, h * BLOCK : (h + 1) * BLOCK] = probs
                    outs.append(dot(probs, value).astype(BF))
                att[rows, :] = dot(jnp.concatenate(outs, axis=1), sel_o[...], 1, 1).astype(BF)
            both = att[rows_at(start, 2 * BLOCK, BLOCK), :]
            part[k] = dot(both, wo[...]).astype(BF)

        part = exchange[0]
        phase.run(attend)
        saved = [keep(src, dst.at[layer]) for src, dst in zip((qkv, prb, att), kept[2:5])]
        nrm_saved = keep(nrm.at[layer], kept[0].at[layer])
        middle = residual + phase.total()
        mid[layer] = middle

        nml[layer, own, :] = (middle * root(middle)).astype(BF)
        phase = Exchange(place, 2 * layer + 1, nml.at[layer], exchange)
        phase.start()
        if layer == 0:
            g_peer.wait_recv()
            g_pass.start()
        slab_keeps.append(weights_here(4 * layer + 2))
        slab_keeps.append(weights_here(4 * layer + 3))
        for copy in pending[3:]:
            forget(copy)

        def perceptron(start, k, layer=layer, wi=wi, wd=wd):
            rows = rows_at(start, 2 * BLOCK, BLOCK)
            for n in range(0, wi.shape[1], BLOCK):
                width = slice(n, n + BLOCK)
                lifted = dot(nml[layer, rows, :], wi[:, width])
                root_two = math.sqrt(2.0 / math.pi)
                square = lifted * lifted
                tanh = jnp.tanh(root_two * lifted * (1.0 + 0.044715 * square))
                act[rows, width] = (0.5 * lifted * (1.0 + tanh)).astype(BF)
                slope = 0.5 * (1.0 + tanh) + 0.5 * lifted * (1.0 - tanh * tanh) * root_two * (
                    1.0 + 3.0 * 0.044715 * square
                )
                gl[rows, width] = slope.astype(BF)
            part[k] = dot(act[rows, :], wd[...]).astype(BF)

        phase.run(perceptron)
        saved += [keep(src, dst.at[layer]) for src, dst in zip((gl, act), kept[5:7])]
        nml_saved = keep(nml.at[layer], kept[1].at[layer])
        pending = saved
        output = middle + phase.total()
        if layer == 0:
            xs[1] = output
            forget(nrm_saved)
            forget(slab_keeps[2])
            loads[2].start()
            loads[0].wait()
            loads[1].wait()
            index = lax.broadcasted_iota(jnp.int32, pick.shape, 0)
            offset = (2 * place.y + place.core) * (pick.shape[0] // (4 * levels))
            pick[...] = jnp.where(index - offset == head_lanes[...], 1.0, 0.0).astype(BF)
            for n in range(0, first.shape[0], 256):
                first_q[n : n + 256, :] = dot(first[n : n + 256, :], pick[...]).astype(BF)
            final_q[...] = dot(pick[...], final[...], 0, 0).astype(BF)

    lines = nrm.at[0]
    lines[own, :] = output.astype(BF)
    phase = Exchange(place, 2 * LAYERS, lines, exchange)
    phase.start()
    g_local.wait()
    for copy in (g_sibling, g_pass):
        copy.wait_recv()
    loads[2].wait()
    bias_q = dot(jnp.broadcast_to(bias_first[...], (16, bias_first.shape[1])), pick[...])[:1]

    def head(start, k):
        rows = rows_at(start, 2 * BLOCK, BLOCK)
        pre = dot(lines[rows, :], first_q[...]) + bias_q
        gate = 1.0 / (1.0 + jnp.exp(-pre))
        hidden[rows, :] = (pre * gate).astype(BF)
        there = g[place.pair(k)].reshape(2 * BLOCK, g.shape[3])
        grad_hidden = dot(there, final_q[...], 1, 1)
        gpre[rows, :] = (grad_hidden * (gate * (1.0 + pre * (1.0 - gate)))).astype(BF)
        part[k] = dot(gpre[rows, :], first_q[...], 1, 1).astype(BF)

        @pl.when(k < 2)
        def _():
            mine = rows_at(start + BLOCK * place.core, BLOCK, BLOCK)
            whole = dot(gpre[mine, :], first_q[...], 1, 1)
            whole = whole + dot(adjoint[(place.x + k) % 2], skip[...], 1, 1)
            part[k, rows_at(BLOCK * place.core, BLOCK, BLOCK), :] = whole.astype(BF)

    phase.run(head)
    grad_out[...] = phase.total()

    keep(lines, kept[7])
    keep(hidden, kept[8])
    keep(gpre, kept[9])
    for n in range(0, lines.shape[0], 2 * BLOCK):
        picked[n : n + 2 * BLOCK, :] = dot(lines[n : n + 2 * BLOCK, :], pick[...]).astype(BF)
    keep(picked, kept[10])
    keep(g, kept[11])
    for x in range(2):
        rows = rows_at(4 * BLOCK * place.y + 2 * BLOCK * x + BLOCK * place.core, BLOCK, BLOCK)
        for n in range(0, first.shape[1], 256):
            pre = dot(lines[rows, :], first[:, n : n + 256])
            pre = pre + bias_first[:, n : n + 256].astype(F32)
            hidden_all[:, n : n + 256] = (pre / (1.0 + jnp.exp(-pre))).astype(BF)
        out = dot(hidden_all[...], final[...]) + bias_last[...].astype(F32)
        out = out + dot(lines[rows, :], skip[...])
        predictions[x * BLOCK : (x + 1) * BLOCK, :] = out.astype(BF)
    for copy in (g_peer, g_sibling, g_pass):
        copy.wait_send()
    for copy in kept_here:
        if not any(copy is other for other in waited):
            copy.wait()


def norm_back(values, q):
    scale = root(values)
    n = values * scale
    return scale * (q - n * jnp.mean(q * n, axis=-1, keepdims=True))


def backward_kernel(levels, *refs):
    (dy_in, rope, sel_q, sel_o, xs, mid) = refs[:6]
    stored, head_stored = refs[6:17], refs[17:22]
    dx_out, small_out = refs[22:24]
    reduced, head_reduced = refs[24:28], refs[28:31]
    exchange, ag = refs[31:36], refs[36]
    loaded = refs[37:48]
    gp = refs[48]
    stages, arrivals = refs[49:56], refs[56:63]
    (small_own, small_x, small_z) = refs[63:66]
    z_sems, load_sems, small_sems = refs[66:]
    (nml, act, gl, wi, wd, nrm, qkv, prb, att, wq, wo) = loaded
    part = exchange[0]
    place = Place()
    z = place.z
    heads = sel_o.shape[1] // BLOCK
    lanes = heads * BLOCK

    def load(layer, i):
        return pltpu.make_async_copy(stored[i].at[layer], loaded[i], load_sems.at[i])

    lines = ag.at[1]
    h_cols, half_width = small_own.shape[2], nrm.shape[1] // 2
    gpre, hidden = gp.at[:, :h_cols], nrm.at[:, :h_cols]
    picked = nrm.at[:, half_width : half_width + h_cols]
    g = qkv.at[:, : stages[5].shape[1]]
    head_loads = [
        pltpu.make_async_copy(src, dst, load_sems.at[11 + i])
        for i, (src, dst) in enumerate(zip(head_stored, (lines, gpre, hidden, picked, g)))
    ]
    mlp_part, attn_part = range(5), range(5, 11)
    for copy in head_loads:
        copy.start()
    for i in mlp_part:
        load(LAYERS - 1, i).start()
    greet(place, levels)

    def count_of(m):
        return arrivals[m].shape[2]

    def slot(m, layer):
        return layer if m < 4 else 0

    def send(layer, m, delta):
        there = (z + delta) % levels
        return remote(
            stages[m].at[rows_at(there * count_of(m), count_of(m))],
            arrivals[m].at[slot(m, layer), delta - 1],
            z_sems.at[0, layer, m, delta - 1],
            z_sems.at[1, layer, m, delta - 1],
            place.level(there),
        )

    def result(layer, m):
        return reduced[m].at[layer] if m < 4 else head_reduced[m - 4]

    def weight_grad(layer, m, left, right, tile):
        width = left.shape[1]
        if m < 4 and layer + 1 < LAYERS:
            for delta in range(1, levels):
                send(layer + 1, m, delta).wait_send()
        if width % tile:
            stages[m][...] = dot(left[...], right[...], 0, 0).astype(BF)
        else:
            def body(i, carry):
                here = rows_at(i * tile, tile, tile)
                stages[m][here, :] = dot(left[:, here], right[...], 0, 0).astype(BF)
                return carry

            lax.fori_loop(0, width // tile, body, 0)
        for delta in range(1, levels):
            send(layer, m, delta).start()
        out = result(layer, m)
        out[...] = stages[m][rows_at(z * count_of(m), count_of(m)), :].astype(out.dtype)

    own = rows_at(2 * BLOCK * place.pair(0) + BLOCK * place.core, BLOCK, BLOCK)
    grad = dy_in[...]
    for step, layer in enumerate(reversed(range(LAYERS))):
        buf = ag.at[0]
        buf[own, :] = grad.astype(BF)
        phase = Exchange(place, 2 * step, buf, exchange)
        phase.start()
        if step == 0:
            for copy in head_loads:
                copy.wait()
            bias_sum = jnp.sum(gpre[...].astype(F32), axis=0, keepdims=True)
            small_own[1] = jnp.broadcast_to(bias_sum, small_own.shape[1:])
            to_x = remote(
                small_own.at[1], small_x, small_sems.at[0, 0], small_sems.at[1, 0], place.peer(1)
            )
            to_x.start()
            weight_grad(layer, 5, hidden, g, 2 * BLOCK)
            weight_grad(layer, 6, picked, g, 2 * BLOCK)
            weight_grad(layer, 4, lines, gpre, 2 * BLOCK)
            g_sum = jnp.sum(g[...].astype(F32), axis=0, keepdims=True)
            to_x.wait()
            small_z[0, :, : g_sum.shape[1]] = jnp.broadcast_to(g_sum, (8, g_sum.shape[1]))
            small_z[0, :, g_sum.shape[1] :] = small_own[1] + small_x[...]
            to_z = [
                remote(
                    small_z.at[0], small_z.at[d], small_sems.at[0, d], small_sems.at[1, d],
                    place.level((z + d) % levels),
                )
                for d in range(1, levels)
            ]
            for copy in to_z:
                copy.start()
            for i in attn_part:
                load(layer, i).start()
        for i in mlp_part:
            load(layer, i).wait()

        def perceptron(start, k, buf=buf):
            rows = rows_at(start, 2 * BLOCK, BLOCK)
            for n in range(0, gl.shape[1], BLOCK):
                width = slice(n, n + BLOCK)
                grad_act = dot(buf[rows, :], wd[width, :], 1, 1)
                gl[rows, width] = (grad_act * gl[rows, width].astype(F32)).astype(BF)
            part[k] = dot(gl[rows, :], wi[...], 1, 1).astype(BF)

        phase.run(perceptron)
        weight_grad(layer, 3, act, buf, BLOCK)
        grad = grad + norm_back(mid[layer], phase.total())

        buf = ag.at[1]
        buf[own, :] = grad.astype(BF)
        phase = Exchange(place, 2 * step + 1, buf, exchange)
        phase.start()
        weight_grad(layer, 2, nml, gl, 2 * BLOCK)
        if layer > 0:
            for i in mlp_part:
                load(layer - 1, i).start()
        for i in attn_part:
            load(layer, i).wait()

        def attend(start, k, buf=buf):
            cosine, sine = rope[:, :BLOCK], rope[:, BLOCK:]
            both = rows_at(start, 2 * BLOCK, BLOCK)
            grad_heads = dot(buf[both, :], wo[...], 1, 1).astype(BF)
            grad_heads = dot(grad_heads, sel_o[...]).astype(BF)
            for half in range(2):
                rows = rows_at(start + half * BLOCK, BLOCK, BLOCK)
                outs = [[], [], []]
                for h in range(heads):
                    def part_of(kind, h=h, rows=rows):
                        low = kind * lanes + h * BLOCK
                        return qkv[rows, low : low + BLOCK]

                    query, key, value = part_of(0), part_of(1), part_of(2)
                    probs = prb[rows, h * BLOCK : (h + 1) * BLOCK]
                    grad_head = grad_heads[
                        half * BLOCK : (half + 1) * BLOCK, h * BLOCK : (h + 1) * BLOCK
                    ]
                    outs[2].append(dot(probs, grad_head, 0, 0).astype(BF))
                    grad_probs = dot(grad_head, value, 1, 1)
                    probs = probs.astype(F32)
                    inner = jnp.sum(probs * grad_probs, axis=-1, keepdims=True)
                    grad_scores = (probs * (grad_probs - inner)).astype(BF)
                    for kind, turned in (
                        (0, dot(grad_scores, key)),
                        (1, dot(grad_scores, query, 0, 0)),
                    ):
                        turned = turned * (1.0 / math.sqrt(HDIM))
                        turned = turned * cosine - pltpu.roll(turned, BLOCK // 2, 1) * sine
                        outs[kind].append(turned.astype(BF))
                packed = jnp.concatenate(outs[0] + outs[1] + outs[2], axis=1)
                gp[rows, :] = dot(packed, sel_q[...], 1, 1).astype(BF)
            part[k] = dot(gp[both, :], wq[...], 1, 1).astype(BF)

        phase.run(attend)
        weight_grad(layer, 1, att, buf, 2 * BLOCK)
        weight_grad(layer, 0, nrm, gp, 2 * BLOCK)
        if layer > 0:
            for i in attn_part:
                load(layer - 1, i).start()
        grad = grad + norm_back(xs[layer], phase.total())
    dx_out[...] = grad

    total = small_z[0]
    for copy, d in zip(to_z, range(1, levels)):
        copy.wait_recv()
        total = total + small_z[d]
    small_out[...] = total
    for copy in to_z:
        copy.wait_send()
    last = LAYERS - 1
    pending = [(last, 5), (last, 6), (last, 4)]
    pending += [(layer, m) for layer in reversed(range(LAYERS)) for m in (3, 2, 1, 0)]
    for layer, m in pending:
        out = result(layer, m)
        total = out[...].astype(F32)
        for delta in range(1, levels):
            send(layer, m, delta).wait_recv()
            total = total + arrivals[m][slot(m, layer), delta - 1].astype(F32)
        out[...] = total.astype(out.dtype)
        if m > 3 or layer == 0:
            for delta in range(1, levels):
                send(layer, m, delta).wait_send()


def shape(*dims, dtype=BF):
    return jax.ShapeDtypeStruct(dims, dtype)


def rope_table():
    position = np.arange(BLOCK) % ROW_LEN
    inverse = ROTARY_BASE ** (-np.arange(HALF) / HALF)
    angles = (position[:, None] * inverse[None, :]).astype(np.float32)
    table = np.zeros((BLOCK, 2, 2, BLOCK // 2), np.float32)
    table[:, 0, :, :HALF] = np.cos(angles)[:, None]
    table[:, 1, 0, :HALF] = -np.sin(angles)
    table[:, 1, 1, :HALF] = np.sin(angles)
    return table.reshape(BLOCK, 2 * BLOCK)


def lane_of(index):
    head, inside = divmod(index, HDIM)
    half, place = divmod(inside, HALF)
    return head * BLOCK + half * (BLOCK // 2) + place


def token_mask(starts, padded):
    within = jnp.arange(BLOCK)
    same_row = within[:, None] // ROW_LEN == within[None, :] // ROW_LEN
    causal = within[None, :] <= within[:, None]
    begun = (within % ROW_LEN)[None, None, :] >= starts[:, :, None]
    open_key = (padded[:, None, :] == 0) | (within[:, None] == within[None, :])[None]
    return ((same_row & causal)[None] & begun & open_key).astype(BF)


def per_device(devices, x, segments, padded, w_qkv, w_out, w_in, w_down, gain_attn, gain_mlp,
               head_first, head_first_bias, head_final, head_bias, head_skip, adjoint):
    levels = devices // PLANE
    width = x.shape[1]
    ff = w_in.shape[2]
    columns = head_final.shape[1]
    everywhere = ("wide", "narrow")
    groups = [[PLANE * z + r for r in range(PLANE)] for z in range(levels)]
    tokens = PLANE * BLOCK
    heads = width // HDIM // PLANE
    span = heads * HDIM
    rows = width // devices
    out_rows = up16(rows)
    ff_rows = ff // devices
    down_rows = up16(ff_rows)
    head_share = 2 * width // devices
    head_rows = up16(head_share)
    used_cols, o_rows, f_cols = 3 * span, levels * out_rows, levels * down_rows
    h_cols = -(-levels * head_rows // 128) * 128
    code_cols = -(-BLOCK // rows)
    q_cols = -(-(used_cols + code_cols) // 128) * 128
    lanes = heads * BLOCK

    sel_q = np.zeros((q_cols, 3 * lanes), np.float32)
    sel_o = np.zeros((o_rows, lanes), np.float32)
    for e in range(span):
        for kind in range(3):
            sel_q[kind * span + e, kind * lanes + lane_of(e)] = 1
        sel_o[e // rows * out_rows + e % rows, lane_of(e)] = 1
    sel_q, sel_o = jnp.asarray(sel_q, BF), jnp.asarray(sel_o, BF)
    rope = jnp.asarray(rope_table())
    head_lanes = np.full((1, h_cols), -width, np.int32)
    for zz in range(levels):
        here = slice(zz * head_rows, zz * head_rows + head_share)
        head_lanes[0, here] = 4 * head_share * zz + np.arange(head_share)
    head_lanes = jnp.asarray(head_lanes)

    seg_rows = segments.reshape(-1, ROW_LEN)
    earlier = jnp.arange(ROW_LEN)[None, :] < jnp.arange(ROW_LEN)[:, None]
    starts = jnp.sum((seg_rows[:, None, :] != seg_rows[:, :, None]) & earlier[None], axis=-1)
    code = (starts.reshape(-1) + ROW_LEN * padded).astype(BF)
    code = jnp.pad(code, (0, code_cols * rows - BLOCK)).reshape(code_cols, rows).T
    code = jnp.pad(code, ((0, 0), (0, q_cols - used_cols - code_cols)))

    def times_gain(w, gain):
        return (w.astype(F32) * gain.astype(F32)[:, :, None]).astype(BF)

    q_part = times_gain(w_qkv, gain_attn).reshape(LAYERS, rows, 3, PLANE, span)
    q_part = q_part.transpose(3, 0, 1, 2, 4).reshape(PLANE, LAYERS, rows, used_cols)
    i_part = times_gain(w_in, gain_mlp).reshape(LAYERS, rows, levels, PLANE, ff_rows)
    i_part = i_part.transpose(3, 0, 1, 2, 4)
    i_part = jnp.pad(i_part, [(0, 0)] * 4 + [(0, down_rows - ff_rows)])
    i_part = i_part.reshape(PLANE, LAYERS, rows, f_cols)
    code = jnp.broadcast_to(code, (PLANE, LAYERS) + code.shape)
    both = jnp.concatenate([q_part, code, i_part], axis=-1)
    both = lax.all_to_all(both, everywhere, 0, 0, axis_index_groups=groups)
    code = both[:, 0, :, used_cols : used_cols + code_cols]
    code = jnp.swapaxes(code, 1, 2).reshape(PLANE, code_cols * rows)[:, :BLOCK]
    code = jnp.swapaxes(code.reshape(2, 2, 2, BLOCK), 1, 2).reshape(PLANE, BLOCK).astype(jnp.int32)
    mask = token_mask(code % ROW_LEN, code // ROW_LEN).reshape(tokens, BLOCK)
    both = jnp.swapaxes(both, 0, 1).reshape(LAYERS, PLANE * rows, q_cols + f_cols)
    q_piece, i_piece = both[..., :q_cols], both[..., q_cols:]
    trade = [(levels * t + zz, PLANE * zz + t) for t in range(PLANE) for zz in range(levels)]
    o_piece = lax.ppermute(w_out, everywhere, trade)
    o_piece = jnp.pad(o_piece, [(0, 0), (0, out_rows - rows), (0, 0)])
    d_piece = jnp.pad(w_down, [(0, 0), (0, down_rows - ff_rows), (0, 0)])

    pieces = (q_piece, o_piece, i_piece, d_piece)
    layer_shapes = [
        (tokens, width), (tokens, width), (tokens, 3 * lanes), (tokens, lanes), (tokens, o_rows),
        (tokens, f_cols), (tokens, f_cols),
    ]
    slab_shapes = [(width, q_cols), (o_rows, width), (width, f_cols), (f_cols, width)]
    blocks = (4, 2, BLOCK, columns)
    outs = [
        shape(2 * BLOCK, columns), shape(BLOCK, width, dtype=F32),
        shape(LAYERS, BLOCK, width, dtype=F32), shape(LAYERS, BLOCK, width, dtype=F32),
    ]
    vmem_outs = len(outs)
    outs += [shape(LAYERS, *dims) for dims in layer_shapes]
    outs += [shape(tokens, width)] + [shape(tokens, h_cols)] * 3 + [shape(*blocks)]
    outs += [shape(LAYERS, *dims) for dims in slab_shapes]
    (predictions, grad_final, xs, mid, nrm, nml, qkv, prb, att, gl, act, lines, hidden, gpre,
     picked, g, wq, wo, wi, wd) = pl.pallas_call(
        lambda *refs: forward_kernel(levels, *refs),
        out_shape=outs,
        in_specs=[VMEM] * 9 + [ANY] * 7,
        out_specs=[VMEM] * vmem_outs + [ANY] * (len(outs) - vmem_outs),
        scratch_shapes=exchange_scratch(width, PHASES + 1)
        + [pltpu.VMEM((LAYERS,) + dims, BF) for dims in layer_shapes[:2]]
        + [pltpu.VMEM(dims, BF) for dims in layer_shapes[2:]]
        + [pltpu.VMEM((LAYERS,) + dims, BF) for dims in slab_shapes]
        + [
            pltpu.VMEM((width, 3 * lanes), BF), pltpu.VMEM((width, width), BF),
            pltpu.VMEM((width, columns), BF), pltpu.VMEM((width, h_cols), BF),
            pltpu.VMEM((width, h_cols), BF), pltpu.VMEM((h_cols, columns), BF),
            pltpu.VMEM(blocks, BF), pltpu.VMEM((tokens, h_cols), BF),
            pltpu.VMEM((tokens, h_cols), BF), pltpu.VMEM((tokens, h_cols), BF),
            pltpu.VMEM((BLOCK, width), BF),
            pltpu.SemaphoreType.DMA((3, LAYERS, 4, levels - 1)),
            pltpu.SemaphoreType.DMA((LAYERS, 4)),
            pltpu.SemaphoreType.DMA((32,)),
            pltpu.SemaphoreType.DMA((3,)),
            pltpu.SemaphoreType.DMA((2, 4)),
        ],
        compiler_params=pltpu.CompilerParams(
            collective_id=1, has_side_effects=True, vmem_limit_bytes=60 * MIB
        ),
        name="decoder_forward",
    )(x, mask, rope, sel_q, sel_o, head_lanes, adjoint.reshape(2, BLOCK, columns),
      head_first_bias[None], head_bias[None], *pieces, head_first, head_final, head_skip)

    chunk = [PLANE * rows, out_rows, PLANE * rows, down_rows, PLANE * rows, head_rows, head_rows]
    cols = [q_cols, width, f_cols, width, h_cols, columns, columns]
    stage_rows = [levels * n for n in chunk[:5]] + [h_cols] * 2
    kept_shapes = [
        (tokens, width), (tokens, f_cols), (tokens, f_cols), (width, f_cols), (f_cols, width),
        (tokens, width), (tokens, 3 * lanes), (tokens, lanes), (tokens, o_rows), (width, q_cols),
        (o_rows, width),
    ]
    small_cols = columns + h_cols
    outs = [shape(BLOCK, width, dtype=F32), shape(8, small_cols, dtype=F32)]
    outs += [shape(LAYERS, chunk[m], cols[m], dtype=F32 if m == 3 else BF) for m in range(4)]
    outs += [shape(chunk[m], cols[m], dtype=F32 if m > 4 else BF) for m in range(4, 7)]
    (input_grad, small, q_grad, o_grad, i_grad, d_grad, g_first, g_out, g_skip) = pl.pallas_call(
        lambda *refs: backward_kernel(levels, *refs),
        out_shape=outs,
        in_specs=[VMEM] * 6 + [ANY] * 16,
        out_specs=[VMEM] * len(outs),
        scratch_shapes=exchange_scratch(width, PHASES)
        + [pltpu.VMEM((2, tokens, width), BF)]
        + [pltpu.VMEM(dims, BF) for dims in kept_shapes]
        + [pltpu.VMEM((tokens, q_cols), BF)]
        + [pltpu.VMEM((stage_rows[m], cols[m]), BF) for m in range(7)]
        + [
            pltpu.VMEM((LAYERS if m < 4 else 1, levels - 1, chunk[m], cols[m]), BF)
            for m in range(7)
        ]
        + [
            pltpu.VMEM((2, 8, h_cols), F32), pltpu.VMEM((8, h_cols), F32),
            pltpu.VMEM((levels, 8, small_cols), F32),
            pltpu.SemaphoreType.DMA((2, LAYERS, 7, levels - 1)),
            pltpu.SemaphoreType.DMA((16,)),
            pltpu.SemaphoreType.DMA((2, levels)),
        ],
        compiler_params=pltpu.CompilerParams(
            collective_id=2, has_side_effects=True, vmem_limit_bytes=60 * MIB
        ),
        name="decoder_backward",
    )(grad_final, rope, sel_q, sel_o, xs, mid, nml, act, gl, wi, wd, nrm, qkv, prb, att, wq, wo,
      lines, gpre, hidden, picked, g.reshape(tokens, columns))

    both = jnp.concatenate([q_grad[..., :used_cols], i_grad], axis=-1)
    both = both.reshape(LAYERS, PLANE, rows, used_cols + f_cols)
    both = jnp.swapaxes(both, 0, 1).reshape(PLANE, -1)
    both = jnp.concatenate([both, g_first.reshape(PLANE, -1)], axis=-1)
    both = lax.all_to_all(both, everywhere, 0, 0, axis_index_groups=groups)
    split = LAYERS * rows * (used_cols + f_cols)
    g_first = both[:, split:].reshape(4, 2, rows, h_cols)[..., : levels * head_rows]
    g_first = g_first.reshape(4, 2, rows, levels, head_rows)[..., :head_share]
    g_first = jnp.sum(g_first.astype(F32), axis=1).transpose(1, 2, 0, 3).reshape(rows, width)
    both = both[:, :split].reshape(PLANE, LAYERS, rows, used_cols + f_cols)
    q_grad = both[..., :used_cols].reshape(PLANE, LAYERS, rows, 3, span)
    q_grad = q_grad.transpose(1, 2, 3, 0, 4).reshape(LAYERS, rows, 3 * width).astype(F32)
    i_grad = both[..., used_cols:].reshape(PLANE, LAYERS, rows, levels, down_rows)[..., :ff_rows]
    i_grad = i_grad.transpose(1, 2, 3, 0, 4).reshape(LAYERS, rows, ff).astype(F32)
    attn_gain_grad = jnp.sum(q_grad * w_qkv.astype(F32), axis=-1)
    mlp_gain_grad = jnp.sum(i_grad * w_in.astype(F32), axis=-1)
    q_grad = q_grad * gain_attn.astype(F32)[:, :, None]
    i_grad = i_grad * gain_mlp.astype(F32)[:, :, None]
    o_grad = lax.ppermute(o_grad[:, :rows], everywhere, [(b, a) for a, b in trade]).astype(F32)
    d_grad = d_grad[:, :ff_rows]
    z, narrow = lax.axis_index("wide") // 4, lax.axis_index("narrow")
    g_first_bias = lax.dynamic_slice(small[0], (columns + z * head_rows + narrow * rows,), (rows,))
    return (
        predictions, input_grad, q_grad, o_grad, i_grad, d_grad, attn_gain_grad, mlp_gain_grad,
        g_first, g_first_bias, g_out[:head_share], small[0, :columns], g_skip[:head_share],
    )


def solution(mesh):
    devices = mesh.shape["wide"] * mesh.shape["narrow"]
    both = ("wide", "narrow")
    weight, gain = P(None, both, None), P(None, both)
    return jax.shard_map(
        lambda *arrays: per_device(devices, *arrays),
        mesh=mesh,
        in_specs=(
            P(both, None), P(both), P(both), weight, weight, weight, weight, gain, gain, P(), P(),
            P(None, "narrow"), P("narrow"), P(None, "narrow"), P("wide", "narrow"),
        ),
        out_specs=(
            P("wide", "narrow"), P(both, None), weight, weight, weight, weight, gain, gain,
            P(both, None), P(both), P("wide", "narrow"), P("narrow"), P("wide", "narrow"),
        ),
        check_vma=False,
    )
```

```python
import math

import jax
import jax.numpy as jnp
import numpy as np
from jax import lax
from jax.experimental import pallas as pl
from jax.experimental.pallas import tpu as pltpu
from jax.sharding import PartitionSpec as P

HDIM = 80
HALF = HDIM // 2
LAYERS = 2
ROW_LEN = 16
BLOCK = 128
HALF_BLOCK = BLOCK // 2
PLANE = 8
PHASES = 2 * LAYERS
WINDOW = 4
MESH = pl.DeviceIdType.MESH
BF = jnp.bfloat16
F32 = jnp.float32
EPS = 1e-06
ROTARY_BASE = 10000.0
MIB = 1024 * 1024
VMEM = pl.BlockSpec(memory_space=pltpu.VMEM)
ANY = pl.BlockSpec(memory_space=pl.ANY)


def up16(rows):
    return -(-rows // 16) * 16


def rows_at(start, count, step=16):
    return pl.ds(pl.multiple_of(start, step), count)


def dot(a, b, ca=1, cb=0):
    return lax.dot_general(a, b, (((ca,), (cb,)), ((), ())), preferred_element_type=F32)


class Place:
    def __init__(self):
        wide = lax.axis_index("wide")
        self.x = lax.axis_index("narrow")
        self.core = wide % 2
        self.y = (wide // 2) % 2
        self.z = wide // 4

    def device(self, z, y, core, x):
        return (z * 4 + y * 2 + core, x)

    def sibling(self):
        return self.device(self.z, self.y, 1 - self.core, self.x)

    def peer(self, k):
        return self.device(self.z, (self.y + k // 2) % 2, self.core, (self.x + k % 2) % 2)

    def pair(self, k):
        return 2 * ((self.y + k // 2) % 2) + (self.x + k % 2) % 2

    def level(self, z):
        return self.device(z, self.y, self.core, self.x)


def greet(place, levels):
    barrier = pltpu.get_barrier_semaphore()
    others = [place.sibling()] + [place.peer(k) for k in (1, 2, 3)]
    others += [place.level((place.z + d) % levels) for d in range(1, levels)]
    for other in others:
        pl.semaphore_signal(barrier, inc=1, device_id=other, device_id_type=MESH)
    pl.semaphore_wait(barrier, len(others))


def remote(src, dst, send, recv, device):
    return pltpu.make_async_remote_copy(
        src_ref=src, dst_ref=dst, send_sem=send, recv_sem=recv, device_id=device,
        device_id_type=MESH,
    )


class Exchange:
    def __init__(self, place, phase, buf, scratch):
        (self.part, self.recv_s, self.recv_c, self.send_c, self.sems) = scratch
        self.place, self.phase, self.buf = place, phase, buf

    def sem(self, s, kind, k):
        return self.sems.at[self.phase, s, kind, k]

    def rows(self, s, k, core):
        start = s * 8 * HALF_BLOCK + self.place.pair(k) * 2 * HALF_BLOCK + core * HALF_BLOCK
        return rows_at(start, HALF_BLOCK, HALF_BLOCK)

    def own(self, s):
        return self.rows(s, 0, self.place.core)

    def to_peer(self, s, k):
        own = self.buf.at[self.own(s)]
        return remote(own, own, self.sem(s, 0, k), self.sem(s, 1, k), self.place.peer(k))

    def from_peer(self, s, k):
        there = self.buf.at[self.rows(s, k, self.place.core)]
        return remote(there, there, self.sem(s, 0, k), self.sem(s, 1, k), self.place.peer(k))

    def to_sibling(self, s, k):
        rows = self.buf.at[self.rows(s, k, self.place.core)]
        return remote(rows, rows, self.sem(s, 2, k), self.sem(s, 3, k), self.place.sibling())

    def from_sibling(self, s, k):
        rows = self.buf.at[self.rows(s, k, 1 - self.place.core)]
        return remote(rows, rows, self.sem(s, 2, k), self.sem(s, 3, k), self.place.sibling())

    def part_rows(self, k, core):
        start = ((self.place.x + k) % 2) * 2 * HALF_BLOCK + core * HALF_BLOCK
        return rows_at(start, HALF_BLOCK, HALF_BLOCK)

    def sum_sibling(self, s, k):
        src = self.part.at[s, k // 2, self.part_rows(k, 1 - self.place.core)]
        return remote(
            src, self.recv_s.at[s, k], self.sem(s, 4, k), self.sem(s, 5, k), self.place.sibling()
        )

    def sum_peer(self, s, k):
        return remote(
            self.send_c.at[s, k - 1], self.recv_c.at[s, k - 1], self.sem(s, 6, k),
            self.sem(s, 7, k), self.place.peer(k),
        )

    def chip_sum(self, s, k):
        own = self.part[s, k // 2, self.part_rows(k, self.place.core), :]
        return own.astype(F32) + self.recv_s[s, k].astype(F32)

    def start(self, s):
        self.to_sibling(s, 0).start()
        for k in (1, 2, 3):
            self.to_peer(s, k).start()

    def finish_chip(self, s, k):
        self.sum_sibling(s, k).wait_recv()
        self.send_c[s, k - 1] = self.chip_sum(s, k).astype(BF)
        self.sum_peer(s, k).start()

    def run(self, compute, hooks):
        def body(i, carry):
            s, half = i // 2, i % 2
            for at, hook in hooks:
                pl.when(i == at)(hook)

            @pl.when(half == 0)
            def _():
                self.from_peer(s, 1).wait_recv()
                self.to_sibling(s, 1).start()

            @pl.when(half == 1)
            def _():
                for k in (2, 3):
                    self.from_peer(s, k).wait_recv()
                    self.to_sibling(s, k).start()

            @pl.when(i == 2)
            def _():
                self.finish_stream(0)

            self.from_sibling(s, 2 * half).wait_recv()
            self.from_sibling(s, 2 * half + 1).wait_recv()
            start = s * 8 * HALF_BLOCK + (self.place.y + half) % 2 * 4 * HALF_BLOCK
            compute(start, s, half)
            self.sum_sibling(s, 2 * half).start()
            self.sum_sibling(s, 2 * half + 1).start()

            @pl.when(half == 1)
            def _():
                self.finish_chip(s, 1)

            return carry

        lax.fori_loop(0, 4, body, 0)

    def finish_stream(self, s):
        for k in (2, 3):
            self.finish_chip(s, k)

    def total(self, s):
        self.sum_sibling(s, 0).wait_recv()
        total = self.chip_sum(s, 0)
        for k in (1, 2, 3):
            self.sum_peer(s, k).wait_recv()
            total = total + self.recv_c[s, k - 1].astype(F32)
        for k in range(4):
            self.to_sibling(s, k).wait_send()
            self.sum_sibling(s, k).wait_send()
            if k:
                self.to_peer(s, k).wait_send()
                self.sum_peer(s, k).wait_send()
        return total


def exchange_scratch(width, phases):
    return [
        pltpu.VMEM((2, 2, 4 * HALF_BLOCK, width), BF),
        pltpu.VMEM((2, 4, HALF_BLOCK, width), BF),
        pltpu.VMEM((2, 3, HALF_BLOCK, width), BF),
        pltpu.VMEM((2, 3, HALF_BLOCK, width), BF),
        pltpu.SemaphoreType.DMA((phases, 2, 8, 4)),
    ]


def root(values):
    return lax.rsqrt(jnp.mean(values * values, axis=-1, keepdims=True) + EPS)


def forward_kernel(levels, *refs):
    (x_in, mask, rope, sel_q, sel_o, head_lanes, adjoint, bias_first, bias_last) = refs[:9]
    pieces, head_weights = refs[9:13], refs[13:16]
    (predictions, grad_out, xs, mid) = refs[16:20]
    kept, (slab_q, slab_o, slab_i, slab_d) = refs[20:32], refs[32:36]
    exchange = refs[36:41]
    (nrm, nml, qkv, prb, att, gl, act) = refs[41:48]
    slabs = refs[48:52]
    (wide_q, first, final, pick, first_q, final_q, g, hidden, gpre, picked, hidden_all) = refs[52:63]
    (z_sems, own_sems, keep_sems, load_sems, g_sems) = refs[63:]
    slab_outs = (slab_q, slab_o, slab_i, slab_d)
    place = Place()
    z = place.z
    heads = sel_o.shape[1] // BLOCK
    lanes = heads * BLOCK
    kept_here, waited = [], []

    def keep(src, dst):
        copy = pltpu.make_async_copy(src, dst, keep_sems.at[len(kept_here)])
        copy.start()
        kept_here.append(copy)
        return copy

    def forget(copy):
        copy.wait()
        waited.append(copy)

    relayed = levels == 4

    def far(delta):
        there = (z + delta) % levels
        return (z + there == 3) & (z * there == 0)

    def rows_of(m, level):
        count = pieces[m].shape[1]
        return rows_at(level * count, count)

    def spread(layer, m, delta):
        return remote(
            pieces[m].at[layer], slabs[m].at[layer, rows_of(m, z)],
            z_sems.at[0, layer, m, delta - 1], z_sems.at[1, layer, m, delta - 1],
            place.level((z + delta) % levels),
        )

    def arriving(layer, m, delta):
        rows = slabs[m].at[layer, rows_of(m, (z + levels - delta) % levels)]
        return remote(
            rows, rows, z_sems.at[0, layer, m, delta - 1], z_sems.at[1, layer, m, delta - 1],
            place.level((z + delta) % levels),
        )

    def relay(layer, m):
        rows = slabs[m].at[layer, rows_of(m, (z + 2) % levels)]
        return remote(
            rows, rows, z_sems.at[2, layer, m, 0], z_sems.at[1, layer, m, 2 * (z - 1)],
            place.level(3 * (z - 1)),
        )

    def for_spread(layer, m, act_on):
        for delta in range(1, levels):
            if relayed and delta != 2:
                @pl.when(jnp.logical_not(far(delta)))
                def _(delta=delta):
                    act_on(spread(layer, m, delta))
            else:
                act_on(spread(layer, m, delta))

    def own_piece(layer, m):
        return pltpu.make_async_copy(
            pieces[m].at[layer], slabs[m].at[layer, rows_of(m, z)], own_sems.at[layer, m]
        )

    order = [(layer, m) for layer in range(LAYERS) for m in range(4)]

    middle = (z == 1) | (z == 2)

    def relay_on(index):
        if relayed and index < len(order):
            @pl.when(middle)
            def _():
                arriving(*order[index], 2).wait_recv()
                relay(*order[index]).start()

    def weights_here(index):
        layer, m = order[index]
        if index + WINDOW < len(order):
            for_spread(*order[index + WINDOW], lambda copy: copy.start())
        for delta in range(1, levels):
            if relayed and delta == 2:
                pl.when(jnp.logical_not(middle))(arriving(layer, m, delta).wait_recv)
            else:
                arriving(layer, m, delta).wait_recv()
        for_spread(layer, m, lambda copy: copy.wait_send())
        own_piece(layer, m).wait()
        if relayed:
            pl.when(middle)(relay(layer, m).wait_send)

        return keep(slabs[m].at[layer], slab_outs[m].at[layer])

    for layer, m in order:
        own_piece(layer, m).start()
    skip = slabs[2].at[0, :, : adjoint.shape[3]]
    loads = [
        pltpu.make_async_copy(src, dst, load_sems.at[i])
        for i, (src, dst) in enumerate(zip(head_weights, (first, final, skip)))
    ]
    loads[0].start()
    loads[1].start()
    greet(place, levels)

    g_own = g.at[:, pl.ds(2 * place.y, 2), place.core]
    g_far = g.at[:, pl.ds(2 * (1 - place.y), 2), place.core]
    g_local = pltpu.make_async_copy(adjoint, g_own, g_sems.at[0, 0])
    g_peer = remote(adjoint, g_own, g_sems.at[0, 1], g_sems.at[1, 1], place.peer(2))
    g_sibling = remote(adjoint, g_own, g_sems.at[0, 2], g_sems.at[1, 2], place.sibling())
    g_pass = remote(g_far, g_far, g_sems.at[0, 3], g_sems.at[1, 3], place.sibling())
    for index in range(WINDOW):
        for_spread(*order[index], lambda copy: copy.start())

    part = exchange[0]
    lines = nrm.at[0]
    bufs = [nrm.at[0], nml.at[0], nrm.at[1], nml.at[1], lines]
    phases = [Exchange(place, p, buf, exchange) for p, buf in enumerate(bufs)]

    def own_half(s):
        return slice(s * HALF_BLOCK, (s + 1) * HALF_BLOCK)

    def enter(p, s, values):
        if p < 2 * LAYERS:
            values = values * root(values)
        bufs[p][phases[p].own(s), :] = values.astype(BF)
        phases[p].start(s)

    def leave(p, s):
        rows = own_half(s)
        total = phases[p].total(s)
        if p == 2 * LAYERS:
            grad_out[rows, :] = total
            return
        layer = p // 2
        if p % 2 == 0:
            values = xs[layer, rows, :] + total
            mid[layer, rows, :] = values
        else:
            values = mid[layer, rows, :] + total
            if layer + 1 < LAYERS:
                xs[layer + 1, rows, :] = values
        enter(p + 1, s, values)

    def run(p, compute, next_weights):
        hooks = [(3, lambda: leave(p, 0))]
        if p:
            hooks += [
                (0, lambda: phases[p - 1].finish_stream(1)),
                (1, lambda: leave(p - 1, 1)),
            ]
        hooks += [(2, lambda index=index: relay_on(index)) for index in next_weights]
        phases[p].run(compute, hooks)

    xs[0] = x_in[...].astype(F32)
    for s in range(2):
        enter(0, s, xs[0, own_half(s), :])
    for copy in (g_local, g_peer, g_sibling):
        copy.start()
    relay_on(0)
    relay_on(1)
    slab_keeps = []
    for layer in range(LAYERS):
        wq, wo, wi, wd = [slab.at[layer] for slab in slabs]
        slab_keeps.append(weights_here(4 * layer))
        for n in range(0, wide_q.shape[1], 256):
            wide_q[:, n : n + 256] = dot(wq[...], sel_q[:, n : n + 256]).astype(BF)
        slab_keeps.append(weights_here(4 * layer + 1))
        if layer:
            for copy in attn_saved:
                forget(copy)

        def attend(start, s, half, layer=layer, wo=wo):
            both = rows_at(start, 2 * BLOCK, 2 * BLOCK)
            projected = dot(nrm[layer, both, :], wide_q[...])
            cosine, sine = rope[:, :BLOCK], rope[:, BLOCK:]
            for block in range(2):
                rows = rows_at(start + block * BLOCK, BLOCK, BLOCK)
                allowed = mask[rows, :] > 0
                here = projected[block * BLOCK : (block + 1) * BLOCK]
                outs = []
                for h in range(heads):
                    def part_of(kind, h=h, here=here):
                        return here[:, kind * lanes + h * BLOCK : kind * lanes + (h + 1) * BLOCK]

                    turned = []
                    for kind in range(2):
                        value = part_of(kind)
                        value = value * cosine + pltpu.roll(value, BLOCK // 2, 1) * sine
                        turned.append(value.astype(BF))
                    query, key = turned
                    value = part_of(2).astype(BF)
                    qkv[rows, h * BLOCK : (h + 1) * BLOCK] = query
                    qkv[rows, lanes + h * BLOCK : lanes + (h + 1) * BLOCK] = key
                    qkv[rows, 2 * lanes + h * BLOCK : 2 * lanes + (h + 1) * BLOCK] = value
                    scores = dot(query, key, 1, 1) * (1.0 / math.sqrt(HDIM))
                    scores = jnp.where(allowed, scores, -1e30)
                    scores = jnp.exp(scores - jnp.max(scores, axis=-1, keepdims=True))
                    probs = (scores / jnp.sum(scores, axis=-1, keepdims=True)).astype(BF)
                    prb[rows, h * BLOCK : (h + 1) * BLOCK] = probs
                    outs.append(dot(probs, value).astype(BF))
                att[rows, :] = dot(jnp.concatenate(outs, axis=1), sel_o[...], 1, 1).astype(BF)
            part[s, half] = dot(att[both, :], wo[...]).astype(BF)

        run(2 * layer, attend, (4 * layer + 2, 4 * layer + 3))
        attn_saved = [keep(src, dst.at[layer]) for src, dst in zip((qkv, prb, att), kept[2:5])]
        nrm_saved = keep(nrm.at[layer], kept[0].at[layer])
        if layer == 0:
            g_peer.wait_recv()
            g_pass.start()
        slab_keeps.append(weights_here(4 * layer + 2))
        slab_keeps.append(weights_here(4 * layer + 3))
        if layer:
            for copy in mlp_saved:
                forget(copy)

        def perceptron(start, s, half, layer=layer, wi=wi, wd=wd):
            rows = rows_at(start, 2 * BLOCK, 2 * BLOCK)
            for n in range(0, wi.shape[1], 2 * BLOCK):
                width = slice(n, min(n + 2 * BLOCK, wi.shape[1]))
                lifted = dot(nml[layer, rows, :], wi[:, width])
                root_two = math.sqrt(2.0 / math.pi)
                square = lifted * lifted
                tanh = jnp.tanh(root_two * lifted * (1.0 + 0.044715 * square))
                act[rows, width] = (0.5 * lifted * (1.0 + tanh)).astype(BF)
                slope = 0.5 * (1.0 + tanh) + 0.5 * lifted * (1.0 - tanh * tanh) * root_two * (
                    1.0 + 3.0 * 0.044715 * square
                )
                gl[rows, width] = slope.astype(BF)
            part[s, half] = dot(act[rows, :], wd[...]).astype(BF)

        run(2 * layer + 1, perceptron, (4 * layer + 4, 4 * layer + 5))
        mlp_saved = [keep(src, dst.at[layer]) for src, dst in zip((gl, act), kept[5:7])]
        keep(nml.at[layer], kept[1].at[layer])
        if layer == 0:
            forget(nrm_saved)
            forget(slab_keeps[2])
            loads[2].start()
            loads[0].wait()
            loads[1].wait()
            index = lax.broadcasted_iota(jnp.int32, pick.shape, 0)
            offset = (2 * place.y + place.core) * (pick.shape[0] // (4 * levels))
            pick[...] = jnp.where(index - offset == head_lanes[...], 1.0, 0.0).astype(BF)
            for n in range(0, first.shape[0], 256):
                first_q[n : n + 256, :] = dot(first[n : n + 256, :], pick[...]).astype(BF)
            final_q[...] = dot(pick[...], final[...], 0, 0).astype(BF)

    g_local.wait()
    for copy in (g_sibling, g_pass):
        copy.wait_recv()
    loads[2].wait()
    bias_q = dot(jnp.broadcast_to(bias_first[...], (16, bias_first.shape[1])), pick[...])[:1]
    columns = g.shape[4]

    def head(start, s, half):
        rows = rows_at(start, 2 * BLOCK, 2 * BLOCK)
        pre = dot(lines[rows, :], first_q[...]) + bias_q
        gate = 1.0 / (1.0 + jnp.exp(-pre))
        hidden[rows, :] = (pre * gate).astype(BF)
        chips = pl.ds((place.y + half) % 2 * 2, 2)
        there = g[s, chips].reshape(2 * BLOCK, columns)
        grad_hidden = dot(there, final_q[...], 1, 1)
        gpre[rows, :] = (grad_hidden * (gate * (1.0 + pre * (1.0 - gate)))).astype(BF)
        whole = dot(gpre[rows, :], first_q[...], 1, 1)
        part[s, half] = whole.astype(BF)

        @pl.when(half == 0)
        def _():
            core = lax.broadcasted_iota(jnp.int32, (2 * BLOCK, 1), 0) // HALF_BLOCK % 2
            mine = jnp.where(core == place.core, there.astype(F32), 0.0).astype(BF)
            part[s, half] = (whole + dot(mine, skip[...], 1, 1)).astype(BF)

    run(2 * LAYERS, head, ())
    phases[2 * LAYERS].finish_stream(1)

    keep(lines, kept[7])
    keep(hidden, kept[8])
    keep(gpre, kept[9])
    for n in range(0, lines.shape[0], 2 * BLOCK):
        picked[n : n + 2 * BLOCK, :] = dot(lines[n : n + 2 * BLOCK, :], pick[...]).astype(BF)
    keep(picked, kept[10])
    keep(g, kept[11])
    leave(2 * LAYERS, 1)
    mine = []
    for x in range(2):
        for s in range(2):
            start = (8 * s + 4 * place.y + 2 * x + place.core) * HALF_BLOCK
            mine.append(lines[rows_at(start, HALF_BLOCK, HALF_BLOCK), :])
    mine = jnp.concatenate(mine, axis=0)
    for n in range(0, first.shape[1], 256):
        pre = dot(mine, first[:, n : n + 256])
        pre = pre + bias_first[:, n : n + 256].astype(F32)
        hidden_all[:, n : n + 256] = (pre / (1.0 + jnp.exp(-pre))).astype(BF)
    out = dot(hidden_all[...], final[...]) + bias_last[...].astype(F32)
    predictions[...] = (out + dot(mine, skip[...])).astype(BF)
    for copy in (g_peer, g_sibling, g_pass):
        copy.wait_send()
    for copy in kept_here:
        if not any(copy is other for other in waited):
            copy.wait()


def norm_back(values, q):
    scale = root(values)
    n = values * scale
    return scale * (q - n * jnp.mean(q * n, axis=-1, keepdims=True))


def backward_kernel(levels, *refs):
    (dy_in, rope, sel_q, sel_o, xs, mid) = refs[:6]
    stored, head_stored = refs[6:17], refs[17:22]
    dx_out, small_out = refs[22:24]
    reduced, head_reduced = refs[24:28], refs[28:31]
    exchange, ag = refs[31:36], refs[36]
    loaded = refs[37:48]
    gp = refs[48]
    stages, arrivals = refs[49:56], refs[56:63]
    (small_own, small_x, small_z) = refs[63:66]
    z_sems, load_sems, small_sems = refs[66:]
    (nml, act, gl, wi, wd, nrm, qkv, prb, att, wq, wo) = loaded
    part = exchange[0]
    place = Place()
    z = place.z
    heads = sel_o.shape[1] // BLOCK
    lanes = heads * BLOCK

    def load(layer, i):
        return pltpu.make_async_copy(stored[i].at[layer], loaded[i], load_sems.at[i])

    lines = ag.at[1]
    h_cols, half_width = small_own.shape[2], nrm.shape[1] // 2
    gpre, hidden = gp.at[:, :h_cols], nrm.at[:, :h_cols]
    picked = nrm.at[:, half_width : half_width + h_cols]
    g = qkv.at[:, : stages[5].shape[1]]
    head_loads = [
        pltpu.make_async_copy(src, dst, load_sems.at[11 + i])
        for i, (src, dst) in enumerate(zip(head_stored, (lines, gpre, hidden, picked, g)))
    ]
    mlp_part, attn_part = range(5), range(5, 11)
    for copy in head_loads:
        copy.start()
    for i in mlp_part:
        load(LAYERS - 1, i).start()
    greet(place, levels)

    def count_of(m):
        return arrivals[m].shape[2]

    def slot(m, layer):
        return layer if m < 4 else 0

    relayed = levels == 4
    middle = (z == 1) | (z == 2)

    def send(layer, m, delta):
        there = (z + delta) % levels
        return remote(
            stages[m].at[rows_at(there * count_of(m), count_of(m))],
            arrivals[m].at[slot(m, layer), delta - 1],
            z_sems.at[0, layer, m, delta - 1],
            z_sems.at[1, layer, m, delta - 1],
            place.level(there),
        )

    def far(delta):
        there = (z + delta) % levels
        return (z + there == 3) & (z * there == 0)

    def hand(layer, m, delta):
        there = (z + delta) % levels
        return remote(
            stages[m].at[rows_at(there * count_of(m), count_of(m))],
            arrivals[m].at[slot(m, layer), levels - 1],
            z_sems.at[0, layer, m, delta - 1],
            z_sems.at[1, layer, m, levels - 1],
            place.level(1 + z // 3),
        )

    def send_first(layer, m):
        for delta in range(1, levels):
            if not relayed:
                send(layer, m, delta).start()
            elif delta == 2:
                pl.when(jnp.logical_not(middle))(send(layer, m, delta).start)
            else:
                pl.when(far(delta))(hand(layer, m, delta).start)
                pl.when(jnp.logical_not(far(delta)))(send(layer, m, delta).start)

    def send_rest(layer, m):
        if relayed:
            @pl.when(middle)
            def _():
                hand(layer, m, 1).wait_recv()
                rows = rows_at((z + 2) % levels * count_of(m), count_of(m))
                total = stages[m][rows, :].astype(F32)
                total = total + arrivals[m][slot(m, layer), levels - 1].astype(F32)
                stages[m][rows, :] = total.astype(BF)
                send(layer, m, 2).start()

    def sent(layer, m):
        for delta in range(1, levels):
            send(layer, m, delta).wait_send()

    def result(layer, m):
        return reduced[m].at[layer] if m < 4 else head_reduced[m - 4]

    def weight_grad(layer, m, left, right, tile):
        width = left.shape[1]
        if m < 4 and layer + 1 < LAYERS:
            sent(layer + 1, m)
        if width % tile:
            stages[m][...] = dot(left[...], right[...], 0, 0).astype(BF)
        else:
            def body(i, carry):
                here = rows_at(i * tile, tile, tile)
                stages[m][here, :] = dot(left[:, here], right[...], 0, 0).astype(BF)
                return carry

            lax.fori_loop(0, width // tile, body, 0)
        send_first(layer, m)
        out = result(layer, m)
        out[...] = stages[m][rows_at(z * count_of(m), count_of(m)), :].astype(out.dtype)

    bufs = [ag.at[p % 2] for p in range(PHASES)]
    phases = [Exchange(place, p, buf, exchange) for p, buf in enumerate(bufs)]

    def own_half(s):
        return slice(s * HALF_BLOCK, (s + 1) * HALF_BLOCK)

    def enter(p, s):
        bufs[p][phases[p].own(s), :] = dx_out[own_half(s), :].astype(BF)
        phases[p].start(s)

    def leave(p, s):
        rows = own_half(s)
        layer = LAYERS - 1 - p // 2
        values = (mid if p % 2 == 0 else xs)[layer, rows, :]
        dx_out[rows, :] += norm_back(values, phases[p].total(s))
        if p + 1 < PHASES:
            enter(p + 1, s)

    def run(p, compute, relays):
        hooks = [(3, lambda: leave(p, 0))]
        hooks += [(2, lambda key=key: send_rest(*key)) for key in relays]
        phases[p].run(compute, hooks)
        phases[p].finish_stream(1)

    dx_out[...] = dy_in[...]
    for s in range(2):
        enter(0, s)

    for copy in head_loads:
        copy.wait()
    last = LAYERS - 1
    bias_sum = jnp.sum(gpre[...].astype(F32), axis=0, keepdims=True)
    small_own[1] = jnp.broadcast_to(bias_sum, small_own.shape[1:])
    to_x = remote(
        small_own.at[1], small_x, small_sems.at[0, 0], small_sems.at[1, 0], place.peer(1)
    )
    to_x.start()
    weight_grad(last, 5, hidden, g, 2 * BLOCK)
    weight_grad(last, 6, picked, g, 2 * BLOCK)
    weight_grad(last, 4, lines, gpre, 2 * BLOCK)
    g_sum = jnp.sum(g[...].astype(F32), axis=0, keepdims=True)
    to_x.wait()
    small_z[0, :, : g_sum.shape[1]] = jnp.broadcast_to(g_sum, (8, g_sum.shape[1]))
    small_z[0, :, g_sum.shape[1] :] = small_own[1] + small_x[...]
    to_z = [
        remote(
            small_z.at[0], small_z.at[d], small_sems.at[0, d], small_sems.at[1, d],
            place.level((z + d) % levels),
        )
        for d in range(1, levels)
    ]
    for copy in to_z:
        copy.start()
    for i in attn_part:
        load(last, i).start()

    relays = [(last, 5), (last, 6), (last, 4)]
    for layer in reversed(range(LAYERS)):
        p = 2 * (LAYERS - 1 - layer)
        buf = bufs[p]
        for i in mlp_part:
            load(layer, i).wait()

        def perceptron(start, s, half, buf=buf):
            rows = rows_at(start, 2 * BLOCK, 2 * BLOCK)
            for n in range(0, gl.shape[1], 2 * BLOCK):
                width = slice(n, min(n + 2 * BLOCK, gl.shape[1]))
                grad_act = dot(buf[rows, :], wd[width, :], 1, 1)
                gl[rows, width] = (grad_act * gl[rows, width].astype(F32)).astype(BF)
            part[s, half] = dot(gl[rows, :], wi[...], 1, 1).astype(BF)

        run(p, perceptron, relays)
        weight_grad(layer, 3, act, buf, BLOCK)
        leave(p, 1)
        weight_grad(layer, 2, nml, gl, 2 * BLOCK)
        if layer > 0:
            for i in mlp_part:
                load(layer - 1, i).start()
        for i in attn_part:
            load(layer, i).wait()
        buf = bufs[p + 1]

        def attend(start, s, half, buf=buf):
            cosine, sine = rope[:, :BLOCK], rope[:, BLOCK:]
            both = rows_at(start, 2 * BLOCK, 2 * BLOCK)
            grad_heads = dot(buf[both, :], wo[...], 1, 1).astype(BF)
            grad_heads = dot(grad_heads, sel_o[...]).astype(BF)
            for block in range(2):
                rows = rows_at(start + block * BLOCK, BLOCK, BLOCK)
                outs = [[], [], []]
                for h in range(heads):
                    def part_of(kind, h=h, rows=rows):
                        low = kind * lanes + h * BLOCK
                        return qkv[rows, low : low + BLOCK]

                    query, key, value = part_of(0), part_of(1), part_of(2)
                    probs = prb[rows, h * BLOCK : (h + 1) * BLOCK]
                    grad_head = grad_heads[
                        block * BLOCK : (block + 1) * BLOCK, h * BLOCK : (h + 1) * BLOCK
                    ]
                    outs[2].append(dot(probs, grad_head, 0, 0).astype(BF))
                    grad_probs = dot(grad_head, value, 1, 1)
                    probs = probs.astype(F32)
                    inner = jnp.sum(probs * grad_probs, axis=-1, keepdims=True)
                    grad_scores = (probs * (grad_probs - inner)).astype(BF)
                    for kind, turned in (
                        (0, dot(grad_scores, key)),
                        (1, dot(grad_scores, query, 0, 0)),
                    ):
                        turned = turned * (1.0 / math.sqrt(HDIM))
                        turned = turned * cosine - pltpu.roll(turned, BLOCK // 2, 1) * sine
                        outs[kind].append(turned.astype(BF))
                packed = jnp.concatenate(outs[0] + outs[1] + outs[2], axis=1)
                gp[rows, :] = dot(packed, sel_q[...], 1, 1).astype(BF)
            part[s, half] = dot(gp[both, :], wq[...], 1, 1).astype(BF)

        run(p + 1, attend, [(layer, 3), (layer, 2)])
        weight_grad(layer, 0, nrm, gp, 2 * BLOCK)
        if layer > 0:
            leave(p + 1, 1)
            weight_grad(layer, 1, att, buf, 2 * BLOCK)
            for i in attn_part:
                load(layer - 1, i).start()
        else:
            weight_grad(layer, 1, att, buf, 2 * BLOCK)
            leave(p + 1, 1)
        relays = [(layer, 0), (layer, 1)]
    for key in relays:
        send_rest(*key)

    total = small_z[0]
    for copy, d in zip(to_z, range(1, levels)):
        copy.wait_recv()
        total = total + small_z[d]
    small_out[...] = total
    for copy in to_z:
        copy.wait_send()
    pending = [(last, 5), (last, 6), (last, 4)]
    pending += [(layer, m) for layer in reversed(range(LAYERS)) for m in (3, 2, 0, 1)]
    for layer, m in pending:
        out = result(layer, m)
        for delta in range(1, levels):
            def add(delta=delta, layer=layer, m=m, out=out):
                send(layer, m, delta).wait_recv()
                total = out[...].astype(F32)
                total = total + arrivals[m][slot(m, layer), delta - 1].astype(F32)
                out[...] = total.astype(out.dtype)

            if relayed and delta != 2:
                source = (z + levels - delta) % levels
                pl.when(jnp.logical_not((z + source == 3) & (z * source == 0)))(add)
            else:
                add()
        if m > 3 or layer == 0:
            sent(layer, m)


def shape(*dims, dtype=BF):
    return jax.ShapeDtypeStruct(dims, dtype)


def rope_table():
    position = np.arange(BLOCK) % ROW_LEN
    inverse = ROTARY_BASE ** (-np.arange(HALF) / HALF)
    angles = (position[:, None] * inverse[None, :]).astype(np.float32)
    table = np.zeros((BLOCK, 2, 2, BLOCK // 2), np.float32)
    table[:, 0, :, :HALF] = np.cos(angles)[:, None]
    table[:, 1, 0, :HALF] = -np.sin(angles)
    table[:, 1, 1, :HALF] = np.sin(angles)
    return table.reshape(BLOCK, 2 * BLOCK)


def lane_of(index):
    head, inside = divmod(index, HDIM)
    half, place = divmod(inside, HALF)
    return head * BLOCK + half * (BLOCK // 2) + place


def token_mask(starts, padded):
    within = jnp.arange(BLOCK)
    same_row = within[:, None] // ROW_LEN == within[None, :] // ROW_LEN
    causal = within[None, :] <= within[:, None]
    begun = (within % ROW_LEN)[None, None, :] >= starts[:, :, None]
    open_key = (padded[:, None, :] == 0) | (within[:, None] == within[None, :])[None]
    return ((same_row & causal)[None] & begun & open_key).astype(BF)


def per_device(devices, x, segments, padded, w_qkv, w_out, w_in, w_down, gain_attn, gain_mlp,
               head_first, head_first_bias, head_final, head_bias, head_skip, adjoint):
    levels = devices // PLANE
    width = x.shape[1]
    ff = w_in.shape[2]
    columns = head_final.shape[1]
    everywhere = ("wide", "narrow")
    groups = [[PLANE * z + r for r in range(PLANE)] for z in range(levels)]
    tokens = PLANE * BLOCK
    heads = width // HDIM // PLANE
    span = heads * HDIM
    rows = width // devices
    out_rows = up16(rows)
    ff_rows = ff // devices
    down_rows = up16(ff_rows)
    head_share = 2 * width // devices
    head_rows = up16(head_share)
    used_cols, o_rows, f_cols = 3 * span, levels * out_rows, levels * down_rows
    h_cols = -(-levels * head_rows // 128) * 128
    code_cols = -(-BLOCK // rows)
    q_cols = -(-(used_cols + code_cols) // 128) * 128
    lanes = heads * BLOCK

    sel_q = np.zeros((q_cols, 3 * lanes), np.float32)
    sel_o = np.zeros((o_rows, lanes), np.float32)
    for e in range(span):
        for kind in range(3):
            sel_q[kind * span + e, kind * lanes + lane_of(e)] = 1
        sel_o[e // rows * out_rows + e % rows, lane_of(e)] = 1
    sel_q, sel_o = jnp.asarray(sel_q, BF), jnp.asarray(sel_o, BF)
    rope = jnp.asarray(rope_table())
    head_lanes = np.full((1, h_cols), -width, np.int32)
    for zz in range(levels):
        here = slice(zz * head_rows, zz * head_rows + head_share)
        head_lanes[0, here] = 4 * head_share * zz + np.arange(head_share)
    head_lanes = jnp.asarray(head_lanes)

    seg_rows = segments.reshape(-1, ROW_LEN)
    earlier = jnp.arange(ROW_LEN)[None, :] < jnp.arange(ROW_LEN)[:, None]
    starts = jnp.sum((seg_rows[:, None, :] != seg_rows[:, :, None]) & earlier[None], axis=-1)
    code = (starts.reshape(-1) + ROW_LEN * padded).astype(BF)
    code = jnp.pad(code, (0, code_cols * rows - BLOCK)).reshape(code_cols, rows).T
    code = jnp.pad(code, ((0, 0), (0, q_cols - used_cols - code_cols)))

    def times_gain(w, gain):
        return (w.astype(F32) * gain.astype(F32)[:, :, None]).astype(BF)

    q_part = times_gain(w_qkv, gain_attn).reshape(LAYERS, rows, 3, PLANE, span)
    q_part = q_part.transpose(3, 0, 1, 2, 4).reshape(PLANE, LAYERS, rows, used_cols)
    i_part = times_gain(w_in, gain_mlp).reshape(LAYERS, rows, levels, PLANE, ff_rows)
    i_part = i_part.transpose(3, 0, 1, 2, 4)
    i_part = jnp.pad(i_part, [(0, 0)] * 4 + [(0, down_rows - ff_rows)])
    i_part = i_part.reshape(PLANE, LAYERS, rows, f_cols)
    code = jnp.broadcast_to(code, (PLANE, LAYERS) + code.shape)
    both = jnp.concatenate([q_part, code, i_part], axis=-1)
    both = lax.all_to_all(both, everywhere, 0, 0, axis_index_groups=groups)
    code = both[:, 0, :, used_cols : used_cols + code_cols]
    code = jnp.swapaxes(code, 1, 2).reshape(PLANE, code_cols * rows)[:, :BLOCK]
    code = code.reshape(2, 2, 2, 2, HALF_BLOCK).transpose(3, 0, 2, 1, 4)
    code = code.reshape(PLANE, BLOCK).astype(jnp.int32)
    mask = token_mask(code % ROW_LEN, code // ROW_LEN).reshape(tokens, BLOCK)
    both = jnp.swapaxes(both, 0, 1).reshape(LAYERS, PLANE * rows, q_cols + f_cols)
    q_piece, i_piece = both[..., :q_cols], both[..., q_cols:]
    trade = [(levels * t + zz, PLANE * zz + t) for t in range(PLANE) for zz in range(levels)]
    o_piece = lax.ppermute(w_out, everywhere, trade)
    o_piece = jnp.pad(o_piece, [(0, 0), (0, out_rows - rows), (0, 0)])
    d_piece = jnp.pad(w_down, [(0, 0), (0, down_rows - ff_rows), (0, 0)])

    pieces = (q_piece, o_piece, i_piece, d_piece)
    layer_shapes = [
        (tokens, width), (tokens, width), (tokens, 3 * lanes), (tokens, lanes), (tokens, o_rows),
        (tokens, f_cols), (tokens, f_cols),
    ]
    slab_shapes = [(width, q_cols), (o_rows, width), (width, f_cols), (f_cols, width)]
    blocks = (2, 4, 2, HALF_BLOCK, columns)
    outs = [
        shape(2 * BLOCK, columns), shape(BLOCK, width, dtype=F32),
        shape(LAYERS, BLOCK, width, dtype=F32), shape(LAYERS, BLOCK, width, dtype=F32),
    ]
    vmem_outs = len(outs)
    outs += [shape(LAYERS, *dims) for dims in layer_shapes]
    outs += [shape(tokens, width)] + [shape(tokens, h_cols)] * 3 + [shape(*blocks)]
    outs += [shape(LAYERS, *dims) for dims in slab_shapes]
    (predictions, grad_final, xs, mid, nrm, nml, qkv, prb, att, gl, act, lines, hidden, gpre,
     picked, g, wq, wo, wi, wd) = pl.pallas_call(
        lambda *refs: forward_kernel(levels, *refs),
        out_shape=outs,
        in_specs=[VMEM] * 9 + [ANY] * 7,
        out_specs=[VMEM] * vmem_outs + [ANY] * (len(outs) - vmem_outs),
        scratch_shapes=exchange_scratch(width, PHASES + 1)
        + [pltpu.VMEM((LAYERS,) + dims, BF) for dims in layer_shapes[:2]]
        + [pltpu.VMEM(dims, BF) for dims in layer_shapes[2:]]
        + [pltpu.VMEM((LAYERS,) + dims, BF) for dims in slab_shapes]
        + [
            pltpu.VMEM((width, 3 * lanes), BF), pltpu.VMEM((width, width), BF),
            pltpu.VMEM((width, columns), BF), pltpu.VMEM((width, h_cols), BF),
            pltpu.VMEM((width, h_cols), BF), pltpu.VMEM((h_cols, columns), BF),
            pltpu.VMEM(blocks, BF), pltpu.VMEM((tokens, h_cols), BF),
            pltpu.VMEM((tokens, h_cols), BF), pltpu.VMEM((tokens, h_cols), BF),
            pltpu.VMEM((2 * BLOCK, width), BF),
            pltpu.SemaphoreType.DMA((3, LAYERS, 4, levels - 1)),
            pltpu.SemaphoreType.DMA((LAYERS, 4)),
            pltpu.SemaphoreType.DMA((32,)),
            pltpu.SemaphoreType.DMA((3,)),
            pltpu.SemaphoreType.DMA((2, 4)),
        ],
        compiler_params=pltpu.CompilerParams(
            collective_id=1, has_side_effects=True, vmem_limit_bytes=60 * MIB
        ),
        name="decoder_forward",
    )(x, mask, rope, sel_q, sel_o, head_lanes, jnp.swapaxes(adjoint.reshape(2, 2, HALF_BLOCK, columns), 0, 1),
      head_first_bias[None], head_bias[None], *pieces, head_first, head_final, head_skip)

    chunk = [PLANE * rows, out_rows, PLANE * rows, down_rows, PLANE * rows, head_rows, head_rows]
    cols = [q_cols, width, f_cols, width, h_cols, columns, columns]
    stage_rows = [levels * n for n in chunk[:5]] + [h_cols] * 2
    kept_shapes = [
        (tokens, width), (tokens, f_cols), (tokens, f_cols), (width, f_cols), (f_cols, width),
        (tokens, width), (tokens, 3 * lanes), (tokens, lanes), (tokens, o_rows), (width, q_cols),
        (o_rows, width),
    ]
    small_cols = columns + h_cols
    outs = [shape(BLOCK, width, dtype=F32), shape(8, small_cols, dtype=F32)]
    outs += [shape(LAYERS, chunk[m], cols[m], dtype=F32 if m == 3 else BF) for m in range(4)]
    outs += [shape(chunk[m], cols[m], dtype=F32 if m > 4 else BF) for m in range(4, 7)]
    (input_grad, small, q_grad, o_grad, i_grad, d_grad, g_first, g_out, g_skip) = pl.pallas_call(
        lambda *refs: backward_kernel(levels, *refs),
        out_shape=outs,
        in_specs=[VMEM] * 6 + [ANY] * 16,
        out_specs=[VMEM] * len(outs),
        scratch_shapes=exchange_scratch(width, PHASES)
        + [pltpu.VMEM((2, tokens, width), BF)]
        + [pltpu.VMEM(dims, BF) for dims in kept_shapes]
        + [pltpu.VMEM((tokens, q_cols), BF)]
        + [pltpu.VMEM((stage_rows[m], cols[m]), BF) for m in range(7)]
        + [
            pltpu.VMEM((LAYERS if m < 4 else 1, levels, chunk[m], cols[m]), BF)
            for m in range(7)
        ]
        + [
            pltpu.VMEM((2, 8, h_cols), F32), pltpu.VMEM((8, h_cols), F32),
            pltpu.VMEM((levels, 8, small_cols), F32),
            pltpu.SemaphoreType.DMA((2, LAYERS, 7, levels)),
            pltpu.SemaphoreType.DMA((16,)),
            pltpu.SemaphoreType.DMA((2, levels)),
        ],
        compiler_params=pltpu.CompilerParams(
            collective_id=2, has_side_effects=True, vmem_limit_bytes=60 * MIB
        ),
        name="decoder_backward",
    )(grad_final, rope, sel_q, sel_o, xs, mid, nml, act, gl, wi, wd, nrm, qkv, prb, att, wq, wo,
      lines, gpre, hidden, picked, g.reshape(tokens, columns))

    both = jnp.concatenate([q_grad[..., :used_cols], i_grad], axis=-1)
    both = both.reshape(LAYERS, PLANE, rows, used_cols + f_cols)
    both = jnp.swapaxes(both, 0, 1).reshape(PLANE, -1)
    both = jnp.concatenate([both, g_first.reshape(PLANE, -1)], axis=-1)
    both = lax.all_to_all(both, everywhere, 0, 0, axis_index_groups=groups)
    split = LAYERS * rows * (used_cols + f_cols)
    g_first = both[:, split:].reshape(4, 2, rows, h_cols)[..., : levels * head_rows]
    g_first = g_first.reshape(4, 2, rows, levels, head_rows)[..., :head_share]
    g_first = jnp.sum(g_first.astype(F32), axis=1).transpose(1, 2, 0, 3).reshape(rows, width)
    both = both[:, :split].reshape(PLANE, LAYERS, rows, used_cols + f_cols)
    q_grad = both[..., :used_cols].reshape(PLANE, LAYERS, rows, 3, span)
    q_grad = q_grad.transpose(1, 2, 3, 0, 4).reshape(LAYERS, rows, 3 * width).astype(F32)
    i_grad = both[..., used_cols:].reshape(PLANE, LAYERS, rows, levels, down_rows)[..., :ff_rows]
    i_grad = i_grad.transpose(1, 2, 3, 0, 4).reshape(LAYERS, rows, ff).astype(F32)
    attn_gain_grad = jnp.sum(q_grad * w_qkv.astype(F32), axis=-1)
    mlp_gain_grad = jnp.sum(i_grad * w_in.astype(F32), axis=-1)
    q_grad = q_grad * gain_attn.astype(F32)[:, :, None]
    i_grad = i_grad * gain_mlp.astype(F32)[:, :, None]
    o_grad = lax.ppermute(o_grad[:, :rows], everywhere, [(b, a) for a, b in trade]).astype(F32)
    d_grad = d_grad[:, :ff_rows]
    z, narrow = lax.axis_index("wide") // 4, lax.axis_index("narrow")
    g_first_bias = lax.dynamic_slice(small[0], (columns + z * head_rows + narrow * rows,), (rows,))
    return (
        predictions, input_grad, q_grad, o_grad, i_grad, d_grad, attn_gain_grad, mlp_gain_grad,
        g_first, g_first_bias, g_out[:head_share], small[0, :columns], g_skip[:head_share],
    )


def solution(mesh):
    devices = mesh.shape["wide"] * mesh.shape["narrow"]
    both = ("wide", "narrow")
    weight, gain = P(None, both, None), P(None, both)
    return jax.shard_map(
        lambda *arrays: per_device(devices, *arrays),
        mesh=mesh,
        in_specs=(
            P(both, None), P(both), P(both), weight, weight, weight, weight, gain, gain, P(), P(),
            P(None, "narrow"), P("narrow"), P(None, "narrow"), P("wide", "narrow"),
        ),
        out_specs=(
            P("wide", "narrow"), P(both, None), weight, weight, weight, weight, gain, gain,
            P(both, None), P(both), P("wide", "narrow"), P("narrow"), P("wide", "narrow"),
        ),
        check_vma=False,
    )
```

```python
import math

import jax
import jax.numpy as jnp
import numpy as np
from jax import lax
from jax.experimental import pallas as pl
from jax.experimental.pallas import tpu as pltpu
from jax.sharding import PartitionSpec as P

HDIM = 80
HALF = HDIM // 2
LAYERS = 2
ROW_LEN = 16
BLOCK = 128
HALF_BLOCK = BLOCK // 2
PLANE = 8
PHASES = 2 * LAYERS
MESH = pl.DeviceIdType.MESH
BF = jnp.bfloat16
F32 = jnp.float32
EPS = 1e-06
ROTARY_BASE = 10000.0
MIB = 1024 * 1024
VMEM = pl.BlockSpec(memory_space=pltpu.VMEM)
ANY = pl.BlockSpec(memory_space=pl.ANY)


def up16(rows):
    return -(-rows // 16) * 16


def rows_at(start, count, step=16):
    return pl.ds(pl.multiple_of(start, step), count)


def dot(a, b, ca=1, cb=0):
    return lax.dot_general(a, b, (((ca,), (cb,)), ((), ())), preferred_element_type=F32)


class Place:
    def __init__(self):
        wide = lax.axis_index("wide")
        self.x = lax.axis_index("narrow")
        self.core = wide % 2
        self.y = (wide // 2) % 2
        self.z = wide // 4

    def device(self, z, y, core, x):
        return (z * 4 + y * 2 + core, x)

    def sibling(self):
        return self.device(self.z, self.y, 1 - self.core, self.x)

    def peer(self, k):
        return self.device(self.z, (self.y + k // 2) % 2, self.core, (self.x + k % 2) % 2)

    def pair(self, k):
        return 2 * ((self.y + k // 2) % 2) + (self.x + k % 2) % 2

    def level(self, z):
        return self.device(z, self.y, self.core, self.x)

    def turned(self, e):
        return (self.y + e // 4) % 2, (self.core + e // 2) % 2, (self.x + e) % 2

    def other(self, e):
        return self.device(self.z, *self.turned(e))

    def rank(self, e=0):
        y, core, x = self.turned(e)
        return 4 * y + 2 * core + x

    def indexed(self, index):
        return (index // 2, index % 2)

    def holder(self, levels):
        index = PLANE * self.z + self.rank()
        return index % levels * PLANE + index // levels

    def held(self, levels):
        return levels * self.rank() + self.z

    def trades(self, levels):
        return self.holder(levels) != PLANE * self.z + self.rank()


def greet(place, levels):
    barrier = pltpu.get_barrier_semaphore()
    others = [place.other(e) for e in range(1, PLANE)]
    others += [place.level((place.z + d) % levels) for d in range(1, levels)]
    for other in others:
        pl.semaphore_signal(barrier, inc=1, device_id=other, device_id_type=MESH)
    trades = place.trades(levels)

    @pl.when(trades)
    def _():
        for index in (place.holder(levels), place.held(levels)):
            pl.semaphore_signal(
                barrier, inc=1, device_id=place.indexed(index), device_id_type=MESH
            )
        pl.semaphore_wait(barrier, len(others) + 2)

    @pl.when(jnp.logical_not(trades))
    def _():
        pl.semaphore_wait(barrier, len(others))


def remote(src, dst, send, recv, device):
    return pltpu.make_async_remote_copy(
        src_ref=src, dst_ref=dst, send_sem=send, recv_sem=recv, device_id=device,
        device_id_type=MESH,
    )


class Exchange:
    def __init__(self, place, phase, buf, scratch):
        (self.part, self.recv_s, self.recv_c, self.send_c, self.sems) = scratch
        self.place, self.phase, self.buf = place, phase, buf

    def sem(self, s, kind, k):
        return self.sems.at[self.phase, s, kind, k]

    def rows(self, s, k, core):
        start = s * 8 * HALF_BLOCK + self.place.pair(k) * 2 * HALF_BLOCK + core * HALF_BLOCK
        return rows_at(start, HALF_BLOCK, HALF_BLOCK)

    def own(self, s):
        return self.rows(s, 0, self.place.core)

    def to_peer(self, s, k):
        own = self.buf.at[self.own(s)]
        return remote(own, own, self.sem(s, 0, k), self.sem(s, 1, k), self.place.peer(k))

    def from_peer(self, s, k):
        there = self.buf.at[self.rows(s, k, self.place.core)]
        return remote(there, there, self.sem(s, 0, k), self.sem(s, 1, k), self.place.peer(k))

    def to_sibling(self, s, k):
        rows = self.buf.at[self.rows(s, k, self.place.core)]
        return remote(rows, rows, self.sem(s, 2, k), self.sem(s, 3, k), self.place.sibling())

    def from_sibling(self, s, k):
        rows = self.buf.at[self.rows(s, k, 1 - self.place.core)]
        return remote(rows, rows, self.sem(s, 2, k), self.sem(s, 3, k), self.place.sibling())

    def part_rows(self, k, core):
        start = ((self.place.x + k) % 2) * 2 * HALF_BLOCK + core * HALF_BLOCK
        return rows_at(start, HALF_BLOCK, HALF_BLOCK)

    def sum_sibling(self, s, k):
        src = self.part.at[s, k // 2, self.part_rows(k, 1 - self.place.core)]
        return remote(
            src, self.recv_s.at[s, k], self.sem(s, 4, k), self.sem(s, 5, k), self.place.sibling()
        )

    def sum_peer(self, s, k):
        return remote(
            self.send_c.at[s, k - 1], self.recv_c.at[s, k - 1], self.sem(s, 6, k),
            self.sem(s, 7, k), self.place.peer(k),
        )

    def chip_sum(self, s, k):
        own = self.part[s, k // 2, self.part_rows(k, self.place.core), :]
        return own.astype(F32) + self.recv_s[s, k].astype(F32)

    def start(self, s):
        self.to_sibling(s, 0).start()
        for k in (1, 2, 3):
            self.to_peer(s, k).start()

    def finish_chip(self, s, k):
        self.sum_sibling(s, k).wait_recv()
        self.send_c[s, k - 1] = self.chip_sum(s, k).astype(BF)
        self.sum_peer(s, k).start()

    def run(self, compute, hooks):
        def body(i, carry):
            s, half = i // 2, i % 2
            for at, hook in hooks:
                pl.when(i == at)(hook)

            @pl.when(half == 0)
            def _():
                self.from_peer(s, 1).wait_recv()
                self.to_sibling(s, 1).start()

            @pl.when(half == 1)
            def _():
                for k in (2, 3):
                    self.from_peer(s, k).wait_recv()
                    self.to_sibling(s, k).start()

            @pl.when(i == 2)
            def _():
                self.finish_stream(0)

            self.from_sibling(s, 2 * half).wait_recv()
            self.from_sibling(s, 2 * half + 1).wait_recv()
            start = s * 8 * HALF_BLOCK + (self.place.y + half) % 2 * 4 * HALF_BLOCK
            compute(start, s, half)
            self.sum_sibling(s, 2 * half).start()
            self.sum_sibling(s, 2 * half + 1).start()

            @pl.when(half == 1)
            def _():
                self.finish_chip(s, 1)

            return carry

        lax.fori_loop(0, 4, body, 0)

    def finish_stream(self, s):
        for k in (2, 3):
            self.finish_chip(s, k)

    def total(self, s):
        self.sum_sibling(s, 0).wait_recv()
        total = self.chip_sum(s, 0)
        for k in (1, 2, 3):
            self.sum_peer(s, k).wait_recv()
            total = total + self.recv_c[s, k - 1].astype(F32)
        for k in range(4):
            self.to_sibling(s, k).wait_send()
            self.sum_sibling(s, k).wait_send()
            if k:
                self.to_peer(s, k).wait_send()
                self.sum_peer(s, k).wait_send()
        return total


def exchange_scratch(width, phases):
    return [
        pltpu.VMEM((2, 2, 4 * HALF_BLOCK, width), BF),
        pltpu.VMEM((2, 4, HALF_BLOCK, width), BF),
        pltpu.VMEM((2, 3, HALF_BLOCK, width), BF),
        pltpu.VMEM((2, 3, HALF_BLOCK, width), BF),
        pltpu.SemaphoreType.DMA((phases, 2, 8, 4)),
    ]


def root(values):
    return lax.rsqrt(jnp.mean(values * values, axis=-1, keepdims=True) + EPS)


def forward_kernel(levels, *refs):
    (x_in, own_mask, rope, sel_q, sel_o, head_lanes, adjoint, bias_first, bias_last) = refs[:9]
    (gains, w_q, w_in, w_out) = refs[9:13]
    w_down, head_weights = refs[13], refs[14:17]
    (predictions, grad_out, xs, mid) = refs[17:21]
    kept, (slab_q, slab_o, slab_i, slab_d) = refs[21:33], refs[33:37]
    exchange = refs[37:42]
    (nrm, nml, qkv, prb, att, gl, act) = refs[42:49]
    slabs = refs[49:53]
    (wide_q, first, final, pick, first_q, final_q, g, hidden, gpre, picked, hidden_all) = refs[53:64]
    (mask, cut, pasted, o_cut, o_piece) = refs[64:69]
    (z_sems, own_sems, keep_sems, load_sems, g_sems, trade_sems, mask_sems, o_sems) = refs[69:]
    slab_outs = (slab_q, slab_o, slab_i, slab_d)
    place = Place()
    z = place.z
    heads = sel_o.shape[1] // BLOCK
    lanes = heads * BLOCK
    kept_here, waited = [], []

    def keep(src, dst):
        copy = pltpu.make_async_copy(src, dst, keep_sems.at[len(kept_here)])
        copy.start()
        kept_here.append(copy)
        return copy

    def forget(copy):
        copy.wait()
        waited.append(copy)

    relayed = levels == 4

    def far(delta):
        there = (z + delta) % levels
        return (z + there == 3) & (z * there == 0)

    counts = [slabs[0].shape[1] // levels, o_piece.shape[1], slabs[2].shape[1] // levels,
              w_down.shape[1]]

    def rows_of(m, level):
        return rows_at(level * counts[m], counts[m])

    def piece(layer, m):
        if m == 1:
            return o_piece.at[layer]
        if m == 3:
            return w_down.at[layer]
        return slabs[m].at[layer, rows_of(m, z)]

    def spread(layer, m, delta):
        return remote(
            piece(layer, m), slabs[m].at[layer, rows_of(m, z)],
            z_sems.at[0, layer, m, delta - 1], z_sems.at[1, layer, m, delta - 1],
            place.level((z + delta) % levels),
        )

    def arriving(layer, m, delta):
        rows = slabs[m].at[layer, rows_of(m, (z + levels - delta) % levels)]
        return remote(
            rows, rows, z_sems.at[0, layer, m, delta - 1], z_sems.at[1, layer, m, delta - 1],
            place.level((z + delta) % levels),
        )

    def relay(layer, m):
        rows = slabs[m].at[layer, rows_of(m, (z + 2) % levels)]
        return remote(
            rows, rows, z_sems.at[2, layer, m, 0], z_sems.at[1, layer, m, 2 * (z - 1)],
            place.level(3 * (z - 1)),
        )

    def for_spread(layer, m, act_on):
        for delta in range(1, levels):
            if relayed and delta != 2:
                @pl.when(jnp.logical_not(far(delta)))
                def _(delta=delta):
                    act_on(spread(layer, m, delta))
            else:
                act_on(spread(layer, m, delta))

    def own_piece(layer, m):
        return pltpu.make_async_copy(
            piece(layer, m), slabs[m].at[layer, rows_of(m, z)], own_sems.at[layer, m]
        )

    def send_weights(layer, m):
        if m % 2:
            own_piece(layer, m).start()
        for_spread(layer, m, lambda copy: copy.start())

    rows, q_cols = w_q.shape[1], slabs[0].shape[2]
    span = w_q.shape[2] // 3 // PLANE
    ff_rows = w_in.shape[2] // PLANE // levels
    padded = slabs[2].shape[2] // levels - ff_rows

    def cut_weights(layer):
        scaled_q = w_q[layer].astype(F32) * gains[0, layer]
        scaled_i = w_in[layer].astype(F32) * gains[1, layer]
        for t in range(PLANE):
            parts = []
            for kind in range(3):
                low = (kind * PLANE + t) * span
                parts.append(scaled_q[:, low : low + span])
            if q_cols > 3 * span:
                parts.append(jnp.zeros((rows, q_cols - 3 * span), F32))
            cut[layer, t, :rows, :q_cols] = jnp.concatenate(parts, axis=1).astype(BF)
            parts = []
            for zz in range(levels):
                low = (zz * PLANE + t) * ff_rows
                parts.append(scaled_i[:, low : low + ff_rows])
                if padded:
                    parts.append(jnp.zeros((rows, padded), F32))
            cut[layer, t, :rows, q_cols:] = jnp.concatenate(parts, axis=1).astype(BF)

    def trade(layer, e):
        return remote(
            cut.at[layer, place.rank(e)], pasted.at[layer, place.rank()],
            trade_sems.at[0, layer, e], trade_sems.at[1, layer, e], place.other(e),
        )

    def traded(layer, e):
        there = pasted.at[layer, place.rank(e)]
        return remote(
            there, there, trade_sems.at[0, layer, e], trade_sems.at[1, layer, e], place.other(e)
        )

    def start_trade(layer):
        for e in range(1, PLANE):
            trade(layer, e).start()
        own = place.rank()
        pltpu.make_async_copy(
            cut.at[layer, own], pasted.at[layer, own], trade_sems.at[0, layer, 0]
        ).start()

    def end_trade(layer):
        own = place.rank()
        pltpu.make_async_copy(
            cut.at[layer, own], pasted.at[layer, own], trade_sems.at[0, layer, 0]
        ).wait()
        for e in range(1, PLANE):
            traded(layer, e).wait_recv()
        for e in range(1, PLANE):
            trade(layer, e).wait_send()
        for m, low in ((0, 0), (2, q_cols)):
            width = slabs[m].shape[2]
            whole = [pasted[layer, t, :rows, low : low + width].astype(F32) for t in range(PLANE)]
            slabs[m][layer, rows_of(m, z), :] = jnp.concatenate(whole, axis=0).astype(BF)

    trades = place.trades(levels)
    o_trade = remote(
        o_cut, o_piece, o_sems.at[0], o_sems.at[1], place.indexed(place.holder(levels))
    )
    o_local = pltpu.make_async_copy(o_cut, o_piece, o_sems.at[0])

    def mask_to(e):
        there = mask.at[:, place.pair(0), place.core]
        return remote(own_mask, there, mask_sems.at[0, e], mask_sems.at[1, e], place.other(e))

    def mask_from(e):
        y, core, x = place.turned(e)
        there = mask.at[:, 2 * y + x, core]
        return remote(there, there, mask_sems.at[0, e], mask_sems.at[1, e], place.other(e))

    mask_local = pltpu.make_async_copy(
        own_mask, mask.at[:, place.pair(0), place.core], mask_sems.at[0, 0]
    )

    middle = (z == 1) | (z == 2)

    def relay_on(layer, m):
        if relayed:
            @pl.when(middle)
            def _():
                arriving(layer, m, 2).wait_recv()
                relay(layer, m).start()

    def weights_here(layer, m):
        for delta in range(1, levels):
            if relayed and delta == 2:
                pl.when(jnp.logical_not(middle))(arriving(layer, m, delta).wait_recv)
            else:
                arriving(layer, m, delta).wait_recv()
        for_spread(layer, m, lambda copy: copy.wait_send())
        if m % 2:
            own_piece(layer, m).wait()
        if relayed:
            pl.when(middle)(relay(layer, m).wait_send)

        return keep(slabs[m].at[layer], slab_outs[m].at[layer])

    skip = slabs[2].at[0, :, : adjoint.shape[3]]
    loads = [
        pltpu.make_async_copy(src, dst, load_sems.at[i])
        for i, (src, dst) in enumerate(zip(head_weights, (first, final, skip)))
    ]
    loads[0].start()
    loads[1].start()
    greet(place, levels)

    g_own = g.at[:, pl.ds(2 * place.y, 2), place.core]
    g_far = g.at[:, pl.ds(2 * (1 - place.y), 2), place.core]
    g_local = pltpu.make_async_copy(adjoint, g_own, g_sems.at[0, 0])
    g_peer = remote(adjoint, g_own, g_sems.at[0, 1], g_sems.at[1, 1], place.peer(2))
    g_sibling = remote(adjoint, g_own, g_sems.at[0, 2], g_sems.at[1, 2], place.sibling())
    g_pass = remote(g_far, g_far, g_sems.at[0, 3], g_sems.at[1, 3], place.sibling())
    part = exchange[0]
    lines = nrm.at[0]
    bufs = [nrm.at[0], nml.at[0], nrm.at[1], nml.at[1], lines]
    phases = [Exchange(place, p, buf, exchange) for p, buf in enumerate(bufs)]

    def own_half(s):
        return slice(s * HALF_BLOCK, (s + 1) * HALF_BLOCK)

    def enter(p, s, values):
        if p < 2 * LAYERS:
            values = values * root(values)
        bufs[p][phases[p].own(s), :] = values.astype(BF)
        phases[p].start(s)

    def leave(p, s):
        rows = own_half(s)
        total = phases[p].total(s)
        if p == 2 * LAYERS:
            grad_out[rows, :] = total
            return
        layer = p // 2
        if p % 2 == 0:
            values = xs[layer, rows, :] + total
            mid[layer, rows, :] = values
        else:
            values = mid[layer, rows, :] + total
            if layer + 1 < LAYERS:
                xs[layer + 1, rows, :] = values
        enter(p + 1, s, values)

    def run(p, compute, next_weights, more=()):
        more = list(more)
        hooks = [(3, lambda: leave(p, 0))]
        if p:
            hooks += [
                (0, lambda: phases[p - 1].finish_stream(1)),
                (1, lambda: leave(p - 1, 1)),
            ]
        hooks += [(2, lambda key=key: relay_on(*key)) for key in next_weights]
        phases[p].run(compute, hooks + more)

    send_weights(0, 3)
    o_cut[...] = jnp.zeros(o_cut.shape, BF)
    for layer in range(LAYERS):
        o_cut[layer, :rows, :] = w_out[layer]
    pl.when(trades)(o_trade.start)
    pl.when(jnp.logical_not(trades))(o_local.start)
    cut_weights(0)
    start_trade(0)
    xs[0] = x_in[...].astype(F32)
    for s in range(2):
        enter(0, s, xs[0, own_half(s), :])
    mask_local.start()
    for e in range(1, PLANE):
        mask_to(e).start()
    cut_weights(1)
    end_trade(0)
    send_weights(0, 0)

    @pl.when(trades)
    def _():
        o_trade.wait_recv()
        o_trade.wait_send()

    pl.when(jnp.logical_not(trades))(o_local.wait)
    send_weights(0, 1)
    send_weights(0, 2)
    start_trade(1)
    for copy in (g_local, g_peer, g_sibling):
        copy.start()
    mask_local.wait()
    for e in range(1, PLANE):
        mask_from(e).wait_recv()
        mask_to(e).wait_send()
    relay_on(0, 0)
    relay_on(0, 1)

    def second_layer():
        end_trade(1)
        send_weights(1, 0)
        send_weights(1, 1)

    slab_keeps = []
    for layer in range(LAYERS):
        wq, wo, wi, wd = [slab.at[layer] for slab in slabs]
        slab_keeps.append(weights_here(layer, 0))
        for n in range(0, wide_q.shape[0], 256):
            wide_q[n : n + 256, :] = dot(wq[n : n + 256, :], sel_q[...]).astype(BF)
        slab_keeps.append(weights_here(layer, 1))
        if layer:
            for copy in attn_saved:
                forget(copy)

        def attend(start, s, half, layer=layer, wo=wo):
            both = rows_at(start, 2 * BLOCK, 2 * BLOCK)
            projected = dot(nrm[layer, both, :], wide_q[...])
            cosine, sine = rope[:, :BLOCK], rope[:, BLOCK:]
            for block in range(2):
                rows = rows_at(start + block * BLOCK, BLOCK, BLOCK)
                chip = (place.y + half) % 2 * 2 + block
                allowed = mask[s, chip].reshape(BLOCK, BLOCK) > 0
                here = projected[block * BLOCK : (block + 1) * BLOCK]
                outs = []
                for h in range(heads):
                    def part_of(kind, h=h, here=here):
                        return here[:, kind * lanes + h * BLOCK : kind * lanes + (h + 1) * BLOCK]

                    turned = []
                    for kind in range(2):
                        value = part_of(kind)
                        value = value * cosine + pltpu.roll(value, BLOCK // 2, 1) * sine
                        turned.append(value.astype(BF))
                    query, key = turned
                    value = part_of(2).astype(BF)
                    qkv[rows, h * BLOCK : (h + 1) * BLOCK] = query
                    qkv[rows, lanes + h * BLOCK : lanes + (h + 1) * BLOCK] = key
                    qkv[rows, 2 * lanes + h * BLOCK : 2 * lanes + (h + 1) * BLOCK] = value
                    scores = dot(query, key, 1, 1) * (1.0 / math.sqrt(HDIM))
                    scores = jnp.where(allowed, scores, -1e30)
                    scores = jnp.exp(scores - jnp.max(scores, axis=-1, keepdims=True))
                    probs = (scores / jnp.sum(scores, axis=-1, keepdims=True)).astype(BF)
                    prb[rows, h * BLOCK : (h + 1) * BLOCK] = probs
                    outs.append(dot(probs, value).astype(BF))
                att[rows, :] = dot(jnp.concatenate(outs, axis=1), sel_o[...], 1, 1).astype(BF)
            part[s, half] = dot(att[both, :], wo[...]).astype(BF)

        more = [(1, second_layer)] if layer == 0 else []
        run(2 * layer, attend, ((layer, 2), (layer, 3)), more)
        attn_saved = [keep(src, dst.at[layer]) for src, dst in zip((qkv, prb, att), kept[2:5])]
        nrm_saved = keep(nrm.at[layer], kept[0].at[layer])
        if layer == 0:
            g_peer.wait_recv()
            g_pass.start()
        slab_keeps.append(weights_here(layer, 2))
        slab_keeps.append(weights_here(layer, 3))
        if layer == 0:
            send_weights(1, 2)
            send_weights(1, 3)
        if layer:
            for copy in mlp_saved:
                forget(copy)

        def perceptron(start, s, half, layer=layer, wi=wi, wd=wd):
            rows = rows_at(start, 2 * BLOCK, 2 * BLOCK)
            lifted = dot(nml[layer, rows, :], wi[...])
            root_two = math.sqrt(2.0 / math.pi)
            square = lifted * lifted
            tanh = jnp.tanh(root_two * lifted * (1.0 + 0.044715 * square))
            act[rows, :] = (0.5 * lifted * (1.0 + tanh)).astype(BF)
            slope = 0.5 * (1.0 + tanh) + 0.5 * lifted * (1.0 - tanh * tanh) * root_two * (
                1.0 + 3.0 * 0.044715 * square
            )
            gl[rows, :] = slope.astype(BF)
            part[s, half] = dot(act[rows, :], wd[...]).astype(BF)

        following = ((layer + 1, 0), (layer + 1, 1)) if layer + 1 < LAYERS else ()
        run(2 * layer + 1, perceptron, following)
        mlp_saved = [keep(src, dst.at[layer]) for src, dst in zip((gl, act), kept[5:7])]
        keep(nml.at[layer], kept[1].at[layer])
        if layer == 0:
            forget(nrm_saved)
            forget(slab_keeps[2])
            loads[2].start()
            loads[0].wait()
            loads[1].wait()
            index = lax.broadcasted_iota(jnp.int32, pick.shape, 0)
            offset = (2 * place.y + place.core) * (pick.shape[0] // (4 * levels))
            pick[...] = jnp.where(index - offset == head_lanes[...], 1.0, 0.0).astype(BF)
            for n in range(0, first.shape[0], 256):
                first_q[n : n + 256, :] = dot(first[n : n + 256, :], pick[...]).astype(BF)
            final_q[...] = dot(pick[...], final[...], 0, 0).astype(BF)

    g_local.wait()
    for copy in (g_sibling, g_pass):
        copy.wait_recv()
    loads[2].wait()
    bias_q = dot(jnp.broadcast_to(bias_first[...], (16, bias_first.shape[1])), pick[...])[:1]
    columns = g.shape[4]

    def head(start, s, half):
        rows = rows_at(start, 2 * BLOCK, 2 * BLOCK)
        pre = dot(lines[rows, :], first_q[...]) + bias_q
        gate = 1.0 / (1.0 + jnp.exp(-pre))
        hidden[rows, :] = (pre * gate).astype(BF)
        chips = pl.ds((place.y + half) % 2 * 2, 2)
        there = g[s, chips].reshape(2 * BLOCK, columns)
        grad_hidden = dot(there, final_q[...], 1, 1)
        gpre[rows, :] = (grad_hidden * (gate * (1.0 + pre * (1.0 - gate)))).astype(BF)
        whole = dot(gpre[rows, :], first_q[...], 1, 1)
        part[s, half] = whole.astype(BF)

        @pl.when(half == 0)
        def _():
            core = lax.broadcasted_iota(jnp.int32, (2 * BLOCK, 1), 0) // HALF_BLOCK % 2
            mine = jnp.where(core == place.core, there.astype(F32), 0.0).astype(BF)
            part[s, half] = (whole + dot(mine, skip[...], 1, 1)).astype(BF)

    run(2 * LAYERS, head, ())
    phases[2 * LAYERS].finish_stream(1)

    keep(lines, kept[7])
    keep(hidden, kept[8])
    keep(gpre, kept[9])
    for n in range(0, lines.shape[0], 2 * BLOCK):
        picked[n : n + 2 * BLOCK, :] = dot(lines[n : n + 2 * BLOCK, :], pick[...]).astype(BF)
    keep(picked, kept[10])
    keep(g, kept[11])
    leave(2 * LAYERS, 1)
    mine = []
    for x in range(2):
        for s in range(2):
            start = (8 * s + 4 * place.y + 2 * x + place.core) * HALF_BLOCK
            mine.append(lines[rows_at(start, HALF_BLOCK, HALF_BLOCK), :])
    mine = jnp.concatenate(mine, axis=0)
    pre = dot(mine, first[...]) + bias_first[...].astype(F32)
    hidden_all[...] = (pre / (1.0 + jnp.exp(-pre))).astype(BF)
    out = dot(hidden_all[...], final[...]) + bias_last[...].astype(F32)
    predictions[...] = (out + dot(mine, skip[...])).astype(BF)
    for copy in (g_peer, g_sibling, g_pass):
        copy.wait_send()
    for copy in kept_here:
        if not any(copy is other for other in waited):
            copy.wait()


def norm_back(values, q):
    scale = root(values)
    n = values * scale
    return scale * (q - n * jnp.mean(q * n, axis=-1, keepdims=True))


def backward_kernel(levels, *refs):
    (rope, sel_q, sel_o, gains, w_q, w_in) = refs[:6]
    dy_in, stored, head_stored = refs[6], refs[7:20], refs[20:25]
    (dx_out, small_out, q_out, o_out, i_out, d_out, q_gain, i_gain) = refs[25:33]
    (first_out, out_out, skip_out) = refs[33:36]
    exchange, ag = refs[36:41], refs[41]
    loaded, gp = refs[42:55], refs[55]
    stages, arrivals = refs[56:63], refs[63:70]
    own_sums, acc, o_acc = refs[70:74], refs[74], refs[75]
    o_cut, o_pasted = refs[76], refs[77]
    (small_own, small_x, small_z) = refs[78:81]
    z_sems, load_sems, small_sems, trade_sems, o_sems = refs[81:]
    (nml, act, gl, wi, wd, mid, nrm, qkv, prb, att, wq, wo, xs) = loaded
    part = exchange[0]
    place = Place()
    z = place.z
    heads = sel_o.shape[1] // BLOCK
    lanes = heads * BLOCK

    def load(layer, i):
        return pltpu.make_async_copy(stored[i].at[layer], loaded[i], load_sems.at[i])

    lines = ag.at[1]
    h_cols, half_width = small_own.shape[2], nrm.shape[1] // 2
    gpre, hidden = gp.at[:, :h_cols], nrm.at[:, :h_cols]
    picked = nrm.at[:, half_width : half_width + h_cols]
    g = qkv.at[:, : stages[5].shape[1]]
    head_loads = [
        pltpu.make_async_copy(src, dst, load_sems.at[len(loaded) + i])
        for i, (src, dst) in enumerate(zip(head_stored, (lines, gpre, hidden, picked, g)))
    ]
    mlp_part, attn_part = range(6), range(6, 13)
    dy_load = pltpu.make_async_copy(dy_in, dx_out, load_sems.at[len(loaded) + 5])
    dy_load.start()
    for copy in head_loads:
        copy.start()
    for i in mlp_part:
        load(LAYERS - 1, i).start()
    greet(place, levels)

    def count_of(m):
        return arrivals[m].shape[2]

    def slot(m, layer):
        return layer if m < 4 else 0

    relayed = levels == 4
    middle = (z == 1) | (z == 2)

    def send(layer, m, delta):
        there = (z + delta) % levels
        return remote(
            stages[m].at[rows_at(there * count_of(m), count_of(m))],
            arrivals[m].at[slot(m, layer), delta - 1],
            z_sems.at[0, layer, m, delta - 1],
            z_sems.at[1, layer, m, delta - 1],
            place.level(there),
        )

    def far(delta):
        there = (z + delta) % levels
        return (z + there == 3) & (z * there == 0)

    def hand(layer, m, delta):
        there = (z + delta) % levels
        return remote(
            stages[m].at[rows_at(there * count_of(m), count_of(m))],
            arrivals[m].at[slot(m, layer), levels - 1],
            z_sems.at[0, layer, m, delta - 1],
            z_sems.at[1, layer, m, levels - 1],
            place.level(1 + z // 3),
        )

    def send_first(layer, m):
        for delta in range(1, levels):
            if not relayed:
                send(layer, m, delta).start()
            elif delta == 2:
                pl.when(jnp.logical_not(middle))(send(layer, m, delta).start)
            else:
                pl.when(far(delta))(hand(layer, m, delta).start)
                pl.when(jnp.logical_not(far(delta)))(send(layer, m, delta).start)

    def send_rest(layer, m):
        if relayed:
            @pl.when(middle)
            def _():
                hand(layer, m, 1).wait_recv()
                rows = rows_at((z + 2) % levels * count_of(m), count_of(m))
                total = stages[m][rows, :].astype(F32)
                total = total + arrivals[m][slot(m, layer), levels - 1].astype(F32)
                stages[m][rows, :] = total.astype(BF)
                send(layer, m, 2).start()

    def sent(layer, m):
        for delta in range(1, levels):
            send(layer, m, delta).wait_send()

    def result(layer, m):
        if m > 4:
            return (out_out, skip_out)[m - 5]
        if m == 3:
            return d_out.at[layer]
        return own_sums[min(m, 3)].at[slot(m, layer)]

    def weight_grad(layer, m, left, right, tile):
        width = left.shape[1]
        if m < 4 and layer + 1 < LAYERS:
            sent(layer + 1, m)
        if width % tile:
            stages[m][...] = dot(left[...], right[...], 0, 0).astype(BF)
        else:
            def body(i, carry):
                here = rows_at(i * tile, tile, tile)
                stages[m][here, :] = dot(left[:, here], right[...], 0, 0).astype(BF)
                return carry

            lax.fori_loop(0, width // tile, body, 0)
        send_first(layer, m)
        out = result(layer, m)
        out[...] = stages[m][rows_at(z * count_of(m), count_of(m)), :].astype(out.dtype)

    bufs = [ag.at[p % 2] for p in range(PHASES)]
    phases = [Exchange(place, p, buf, exchange) for p, buf in enumerate(bufs)]

    def own_half(s):
        return slice(s * HALF_BLOCK, (s + 1) * HALF_BLOCK)

    def enter(p, s):
        bufs[p][phases[p].own(s), :] = dx_out[own_half(s), :].astype(BF)
        phases[p].start(s)

    def leave(p, s):
        rows = own_half(s)
        values = (mid if p % 2 == 0 else xs)[rows, :]
        dx_out[rows, :] += norm_back(values, phases[p].total(s))
        if p + 1 < PHASES:
            enter(p + 1, s)

    def run(p, compute, relays):
        hooks = [(3, lambda: leave(p, 0))]
        hooks += [(2, lambda key=key: send_rest(*key)) for key in relays]
        phases[p].run(compute, hooks)
        phases[p].finish_stream(1)

    dy_load.wait()
    for s in range(2):
        enter(0, s)

    for copy in head_loads:
        copy.wait()
    last = LAYERS - 1
    bias_sum = jnp.sum(gpre[...].astype(F32), axis=0, keepdims=True)
    small_own[1] = jnp.broadcast_to(bias_sum, small_own.shape[1:])
    to_x = remote(
        small_own.at[1], small_x, small_sems.at[0, 0], small_sems.at[1, 0], place.peer(1)
    )
    to_x.start()
    weight_grad(last, 5, hidden, g, 2 * BLOCK)
    weight_grad(last, 6, picked, g, 2 * BLOCK)
    weight_grad(last, 4, lines, gpre, 2 * BLOCK)
    g_sum = jnp.sum(g[...].astype(F32), axis=0, keepdims=True)
    to_x.wait()
    small_z[0, :, : g_sum.shape[1]] = jnp.broadcast_to(g_sum, (8, g_sum.shape[1]))
    small_z[0, :, g_sum.shape[1] :] = small_own[1] + small_x[...]
    to_z = [
        remote(
            small_z.at[0], small_z.at[d], small_sems.at[0, d], small_sems.at[1, d],
            place.level((z + d) % levels),
        )
        for d in range(1, levels)
    ]
    for copy in to_z:
        copy.start()
    for i in attn_part:
        load(last, i).start()

    relays = [(last, 5), (last, 6), (last, 4)]
    for layer in reversed(range(LAYERS)):
        p = 2 * (LAYERS - 1 - layer)
        buf = bufs[p]
        for i in mlp_part:
            load(layer, i).wait()

        def perceptron(start, s, half, buf=buf):
            rows = rows_at(start, 2 * BLOCK, 2 * BLOCK)
            grad_act = dot(buf[rows, :], wd[...], 1, 1)
            gl[rows, :] = (grad_act * gl[rows, :].astype(F32)).astype(BF)
            part[s, half] = dot(gl[rows, :], wi[...], 1, 1).astype(BF)

        run(p, perceptron, relays)
        weight_grad(layer, 3, act, buf, BLOCK)
        leave(p, 1)
        weight_grad(layer, 2, nml, gl, 2 * BLOCK)
        if layer > 0:
            for i in mlp_part:
                load(layer - 1, i).start()
        for i in attn_part:
            load(layer, i).wait()
        buf = bufs[p + 1]

        def attend(start, s, half, buf=buf):
            cosine, sine = rope[:, :BLOCK], rope[:, BLOCK:]
            both = rows_at(start, 2 * BLOCK, 2 * BLOCK)
            grad_heads = dot(buf[both, :], wo[...], 1, 1).astype(BF)
            grad_heads = dot(grad_heads, sel_o[...]).astype(BF)
            for block in range(2):
                rows = rows_at(start + block * BLOCK, BLOCK, BLOCK)
                outs = [[], [], []]
                for h in range(heads):
                    def part_of(kind, h=h, rows=rows):
                        low = kind * lanes + h * BLOCK
                        return qkv[rows, low : low + BLOCK]

                    query, key, value = part_of(0), part_of(1), part_of(2)
                    probs = prb[rows, h * BLOCK : (h + 1) * BLOCK]
                    grad_head = grad_heads[
                        block * BLOCK : (block + 1) * BLOCK, h * BLOCK : (h + 1) * BLOCK
                    ]
                    outs[2].append(dot(probs, grad_head, 0, 0).astype(BF))
                    grad_probs = dot(grad_head, value, 1, 1)
                    probs = probs.astype(F32)
                    inner = jnp.sum(probs * grad_probs, axis=-1, keepdims=True)
                    grad_scores = (probs * (grad_probs - inner)).astype(BF)
                    for kind, turned in (
                        (0, dot(grad_scores, key)),
                        (1, dot(grad_scores, query, 0, 0)),
                    ):
                        turned = turned * (1.0 / math.sqrt(HDIM))
                        turned = turned * cosine - pltpu.roll(turned, BLOCK // 2, 1) * sine
                        outs[kind].append(turned.astype(BF))
                packed = jnp.concatenate(outs[0] + outs[1] + outs[2], axis=1)
                gp[rows, :] = dot(packed, sel_q[...], 1, 1).astype(BF)
            part[s, half] = dot(gp[both, :], wq[...], 1, 1).astype(BF)

        run(p + 1, attend, [(layer, 3), (layer, 2)])
        weight_grad(layer, 0, nrm, gp, 2 * BLOCK)
        if layer > 0:
            leave(p + 1, 1)
            weight_grad(layer, 1, att, buf, 2 * BLOCK)
            for i in attn_part:
                load(layer - 1, i).start()
        else:
            weight_grad(layer, 1, att, buf, 2 * BLOCK)
            leave(p + 1, 1)
        relays = [(layer, 0), (layer, 1)]
    for key in relays:
        send_rest(*key)

    total = small_z[0]
    for copy, d in zip(to_z, range(1, levels)):
        copy.wait_recv()
        total = total + small_z[d]
    small_out[...] = total
    for copy in to_z:
        copy.wait_send()
    rows = w_q.shape[1]
    pad_rows = up16(rows)
    kinds = {0: 0, 2: 1, 4: 2}

    def cut_at(m, t):
        start = rows_at((t + (PLANE if m == 2 else 0)) * pad_rows, pad_rows)
        low = {0: 0, 2: 0, 4: nml.shape[1] // 2}[m]
        return nml.at[start, low : low + stages[m].shape[1]]

    def pasted_at(layer, m, t):
        start = rows_at((slot(m, layer) * PLANE + t) * pad_rows, pad_rows)
        return {0: gl, 2: act, 4: wd}[m].at[start, : stages[m].shape[1]]

    def trade(layer, m, e):
        kind = kinds[m]
        return remote(
            cut_at(m, place.rank(e)), pasted_at(layer, m, place.rank()),
            trade_sems.at[0, layer, kind, e], trade_sems.at[1, layer, kind, e], place.other(e),
        )

    def traded(layer, m, e):
        there = pasted_at(layer, m, place.rank(e))
        return remote(
            there, there, trade_sems.at[0, layer, kinds[m], e],
            trade_sems.at[1, layer, kinds[m], e], place.other(e),
        )

    def own_trade(layer, m):
        own = place.rank()
        return pltpu.make_async_copy(
            cut_at(m, own), pasted_at(layer, m, own), trade_sems.at[0, layer, kinds[m], 0]
        )

    stayed = set()

    def wait_own_trade(layer, m):
        if (layer, m) not in stayed:
            own_trade(layer, m).wait()
            stayed.add((layer, m))

    def pasted(layer, m, t):
        return pasted_at(layer, m, t)[:rows, :].astype(F32)

    trades = place.trades(levels)

    def o_trade(layer):
        return remote(
            o_cut.at[layer], o_pasted.at[layer], o_sems.at[0, layer], o_sems.at[1, layer],
            place.indexed(place.held(levels)),
        )

    def o_local(layer):
        return pltpu.make_async_copy(o_cut.at[layer], o_pasted.at[layer], o_sems.at[0, layer])

    def finalize(layer, m):
        own = result(layer, m)
        if m == 3 or m > 4:
            total = own
        else:
            total = o_acc if m == 1 else acc.at[:, : own.shape[1]]
            total[...] = own[...].astype(F32)
        for delta in range(1, levels):
            def add(delta=delta):
                send(layer, m, delta).wait_recv()
                total[...] += arrivals[m][slot(m, layer), delta - 1].astype(F32)

            if relayed and delta != 2:
                source = (z + levels - delta) % levels
                pl.when(jnp.logical_not((z + source == 3) & (z * source == 0)))(add)
            else:
                add()
        if m > 3 or layer == 0:
            sent(layer, m)
        if m == 1:
            o_cut[layer] = total[...].astype(BF)
            pl.when(trades)(o_trade(layer).start)
            pl.when(jnp.logical_not(trades))(o_local(layer).start)
        elif m in kinds:
            if m < 4 and layer + 1 < LAYERS:
                wait_own_trade(layer + 1, m)
                for e in range(1, PLANE):
                    trade(layer + 1, m, e).wait_send()
            values = total[...].astype(BF).astype(F32)
            for t in range(PLANE):
                cut_at(m, t)[:rows, :] = values[t * rows : (t + 1) * rows].astype(BF)
            own_trade(layer, m).start()
            for e in range(1, PLANE):
                trade(layer, m, e).start()

    def wait_trade(layer, m):
        wait_own_trade(layer, m)
        for e in range(1, PLANE):
            traded(layer, m, e).wait_recv()
        if m > 3 or layer == 0:
            for e in range(1, PLANE):
                trade(layer, m, e).wait_send()

    span = w_q.shape[2] // 3 // PLANE
    ff_rows = w_in.shape[2] // PLANE // levels
    padded_rows = stages[2].shape[1] // levels

    def assemble(layer):
        wait_trade(layer, 0)
        ranks = [pasted(layer, 0, t) for t in range(PLANE)]
        parts = [rank[:, kind * span : (kind + 1) * span] for kind in range(3) for rank in ranks]
        whole = jnp.concatenate(parts, axis=1)
        q_out[layer] = whole * gains[0, layer]
        q_gain[layer] = jnp.sum(whole * w_q[layer].astype(F32), axis=1, keepdims=True)

    def assemble_mlp(layer):
        wait_trade(layer, 2)
        ranks = [pasted(layer, 2, t) for t in range(PLANE)]
        parts = [
            rank[:, zz * padded_rows : zz * padded_rows + ff_rows]
            for zz in range(levels) for rank in ranks
        ]
        whole = jnp.concatenate(parts, axis=1)
        i_out[layer] = whole * gains[1, layer]
        i_gain[layer] = jnp.sum(whole * w_in[layer].astype(F32), axis=1, keepdims=True)

    def assemble_out(layer):
        @pl.when(trades)
        def _():
            o_trade(layer).wait_recv()
            o_trade(layer).wait_send()

        pl.when(jnp.logical_not(trades))(o_local(layer).wait)
        o_out[layer] = o_pasted[layer, :rows, :].astype(F32)

    head_rows, head_share = out_out.shape[0], first_out.shape[1] // 4 // levels

    def assemble_head():
        wait_trade(last, 4)
        sums = []
        for q in range(4):
            sums.append(pasted(last, 4, 2 * q) + pasted(last, 4, 2 * q + 1))
        parts = []
        for zz in range(levels):
            for q in range(4):
                parts.append(sums[q][:, zz * head_rows : zz * head_rows + head_share])
        first_out[...] = jnp.concatenate(parts, axis=1)

    for key in [(last, 5), (last, 6), (last, 4)] + [(last, m) for m in (3, 2, 0, 1)]:
        finalize(*key)
    for layer in reversed(range(LAYERS - 1)):
        finalize(layer, 3)
        finalize(layer, 2)
    assemble_head()
    for layer in reversed(range(LAYERS)):
        if layer == 0:
            finalize(layer, 0)
            finalize(layer, 1)
        assemble_mlp(layer)
        assemble(layer)
        assemble_out(layer)


def shape(*dims, dtype=BF):
    return jax.ShapeDtypeStruct(dims, dtype)


def rope_table():
    position = np.arange(BLOCK) % ROW_LEN
    inverse = ROTARY_BASE ** (-np.arange(HALF) / HALF)
    angles = (position[:, None] * inverse[None, :]).astype(np.float32)
    table = np.zeros((BLOCK, 2, 2, BLOCK // 2), np.float32)
    table[:, 0, :, :HALF] = np.cos(angles)[:, None]
    table[:, 1, 0, :HALF] = -np.sin(angles)
    table[:, 1, 1, :HALF] = np.sin(angles)
    return table.reshape(BLOCK, 2 * BLOCK)


def lane_of(index):
    head, inside = divmod(index, HDIM)
    half, place = divmod(inside, HALF)
    return head * BLOCK + half * (BLOCK // 2) + place


def per_device(devices, x, segments, padded, w_qkv, w_out, w_in, w_down, gain_attn, gain_mlp,
               head_first, head_first_bias, head_final, head_bias, head_skip, adjoint):
    levels = devices // PLANE
    width = x.shape[1]
    ff = w_in.shape[2]
    columns = head_final.shape[1]
    tokens = PLANE * BLOCK
    heads = width // HDIM // PLANE
    span = heads * HDIM
    rows = width // devices
    out_rows = up16(rows)
    ff_rows = ff // devices
    down_rows = up16(ff_rows)
    head_share = 2 * width // devices
    head_rows = up16(head_share)
    used_cols, o_rows, f_cols = 3 * span, levels * out_rows, levels * down_rows
    h_cols = -(-levels * head_rows // 128) * 128
    q_cols = -(-used_cols // 128) * 128
    lanes = heads * BLOCK

    sel_q = np.zeros((q_cols, 3 * lanes), np.float32)
    sel_o = np.zeros((o_rows, lanes), np.float32)
    for e in range(span):
        for kind in range(3):
            sel_q[kind * span + e, kind * lanes + lane_of(e)] = 1
        sel_o[e // rows * out_rows + e % rows, lane_of(e)] = 1
    sel_q, sel_o = jnp.asarray(sel_q, BF), jnp.asarray(sel_o, BF)
    rope = jnp.asarray(rope_table())
    head_lanes = np.full((1, h_cols), -width, np.int32)
    for zz in range(levels):
        here = slice(zz * head_rows, zz * head_rows + head_share)
        head_lanes[0, here] = 4 * head_share * zz + np.arange(head_share)
    head_lanes = jnp.asarray(head_lanes)

    seg = segments.reshape(2, HALF_BLOCK)
    open_key = padded.reshape(2, HALF_BLOCK) == 0
    within = jnp.arange(HALF_BLOCK)
    static = within[:, None] // ROW_LEN == within[None, :] // ROW_LEN
    static = static & (within[None, :] <= within[:, None])
    allowed = static[None] & (seg[:, :, None] == seg[:, None, :])
    allowed = allowed & (open_key[:, None, :] | (within[:, None] == within[None, :])[None])
    core = lax.axis_index("wide") % 2
    side = jnp.arange(BLOCK)[None, None, :] // HALF_BLOCK == core
    own_mask = (jnp.concatenate([allowed, allowed], axis=-1) & side).astype(BF)

    gains = jnp.stack([gain_attn, gain_mlp]).astype(F32)[..., None]
    d_piece = w_down
    if down_rows != ff_rows:
        d_piece = jnp.pad(w_down, [(0, 0), (0, down_rows - ff_rows), (0, 0)])
    pad_rows = up16(rows)

    layer_shapes = [
        (tokens, width), (tokens, width), (tokens, 3 * lanes), (tokens, lanes), (tokens, o_rows),
        (tokens, f_cols), (tokens, f_cols),
    ]
    slab_shapes = [(width, q_cols), (o_rows, width), (width, f_cols), (f_cols, width)]
    blocks = (2, 4, 2, HALF_BLOCK, columns)
    outs = [
        shape(2 * BLOCK, columns), shape(BLOCK, width, dtype=F32),
        shape(LAYERS, BLOCK, width, dtype=F32), shape(LAYERS, BLOCK, width, dtype=F32),
    ]
    vmem_outs = len(outs)
    outs += [shape(LAYERS, *dims) for dims in layer_shapes]
    outs += [shape(tokens, width)] + [shape(tokens, h_cols)] * 3 + [shape(*blocks)]
    outs += [shape(LAYERS, *dims) for dims in slab_shapes]
    (predictions, grad_final, xs, mid, nrm, nml, qkv, prb, att, gl, act, lines, hidden, gpre,
     picked, g, wq, wo, wi, wd) = pl.pallas_call(
        lambda *refs: forward_kernel(levels, *refs),
        out_shape=outs,
        in_specs=[VMEM] * 13 + [ANY] * 4,
        out_specs=[VMEM] * vmem_outs + [ANY] * (len(outs) - vmem_outs),
        scratch_shapes=exchange_scratch(width, PHASES + 1)
        + [pltpu.VMEM((LAYERS,) + dims, BF) for dims in layer_shapes[:2]]
        + [pltpu.VMEM(dims, BF) for dims in layer_shapes[2:]]
        + [pltpu.VMEM((LAYERS,) + dims, BF) for dims in slab_shapes]
        + [
            pltpu.VMEM((width, 3 * lanes), BF), pltpu.VMEM((width, width), BF),
            pltpu.VMEM((width, columns), BF), pltpu.VMEM((width, h_cols), BF),
            pltpu.VMEM((width, h_cols), BF), pltpu.VMEM((h_cols, columns), BF),
            pltpu.VMEM(blocks, BF), pltpu.VMEM((tokens, h_cols), BF),
            pltpu.VMEM((tokens, h_cols), BF), pltpu.VMEM((tokens, h_cols), BF),
            pltpu.VMEM((2 * BLOCK, width), BF),
            pltpu.VMEM((2, 4, 2, HALF_BLOCK, BLOCK), BF),
            pltpu.VMEM((LAYERS, PLANE, pad_rows, q_cols + f_cols), BF),
            pltpu.VMEM((LAYERS, PLANE, pad_rows, q_cols + f_cols), BF),
            pltpu.VMEM((LAYERS, out_rows, width), BF),
            pltpu.VMEM((LAYERS, out_rows, width), BF),
            pltpu.SemaphoreType.DMA((3, LAYERS, 4, levels - 1)),
            pltpu.SemaphoreType.DMA((LAYERS, 4)),
            pltpu.SemaphoreType.DMA((32,)),
            pltpu.SemaphoreType.DMA((3,)),
            pltpu.SemaphoreType.DMA((2, 4)),
            pltpu.SemaphoreType.DMA((2, LAYERS, PLANE)),
            pltpu.SemaphoreType.DMA((2, PLANE)),
            pltpu.SemaphoreType.DMA((2,)),
        ],
        compiler_params=pltpu.CompilerParams(
            collective_id=1, has_side_effects=True, vmem_limit_bytes=62 * MIB
        ),
        name="decoder_forward",
    )(x, own_mask, rope, sel_q, sel_o, head_lanes,
      jnp.swapaxes(adjoint.reshape(2, 2, HALF_BLOCK, columns), 0, 1), head_first_bias[None],
      head_bias[None], gains, w_qkv, w_in, w_out, d_piece, head_first, head_final, head_skip)

    chunk = [PLANE * rows, out_rows, PLANE * rows, down_rows, PLANE * rows, head_rows, head_rows]
    cols = [q_cols, width, f_cols, width, h_cols, columns, columns]
    stage_rows = [levels * n for n in chunk[:5]] + [h_cols] * 2
    kept_shapes = [
        (tokens, width), (tokens, f_cols), (tokens, f_cols), (width, f_cols), (f_cols, width),
        (BLOCK, width), (tokens, width), (tokens, 3 * lanes), (tokens, lanes), (tokens, o_rows),
        (width, q_cols), (o_rows, width), (BLOCK, width),
    ]
    small_cols = columns + h_cols
    outs = [
        shape(BLOCK, width, dtype=F32), shape(8, small_cols, dtype=F32),
        shape(LAYERS, rows, 3 * width, dtype=F32), shape(LAYERS, rows, width, dtype=F32),
        shape(LAYERS, rows, ff, dtype=F32), shape(LAYERS, down_rows, width, dtype=F32),
        shape(LAYERS, rows, 1, dtype=F32), shape(LAYERS, rows, 1, dtype=F32),
        shape(rows, width, dtype=F32), shape(head_rows, columns, dtype=F32),
        shape(head_rows, columns, dtype=F32),
    ]
    (input_grad, small, q_grad, o_grad, i_grad, d_grad, q_gain, i_gain, g_first, g_out,
     g_skip) = pl.pallas_call(
        lambda *refs: backward_kernel(levels, *refs),
        out_shape=outs,
        in_specs=[VMEM] * 6 + [ANY] * 19,
        out_specs=[VMEM] * len(outs),
        scratch_shapes=exchange_scratch(width, PHASES)
        + [pltpu.VMEM((2, tokens, width), BF)]
        + [pltpu.VMEM(dims, F32 if dims[0] == BLOCK else BF) for dims in kept_shapes]
        + [pltpu.VMEM((tokens, q_cols), BF)]
        + [pltpu.VMEM((stage_rows[m], cols[m]), BF) for m in range(7)]
        + [
            pltpu.VMEM((LAYERS if m < 4 else 1, levels, chunk[m], cols[m]), BF)
            for m in range(7)
        ]
        + [
            pltpu.VMEM((LAYERS if m < 4 else 1, chunk[m], cols[m]), BF) for m in (0, 1, 2, 4)
        ]
        + [pltpu.VMEM((chunk[0], max(f_cols, q_cols)), F32), pltpu.VMEM((out_rows, width), F32)]
        + [pltpu.VMEM((LAYERS, out_rows, width), BF)] * 2
        + [
            pltpu.VMEM((2, 8, h_cols), F32), pltpu.VMEM((8, h_cols), F32),
            pltpu.VMEM((levels, 8, small_cols), F32),
            pltpu.SemaphoreType.DMA((2, LAYERS, 7, levels)),
            pltpu.SemaphoreType.DMA((20,)),
            pltpu.SemaphoreType.DMA((2, levels)),
            pltpu.SemaphoreType.DMA((2, LAYERS, 3, PLANE)),
            pltpu.SemaphoreType.DMA((2, LAYERS)),
        ],
        compiler_params=pltpu.CompilerParams(
            collective_id=2, has_side_effects=True, vmem_limit_bytes=62 * MIB
        ),
        name="decoder_backward",
    )(rope, sel_q, sel_o, gains, w_qkv, w_in, grad_final, nml, act, gl, wi, wd, mid, nrm, qkv, prb,
      att, wq, wo, xs, lines, gpre, hidden, picked, g.reshape(tokens, columns))

    z, narrow = lax.axis_index("wide") // 4, lax.axis_index("narrow")
    g_first_bias = lax.dynamic_slice(small[0], (columns + z * head_rows + narrow * rows,), (rows,))
    return (
        predictions, input_grad, q_grad, o_grad, i_grad, d_grad[:, :ff_rows], q_gain[..., 0],
        i_gain[..., 0], g_first, g_first_bias, g_out[:head_share], small[0, :columns],
        g_skip[:head_share],
    )


def solution(mesh):
    devices = mesh.shape["wide"] * mesh.shape["narrow"]
    both = ("wide", "narrow")
    weight, gain = P(None, both, None), P(None, both)
    return jax.shard_map(
        lambda *arrays: per_device(devices, *arrays),
        mesh=mesh,
        in_specs=(
            P(both, None), P(both), P(both), weight, weight, weight, weight, gain, gain, P(), P(),
            P(None, "narrow"), P("narrow"), P(None, "narrow"), P("wide", "narrow"),
        ),
        out_specs=(
            P("wide", "narrow"), P(both, None), weight, weight, weight, weight, gain, gain,
            P(both, None), P(both), P("wide", "narrow"), P("narrow"), P("wide", "narrow"),
        ),
        check_vma=False,
    )
```

```python
import math

import jax
import jax.numpy as jnp
import numpy as np
from jax import lax
from jax.experimental import pallas as pl
from jax.experimental.pallas import tpu as pltpu
from jax.sharding import PartitionSpec as P

HDIM = 80
HALF = HDIM // 2
LAYERS = 2
ROW_LEN = 16
BLOCK = 128
HALF_BLOCK = BLOCK // 2
PLANE = 8
PHASES = 2 * LAYERS
MESH = pl.DeviceIdType.MESH
BF = jnp.bfloat16
F32 = jnp.float32
EPS = 1e-06
ROTARY_BASE = 10000.0
MIB = 1024 * 1024
VMEM = pl.BlockSpec(memory_space=pltpu.VMEM)
ANY = pl.BlockSpec(memory_space=pl.ANY)


def up16(rows):
    return -(-rows // 16) * 16


def rows_at(start, count, step=16):
    return pl.ds(pl.multiple_of(start, step), count)


def dot(a, b, ca=1, cb=0):
    return lax.dot_general(a, b, (((ca,), (cb,)), ((), ())), preferred_element_type=F32)


class Place:
    def __init__(self):
        wide = lax.axis_index("wide")
        self.x = lax.axis_index("narrow")
        self.core = wide % 2
        self.y = (wide // 2) % 2
        self.z = wide // 4

    def device(self, z, y, core, x):
        return (z * 4 + y * 2 + core, x)

    def sibling(self):
        return self.device(self.z, self.y, 1 - self.core, self.x)

    def major(self, s, far=0):
        return (self.y + s * (self.x - self.y) + far) % 2

    def minor(self, s, near=0):
        return (self.x + s * (self.y - self.x) + near) % 2

    def near(self, s):
        return self.device(self.z, (self.y + s) % 2, self.core, (self.x + 1 - s) % 2)

    def far(self, s):
        return self.device(self.z, (self.y + 1 - s) % 2, self.core, (self.x + s) % 2)

    def level(self, z):
        return self.device(z, self.y, self.core, self.x)

    def turned(self, e):
        return (self.y + e // 4) % 2, (self.core + e // 2) % 2, (self.x + e) % 2

    def other(self, e):
        return self.device(self.z, *self.turned(e))

    def rank(self, e=0):
        y, core, x = self.turned(e)
        return 4 * y + 2 * core + x

    def indexed(self, index):
        return (index // 2, index % 2)

    def holder(self, levels):
        index = PLANE * self.z + self.rank()
        return index % levels * PLANE + index // levels

    def held(self, levels):
        return levels * self.rank() + self.z

    def trades(self, levels):
        return self.holder(levels) != PLANE * self.z + self.rank()


def greet(place, levels):
    barrier = pltpu.get_barrier_semaphore()
    others = [place.other(e) for e in range(1, PLANE)]
    others += [place.level((place.z + d) % levels) for d in range(1, levels)]
    for other in others:
        pl.semaphore_signal(barrier, inc=1, device_id=other, device_id_type=MESH)
    trades = place.trades(levels)

    @pl.when(trades)
    def _():
        for index in (place.holder(levels), place.held(levels)):
            pl.semaphore_signal(
                barrier, inc=1, device_id=place.indexed(index), device_id_type=MESH
            )
        pl.semaphore_wait(barrier, len(others) + 2)

    @pl.when(jnp.logical_not(trades))
    def _():
        pl.semaphore_wait(barrier, len(others))


def remote(src, dst, send, recv, device):
    return pltpu.make_async_remote_copy(
        src_ref=src, dst_ref=dst, send_sem=send, recv_sem=recv, device_id=device,
        device_id_type=MESH,
    )


class Exchange:
    def __init__(self, place, phase, buf, scratch):
        (self.part, self.recv_s, self.send_f, self.recv_f, self.send_n, self.recv_n, self.sems) = scratch
        self.place, self.phase, self.buf = place, phase, buf

    def copy(self, s, kind, src, dst, device):
        sems = self.sems
        return remote(
            src, dst, sems.at[self.phase, s, 0, kind], sems.at[self.phase, s, 1, kind], device
        )

    def block(self, s, far, near, core):
        place = self.place
        return self.buf.at[s, place.major(s, far), place.minor(s, near), core]

    def own(self, s):
        return (s, self.place.major(s), self.place.minor(s), self.place.core)

    def to_near(self, s, far=0, near=0):
        rows = self.block(s, far, near, self.place.core)
        return self.copy(s, 0, rows, rows, self.place.near(s))

    def to_far(self, s, far=0, near=0):
        rows = self.block(s, far, near, self.place.core)
        return self.copy(s, 1, rows, rows, self.place.far(s))

    def pass_far(self, s, far=0, near=1):
        rows = self.block(s, far, near, self.place.core)
        return self.copy(s, 2, rows, rows, self.place.far(s))

    def sibling(self, s, kind, core):
        if kind < 2:
            rows = self.block(s, 0, kind, core)
        else:
            rows = self.buf.at[s, self.place.major(s, 1), :, core]
        return self.copy(s, 3 + kind, rows, rows, self.place.sibling())

    def to_sibling(self, s, kind):
        return self.sibling(s, kind, self.place.core)

    def from_sibling(self, s, kind):
        return self.sibling(s, kind, 1 - self.place.core)

    def sum_sibling(self, s, half):
        src = self.part.at[s, half, :, 1 - self.place.core]
        sems = self.sems
        return remote(
            src, self.recv_s.at[s, half], sems.at[self.phase, s, 0, 6 + half],
            sems.at[self.phase, s, 1, 6 + half], self.place.sibling(),
        )

    def sum_far(self, s):
        return self.copy(s, 8, self.send_f.at[s], self.recv_f.at[s], self.place.far(s))

    def sum_near(self, s):
        return self.copy(s, 9, self.send_n.at[s], self.recv_n.at[s], self.place.near(s))

    def start(self, s):
        self.to_near(s).start()
        self.to_far(s).start()
        self.to_sibling(s, 0).start()

    def far_stage(self, s):
        self.sum_sibling(s, 1).wait_recv()
        own = self.part[s, 1, :, self.place.core].astype(F32)
        self.send_f[s] = (own + self.recv_s[s, 1].astype(F32)).astype(BF)
        self.sum_far(s).start()

    def summed(self, s, minor):
        own = self.part[s, 0, minor, self.place.core].astype(F32)
        return own + self.recv_s[s, 0, minor].astype(F32) + self.recv_f[s, minor].astype(F32)

    def near_stage(self, s):
        self.sum_sibling(s, 0).wait_recv()
        self.sum_far(s).wait_recv()
        self.send_n[s] = self.summed(s, self.place.minor(s, 1)).astype(BF)
        self.sum_near(s).start()

    def total(self, s):
        self.sum_near(s).wait_recv()
        total = self.summed(s, self.place.minor(s)) + self.recv_n[s].astype(F32)
        self.to_near(s).wait_send()
        self.to_far(s).wait_send()
        self.pass_far(s).wait_send()
        for kind in range(3):
            self.to_sibling(s, kind).wait_send()
        for half in range(2):
            self.sum_sibling(s, half).wait_send()
        self.sum_far(s).wait_send()
        self.sum_near(s).wait_send()
        return total

    def run(self, compute, hooks):
        def body(i, carry):
            s, half = i // 2, i % 2

            @pl.when(half == 0)
            def _():
                self.to_near(s, 0, 1).wait_recv()
                self.pass_far(s).start()
                self.to_sibling(s, 1).start()

            for at, hook in hooks:
                pl.when(i == at)(hook)

            @pl.when(half == 0)
            def _():
                self.from_sibling(s, 0).wait_recv()
                self.from_sibling(s, 1).wait_recv()

            @pl.when(half == 1)
            def _():
                self.to_far(s, 1, 0).wait_recv()
                self.pass_far(s, 1, 1).wait_recv()
                self.to_sibling(s, 2).start()

            @pl.when(i == 2)
            def _():
                self.far_stage(0)

            @pl.when(half == 1)
            def _():
                self.from_sibling(s, 2).wait_recv()

            major = self.place.major(s, half)
            compute(s * 8 * HALF_BLOCK + major * 4 * HALF_BLOCK, s, half, major)
            self.sum_sibling(s, half).start()
            return carry

        lax.fori_loop(0, 4, body, 0)
        self.near_stage(0)
        self.far_stage(1)


def exchange_scratch(width, phases):
    return [
        pltpu.VMEM((2, 2, 2, 2, HALF_BLOCK, width), BF),
        pltpu.VMEM((2, 2, 2, HALF_BLOCK, width), BF),
        pltpu.VMEM((2, 2, HALF_BLOCK, width), BF),
        pltpu.VMEM((2, 2, HALF_BLOCK, width), BF),
        pltpu.VMEM((2, HALF_BLOCK, width), BF),
        pltpu.VMEM((2, HALF_BLOCK, width), BF),
        pltpu.SemaphoreType.DMA((phases, 2, 2, 10)),
    ]


def flat(ref, columns=slice(None)):
    if len(ref.shape) == 2:
        return ref[:, columns]
    values = ref[(slice(None),) * 5 + (columns,)]
    return values.reshape(-1, values.shape[-1])


def write_part(part, s, half, values, w, contracted):
    width = part.shape[-1]
    step = width // 2
    for n in range(0, width, step):
        columns = slice(n, n + step)
        side = w[:, columns] if contracted == 0 else w[columns, :]
        part[s, half, :, :, :, columns] = blocked(dot(values, side, 1, contracted).astype(BF))


def blocked(values):
    return values.reshape(2, 2, HALF_BLOCK, values.shape[-1])


def root(values):
    return lax.rsqrt(jnp.mean(values * values, axis=-1, keepdims=True) + EPS)


def forward_kernel(levels, *refs):
    (x_in, own_mask, rope, sel_q, sel_o, head_lanes, adjoint, bias_first, bias_last) = refs[:9]
    (gains, w_q, w_in, w_out) = refs[9:13]
    w_down, head_weights = refs[13], refs[14:17]
    (predictions, grad_out, xs, mid) = refs[17:21]
    kept, (slab_q, slab_o, slab_i, slab_d) = refs[21:33], refs[33:37]
    exchange = refs[37:44]
    (nrm, nml, qkv, prb, att, gl, act) = refs[44:51]
    slabs = refs[51:55]
    (wide_q, first, final, pick, first_q, final_q) = refs[55:61]
    (g, g_rows, hidden, gpre, picked, hidden_all) = refs[61:67]
    (mask, cut, pasted, o_cut, o_piece) = refs[67:72]
    (z_sems, own_sems, keep_sems, load_sems, g_sems, trade_sems, mask_sems, o_sems) = refs[72:]
    slab_outs = (slab_q, slab_o, slab_i, slab_d)
    place = Place()
    z = place.z
    heads = sel_o.shape[1] // BLOCK
    lanes = heads * BLOCK
    kept_here, waited = [], []

    def keep(src, dst):
        copy = pltpu.make_async_copy(src, dst, keep_sems.at[len(kept_here)])
        copy.start()
        kept_here.append(copy)
        return copy

    def forget(copy):
        copy.wait()
        waited.append(copy)

    relayed = levels == 4

    def far(delta):
        there = (z + delta) % levels
        return (z + there == 3) & (z * there == 0)

    counts = [slabs[0].shape[1] // levels, o_piece.shape[1], slabs[2].shape[1] // levels,
              w_down.shape[1]]

    def rows_of(m, level):
        return rows_at(level * counts[m], counts[m])

    def piece(layer, m):
        if m == 1:
            return o_piece.at[layer]
        if m == 3:
            return w_down.at[layer]
        return slabs[m].at[layer, rows_of(m, z)]

    def spread(layer, m, delta):
        return remote(
            piece(layer, m), slabs[m].at[layer, rows_of(m, z)],
            z_sems.at[0, layer, m, delta - 1], z_sems.at[1, layer, m, delta - 1],
            place.level((z + delta) % levels),
        )

    def arriving(layer, m, delta):
        rows = slabs[m].at[layer, rows_of(m, (z + levels - delta) % levels)]
        return remote(
            rows, rows, z_sems.at[0, layer, m, delta - 1], z_sems.at[1, layer, m, delta - 1],
            place.level((z + delta) % levels),
        )

    def relay(layer, m):
        rows = slabs[m].at[layer, rows_of(m, (z + 2) % levels)]
        return remote(
            rows, rows, z_sems.at[2, layer, m, 0], z_sems.at[1, layer, m, 2 * (z - 1)],
            place.level(3 * (z - 1)),
        )

    def for_spread(layer, m, act_on):
        for delta in range(1, levels):
            if relayed and delta != 2:
                @pl.when(jnp.logical_not(far(delta)))
                def _(delta=delta):
                    act_on(spread(layer, m, delta))
            else:
                act_on(spread(layer, m, delta))

    def own_piece(layer, m):
        return pltpu.make_async_copy(
            piece(layer, m), slabs[m].at[layer, rows_of(m, z)], own_sems.at[layer, m]
        )

    def send_weights(layer, m):
        if m % 2:
            own_piece(layer, m).start()
        for_spread(layer, m, lambda copy: copy.start())

    rows, q_cols = w_q.shape[1], slabs[0].shape[2]
    span = w_q.shape[2] // 3 // PLANE
    ff_rows = w_in.shape[2] // PLANE // levels
    padded = slabs[2].shape[2] // levels - ff_rows

    def cut_weights(layer):
        scaled_q = w_q[layer].astype(F32) * gains[0, layer]
        scaled_i = w_in[layer].astype(F32) * gains[1, layer]
        for t in range(PLANE):
            parts = []
            for kind in range(3):
                low = (kind * PLANE + t) * span
                parts.append(scaled_q[:, low : low + span])
            if q_cols > 3 * span:
                parts.append(jnp.zeros((rows, q_cols - 3 * span), F32))
            cut[layer, t, :rows, :q_cols] = jnp.concatenate(parts, axis=1).astype(BF)
            parts = []
            for zz in range(levels):
                low = (zz * PLANE + t) * ff_rows
                parts.append(scaled_i[:, low : low + ff_rows])
                if padded:
                    parts.append(jnp.zeros((rows, padded), F32))
            cut[layer, t, :rows, q_cols:] = jnp.concatenate(parts, axis=1).astype(BF)

    def trade(layer, e):
        return remote(
            cut.at[layer, place.rank(e)], pasted.at[layer, place.rank()],
            trade_sems.at[0, layer, e], trade_sems.at[1, layer, e], place.other(e),
        )

    def traded(layer, e):
        there = pasted.at[layer, place.rank(e)]
        return remote(
            there, there, trade_sems.at[0, layer, e], trade_sems.at[1, layer, e], place.other(e)
        )

    def start_trade(layer):
        for e in range(1, PLANE):
            trade(layer, e).start()
        own = place.rank()
        pltpu.make_async_copy(
            cut.at[layer, own], pasted.at[layer, own], trade_sems.at[0, layer, 0]
        ).start()

    def end_trade(layer):
        own = place.rank()
        pltpu.make_async_copy(
            cut.at[layer, own], pasted.at[layer, own], trade_sems.at[0, layer, 0]
        ).wait()
        for e in range(1, PLANE):
            traded(layer, e).wait_recv()
        for e in range(1, PLANE):
            trade(layer, e).wait_send()
        for m, low in ((0, 0), (2, q_cols)):
            width = slabs[m].shape[2]
            whole = [pasted[layer, t, :rows, low : low + width].astype(F32) for t in range(PLANE)]
            slabs[m][layer, rows_of(m, z), :] = jnp.concatenate(whole, axis=0).astype(BF)

    trades = place.trades(levels)
    o_trade = remote(
        o_cut, o_piece, o_sems.at[0], o_sems.at[1], place.indexed(place.holder(levels))
    )
    o_local = pltpu.make_async_copy(o_cut, o_piece, o_sems.at[0])

    def mask_to(e):
        there = mask.at[place.y, place.x, :, place.core]
        return remote(own_mask, there, mask_sems.at[0, e], mask_sems.at[1, e], place.other(e))

    def mask_from(e):
        y, core, x = place.turned(e)
        there = mask.at[y, x, :, core]
        return remote(there, there, mask_sems.at[0, e], mask_sems.at[1, e], place.other(e))

    mask_local = pltpu.make_async_copy(
        own_mask, mask.at[place.y, place.x, :, place.core], mask_sems.at[0, 0]
    )

    middle = (z == 1) | (z == 2)

    def relay_on(layer, m):
        if relayed:
            @pl.when(middle)
            def _():
                arriving(layer, m, 2).wait_recv()
                relay(layer, m).start()

    def weights_here(layer, m):
        for delta in range(1, levels):
            if relayed and delta == 2:
                pl.when(jnp.logical_not(middle))(arriving(layer, m, delta).wait_recv)
            else:
                arriving(layer, m, delta).wait_recv()
        for_spread(layer, m, lambda copy: copy.wait_send())
        if m % 2:
            own_piece(layer, m).wait()
        if relayed:
            pl.when(middle)(relay(layer, m).wait_send)

        return keep(slabs[m].at[layer], slab_outs[m].at[layer])

    skip = slabs[2].at[0, :, : adjoint.shape[3]]
    loads = [
        pltpu.make_async_copy(src, dst, load_sems.at[i])
        for i, (src, dst) in enumerate(zip(head_weights, (first, final, skip)))
    ]
    loads[0].start()
    loads[1].start()
    greet(place, levels)

    g_own = g.at[place.y, :, :, place.core]
    g_far = g.at[1 - place.y, :, :, place.core]
    g_local = pltpu.make_async_copy(adjoint, g_own, g_sems.at[0, 0])
    g_peer = remote(adjoint, g_own, g_sems.at[0, 1], g_sems.at[1, 1], place.far(0))
    g_sibling = remote(adjoint, g_own, g_sems.at[0, 2], g_sems.at[1, 2], place.sibling())
    g_pass = remote(g_far, g_far, g_sems.at[0, 3], g_sems.at[1, 3], place.sibling())
    part = exchange[0]
    lines = nrm.at[0]
    bufs = [nrm.at[0], nml.at[0], nrm.at[1], nml.at[1], lines]
    phases = [Exchange(place, p, buf, exchange) for p, buf in enumerate(bufs)]

    def own_half(s):
        return slice(s * HALF_BLOCK, (s + 1) * HALF_BLOCK)

    def chip_of(s, major, minor):
        return (major + s * (minor - major), minor + s * (major - minor))

    def enter(p, s, values):
        if p < 2 * LAYERS:
            values = values * root(values)
        bufs[p][phases[p].own(s)] = values.astype(BF)
        phases[p].start(s)

    def leave(p, s):
        rows = own_half(s)
        total = phases[p].total(s)
        if p == 2 * LAYERS:
            grad_out[rows, :] = total
            return
        layer = p // 2
        if p % 2 == 0:
            values = xs[layer, rows, :] + total
            mid[layer, rows, :] = values
        else:
            values = mid[layer, rows, :] + total
            if layer + 1 < LAYERS:
                xs[layer + 1, rows, :] = values
        enter(p + 1, s, values)

    def run(p, compute, next_weights, more=()):
        more = list(more)
        hooks = [(1, lambda: leave(p - 1, 1))] if p else []
        hooks += [(2, lambda key=key: relay_on(*key)) for key in next_weights]
        phases[p].run(compute, hooks + more)
        leave(p, 0)
        phases[p].near_stage(1)

    send_weights(0, 3)
    o_cut[...] = jnp.zeros(o_cut.shape, BF)
    for layer in range(LAYERS):
        o_cut[layer, :rows, :] = w_out[layer]
    pl.when(trades)(o_trade.start)
    pl.when(jnp.logical_not(trades))(o_local.start)
    cut_weights(0)
    start_trade(0)
    xs[0] = x_in[...].astype(F32)
    for s in range(2):
        enter(0, s, xs[0, own_half(s), :])
    mask_local.start()
    for e in range(1, PLANE):
        mask_to(e).start()
    cut_weights(1)
    end_trade(0)
    send_weights(0, 0)

    @pl.when(trades)
    def _():
        o_trade.wait_recv()
        o_trade.wait_send()

    pl.when(jnp.logical_not(trades))(o_local.wait)
    send_weights(0, 1)
    start_trade(1)
    for copy in (g_local, g_peer, g_sibling):
        copy.start()
    mask_local.wait()
    for e in range(1, PLANE):
        mask_from(e).wait_recv()
        mask_to(e).wait_send()
    relay_on(0, 0)
    relay_on(0, 1)

    def second_layer():
        end_trade(1)
        send_weights(1, 0)
        send_weights(1, 1)

    slab_keeps = []
    for layer in range(LAYERS):
        wq, wo, wi, wd = [slab.at[layer] for slab in slabs]
        slab_keeps.append(weights_here(layer, 0))
        if layer == 0:
            send_weights(0, 2)
        for n in range(0, wide_q.shape[0], 256):
            wide_q[n : n + 256, :] = dot(wq[n : n + 256, :], sel_q[...]).astype(BF)
        slab_keeps.append(weights_here(layer, 1))
        if layer:
            for copy in attn_saved:
                forget(copy)

        def attend(start, s, half, major, layer=layer, wo=wo):
            both = rows_at(start, 2 * BLOCK, 2 * BLOCK)
            projected = dot(nrm[layer, s, major].reshape(2 * BLOCK, nrm.shape[-1]), wide_q[...])
            cosine, sine = rope[:, :BLOCK], rope[:, BLOCK:]
            for block in range(2):
                rows = rows_at(start + block * BLOCK, BLOCK, BLOCK)
                allowed = mask[chip_of(s, major, block) + (s,)].reshape(BLOCK, BLOCK) > 0
                here = projected[block * BLOCK : (block + 1) * BLOCK]
                outs = []
                for h in range(heads):
                    def part_of(kind, h=h, here=here):
                        return here[:, kind * lanes + h * BLOCK : kind * lanes + (h + 1) * BLOCK]

                    turned = []
                    for kind in range(2):
                        value = part_of(kind)
                        value = value * cosine + pltpu.roll(value, BLOCK // 2, 1) * sine
                        turned.append(value.astype(BF))
                    query, key = turned
                    value = part_of(2).astype(BF)
                    qkv[rows, h * BLOCK : (h + 1) * BLOCK] = query
                    qkv[rows, lanes + h * BLOCK : lanes + (h + 1) * BLOCK] = key
                    qkv[rows, 2 * lanes + h * BLOCK : 2 * lanes + (h + 1) * BLOCK] = value
                    scores = dot(query, key, 1, 1) * (1.0 / math.sqrt(HDIM))
                    scores = jnp.where(allowed, scores, -1e30)
                    scores = jnp.exp(scores - jnp.max(scores, axis=-1, keepdims=True))
                    probs = (scores / jnp.sum(scores, axis=-1, keepdims=True)).astype(BF)
                    prb[rows, h * BLOCK : (h + 1) * BLOCK] = probs
                    outs.append(dot(probs, value).astype(BF))
                att[rows, :] = dot(jnp.concatenate(outs, axis=1), sel_o[...], 1, 1).astype(BF)
            part[s, half] = blocked(dot(att[both, :], wo[...]).astype(BF))

        more = [(1, second_layer)] if layer == 0 else []
        run(2 * layer, attend, ((layer, 2), (layer, 3)), more)
        attn_saved = [keep(src, dst.at[layer]) for src, dst in zip((qkv, prb, att), kept[2:5])]
        nrm_saved = keep(nrm.at[layer], kept[0].at[layer])
        if layer == 0:
            g_peer.wait_recv()
            g_pass.start()
        slab_keeps.append(weights_here(layer, 2))
        slab_keeps.append(weights_here(layer, 3))
        if layer == 0:
            send_weights(1, 2)
            send_weights(1, 3)
        if layer:
            for copy in mlp_saved:
                forget(copy)

        def perceptron(start, s, half, major, layer=layer, wi=wi, wd=wd):
            rows = rows_at(start, 2 * BLOCK, 2 * BLOCK)
            lifted = dot(nml[layer, s, major].reshape(2 * BLOCK, nml.shape[-1]), wi[...])
            root_two = math.sqrt(2.0 / math.pi)
            square = lifted * lifted
            tanh = jnp.tanh(root_two * lifted * (1.0 + 0.044715 * square))
            act[rows, :] = (0.5 * lifted * (1.0 + tanh)).astype(BF)
            slope = 0.5 * (1.0 + tanh) + 0.5 * lifted * (1.0 - tanh * tanh) * root_two * (
                1.0 + 3.0 * 0.044715 * square
            )
            gl[rows, :] = slope.astype(BF)
            part[s, half] = blocked(dot(act[rows, :], wd[...]).astype(BF))

        following = ((layer + 1, 0), (layer + 1, 1)) if layer + 1 < LAYERS else ()
        run(2 * layer + 1, perceptron, following)
        mlp_saved = [keep(src, dst.at[layer]) for src, dst in zip((gl, act), kept[5:7])]
        keep(nml.at[layer], kept[1].at[layer])
        if layer == 0:
            forget(nrm_saved)
            forget(slab_keeps[2])
            loads[2].start()
            loads[0].wait()
            loads[1].wait()
            index = lax.broadcasted_iota(jnp.int32, pick.shape, 0)
            offset = (2 * place.y + place.core) * (pick.shape[0] // (4 * levels))
            pick[...] = jnp.where(index - offset == head_lanes[...], 1.0, 0.0).astype(BF)
            for n in range(0, first.shape[0], 256):
                first_q[n : n + 256, :] = dot(first[n : n + 256, :], pick[...]).astype(BF)
            final_q[...] = dot(pick[...], final[...], 0, 0).astype(BF)

    g_local.wait()
    for copy in (g_sibling, g_pass):
        copy.wait_recv()
    loads[2].wait()
    bias_q = dot(jnp.broadcast_to(bias_first[...], (16, bias_first.shape[1])), pick[...])[:1]
    columns = g.shape[-1]

    def head(start, s, half, major):
        rows = rows_at(start, 2 * BLOCK, 2 * BLOCK)
        pre = dot(lines[s, major].reshape(2 * BLOCK, lines.shape[-1]), first_q[...]) + bias_q
        gate = 1.0 / (1.0 + jnp.exp(-pre))
        hidden[rows, :] = (pre * gate).astype(BF)
        for block in range(2):
            here = rows_at(start + block * BLOCK, BLOCK, BLOCK)
            g_rows[here, :] = g[chip_of(s, major, block) + (s,)].reshape(BLOCK, columns)
        there = g_rows[rows, :]
        grad_hidden = dot(there, final_q[...], 1, 1)
        gpre[rows, :] = (grad_hidden * (gate * (1.0 + pre * (1.0 - gate)))).astype(BF)
        row = lax.broadcasted_iota(jnp.int32, (2 * BLOCK, 1), 0)
        y = major + s * (row // BLOCK - major)
        mine = (row // HALF_BLOCK % 2 == place.core) & (y == place.y)
        mine = jnp.where(mine, there.astype(F32), 0.0).astype(BF)
        whole = dot(gpre[rows, :], first_q[...], 1, 1) + dot(mine, skip[...], 1, 1)
        part[s, half] = blocked(whole.astype(BF))

    run(2 * LAYERS, head, ())

    keep(lines, kept[7])
    keep(hidden, kept[8])
    keep(gpre, kept[9])
    keep(g_rows, kept[11])
    for s in range(2):
        for major in range(2):
            n = (2 * s + major) * 2 * BLOCK
            rows = lines[s, major].reshape(2 * BLOCK, lines.shape[-1])
            picked[n : n + 2 * BLOCK, :] = dot(rows, pick[...]).astype(BF)
    keep(picked, kept[10])
    mine = []
    for x in range(2):
        mine += [lines[0, place.y, x, place.core], lines[1, x, place.y, place.core]]
    mine = jnp.concatenate(mine, axis=0)
    pre = dot(mine, first[...]) + bias_first[...].astype(F32)
    hidden_all[...] = (pre / (1.0 + jnp.exp(-pre))).astype(BF)
    out = dot(hidden_all[...], final[...]) + bias_last[...].astype(F32)
    predictions[...] = (out + dot(mine, skip[...])).astype(BF)
    leave(2 * LAYERS, 1)
    for copy in (g_peer, g_sibling, g_pass):
        copy.wait_send()
    for copy in kept_here:
        if not any(copy is other for other in waited):
            copy.wait()


def norm_back(values, q):
    scale = root(values)
    n = values * scale
    return scale * (q - n * jnp.mean(q * n, axis=-1, keepdims=True))


def backward_kernel(levels, *refs):
    (rope, sel_q, sel_o, gains, w_q, w_in) = refs[:6]
    dy_in, stored, head_stored = refs[6], refs[7:20], refs[20:25]
    (dx_out, small_out, q_out, o_out, i_out, d_out, q_gain, i_gain) = refs[25:33]
    (first_out, out_out, skip_out) = refs[33:36]
    exchange, ag = refs[36:43], refs[43]
    loaded, gp = refs[44:57], refs[57]
    stages, arrivals = refs[58:65], refs[65:72]
    own_sums, acc, o_acc = refs[72:76], refs[76], refs[77]
    o_cut, o_pasted = refs[78], refs[79]
    (small_own, small_x, small_z) = refs[80:83]
    row_buf = refs[83]
    z_sems, load_sems, small_sems, trade_sems, o_sems, row_sem = refs[84:]
    (nml, act, gl, wi, wd, mid, nrm, qkv, prb, att, wq, wo, xs) = loaded
    part = exchange[0]
    place = Place()
    z = place.z
    heads = sel_o.shape[1] // BLOCK
    lanes = heads * BLOCK

    def load(layer, i):
        return pltpu.make_async_copy(stored[i].at[layer], loaded[i], load_sems.at[i])

    lines = ag.at[1]
    h_cols, half_width = small_own.shape[2], nrm.shape[-1] // 2
    gpre, hidden = gp.at[:, :h_cols], nrm.at[:, :, :, :, :, :h_cols]
    picked = nrm.at[:, :, :, :, :, half_width : half_width + h_cols]
    g = qkv.at[:, : stages[5].shape[1]]
    head_loads = [
        pltpu.make_async_copy(src, dst, load_sems.at[len(loaded) + i])
        for i, (src, dst) in enumerate(zip(head_stored, (lines, gpre, hidden, picked, g)))
    ]
    mlp_part, attn_part = range(5), range(6, 12)
    norm_loads = [pltpu.make_async_copy(stored[i], loaded[i], load_sems.at[i]) for i in (5, 12)]
    for copy in norm_loads:
        copy.start()
    dy_load = pltpu.make_async_copy(dy_in, dx_out, load_sems.at[len(loaded) + 5])
    dy_load.start()
    for copy in head_loads:
        copy.start()
    for i in mlp_part:
        load(LAYERS - 1, i).start()
    greet(place, levels)

    def count_of(m):
        return arrivals[m].shape[2]

    def slot(m, layer):
        return layer if m < 4 else 0

    relayed = levels == 4
    middle = (z == 1) | (z == 2)

    def send(layer, m, delta):
        there = (z + delta) % levels
        return remote(
            stages[m].at[rows_at(there * count_of(m), count_of(m))],
            arrivals[m].at[slot(m, layer), delta - 1],
            z_sems.at[0, layer, m, delta - 1],
            z_sems.at[1, layer, m, delta - 1],
            place.level(there),
        )

    def far(delta):
        there = (z + delta) % levels
        return (z + there == 3) & (z * there == 0)

    def hand(layer, m, delta):
        there = (z + delta) % levels
        return remote(
            stages[m].at[rows_at(there * count_of(m), count_of(m))],
            arrivals[m].at[slot(m, layer), levels - 1],
            z_sems.at[0, layer, m, delta - 1],
            z_sems.at[1, layer, m, levels - 1],
            place.level(1 + z // 3),
        )

    def send_first(layer, m):
        for delta in range(1, levels):
            if not relayed:
                send(layer, m, delta).start()
            elif delta == 2:
                pl.when(jnp.logical_not(middle))(send(layer, m, delta).start)
            else:
                pl.when(far(delta))(hand(layer, m, delta).start)
                pl.when(jnp.logical_not(far(delta)))(send(layer, m, delta).start)

    def send_rest(layer, m):
        if relayed:
            @pl.when(middle)
            def _():
                hand(layer, m, 1).wait_recv()
                rows = rows_at((z + 2) % levels * count_of(m), count_of(m))
                total = stages[m][rows, :].astype(F32)
                total = total + arrivals[m][slot(m, layer), levels - 1].astype(F32)
                stages[m][rows, :] = total.astype(BF)
                send(layer, m, 2).start()

    def sent(layer, m):
        for delta in range(1, levels):
            send(layer, m, delta).wait_send()

    def result(layer, m):
        if m > 4:
            return (out_out, skip_out)[m - 5]
        if m == 3:
            return d_out.at[layer]
        return own_sums[min(m, 3)].at[slot(m, layer)]

    def weight_grad(layer, m, left, right, tile):
        width = left.shape[-1]
        if m < 4 and layer + 1 < LAYERS:
            sent(layer + 1, m)
        if width % tile:
            stages[m][...] = dot(flat(left), flat(right), 0, 0).astype(BF)
        else:
            def body(i, carry):
                here = rows_at(i * tile, tile, tile)
                stages[m][here, :] = dot(flat(left, here), flat(right), 0, 0).astype(BF)
                return carry

            lax.fori_loop(0, width // tile, body, 0)
        send_first(layer, m)
        out = result(layer, m)
        out[...] = stages[m][rows_at(z * count_of(m), count_of(m)), :].astype(out.dtype)

    bufs = [ag.at[p % 2] for p in range(PHASES)]
    phases = [Exchange(place, p, buf, exchange) for p, buf in enumerate(bufs)]

    def own_half(s):
        return slice(s * HALF_BLOCK, (s + 1) * HALF_BLOCK)

    def enter(p, s):
        bufs[p][phases[p].own(s)] = dx_out[own_half(s), :].astype(BF)
        phases[p].start(s)

    def leave(p, s):
        rows = own_half(s)
        values = (mid if p % 2 == 0 else xs)[LAYERS - 1 - p // 2, rows, :]
        dx_out[rows, :] += norm_back(values, phases[p].total(s))
        if p + 1 < PHASES:
            enter(p + 1, s)

    def run(p, compute, relays):
        hooks = [(1, lambda: leave(p - 1, 1))] if p else []
        hooks += [(2, lambda key=key: send_rest(*key)) for key in relays]
        phases[p].run(compute, hooks)

    dy_load.wait()
    for copy in norm_loads:
        copy.wait()
    for s in range(2):
        enter(0, s)

    for copy in head_loads:
        copy.wait()
    last = LAYERS - 1
    bias_sum = jnp.sum(gpre[...].astype(F32), axis=0, keepdims=True)
    small_own[1] = jnp.broadcast_to(bias_sum, small_own.shape[1:])
    to_x = remote(
        small_own.at[1], small_x, small_sems.at[0, 0], small_sems.at[1, 0], place.near(0)
    )
    to_x.start()
    weight_grad(last, 5, hidden, g, 2 * BLOCK)
    weight_grad(last, 6, picked, g, 2 * BLOCK)
    weight_grad(last, 4, lines, gpre, 2 * BLOCK)
    g_sum = jnp.sum(g[...].astype(F32), axis=0, keepdims=True)
    to_x.wait()
    small_z[0, :, : g_sum.shape[1]] = jnp.broadcast_to(g_sum, (8, g_sum.shape[1]))
    small_z[0, :, g_sum.shape[1] :] = small_own[1] + small_x[...]
    to_z = [
        remote(
            small_z.at[0], small_z.at[d], small_sems.at[0, d], small_sems.at[1, d],
            place.level((z + d) % levels),
        )
        for d in range(1, levels)
    ]
    for copy in to_z:
        copy.start()
    for i in attn_part:
        load(last, i).start()

    relays = [(last, 5), (last, 6), (last, 4)]
    for layer in reversed(range(LAYERS)):
        p = 2 * (LAYERS - 1 - layer)
        buf = bufs[p]
        for i in mlp_part:
            load(layer, i).wait()

        def perceptron(start, s, half, major, buf=buf):
            rows = rows_at(start, 2 * BLOCK, 2 * BLOCK)
            grad_act = dot(buf[s, major].reshape(2 * BLOCK, buf.shape[-1]), wd[...], 1, 1)
            gl[rows, :] = (grad_act * gl[rows, :].astype(F32)).astype(BF)
            write_part(part, s, half, gl[rows, :], wi, 1)

        run(p, perceptron, relays)
        weight_grad(layer, 3, act, buf, BLOCK)
        leave(p, 0)
        weight_grad(layer, 2, nml, gl, 2 * BLOCK)
        phases[p].near_stage(1)
        if layer > 0:
            for i in mlp_part:
                load(layer - 1, i).start()
        for i in attn_part:
            load(layer, i).wait()
        buf = bufs[p + 1]

        def attend(start, s, half, major, buf=buf):
            cosine, sine = rope[:, :BLOCK], rope[:, BLOCK:]
            both = rows_at(start, 2 * BLOCK, 2 * BLOCK)
            there = buf[s, major].reshape(2 * BLOCK, buf.shape[-1])
            grad_heads = dot(there, wo[...], 1, 1).astype(BF)
            grad_heads = dot(grad_heads, sel_o[...]).astype(BF)
            for block in range(2):
                rows = rows_at(start + block * BLOCK, BLOCK, BLOCK)
                outs = [[], [], []]
                for h in range(heads):
                    def part_of(kind, h=h, rows=rows):
                        low = kind * lanes + h * BLOCK
                        return qkv[rows, low : low + BLOCK]

                    query, key, value = part_of(0), part_of(1), part_of(2)
                    probs = prb[rows, h * BLOCK : (h + 1) * BLOCK]
                    grad_head = grad_heads[
                        block * BLOCK : (block + 1) * BLOCK, h * BLOCK : (h + 1) * BLOCK
                    ]
                    outs[2].append(dot(probs, grad_head, 0, 0).astype(BF))
                    grad_probs = dot(grad_head, value, 1, 1)
                    probs = probs.astype(F32)
                    inner = jnp.sum(probs * grad_probs, axis=-1, keepdims=True)
                    grad_scores = (probs * (grad_probs - inner)).astype(BF)
                    for kind, turned in (
                        (0, dot(grad_scores, key)),
                        (1, dot(grad_scores, query, 0, 0)),
                    ):
                        turned = turned * (1.0 / math.sqrt(HDIM))
                        turned = turned * cosine - pltpu.roll(turned, BLOCK // 2, 1) * sine
                        outs[kind].append(turned.astype(BF))
                packed = jnp.concatenate(outs[0] + outs[1] + outs[2], axis=1)
                gp[rows, :] = dot(packed, sel_q[...], 1, 1).astype(BF)
            write_part(part, s, half, gp[both, :], wq, 1)

        run(p + 1, attend, [(layer, 3), (layer, 2)])
        weight_grad(layer, 0, nrm, gp, 2 * BLOCK)
        leave(p + 1, 0)
        weight_grad(layer, 1, att, buf, 2 * BLOCK)
        phases[p + 1].near_stage(1)
        if layer > 0:
            for i in attn_part:
                load(layer - 1, i).start()
        relays = [(layer, 0), (layer, 1)]
    leave(PHASES - 1, 1)
    for key in relays:
        send_rest(*key)

    total = small_z[0]
    for copy, d in zip(to_z, range(1, levels)):
        copy.wait_recv()
        total = total + small_z[d]
    small_out[...] = total
    for copy in to_z:
        copy.wait_send()
    rows = w_q.shape[1]
    pad_rows = up16(rows)
    kinds = {0: 0, 2: 1, 4: 2}

    def cut_at(m, t):
        start = rows_at((t + PLANE * kinds[m]) * pad_rows, pad_rows)
        return wi.at[start, : stages[m].shape[1]]

    def pasted_at(layer, m, t):
        start = rows_at((slot(m, layer) * PLANE + t) * pad_rows, pad_rows)
        return {0: gl, 2: act, 4: wd}[m].at[start, : stages[m].shape[1]]

    def trade(layer, m, e):
        kind = kinds[m]
        return remote(
            cut_at(m, place.rank(e)), pasted_at(layer, m, place.rank()),
            trade_sems.at[0, layer, kind, e], trade_sems.at[1, layer, kind, e], place.other(e),
        )

    def traded(layer, m, e):
        there = pasted_at(layer, m, place.rank(e))
        return remote(
            there, there, trade_sems.at[0, layer, kinds[m], e],
            trade_sems.at[1, layer, kinds[m], e], place.other(e),
        )

    def own_trade(layer, m):
        own = place.rank()
        return pltpu.make_async_copy(
            cut_at(m, own), pasted_at(layer, m, own), trade_sems.at[0, layer, kinds[m], 0]
        )

    stayed = set()

    def wait_own_trade(layer, m):
        if (layer, m) not in stayed:
            own_trade(layer, m).wait()
            stayed.add((layer, m))

    def pasted(layer, m, t):
        return pasted_at(layer, m, t)[:rows, :].astype(F32)

    trades = place.trades(levels)

    def o_trade(layer):
        return remote(
            o_cut.at[layer], o_pasted.at[layer], o_sems.at[0, layer], o_sems.at[1, layer],
            place.indexed(place.held(levels)),
        )

    def o_local(layer):
        return pltpu.make_async_copy(o_cut.at[layer], o_pasted.at[layer], o_sems.at[0, layer])

    def finalize(layer, m):
        own = result(layer, m)
        if m == 3 or m > 4:
            total = own
        else:
            total = o_acc if m == 1 else acc.at[:, : own.shape[1]]
            total[...] = own[...].astype(F32)
        for delta in range(1, levels):
            def add(delta=delta):
                send(layer, m, delta).wait_recv()
                total[...] += arrivals[m][slot(m, layer), delta - 1].astype(F32)

            if relayed and delta != 2:
                source = (z + levels - delta) % levels
                pl.when(jnp.logical_not((z + source == 3) & (z * source == 0)))(add)
            else:
                add()
        if m > 3 or layer == 0:
            sent(layer, m)
        if m == 1:
            o_cut[layer] = total[...].astype(BF)
            pl.when(trades)(o_trade(layer).start)
            pl.when(jnp.logical_not(trades))(o_local(layer).start)
        elif m in kinds:
            if m < 4 and layer + 1 < LAYERS:
                wait_own_trade(layer + 1, m)
                for e in range(1, PLANE):
                    trade(layer + 1, m, e).wait_send()
            values = total[...].astype(BF).astype(F32)
            for t in range(PLANE):
                cut_at(m, t)[:rows, :] = values[t * rows : (t + 1) * rows].astype(BF)
            own_trade(layer, m).start()
            for e in range(1, PLANE):
                trade(layer, m, e).start()

    def wait_trade(layer, m):
        wait_own_trade(layer, m)
        for e in range(1, PLANE):
            traded(layer, m, e).wait_recv()
        if m > 3 or layer == 0:
            for e in range(1, PLANE):
                trade(layer, m, e).wait_send()

    span = w_q.shape[2] // 3 // PLANE
    ff_rows = w_in.shape[2] // PLANE // levels
    padded_rows = stages[2].shape[1] // levels

    def rows_out(layer, out):
        here = row_buf.at[:, : out.shape[2]]
        return pltpu.make_async_copy(here, out.at[layer], row_sem.at[0])

    on_the_way = []

    def write_rows(layer, parts, out, kind, w, gain_out):
        whole = jnp.concatenate(parts, axis=1)
        gain_out[layer] = jnp.sum(whole * w[layer].astype(F32), axis=1, keepdims=True)
        if on_the_way:
            on_the_way.pop().wait()
        row_buf[:, : out.shape[2]] = whole * gains[kind, layer]
        copy = rows_out(layer, out)
        copy.start()
        on_the_way.append(copy)

    def assemble(layer):
        wait_trade(layer, 0)
        ranks = [pasted(layer, 0, t) for t in range(PLANE)]
        parts = [rank[:, kind * span : (kind + 1) * span] for kind in range(3) for rank in ranks]
        write_rows(layer, parts, q_out, 0, w_q, q_gain)

    def assemble_mlp(layer):
        wait_trade(layer, 2)
        ranks = [pasted(layer, 2, t) for t in range(PLANE)]
        parts = [
            rank[:, zz * padded_rows : zz * padded_rows + ff_rows]
            for zz in range(levels) for rank in ranks
        ]
        write_rows(layer, parts, i_out, 1, w_in, i_gain)

    def assemble_out(layer):
        @pl.when(trades)
        def _():
            o_trade(layer).wait_recv()
            o_trade(layer).wait_send()

        pl.when(jnp.logical_not(trades))(o_local(layer).wait)
        o_out[layer] = o_pasted[layer, :rows, :].astype(F32)

    head_rows, head_share = out_out.shape[0], first_out.shape[1] // 4 // levels

    def assemble_head():
        wait_trade(last, 4)
        sums = []
        for q in range(4):
            sums.append(pasted(last, 4, 2 * q) + pasted(last, 4, 2 * q + 1))
        parts = []
        for zz in range(levels):
            for q in range(4):
                parts.append(sums[q][:, zz * head_rows : zz * head_rows + head_share])
        first_out[...] = jnp.concatenate(parts, axis=1)

    for key in [(last, 5), (last, 6), (last, 4)] + [(last, m) for m in (3, 2, 0, 1)]:
        finalize(*key)
    for layer in reversed(range(LAYERS - 1)):
        finalize(layer, 3)
        finalize(layer, 2)
    assemble_head()
    for layer in reversed(range(LAYERS)):
        if layer == 0:
            finalize(layer, 0)
            finalize(layer, 1)
        assemble_mlp(layer)
        assemble(layer)
        assemble_out(layer)
    on_the_way.pop().wait()


def shape(*dims, dtype=BF):
    return jax.ShapeDtypeStruct(dims, dtype)


def rope_table():
    position = np.arange(BLOCK) % ROW_LEN
    inverse = ROTARY_BASE ** (-np.arange(HALF) / HALF)
    angles = (position[:, None] * inverse[None, :]).astype(np.float32)
    table = np.zeros((BLOCK, 2, 2, BLOCK // 2), np.float32)
    table[:, 0, :, :HALF] = np.cos(angles)[:, None]
    table[:, 1, 0, :HALF] = -np.sin(angles)
    table[:, 1, 1, :HALF] = np.sin(angles)
    return table.reshape(BLOCK, 2 * BLOCK)


def lane_of(index):
    head, inside = divmod(index, HDIM)
    half, place = divmod(inside, HALF)
    return head * BLOCK + half * (BLOCK // 2) + place


def per_device(devices, x, segments, padded, w_qkv, w_out, w_in, w_down, gain_attn, gain_mlp,
               head_first, head_first_bias, head_final, head_bias, head_skip, adjoint):
    levels = devices // PLANE
    width = x.shape[1]
    ff = w_in.shape[2]
    columns = head_final.shape[1]
    tokens = PLANE * BLOCK
    heads = width // HDIM // PLANE
    span = heads * HDIM
    rows = width // devices
    out_rows = up16(rows)
    ff_rows = ff // devices
    down_rows = up16(ff_rows)
    head_share = 2 * width // devices
    head_rows = up16(head_share)
    used_cols, o_rows, f_cols = 3 * span, levels * out_rows, levels * down_rows
    h_cols = -(-levels * head_rows // 128) * 128
    q_cols = -(-used_cols // 128) * 128
    lanes = heads * BLOCK

    sel_q = np.zeros((q_cols, 3 * lanes), np.float32)
    sel_o = np.zeros((o_rows, lanes), np.float32)
    for e in range(span):
        for kind in range(3):
            sel_q[kind * span + e, kind * lanes + lane_of(e)] = 1
        sel_o[e // rows * out_rows + e % rows, lane_of(e)] = 1
    sel_q, sel_o = jnp.asarray(sel_q, BF), jnp.asarray(sel_o, BF)
    rope = jnp.asarray(rope_table())
    head_lanes = np.full((1, h_cols), -width, np.int32)
    for zz in range(levels):
        here = slice(zz * head_rows, zz * head_rows + head_share)
        head_lanes[0, here] = 4 * head_share * zz + np.arange(head_share)
    head_lanes = jnp.asarray(head_lanes)

    seg = segments.reshape(2, HALF_BLOCK)
    open_key = padded.reshape(2, HALF_BLOCK) == 0
    within = jnp.arange(HALF_BLOCK)
    static = within[:, None] // ROW_LEN == within[None, :] // ROW_LEN
    static = static & (within[None, :] <= within[:, None])
    allowed = static[None] & (seg[:, :, None] == seg[:, None, :])
    allowed = allowed & (open_key[:, None, :] | (within[:, None] == within[None, :])[None])
    core = lax.axis_index("wide") % 2
    side = jnp.arange(BLOCK)[None, None, :] // HALF_BLOCK == core
    own_mask = (jnp.concatenate([allowed, allowed], axis=-1) & side).astype(BF)

    gains = jnp.stack([gain_attn, gain_mlp]).astype(F32)[..., None]
    d_piece = w_down
    if down_rows != ff_rows:
        d_piece = jnp.pad(w_down, [(0, 0), (0, down_rows - ff_rows), (0, 0)])
    pad_rows = up16(rows)

    in_blocks = (2, 2, 2, 2, HALF_BLOCK)
    layer_shapes = [
        in_blocks + (width,), in_blocks + (width,), (tokens, 3 * lanes), (tokens, lanes), (tokens, o_rows),
        (tokens, f_cols), (tokens, f_cols),
    ]
    slab_shapes = [(width, q_cols), (o_rows, width), (width, f_cols), (f_cols, width)]
    outs = [
        shape(2 * BLOCK, columns), shape(BLOCK, width, dtype=F32),
        shape(LAYERS, BLOCK, width, dtype=F32), shape(LAYERS, BLOCK, width, dtype=F32),
    ]
    vmem_outs = len(outs)
    outs += [shape(LAYERS, *dims) for dims in layer_shapes]
    outs += [shape(*in_blocks, width)] + [shape(tokens, h_cols)] * 3 + [shape(tokens, columns)]
    outs += [shape(LAYERS, *dims) for dims in slab_shapes]
    (predictions, grad_final, xs, mid, nrm, nml, qkv, prb, att, gl, act, lines, hidden, gpre,
     picked, g, wq, wo, wi, wd) = pl.pallas_call(
        lambda *refs: forward_kernel(levels, *refs),
        out_shape=outs,
        in_specs=[VMEM] * 13 + [ANY] * 4,
        out_specs=[VMEM] * vmem_outs + [ANY] * (len(outs) - vmem_outs),
        scratch_shapes=exchange_scratch(width, PHASES + 1)
        + [pltpu.VMEM((LAYERS,) + dims, BF) for dims in layer_shapes[:2]]
        + [pltpu.VMEM(dims, BF) for dims in layer_shapes[2:]]
        + [pltpu.VMEM((LAYERS,) + dims, BF) for dims in slab_shapes]
        + [
            pltpu.VMEM((width, 3 * lanes), BF), pltpu.VMEM((width, width), BF),
            pltpu.VMEM((width, columns), BF), pltpu.VMEM((width, h_cols), BF),
            pltpu.VMEM((width, h_cols), BF), pltpu.VMEM((h_cols, columns), BF),
            pltpu.VMEM(in_blocks + (columns,), BF), pltpu.VMEM((tokens, columns), BF),
            pltpu.VMEM((tokens, h_cols), BF),
            pltpu.VMEM((tokens, h_cols), BF), pltpu.VMEM((tokens, h_cols), BF),
            pltpu.VMEM((2 * BLOCK, width), BF),
            pltpu.VMEM(in_blocks + (BLOCK,), BF),
            pltpu.VMEM((LAYERS, PLANE, pad_rows, q_cols + f_cols), BF),
            pltpu.VMEM((LAYERS, PLANE, pad_rows, q_cols + f_cols), BF),
            pltpu.VMEM((LAYERS, out_rows, width), BF),
            pltpu.VMEM((LAYERS, out_rows, width), BF),
            pltpu.SemaphoreType.DMA((3, LAYERS, 4, levels - 1)),
            pltpu.SemaphoreType.DMA((LAYERS, 4)),
            pltpu.SemaphoreType.DMA((32,)),
            pltpu.SemaphoreType.DMA((3,)),
            pltpu.SemaphoreType.DMA((2, 4)),
            pltpu.SemaphoreType.DMA((2, LAYERS, PLANE)),
            pltpu.SemaphoreType.DMA((2, PLANE)),
            pltpu.SemaphoreType.DMA((2,)),
        ],
        compiler_params=pltpu.CompilerParams(
            collective_id=1, has_side_effects=True, vmem_limit_bytes=62 * MIB
        ),
        name="decoder_forward",
    )(x, own_mask, rope, sel_q, sel_o, head_lanes,
      adjoint.reshape(2, 2, HALF_BLOCK, columns), head_first_bias[None], head_bias[None], gains,
      w_qkv, w_in, w_out, d_piece, head_first, head_final, head_skip)

    chunk = [PLANE * rows, out_rows, PLANE * rows, down_rows, PLANE * rows, head_rows, head_rows]
    cols = [q_cols, width, f_cols, width, h_cols, columns, columns]
    stage_rows = [levels * n for n in chunk[:5]] + [h_cols] * 2
    kept_shapes = [
        in_blocks + (width,), (tokens, f_cols), (tokens, f_cols), (width, f_cols), (f_cols, width),
        (LAYERS, BLOCK, width), in_blocks + (width,), (tokens, 3 * lanes), (tokens, lanes),
        (tokens, o_rows), (width, q_cols), (o_rows, width), (LAYERS, BLOCK, width),
    ]
    small_cols = columns + h_cols
    outs = [
        shape(BLOCK, width, dtype=F32), shape(8, small_cols, dtype=F32),
        shape(LAYERS, rows, 3 * width, dtype=F32), shape(LAYERS, rows, width, dtype=F32),
        shape(LAYERS, rows, ff, dtype=F32), shape(LAYERS, down_rows, width, dtype=F32),
        shape(LAYERS, rows, 1, dtype=F32), shape(LAYERS, rows, 1, dtype=F32),
        shape(rows, width, dtype=F32), shape(head_rows, columns, dtype=F32),
        shape(head_rows, columns, dtype=F32),
    ]
    (input_grad, small, q_grad, o_grad, i_grad, d_grad, q_gain, i_gain, g_first, g_out,
     g_skip) = pl.pallas_call(
        lambda *refs: backward_kernel(levels, *refs),
        out_shape=outs,
        in_specs=[VMEM] * 6 + [ANY] * 19,
        out_specs=[VMEM, VMEM, ANY, VMEM, ANY] + [VMEM] * (len(outs) - 5),
        scratch_shapes=exchange_scratch(width, PHASES)
        + [pltpu.VMEM((2,) + in_blocks + (width,), BF)]
        + [pltpu.VMEM(dims, F32 if dims[0] == LAYERS and dims[1] == BLOCK else BF) for dims in kept_shapes]
        + [pltpu.VMEM((tokens, q_cols), BF)]
        + [pltpu.VMEM((stage_rows[m], cols[m]), BF) for m in range(7)]
        + [
            pltpu.VMEM((LAYERS if m < 4 else 1, levels, chunk[m], cols[m]), BF)
            for m in range(7)
        ]
        + [
            pltpu.VMEM((LAYERS if m < 4 else 1, chunk[m], cols[m]), BF) for m in (0, 1, 2, 4)
        ]
        + [pltpu.VMEM((chunk[0], max(f_cols, q_cols)), F32), pltpu.VMEM((out_rows, width), F32)]
        + [pltpu.VMEM((LAYERS, out_rows, width), BF)] * 2
        + [
            pltpu.VMEM((2, 8, h_cols), F32), pltpu.VMEM((8, h_cols), F32),
            pltpu.VMEM((levels, 8, small_cols), F32),
            pltpu.VMEM((rows, max(ff, 3 * width)), F32),
            pltpu.SemaphoreType.DMA((2, LAYERS, 7, levels)),
            pltpu.SemaphoreType.DMA((20,)),
            pltpu.SemaphoreType.DMA((2, levels)),
            pltpu.SemaphoreType.DMA((2, LAYERS, 3, PLANE)),
            pltpu.SemaphoreType.DMA((2, LAYERS)),
            pltpu.SemaphoreType.DMA((1,)),
        ],
        compiler_params=pltpu.CompilerParams(
            collective_id=2, has_side_effects=True, vmem_limit_bytes=62 * MIB
        ),
        name="decoder_backward",
    )(rope, sel_q, sel_o, gains, w_qkv, w_in, grad_final, nml, act, gl, wi, wd, mid, nrm, qkv, prb,
      att, wq, wo, xs, lines, gpre, hidden.reshape(in_blocks + (h_cols,)),
      picked.reshape(in_blocks + (h_cols,)), g)

    z, narrow = lax.axis_index("wide") // 4, lax.axis_index("narrow")
    g_first_bias = lax.dynamic_slice(small[0], (columns + z * head_rows + narrow * rows,), (rows,))
    return (
        predictions, input_grad, q_grad, o_grad, i_grad, d_grad[:, :ff_rows], q_gain[..., 0],
        i_gain[..., 0], g_first, g_first_bias, g_out[:head_share], small[0, :columns],
        g_skip[:head_share],
    )


def solution(mesh):
    devices = mesh.shape["wide"] * mesh.shape["narrow"]
    both = ("wide", "narrow")
    weight, gain = P(None, both, None), P(None, both)
    return jax.shard_map(
        lambda *arrays: per_device(devices, *arrays),
        mesh=mesh,
        in_specs=(
            P(both, None), P(both), P(both), weight, weight, weight, weight, gain, gain, P(), P(),
            P(None, "narrow"), P("narrow"), P(None, "narrow"), P("wide", "narrow"),
        ),
        out_specs=(
            P("wide", "narrow"), P(both, None), weight, weight, weight, weight, gain, gain,
            P(both, None), P(both), P("wide", "narrow"), P("narrow"), P("wide", "narrow"),
        ),
        check_vma=False,
    )
```

```python
import math

import jax
import jax.numpy as jnp
import numpy as np
from jax import lax
from jax.experimental import pallas as pl
from jax.experimental.pallas import tpu as pltpu
from jax.sharding import PartitionSpec as P

HDIM = 80
HALF = HDIM // 2
LAYERS = 2
ROW_LEN = 16
BLOCK = 128
HALF_BLOCK = BLOCK // 2
PLANE = 8
PHASES = 2 * LAYERS
MESH = pl.DeviceIdType.MESH
BF = jnp.bfloat16
F32 = jnp.float32
EPS = 1e-06
ROTARY_BASE = 10000.0
MIB = 1024 * 1024
VMEM = pl.BlockSpec(memory_space=pltpu.VMEM)
ANY = pl.BlockSpec(memory_space=pl.ANY)


def up16(rows):
    return -(-rows // 16) * 16


def rows_at(start, count, step=16):
    return pl.ds(pl.multiple_of(start, step), count)


def dot(a, b, ca=1, cb=0):
    return lax.dot_general(a, b, (((ca,), (cb,)), ((), ())), preferred_element_type=F32)


class Place:
    def __init__(self):
        wide = lax.axis_index("wide")
        self.x = lax.axis_index("narrow")
        self.core = wide % 2
        self.y = (wide // 2) % 2
        self.z = wide // 4

    def device(self, z, y, core, x):
        return (z * 4 + y * 2 + core, x)

    def sibling(self):
        return self.device(self.z, self.y, 1 - self.core, self.x)

    def major(self, s, far=0):
        return (self.y + s * (self.x - self.y) + far) % 2

    def minor(self, s, near=0):
        return (self.x + s * (self.y - self.x) + near) % 2

    def near(self, s):
        return self.device(self.z, (self.y + s) % 2, self.core, (self.x + 1 - s) % 2)

    def far(self, s):
        return self.device(self.z, (self.y + 1 - s) % 2, self.core, (self.x + s) % 2)

    def level(self, z):
        return self.device(z, self.y, self.core, self.x)

    def turned(self, e):
        return (self.y + e // 4) % 2, (self.core + e // 2) % 2, (self.x + e) % 2

    def other(self, e):
        return self.device(self.z, *self.turned(e))

    def rank(self, e=0):
        y, core, x = self.turned(e)
        return 4 * y + 2 * core + x

    def indexed(self, index):
        return (index // 2, index % 2)

    def holder(self, levels):
        index = PLANE * self.z + self.rank()
        return index % levels * PLANE + index // levels

    def held(self, levels):
        return levels * self.rank() + self.z

    def trades(self, levels):
        return self.holder(levels) != PLANE * self.z + self.rank()


def greet(place, levels):
    barrier = pltpu.get_barrier_semaphore()
    others = [place.other(e) for e in range(1, PLANE)]
    others += [place.level((place.z + d) % levels) for d in range(1, levels)]
    for other in others:
        pl.semaphore_signal(barrier, inc=1, device_id=other, device_id_type=MESH)
    trades = place.trades(levels)

    @pl.when(trades)
    def _():
        for index in (place.holder(levels), place.held(levels)):
            pl.semaphore_signal(
                barrier, inc=1, device_id=place.indexed(index), device_id_type=MESH
            )
        pl.semaphore_wait(barrier, len(others) + 2)

    @pl.when(jnp.logical_not(trades))
    def _():
        pl.semaphore_wait(barrier, len(others))


def remote(src, dst, send, recv, device):
    return pltpu.make_async_remote_copy(
        src_ref=src, dst_ref=dst, send_sem=send, recv_sem=recv, device_id=device,
        device_id_type=MESH,
    )


class Exchange:
    def __init__(self, place, phase, buf, scratch):
        (self.part, self.recv_s, self.send_f, self.recv_f, self.send_n, self.recv_n, self.sems) = scratch
        self.place, self.phase, self.buf = place, phase, buf

    def copy(self, s, kind, src, dst, device):
        sems = self.sems
        return remote(
            src, dst, sems.at[self.phase, s, 0, kind], sems.at[self.phase, s, 1, kind], device
        )

    def block(self, s, far, near, core):
        place = self.place
        return self.buf.at[s, place.major(s, far), place.minor(s, near), core]

    def own(self, s):
        return (s, self.place.major(s), self.place.minor(s), self.place.core)

    def to_near(self, s, far=0, near=0):
        rows = self.block(s, far, near, self.place.core)
        return self.copy(s, 0, rows, rows, self.place.near(s))

    def to_far(self, s, far=0, near=0):
        rows = self.block(s, far, near, self.place.core)
        return self.copy(s, 1, rows, rows, self.place.far(s))

    def pass_far(self, s, far=0, near=1):
        rows = self.block(s, far, near, self.place.core)
        return self.copy(s, 2, rows, rows, self.place.far(s))

    def sibling(self, s, kind, core):
        if kind < 2:
            rows = self.block(s, 0, kind, core)
        else:
            rows = self.buf.at[s, self.place.major(s, 1), :, core]
        return self.copy(s, 3 + kind, rows, rows, self.place.sibling())

    def to_sibling(self, s, kind):
        return self.sibling(s, kind, self.place.core)

    def from_sibling(self, s, kind):
        return self.sibling(s, kind, 1 - self.place.core)

    def sum_sibling(self, s, half):
        src = self.part.at[s, half, :, 1 - self.place.core]
        sems = self.sems
        return remote(
            src, self.recv_s.at[s, half], sems.at[self.phase, s, 0, 6 + half],
            sems.at[self.phase, s, 1, 6 + half], self.place.sibling(),
        )

    def sum_far(self, s):
        return self.copy(s, 8, self.send_f.at[s], self.recv_f.at[s], self.place.far(s))

    def sum_near(self, s):
        return self.copy(s, 9, self.send_n.at[s], self.recv_n.at[s], self.place.near(s))

    def start(self, s):
        self.to_near(s).start()
        self.to_far(s).start()
        self.to_sibling(s, 0).start()

    def far_stage(self, s):
        self.sum_sibling(s, 1).wait_recv()
        own = self.part[s, 1, :, self.place.core].astype(F32)
        self.send_f[s] = (own + self.recv_s[s, 1].astype(F32)).astype(BF)
        self.sum_far(s).start()

    def summed(self, s, minor):
        own = self.part[s, 0, minor, self.place.core].astype(F32)
        return own + self.recv_s[s, 0, minor].astype(F32) + self.recv_f[s, minor].astype(F32)

    def near_stage(self, s):
        self.sum_sibling(s, 0).wait_recv()
        self.sum_far(s).wait_recv()
        self.send_n[s] = self.summed(s, self.place.minor(s, 1)).astype(BF)
        self.sum_near(s).start()

    def total(self, s):
        self.sum_near(s).wait_recv()
        total = self.summed(s, self.place.minor(s)) + self.recv_n[s].astype(F32)
        self.to_near(s).wait_send()
        self.to_far(s).wait_send()
        self.pass_far(s).wait_send()
        for kind in range(3):
            self.to_sibling(s, kind).wait_send()
        for half in range(2):
            self.sum_sibling(s, half).wait_send()
        self.sum_far(s).wait_send()
        self.sum_near(s).wait_send()
        return total

    def run(self, compute, hooks):
        def body(i, carry):
            s, half = i // 2, i % 2

            @pl.when(half == 0)
            def _():
                self.to_near(s, 0, 1).wait_recv()
                self.pass_far(s).start()
                self.to_sibling(s, 1).start()

            for at, hook in hooks:
                pl.when(i == at)(hook)

            @pl.when(half == 0)
            def _():
                self.from_sibling(s, 0).wait_recv()
                self.from_sibling(s, 1).wait_recv()

            @pl.when(half == 1)
            def _():
                self.to_far(s, 1, 0).wait_recv()
                self.pass_far(s, 1, 1).wait_recv()
                self.to_sibling(s, 2).start()

            @pl.when(i == 2)
            def _():
                self.far_stage(0)

            @pl.when(half == 1)
            def _():
                self.from_sibling(s, 2).wait_recv()

            major = self.place.major(s, half)
            compute(s * 8 * HALF_BLOCK + major * 4 * HALF_BLOCK, s, half, major)
            self.sum_sibling(s, half).start()
            return carry

        lax.fori_loop(0, 4, body, 0)
        self.near_stage(0)
        self.far_stage(1)


def exchange_scratch(width, phases):
    return [
        pltpu.VMEM((2, 2, 2, 2, HALF_BLOCK, width), BF),
        pltpu.VMEM((2, 2, 2, HALF_BLOCK, width), BF),
        pltpu.VMEM((2, 2, HALF_BLOCK, width), BF),
        pltpu.VMEM((2, 2, HALF_BLOCK, width), BF),
        pltpu.VMEM((2, HALF_BLOCK, width), BF),
        pltpu.VMEM((2, HALF_BLOCK, width), BF),
        pltpu.SemaphoreType.DMA((phases, 2, 2, 10)),
    ]


def flat(ref, columns=slice(None)):
    if len(ref.shape) == 2:
        return ref[:, columns]
    values = ref[(slice(None),) * 5 + (columns,)]
    return values.reshape(-1, values.shape[-1])


def write_part(part, s, half, values, w, contracted):
    width = part.shape[-1]
    step = width // 2
    for n in range(0, width, step):
        columns = slice(n, n + step)
        side = w[:, columns] if contracted == 0 else w[columns, :]
        part[s, half, :, :, :, columns] = blocked(dot(values, side, 1, contracted).astype(BF))


def blocked(values):
    return values.reshape(2, 2, HALF_BLOCK, values.shape[-1])


def root(values):
    return lax.rsqrt(jnp.mean(values * values, axis=-1, keepdims=True) + EPS)


def forward_kernel(levels, *refs):
    (x_in, own_mask, rope, sel_q, sel_o, head_lanes, adjoint, bias_first, bias_last) = refs[:9]
    (gains, w_q, w_in, w_out) = refs[9:13]
    w_down, head_weights = refs[13], refs[14:17]
    (predictions, grad_out, xs, mid) = refs[17:21]
    kept, (slab_q, slab_o, slab_i, slab_d) = refs[21:33], refs[33:37]
    exchange = refs[37:44]
    (nrm, nml, qkv, prb, att, gl, act) = refs[44:51]
    slabs = refs[51:55]
    (wide_q, first, final, pick, first_q, final_q) = refs[55:61]
    (g, g_rows, hidden, gpre, picked, hidden_all) = refs[61:67]
    (mask, cut, pasted, o_cut, o_piece) = refs[67:72]
    (z_sems, own_sems, keep_sems, load_sems, g_sems, trade_sems, mask_sems, o_sems) = refs[72:]
    slab_outs = (slab_q, slab_o, slab_i, slab_d)
    place = Place()
    z = place.z
    heads = sel_o.shape[1] // BLOCK
    lanes = heads * BLOCK
    kept_here, waited = [], []

    def keep(src, dst):
        copy = pltpu.make_async_copy(src, dst, keep_sems.at[len(kept_here)])
        copy.start()
        kept_here.append(copy)
        return copy

    def forget(copy):
        copy.wait()
        waited.append(copy)

    relayed = levels == 4

    def far(delta):
        there = (z + delta) % levels
        return (z + there == 3) & (z * there == 0)

    counts = [slabs[0].shape[1] // levels, o_piece.shape[1], slabs[2].shape[1] // levels,
              w_down.shape[1]]

    def rows_of(m, level):
        return rows_at(level * counts[m], counts[m])

    def piece(layer, m):
        if m == 1:
            return o_piece.at[layer]
        if m == 3:
            return w_down.at[layer]
        return slabs[m].at[layer, rows_of(m, z)]

    def spread(layer, m, delta):
        return remote(
            piece(layer, m), slabs[m].at[layer, rows_of(m, z)],
            z_sems.at[0, layer, m, delta - 1], z_sems.at[1, layer, m, delta - 1],
            place.level((z + delta) % levels),
        )

    def arriving(layer, m, delta):
        rows = slabs[m].at[layer, rows_of(m, (z + levels - delta) % levels)]
        return remote(
            rows, rows, z_sems.at[0, layer, m, delta - 1], z_sems.at[1, layer, m, delta - 1],
            place.level((z + delta) % levels),
        )

    def relay(layer, m):
        rows = slabs[m].at[layer, rows_of(m, (z + 2) % levels)]
        return remote(
            rows, rows, z_sems.at[2, layer, m, 0], z_sems.at[1, layer, m, 2 * (z - 1)],
            place.level(3 * (z - 1)),
        )

    def for_spread(layer, m, act_on):
        for delta in range(1, levels):
            if relayed and delta != 2:
                @pl.when(jnp.logical_not(far(delta)))
                def _(delta=delta):
                    act_on(spread(layer, m, delta))
            else:
                act_on(spread(layer, m, delta))

    def own_piece(layer, m):
        return pltpu.make_async_copy(
            piece(layer, m), slabs[m].at[layer, rows_of(m, z)], own_sems.at[layer, m]
        )

    def send_weights(layer, m):
        if m % 2:
            own_piece(layer, m).start()
        for_spread(layer, m, lambda copy: copy.start())

    rows, q_cols = w_q.shape[1], slabs[0].shape[2]
    span = w_q.shape[2] // 3 // PLANE
    ff_rows = w_in.shape[2] // PLANE // levels
    padded = slabs[2].shape[2] // levels - ff_rows

    def cut_weights(layer):
        scaled_q = w_q[layer].astype(F32) * gains[0, layer]
        scaled_i = w_in[layer].astype(F32) * gains[1, layer]
        for t in range(PLANE):
            parts = []
            for kind in range(3):
                low = (kind * PLANE + t) * span
                parts.append(scaled_q[:, low : low + span])
            if q_cols > 3 * span:
                parts.append(jnp.zeros((rows, q_cols - 3 * span), F32))
            cut[layer, t, :rows, :q_cols] = jnp.concatenate(parts, axis=1).astype(BF)
            parts = []
            for zz in range(levels):
                low = (zz * PLANE + t) * ff_rows
                parts.append(scaled_i[:, low : low + ff_rows])
                if padded:
                    parts.append(jnp.zeros((rows, padded), F32))
            cut[layer, t, :rows, q_cols:] = jnp.concatenate(parts, axis=1).astype(BF)

    def trade(layer, e):
        return remote(
            cut.at[layer, place.rank(e)], pasted.at[layer, place.rank()],
            trade_sems.at[0, layer, e], trade_sems.at[1, layer, e], place.other(e),
        )

    def traded(layer, e):
        there = pasted.at[layer, place.rank(e)]
        return remote(
            there, there, trade_sems.at[0, layer, e], trade_sems.at[1, layer, e], place.other(e)
        )

    def start_trade(layer):
        for e in range(1, PLANE):
            trade(layer, e).start()
        own = place.rank()
        pltpu.make_async_copy(
            cut.at[layer, own], pasted.at[layer, own], trade_sems.at[0, layer, 0]
        ).start()

    def end_trade(layer):
        own = place.rank()
        pltpu.make_async_copy(
            cut.at[layer, own], pasted.at[layer, own], trade_sems.at[0, layer, 0]
        ).wait()
        for e in range(1, PLANE):
            traded(layer, e).wait_recv()
        for e in range(1, PLANE):
            trade(layer, e).wait_send()
        for m, low in ((0, 0), (2, q_cols)):
            width = slabs[m].shape[2]
            whole = [pasted[layer, t, :rows, low : low + width].astype(F32) for t in range(PLANE)]
            slabs[m][layer, rows_of(m, z), :] = jnp.concatenate(whole, axis=0).astype(BF)

    trades = place.trades(levels)
    o_trade = remote(
        o_cut, o_piece, o_sems.at[0], o_sems.at[1], place.indexed(place.holder(levels))
    )
    o_local = pltpu.make_async_copy(o_cut, o_piece, o_sems.at[0])

    def mask_to(e):
        there = mask.at[place.y, place.x, :, place.core]
        return remote(own_mask, there, mask_sems.at[0, e], mask_sems.at[1, e], place.other(e))

    def mask_from(e):
        y, core, x = place.turned(e)
        there = mask.at[y, x, :, core]
        return remote(there, there, mask_sems.at[0, e], mask_sems.at[1, e], place.other(e))

    mask_local = pltpu.make_async_copy(
        own_mask, mask.at[place.y, place.x, :, place.core], mask_sems.at[0, 0]
    )

    middle = (z == 1) | (z == 2)

    def relay_on(layer, m):
        if relayed:
            @pl.when(middle)
            def _():
                arriving(layer, m, 2).wait_recv()
                relay(layer, m).start()

    def weights_here(layer, m):
        for delta in range(1, levels):
            if relayed and delta == 2:
                pl.when(jnp.logical_not(middle))(arriving(layer, m, delta).wait_recv)
            else:
                arriving(layer, m, delta).wait_recv()
        for_spread(layer, m, lambda copy: copy.wait_send())
        if m % 2:
            own_piece(layer, m).wait()
        if relayed:
            pl.when(middle)(relay(layer, m).wait_send)

        return keep(slabs[m].at[layer], slab_outs[m].at[layer])

    skip = slabs[2].at[0, :, : adjoint.shape[3]]
    loads = [
        pltpu.make_async_copy(src, dst, load_sems.at[i])
        for i, (src, dst) in enumerate(zip(head_weights, (first, final, skip)))
    ]
    loads[0].start()
    loads[1].start()
    greet(place, levels)

    g_own = g.at[place.y, :, :, place.core]
    g_far = g.at[1 - place.y, :, :, place.core]
    g_local = pltpu.make_async_copy(adjoint, g_own, g_sems.at[0, 0])
    g_peer = remote(adjoint, g_own, g_sems.at[0, 1], g_sems.at[1, 1], place.far(0))
    g_sibling = remote(adjoint, g_own, g_sems.at[0, 2], g_sems.at[1, 2], place.sibling())
    g_pass = remote(g_far, g_far, g_sems.at[0, 3], g_sems.at[1, 3], place.sibling())
    part = exchange[0]
    lines = nrm.at[0]
    bufs = [nrm.at[0], nml.at[0], nrm.at[1], nml.at[1], lines]
    phases = [Exchange(place, p, buf, exchange) for p, buf in enumerate(bufs)]

    def own_half(s):
        return slice(s * HALF_BLOCK, (s + 1) * HALF_BLOCK)

    def chip_of(s, major, minor):
        return (major + s * (minor - major), minor + s * (major - minor))

    def enter(p, s, values):
        if p < 2 * LAYERS:
            values = values * root(values)
        bufs[p][phases[p].own(s)] = values.astype(BF)
        phases[p].start(s)

    def leave(p, s):
        rows = own_half(s)
        total = phases[p].total(s)
        if p == 2 * LAYERS:
            grad_out[rows, :] = total
            return
        layer = p // 2
        if p % 2 == 0:
            values = xs[layer, rows, :] + total
            mid[layer, rows, :] = values
        else:
            values = mid[layer, rows, :] + total
            if layer + 1 < LAYERS:
                xs[layer + 1, rows, :] = values
        enter(p + 1, s, values)

    def run(p, compute, next_weights, more=()):
        more = list(more)
        hooks = [(1, lambda: leave(p - 1, 1))] if p else []
        hooks += [(2, lambda key=key: relay_on(*key)) for key in next_weights]
        phases[p].run(compute, hooks + more)
        leave(p, 0)
        phases[p].near_stage(1)

    send_weights(0, 3)
    o_cut[...] = jnp.zeros(o_cut.shape, BF)
    for layer in range(LAYERS):
        o_cut[layer, :rows, :] = w_out[layer]
    pl.when(trades)(o_trade.start)
    pl.when(jnp.logical_not(trades))(o_local.start)
    cut_weights(0)
    start_trade(0)
    xs[0] = x_in[...].astype(F32)
    for s in range(2):
        enter(0, s, xs[0, own_half(s), :])
    mask_local.start()
    for e in range(1, PLANE):
        mask_to(e).start()
    cut_weights(1)
    end_trade(0)
    send_weights(0, 0)

    @pl.when(trades)
    def _():
        o_trade.wait_recv()
        o_trade.wait_send()

    pl.when(jnp.logical_not(trades))(o_local.wait)
    send_weights(0, 1)
    start_trade(1)
    for copy in (g_local, g_peer, g_sibling):
        copy.start()
    mask_local.wait()
    for e in range(1, PLANE):
        mask_from(e).wait_recv()
        mask_to(e).wait_send()
    relay_on(0, 0)
    relay_on(0, 1)

    def second_layer():
        end_trade(1)
        send_weights(1, 0)
        send_weights(1, 1)

    slab_keeps = []
    for layer in range(LAYERS):
        wq, wo, wi, wd = [slab.at[layer] for slab in slabs]
        slab_keeps.append(weights_here(layer, 0))
        if layer == 0:
            send_weights(0, 2)
        for n in range(0, wide_q.shape[0], 256):
            wide_q[n : n + 256, :] = dot(wq[n : n + 256, :], sel_q[...]).astype(BF)
        slab_keeps.append(weights_here(layer, 1))
        if layer:
            for copy in attn_saved:
                forget(copy)

        def attend(start, s, half, major, layer=layer, wo=wo):
            both = rows_at(start, 2 * BLOCK, 2 * BLOCK)
            projected = dot(nrm[layer, s, major].reshape(2 * BLOCK, nrm.shape[-1]), wide_q[...])
            cosine, sine = rope[:, :BLOCK], rope[:, BLOCK:]
            allowed = [
                mask[chip_of(s, major, block) + (s,)].reshape(BLOCK, BLOCK) > 0 for block in range(2)
            ]
            units = [(block, h) for block in range(2) for h in range(heads)]
            turned = []
            for low in range(0, 2 * lanes, BLOCK):
                value = projected[:, low : low + BLOCK]
                value = value * cosine + pltpu.roll(value, BLOCK // 2, 1) * sine
                turned.append(value.astype(BF))
            values = projected[:, 2 * lanes :].astype(BF)

            def rows_in(array, block):
                return array[block * BLOCK : (block + 1) * BLOCK]

            scores = [
                dot(rows_in(turned[h], block), rows_in(turned[heads + h], block), 1, 1)
                for block, h in units
            ]
            scores = [
                jnp.where(allowed[block], score * (1.0 / math.sqrt(HDIM)), -1e30)
                for (block, h), score in zip(units, scores)
            ]
            tops = [jnp.max(score, axis=-1, keepdims=True) for score in scores]
            scores = [jnp.exp(score - top) for score, top in zip(scores, tops)]
            sums = [jnp.sum(score, axis=-1, keepdims=True) for score in scores]
            probs = [(score / total).astype(BF) for score, total in zip(scores, sums)]
            outs = [
                dot(prob, rows_in(values, block)[:, h * BLOCK : (h + 1) * BLOCK]).astype(BF)
                for (block, h), prob in zip(units, probs)
            ]

            def joined(parts):
                side = [
                    jnp.concatenate(parts[block * heads : (block + 1) * heads], axis=1)
                    for block in range(2)
                ]
                return jnp.concatenate(side, axis=0)

            attended = dot(joined(outs), sel_o[...], 1, 1).astype(BF)
            write_part(part, s, half, attended, wo, 0)
            att[both, :] = attended
            prb[both, :] = joined(probs)
            qkv[both, :] = jnp.concatenate(turned + [values], axis=1)

        more = [(1, second_layer)] if layer == 0 else []
        run(2 * layer, attend, ((layer, 2), (layer, 3)), more)
        attn_saved = [keep(src, dst.at[layer]) for src, dst in zip((qkv, prb, att), kept[2:5])]
        nrm_saved = keep(nrm.at[layer], kept[0].at[layer])
        if layer == 0:
            g_peer.wait_recv()
            g_pass.start()
        slab_keeps.append(weights_here(layer, 2))
        slab_keeps.append(weights_here(layer, 3))
        if layer == 0:
            send_weights(1, 2)
            send_weights(1, 3)
        if layer:
            for copy in mlp_saved:
                forget(copy)

        def perceptron(start, s, half, major, layer=layer, wi=wi, wd=wd):
            rows = rows_at(start, 2 * BLOCK, 2 * BLOCK)
            lifted = dot(nml[layer, s, major].reshape(2 * BLOCK, nml.shape[-1]), wi[...])
            root_two = math.sqrt(2.0 / math.pi)
            square = lifted * lifted
            tanh = jnp.tanh(root_two * lifted * (1.0 + 0.044715 * square))
            activated = (0.5 * lifted * (1.0 + tanh)).astype(BF)
            slope = 0.5 * (1.0 + tanh) + 0.5 * lifted * (1.0 - tanh * tanh) * root_two * (
                1.0 + 3.0 * 0.044715 * square
            )
            write_part(part, s, half, activated, wd, 0)
            act[rows, :] = activated
            gl[rows, :] = slope.astype(BF)

        following = ((layer + 1, 0), (layer + 1, 1)) if layer + 1 < LAYERS else ()
        run(2 * layer + 1, perceptron, following)
        mlp_saved = [keep(src, dst.at[layer]) for src, dst in zip((gl, act), kept[5:7])]
        keep(nml.at[layer], kept[1].at[layer])
        if layer == 0:
            forget(nrm_saved)
            forget(slab_keeps[2])
            loads[2].start()
            loads[0].wait()
            loads[1].wait()
            index = lax.broadcasted_iota(jnp.int32, pick.shape, 0)
            offset = (2 * place.y + place.core) * (pick.shape[0] // (4 * levels))
            pick[...] = jnp.where(index - offset == head_lanes[...], 1.0, 0.0).astype(BF)
            for n in range(0, first.shape[0], 256):
                first_q[n : n + 256, :] = dot(first[n : n + 256, :], pick[...]).astype(BF)
            final_q[...] = dot(pick[...], final[...], 0, 0).astype(BF)

    g_local.wait()
    for copy in (g_sibling, g_pass):
        copy.wait_recv()
    loads[2].wait()
    bias_q = dot(jnp.broadcast_to(bias_first[...], (16, bias_first.shape[1])), pick[...])[:1]
    columns = g.shape[-1]

    def head(start, s, half, major):
        rows = rows_at(start, 2 * BLOCK, 2 * BLOCK)
        pre = dot(lines[s, major].reshape(2 * BLOCK, lines.shape[-1]), first_q[...]) + bias_q
        gate = 1.0 / (1.0 + jnp.exp(-pre))
        hidden[rows, :] = (pre * gate).astype(BF)
        for block in range(2):
            here = rows_at(start + block * BLOCK, BLOCK, BLOCK)
            g_rows[here, :] = g[chip_of(s, major, block) + (s,)].reshape(BLOCK, columns)
        there = g_rows[rows, :]
        grad_hidden = dot(there, final_q[...], 1, 1)
        gpre[rows, :] = (grad_hidden * (gate * (1.0 + pre * (1.0 - gate)))).astype(BF)
        row = lax.broadcasted_iota(jnp.int32, (2 * BLOCK, 1), 0)
        y = major + s * (row // BLOCK - major)
        mine = (row // HALF_BLOCK % 2 == place.core) & (y == place.y)
        mine = jnp.where(mine, there.astype(F32), 0.0).astype(BF)
        whole = dot(gpre[rows, :], first_q[...], 1, 1) + dot(mine, skip[...], 1, 1)
        part[s, half] = blocked(whole.astype(BF))

    run(2 * LAYERS, head, ())

    keep(lines, kept[7])
    keep(hidden, kept[8])
    keep(gpre, kept[9])
    keep(g_rows, kept[11])
    for s in range(2):
        for major in range(2):
            n = (2 * s + major) * 2 * BLOCK
            rows = lines[s, major].reshape(2 * BLOCK, lines.shape[-1])
            picked[n : n + 2 * BLOCK, :] = dot(rows, pick[...]).astype(BF)
    keep(picked, kept[10])
    mine = []
    for x in range(2):
        mine += [lines[0, place.y, x, place.core], lines[1, x, place.y, place.core]]
    mine = jnp.concatenate(mine, axis=0)
    pre = dot(mine, first[...]) + bias_first[...].astype(F32)
    hidden_all[...] = (pre / (1.0 + jnp.exp(-pre))).astype(BF)
    out = dot(hidden_all[...], final[...]) + bias_last[...].astype(F32)
    predictions[...] = (out + dot(mine, skip[...])).astype(BF)
    leave(2 * LAYERS, 1)
    for copy in (g_peer, g_sibling, g_pass):
        copy.wait_send()
    for copy in kept_here:
        if not any(copy is other for other in waited):
            copy.wait()


def norm_back(values, q):
    scale = root(values)
    n = values * scale
    return scale * (q - n * jnp.mean(q * n, axis=-1, keepdims=True))


def backward_kernel(levels, *refs):
    (rope, sel_q, sel_o, gains, w_q, w_in) = refs[:6]
    dy_in, stored, head_stored = refs[6], refs[7:20], refs[20:25]
    (dx_out, small_out, q_out, o_out, i_out, d_out, q_gain, i_gain) = refs[25:33]
    (first_out, out_out, skip_out) = refs[33:36]
    exchange, ag = refs[36:43], refs[43]
    loaded, gp = refs[44:57], refs[57]
    stages, arrivals = refs[58:65], refs[65:72]
    own_sums, acc, o_acc = refs[72:76], refs[76], refs[77]
    o_cut, o_pasted = refs[78], refs[79]
    (small_own, small_x, small_z) = refs[80:83]
    row_buf = refs[83]
    z_sems, load_sems, small_sems, trade_sems, o_sems, row_sem = refs[84:]
    (nml, act, gl, wi, wd, mid, nrm, qkv, prb, att, wq, wo, xs) = loaded
    part = exchange[0]
    place = Place()
    z = place.z
    heads = sel_o.shape[1] // BLOCK
    lanes = heads * BLOCK

    def load(layer, i):
        return pltpu.make_async_copy(stored[i].at[layer], loaded[i], load_sems.at[i])

    lines = ag.at[1]
    h_cols, half_width = small_own.shape[2], nrm.shape[-1] // 2
    gpre, hidden = gp.at[:, :h_cols], nrm.at[:, :, :, :, :, :h_cols]
    picked = nrm.at[:, :, :, :, :, half_width : half_width + h_cols]
    g = qkv.at[:, : stages[5].shape[1]]
    head_loads = [
        pltpu.make_async_copy(src, dst, load_sems.at[len(loaded) + i])
        for i, (src, dst) in enumerate(zip(head_stored, (lines, gpre, hidden, picked, g)))
    ]
    mlp_part, attn_part = range(5), range(6, 12)
    norm_loads = [pltpu.make_async_copy(stored[i], loaded[i], load_sems.at[i]) for i in (5, 12)]
    for copy in norm_loads:
        copy.start()
    dy_load = pltpu.make_async_copy(dy_in, dx_out, load_sems.at[len(loaded) + 5])
    dy_load.start()
    for copy in head_loads:
        copy.start()
    for i in mlp_part:
        load(LAYERS - 1, i).start()
    greet(place, levels)

    def count_of(m):
        return arrivals[m].shape[2]

    def slot(m, layer):
        return layer if m < 4 else 0

    relayed = levels == 4
    middle = (z == 1) | (z == 2)

    def send(layer, m, delta):
        there = (z + delta) % levels
        return remote(
            stages[m].at[rows_at(there * count_of(m), count_of(m))],
            arrivals[m].at[slot(m, layer), delta - 1],
            z_sems.at[0, layer, m, delta - 1],
            z_sems.at[1, layer, m, delta - 1],
            place.level(there),
        )

    def far(delta):
        there = (z + delta) % levels
        return (z + there == 3) & (z * there == 0)

    def hand(layer, m, delta):
        there = (z + delta) % levels
        return remote(
            stages[m].at[rows_at(there * count_of(m), count_of(m))],
            arrivals[m].at[slot(m, layer), levels - 1],
            z_sems.at[0, layer, m, delta - 1],
            z_sems.at[1, layer, m, levels - 1],
            place.level(1 + z // 3),
        )

    def send_first(layer, m):
        for delta in range(1, levels):
            if not relayed:
                send(layer, m, delta).start()
            elif delta == 2:
                pl.when(jnp.logical_not(middle))(send(layer, m, delta).start)
            else:
                pl.when(far(delta))(hand(layer, m, delta).start)
                pl.when(jnp.logical_not(far(delta)))(send(layer, m, delta).start)

    def send_rest(layer, m):
        if relayed:
            @pl.when(middle)
            def _():
                hand(layer, m, 1).wait_recv()
                rows = rows_at((z + 2) % levels * count_of(m), count_of(m))
                total = stages[m][rows, :].astype(F32)
                total = total + arrivals[m][slot(m, layer), levels - 1].astype(F32)
                stages[m][rows, :] = total.astype(BF)
                send(layer, m, 2).start()

    def sent(layer, m):
        for delta in range(1, levels):
            send(layer, m, delta).wait_send()

    def result(layer, m):
        if m > 4:
            return (out_out, skip_out)[m - 5]
        if m == 3:
            return d_out.at[layer]
        return own_sums[min(m, 3)].at[slot(m, layer)]

    def weight_grad(layer, m, left, right, tile):
        width = left.shape[-1]
        if m < 4 and layer + 1 < LAYERS:
            sent(layer + 1, m)
        for low in range(0, width, tile):
            here = slice(low, min(low + tile, width))
            stages[m][here, :] = dot(flat(left, here), flat(right), 0, 0).astype(BF)
        send_first(layer, m)
        out = result(layer, m)
        out[...] = stages[m][rows_at(z * count_of(m), count_of(m)), :].astype(out.dtype)

    bufs = [ag.at[p % 2] for p in range(PHASES)]
    phases = [Exchange(place, p, buf, exchange) for p, buf in enumerate(bufs)]

    def own_half(s):
        return slice(s * HALF_BLOCK, (s + 1) * HALF_BLOCK)

    def enter(p, s):
        bufs[p][phases[p].own(s)] = dx_out[own_half(s), :].astype(BF)
        phases[p].start(s)

    def leave(p, s):
        rows = own_half(s)
        values = (mid if p % 2 == 0 else xs)[LAYERS - 1 - p // 2, rows, :]
        dx_out[rows, :] += norm_back(values, phases[p].total(s))
        if p + 1 < PHASES:
            enter(p + 1, s)

    def run(p, compute, relays):
        hooks = [(1, lambda: leave(p - 1, 1))] if p else []
        hooks += [(2, lambda key=key: send_rest(*key)) for key in relays]
        phases[p].run(compute, hooks)

    dy_load.wait()
    for copy in norm_loads:
        copy.wait()
    for s in range(2):
        enter(0, s)

    for copy in head_loads:
        copy.wait()
    last = LAYERS - 1
    bias_sum = jnp.sum(gpre[...].astype(F32), axis=0, keepdims=True)
    small_own[1] = jnp.broadcast_to(bias_sum, small_own.shape[1:])
    to_x = remote(
        small_own.at[1], small_x, small_sems.at[0, 0], small_sems.at[1, 0], place.near(0)
    )
    to_x.start()
    weight_grad(last, 5, hidden, g, 4 * BLOCK)
    weight_grad(last, 6, picked, g, 4 * BLOCK)
    weight_grad(last, 4, lines, gpre, 5 * BLOCK)
    g_sum = jnp.sum(g[...].astype(F32), axis=0, keepdims=True)
    to_x.wait()
    small_z[0, :, : g_sum.shape[1]] = jnp.broadcast_to(g_sum, (8, g_sum.shape[1]))
    small_z[0, :, g_sum.shape[1] :] = small_own[1] + small_x[...]
    to_z = [
        remote(
            small_z.at[0], small_z.at[d], small_sems.at[0, d], small_sems.at[1, d],
            place.level((z + d) % levels),
        )
        for d in range(1, levels)
    ]
    for copy in to_z:
        copy.start()
    for i in attn_part:
        load(last, i).start()

    relays = [(last, 5), (last, 6), (last, 4)]
    for layer in reversed(range(LAYERS)):
        p = 2 * (LAYERS - 1 - layer)
        buf = bufs[p]
        for i in mlp_part:
            load(layer, i).wait()

        def perceptron(start, s, half, major, buf=buf):
            rows = rows_at(start, 2 * BLOCK, 2 * BLOCK)
            grad_act = dot(buf[s, major].reshape(2 * BLOCK, buf.shape[-1]), wd[...], 1, 1)
            grad_lift = (grad_act * gl[rows, :].astype(F32)).astype(BF)
            write_part(part, s, half, grad_lift, wi, 1)
            gl[rows, :] = grad_lift

        run(p, perceptron, relays)
        weight_grad(layer, 3, act, buf, 2 * BLOCK)
        leave(p, 0)
        weight_grad(layer, 2, nml, gl, 5 * BLOCK)
        phases[p].near_stage(1)
        if layer > 0:
            for i in mlp_part:
                load(layer - 1, i).start()
        for i in attn_part:
            load(layer, i).wait()
        buf = bufs[p + 1]

        def attend(start, s, half, major, buf=buf):
            cosine, sine = rope[:, :BLOCK], rope[:, BLOCK:]
            both = rows_at(start, 2 * BLOCK, 2 * BLOCK)
            there = buf[s, major].reshape(2 * BLOCK, buf.shape[-1])
            grad_heads = dot(there, wo[...], 1, 1).astype(BF)
            grad_heads = dot(grad_heads, sel_o[...]).astype(BF)
            kept, probs = qkv[both, :], prb[both, :]
            units = [(block, h) for block in range(2) for h in range(heads)]

            def unit(array, block, h, kind=0):
                low = kind * lanes + h * BLOCK
                return array[block * BLOCK : (block + 1) * BLOCK, low : low + BLOCK]

            queries, keys, values = [[unit(kept, *u, kind) for u in units] for kind in range(3)]
            probs = [unit(probs, *u) for u in units]
            grads = [unit(grad_heads, *u) for u in units]
            grad_probs = [dot(grad, value, 1, 1) for grad, value in zip(grads, values)]
            grad_values = [dot(prob, grad, 0, 0).astype(BF) for prob, grad in zip(probs, grads)]
            wide = [prob.astype(F32) for prob in probs]
            inner = [
                jnp.sum(prob * grad, axis=-1, keepdims=True) for prob, grad in zip(wide, grad_probs)
            ]
            grad_scores = [
                (prob * (grad - total)).astype(BF)
                for prob, grad, total in zip(wide, grad_probs, inner)
            ]
            grad_queries = [dot(grad, key) for grad, key in zip(grad_scores, keys)]
            grad_keys = [dot(grad, query, 0, 0) for grad, query in zip(grad_scores, queries)]
            packed = []
            for parts in (grad_queries, grad_keys):
                for h in range(heads):
                    turned = jnp.concatenate([parts[h], parts[heads + h]], axis=0)
                    turned = turned * (1.0 / math.sqrt(HDIM))
                    turned = turned * cosine - pltpu.roll(turned, BLOCK // 2, 1) * sine
                    packed.append(turned.astype(BF))
            for h in range(heads):
                packed.append(jnp.concatenate([grad_values[h], grad_values[heads + h]], axis=0))
            packed = dot(jnp.concatenate(packed, axis=1), sel_q[...], 1, 1).astype(BF)
            write_part(part, s, half, packed, wq, 1)
            gp[both, :] = packed

        run(p + 1, attend, [(layer, 3), (layer, 2)])
        weight_grad(layer, 0, nrm, gp, 5 * BLOCK)
        leave(p + 1, 0)
        weight_grad(layer, 1, att, buf, 2 * BLOCK)
        phases[p + 1].near_stage(1)
        if layer > 0:
            for i in attn_part:
                load(layer - 1, i).start()
        relays = [(layer, 0), (layer, 1)]
    leave(PHASES - 1, 1)
    for key in relays:
        send_rest(*key)

    total = small_z[0]
    for copy, d in zip(to_z, range(1, levels)):
        copy.wait_recv()
        total = total + small_z[d]
    small_out[...] = total
    for copy in to_z:
        copy.wait_send()
    rows = w_q.shape[1]
    pad_rows = up16(rows)
    kinds = {0: 0, 2: 1, 4: 2}

    def cut_at(m, t):
        start = rows_at((t + PLANE * kinds[m]) * pad_rows, pad_rows)
        return wi.at[start, : stages[m].shape[1]]

    def pasted_at(layer, m, t):
        start = rows_at((slot(m, layer) * PLANE + t) * pad_rows, pad_rows)
        return {0: gl, 2: act, 4: wd}[m].at[start, : stages[m].shape[1]]

    def trade(layer, m, e):
        kind = kinds[m]
        return remote(
            cut_at(m, place.rank(e)), pasted_at(layer, m, place.rank()),
            trade_sems.at[0, layer, kind, e], trade_sems.at[1, layer, kind, e], place.other(e),
        )

    def traded(layer, m, e):
        there = pasted_at(layer, m, place.rank(e))
        return remote(
            there, there, trade_sems.at[0, layer, kinds[m], e],
            trade_sems.at[1, layer, kinds[m], e], place.other(e),
        )

    def own_trade(layer, m):
        own = place.rank()
        return pltpu.make_async_copy(
            cut_at(m, own), pasted_at(layer, m, own), trade_sems.at[0, layer, kinds[m], 0]
        )

    stayed = set()

    def wait_own_trade(layer, m):
        if (layer, m) not in stayed:
            own_trade(layer, m).wait()
            stayed.add((layer, m))

    def pasted(layer, m, t):
        return pasted_at(layer, m, t)[:rows, :].astype(F32)

    trades = place.trades(levels)

    def o_trade(layer):
        return remote(
            o_cut.at[layer], o_pasted.at[layer], o_sems.at[0, layer], o_sems.at[1, layer],
            place.indexed(place.held(levels)),
        )

    def o_local(layer):
        return pltpu.make_async_copy(o_cut.at[layer], o_pasted.at[layer], o_sems.at[0, layer])

    def finalize(layer, m):
        own = result(layer, m)
        if m == 3 or m > 4:
            total = own
        else:
            total = o_acc if m == 1 else acc.at[:, : own.shape[1]]
            total[...] = own[...].astype(F32)
        for delta in range(1, levels):
            def add(delta=delta):
                send(layer, m, delta).wait_recv()
                total[...] += arrivals[m][slot(m, layer), delta - 1].astype(F32)

            if relayed and delta != 2:
                source = (z + levels - delta) % levels
                pl.when(jnp.logical_not((z + source == 3) & (z * source == 0)))(add)
            else:
                add()
        if m > 3 or layer == 0:
            sent(layer, m)
        if m == 1:
            o_cut[layer] = total[...].astype(BF)
            pl.when(trades)(o_trade(layer).start)
            pl.when(jnp.logical_not(trades))(o_local(layer).start)
        elif m in kinds:
            if m < 4 and layer + 1 < LAYERS:
                wait_own_trade(layer + 1, m)
                for e in range(1, PLANE):
                    trade(layer + 1, m, e).wait_send()
            values = total[...].astype(BF).astype(F32)
            for t in range(PLANE):
                cut_at(m, t)[:rows, :] = values[t * rows : (t + 1) * rows].astype(BF)
            own_trade(layer, m).start()
            for e in range(1, PLANE):
                trade(layer, m, e).start()

    def wait_trade(layer, m):
        wait_own_trade(layer, m)
        for e in range(1, PLANE):
            traded(layer, m, e).wait_recv()
        if m > 3 or layer == 0:
            for e in range(1, PLANE):
                trade(layer, m, e).wait_send()

    span = w_q.shape[2] // 3 // PLANE
    ff_rows = w_in.shape[2] // PLANE // levels
    padded_rows = stages[2].shape[1] // levels

    def rows_out(layer, out):
        here = row_buf.at[:, : out.shape[2]]
        return pltpu.make_async_copy(here, out.at[layer], row_sem.at[0])

    on_the_way = []

    def write_rows(layer, parts, out, kind, w, gain_out):
        whole = jnp.concatenate(parts, axis=1)
        gain_out[layer] = jnp.sum(whole * w[layer].astype(F32), axis=1, keepdims=True)
        if on_the_way:
            on_the_way.pop().wait()
        row_buf[:, : out.shape[2]] = whole * gains[kind, layer]
        copy = rows_out(layer, out)
        copy.start()
        on_the_way.append(copy)

    def assemble(layer):
        wait_trade(layer, 0)
        ranks = [pasted(layer, 0, t) for t in range(PLANE)]
        parts = [rank[:, kind * span : (kind + 1) * span] for kind in range(3) for rank in ranks]
        write_rows(layer, parts, q_out, 0, w_q, q_gain)

    def assemble_mlp(layer):
        wait_trade(layer, 2)
        ranks = [pasted(layer, 2, t) for t in range(PLANE)]
        parts = [
            rank[:, zz * padded_rows : zz * padded_rows + ff_rows]
            for zz in range(levels) for rank in ranks
        ]
        write_rows(layer, parts, i_out, 1, w_in, i_gain)

    def assemble_out(layer):
        @pl.when(trades)
        def _():
            o_trade(layer).wait_recv()
            o_trade(layer).wait_send()

        pl.when(jnp.logical_not(trades))(o_local(layer).wait)
        o_out[layer] = o_pasted[layer, :rows, :].astype(F32)

    head_rows, head_share = out_out.shape[0], first_out.shape[1] // 4 // levels

    def assemble_head():
        wait_trade(last, 4)
        sums = []
        for q in range(4):
            sums.append(pasted(last, 4, 2 * q) + pasted(last, 4, 2 * q + 1))
        parts = []
        for zz in range(levels):
            for q in range(4):
                parts.append(sums[q][:, zz * head_rows : zz * head_rows + head_share])
        first_out[...] = jnp.concatenate(parts, axis=1)

    for key in [(last, 5), (last, 6), (last, 4)] + [(last, m) for m in (3, 2, 0, 1)]:
        finalize(*key)
    for layer in reversed(range(LAYERS - 1)):
        finalize(layer, 3)
        finalize(layer, 2)
    assemble_head()
    for layer in reversed(range(LAYERS)):
        if layer == 0:
            finalize(layer, 0)
            finalize(layer, 1)
        assemble_mlp(layer)
        assemble(layer)
        assemble_out(layer)
    on_the_way.pop().wait()


def shape(*dims, dtype=BF):
    return jax.ShapeDtypeStruct(dims, dtype)


def rope_table():
    position = np.arange(2 * BLOCK) % ROW_LEN
    inverse = ROTARY_BASE ** (-np.arange(HALF) / HALF)
    angles = (position[:, None] * inverse[None, :]).astype(np.float32)
    table = np.zeros((2 * BLOCK, 2, 2, BLOCK // 2), np.float32)
    table[:, 0, :, :HALF] = np.cos(angles)[:, None]
    table[:, 1, 0, :HALF] = -np.sin(angles)
    table[:, 1, 1, :HALF] = np.sin(angles)
    return table.reshape(2 * BLOCK, 2 * BLOCK)


def lane_of(index):
    head, inside = divmod(index, HDIM)
    half, place = divmod(inside, HALF)
    return head * BLOCK + half * (BLOCK // 2) + place


def per_device(devices, x, segments, padded, w_qkv, w_out, w_in, w_down, gain_attn, gain_mlp,
               head_first, head_first_bias, head_final, head_bias, head_skip, adjoint):
    levels = devices // PLANE
    width = x.shape[1]
    ff = w_in.shape[2]
    columns = head_final.shape[1]
    tokens = PLANE * BLOCK
    heads = width // HDIM // PLANE
    span = heads * HDIM
    rows = width // devices
    out_rows = up16(rows)
    ff_rows = ff // devices
    down_rows = up16(ff_rows)
    head_share = 2 * width // devices
    head_rows = up16(head_share)
    used_cols, o_rows, f_cols = 3 * span, levels * out_rows, levels * down_rows
    h_cols = -(-levels * head_rows // 128) * 128
    q_cols = -(-used_cols // 128) * 128
    lanes = heads * BLOCK

    sel_q = np.zeros((q_cols, 3 * lanes), np.float32)
    sel_o = np.zeros((o_rows, lanes), np.float32)
    for e in range(span):
        for kind in range(3):
            sel_q[kind * span + e, kind * lanes + lane_of(e)] = 1
        sel_o[e // rows * out_rows + e % rows, lane_of(e)] = 1
    sel_q, sel_o = jnp.asarray(sel_q, BF), jnp.asarray(sel_o, BF)
    rope = jnp.asarray(rope_table())
    head_lanes = np.full((1, h_cols), -width, np.int32)
    for zz in range(levels):
        here = slice(zz * head_rows, zz * head_rows + head_share)
        head_lanes[0, here] = 4 * head_share * zz + np.arange(head_share)
    head_lanes = jnp.asarray(head_lanes)

    seg = segments.reshape(2, HALF_BLOCK)
    open_key = padded.reshape(2, HALF_BLOCK) == 0
    within = jnp.arange(HALF_BLOCK)
    static = within[:, None] // ROW_LEN == within[None, :] // ROW_LEN
    static = static & (within[None, :] <= within[:, None])
    allowed = static[None] & (seg[:, :, None] == seg[:, None, :])
    allowed = allowed & (open_key[:, None, :] | (within[:, None] == within[None, :])[None])
    core = lax.axis_index("wide") % 2
    side = jnp.arange(BLOCK)[None, None, :] // HALF_BLOCK == core
    own_mask = (jnp.concatenate([allowed, allowed], axis=-1) & side).astype(BF)

    gains = jnp.stack([gain_attn, gain_mlp]).astype(F32)[..., None]
    d_piece = w_down
    if down_rows != ff_rows:
        d_piece = jnp.pad(w_down, [(0, 0), (0, down_rows - ff_rows), (0, 0)])
    pad_rows = up16(rows)

    in_blocks = (2, 2, 2, 2, HALF_BLOCK)
    layer_shapes = [
        in_blocks + (width,), in_blocks + (width,), (tokens, 3 * lanes), (tokens, lanes), (tokens, o_rows),
        (tokens, f_cols), (tokens, f_cols),
    ]
    slab_shapes = [(width, q_cols), (o_rows, width), (width, f_cols), (f_cols, width)]
    outs = [
        shape(2 * BLOCK, columns), shape(BLOCK, width, dtype=F32),
        shape(LAYERS, BLOCK, width, dtype=F32), shape(LAYERS, BLOCK, width, dtype=F32),
    ]
    vmem_outs = len(outs)
    outs += [shape(LAYERS, *dims) for dims in layer_shapes]
    outs += [shape(*in_blocks, width)] + [shape(tokens, h_cols)] * 3 + [shape(tokens, columns)]
    outs += [shape(LAYERS, *dims) for dims in slab_shapes]
    (predictions, grad_final, xs, mid, nrm, nml, qkv, prb, att, gl, act, lines, hidden, gpre,
     picked, g, wq, wo, wi, wd) = pl.pallas_call(
        lambda *refs: forward_kernel(levels, *refs),
        out_shape=outs,
        in_specs=[VMEM] * 13 + [ANY] * 4,
        out_specs=[VMEM] * vmem_outs + [ANY] * (len(outs) - vmem_outs),
        scratch_shapes=exchange_scratch(width, PHASES + 1)
        + [pltpu.VMEM((LAYERS,) + dims, BF) for dims in layer_shapes[:2]]
        + [pltpu.VMEM(dims, BF) for dims in layer_shapes[2:]]
        + [pltpu.VMEM((LAYERS,) + dims, BF) for dims in slab_shapes]
        + [
            pltpu.VMEM((width, 3 * lanes), BF), pltpu.VMEM((width, width), BF),
            pltpu.VMEM((width, columns), BF), pltpu.VMEM((width, h_cols), BF),
            pltpu.VMEM((width, h_cols), BF), pltpu.VMEM((h_cols, columns), BF),
            pltpu.VMEM(in_blocks + (columns,), BF), pltpu.VMEM((tokens, columns), BF),
            pltpu.VMEM((tokens, h_cols), BF),
            pltpu.VMEM((tokens, h_cols), BF), pltpu.VMEM((tokens, h_cols), BF),
            pltpu.VMEM((2 * BLOCK, width), BF),
            pltpu.VMEM(in_blocks + (BLOCK,), BF),
            pltpu.VMEM((LAYERS, PLANE, pad_rows, q_cols + f_cols), BF),
            pltpu.VMEM((LAYERS, PLANE, pad_rows, q_cols + f_cols), BF),
            pltpu.VMEM((LAYERS, out_rows, width), BF),
            pltpu.VMEM((LAYERS, out_rows, width), BF),
            pltpu.SemaphoreType.DMA((3, LAYERS, 4, levels - 1)),
            pltpu.SemaphoreType.DMA((LAYERS, 4)),
            pltpu.SemaphoreType.DMA((32,)),
            pltpu.SemaphoreType.DMA((3,)),
            pltpu.SemaphoreType.DMA((2, 4)),
            pltpu.SemaphoreType.DMA((2, LAYERS, PLANE)),
            pltpu.SemaphoreType.DMA((2, PLANE)),
            pltpu.SemaphoreType.DMA((2,)),
        ],
        compiler_params=pltpu.CompilerParams(
            collective_id=1, has_side_effects=True, vmem_limit_bytes=62 * MIB
        ),
        name="decoder_forward",
    )(x, own_mask, rope, sel_q, sel_o, head_lanes,
      adjoint.reshape(2, 2, HALF_BLOCK, columns), head_first_bias[None], head_bias[None], gains,
      w_qkv, w_in, w_out, d_piece, head_first, head_final, head_skip)

    chunk = [PLANE * rows, out_rows, PLANE * rows, down_rows, PLANE * rows, head_rows, head_rows]
    cols = [q_cols, width, f_cols, width, h_cols, columns, columns]
    stage_rows = [levels * n for n in chunk[:5]] + [h_cols] * 2
    kept_shapes = [
        in_blocks + (width,), (tokens, f_cols), (tokens, f_cols), (width, f_cols), (f_cols, width),
        (LAYERS, BLOCK, width), in_blocks + (width,), (tokens, 3 * lanes), (tokens, lanes),
        (tokens, o_rows), (width, q_cols), (o_rows, width), (LAYERS, BLOCK, width),
    ]
    small_cols = columns + h_cols
    outs = [
        shape(BLOCK, width, dtype=F32), shape(8, small_cols, dtype=F32),
        shape(LAYERS, rows, 3 * width, dtype=F32), shape(LAYERS, rows, width, dtype=F32),
        shape(LAYERS, rows, ff, dtype=F32), shape(LAYERS, down_rows, width, dtype=F32),
        shape(LAYERS, rows, 1, dtype=F32), shape(LAYERS, rows, 1, dtype=F32),
        shape(rows, width, dtype=F32), shape(head_rows, columns, dtype=F32),
        shape(head_rows, columns, dtype=F32),
    ]
    (input_grad, small, q_grad, o_grad, i_grad, d_grad, q_gain, i_gain, g_first, g_out,
     g_skip) = pl.pallas_call(
        lambda *refs: backward_kernel(levels, *refs),
        out_shape=outs,
        in_specs=[VMEM] * 6 + [ANY] * 19,
        out_specs=[VMEM, VMEM, ANY, VMEM, ANY] + [VMEM] * (len(outs) - 5),
        scratch_shapes=exchange_scratch(width, PHASES)
        + [pltpu.VMEM((2,) + in_blocks + (width,), BF)]
        + [pltpu.VMEM(dims, F32 if dims[0] == LAYERS and dims[1] == BLOCK else BF) for dims in kept_shapes]
        + [pltpu.VMEM((tokens, q_cols), BF)]
        + [pltpu.VMEM((stage_rows[m], cols[m]), BF) for m in range(7)]
        + [
            pltpu.VMEM((LAYERS if m < 4 else 1, levels, chunk[m], cols[m]), BF)
            for m in range(7)
        ]
        + [
            pltpu.VMEM((LAYERS if m < 4 else 1, chunk[m], cols[m]), BF) for m in (0, 1, 2, 4)
        ]
        + [pltpu.VMEM((chunk[0], max(f_cols, q_cols)), F32), pltpu.VMEM((out_rows, width), F32)]
        + [pltpu.VMEM((LAYERS, out_rows, width), BF)] * 2
        + [
            pltpu.VMEM((2, 8, h_cols), F32), pltpu.VMEM((8, h_cols), F32),
            pltpu.VMEM((levels, 8, small_cols), F32),
            pltpu.VMEM((rows, max(ff, 3 * width)), F32),
            pltpu.SemaphoreType.DMA((2, LAYERS, 7, levels)),
            pltpu.SemaphoreType.DMA((20,)),
            pltpu.SemaphoreType.DMA((2, levels)),
            pltpu.SemaphoreType.DMA((2, LAYERS, 3, PLANE)),
            pltpu.SemaphoreType.DMA((2, LAYERS)),
            pltpu.SemaphoreType.DMA((1,)),
        ],
        compiler_params=pltpu.CompilerParams(
            collective_id=2, has_side_effects=True, vmem_limit_bytes=62 * MIB
        ),
        name="decoder_backward",
    )(rope, sel_q, sel_o, gains, w_qkv, w_in, grad_final, nml, act, gl, wi, wd, mid, nrm, qkv, prb,
      att, wq, wo, xs, lines, gpre, hidden.reshape(in_blocks + (h_cols,)),
      picked.reshape(in_blocks + (h_cols,)), g)

    z, narrow = lax.axis_index("wide") // 4, lax.axis_index("narrow")
    g_first_bias = lax.dynamic_slice(small[0], (columns + z * head_rows + narrow * rows,), (rows,))
    return (
        predictions, input_grad, q_grad, o_grad, i_grad, d_grad[:, :ff_rows], q_gain[..., 0],
        i_gain[..., 0], g_first, g_first_bias, g_out[:head_share], small[0, :columns],
        g_skip[:head_share],
    )


def solution(mesh):
    devices = mesh.shape["wide"] * mesh.shape["narrow"]
    both = ("wide", "narrow")
    weight, gain = P(None, both, None), P(None, both)
    return jax.shard_map(
        lambda *arrays: per_device(devices, *arrays),
        mesh=mesh,
        in_specs=(
            P(both, None), P(both), P(both), weight, weight, weight, weight, gain, gain, P(), P(),
            P(None, "narrow"), P("narrow"), P(None, "narrow"), P("wide", "narrow"),
        ),
        out_specs=(
            P("wide", "narrow"), P(both, None), weight, weight, weight, weight, gain, gain,
            P(both, None), P(both), P("wide", "narrow"), P("narrow"), P("wide", "narrow"),
        ),
        check_vma=False,
    )
```

```python
import math

import jax
import jax.numpy as jnp
import numpy as np
from jax import lax
from jax.experimental import pallas as pl
from jax.experimental.pallas import tpu as pltpu
from jax.sharding import PartitionSpec as P

HDIM = 80
HALF = HDIM // 2
LAYERS = 2
ROW_LEN = 16
BLOCK = 128
HALF_BLOCK = BLOCK // 2
PLANE = 8
PHASES = 2 * LAYERS
MESH = pl.DeviceIdType.MESH
BF = jnp.bfloat16
F32 = jnp.float32
EPS = 1e-06
ROTARY_BASE = 10000.0
MIB = 1024 * 1024
VMEM = pl.BlockSpec(memory_space=pltpu.VMEM)
ANY = pl.BlockSpec(memory_space=pl.ANY)


def up16(rows):
    return -(-rows // 16) * 16


def rows_at(start, count, step=16):
    return pl.ds(pl.multiple_of(start, step), count)


def dot(a, b, ca=1, cb=0):
    return lax.dot_general(a, b, (((ca,), (cb,)), ((), ())), preferred_element_type=F32)


class Place:
    def __init__(self):
        wide = lax.axis_index("wide")
        self.x = lax.axis_index("narrow")
        self.core = wide % 2
        self.y = (wide // 2) % 2
        self.z = wide // 4

    def device(self, z, y, core, x):
        return (z * 4 + y * 2 + core, x)

    def sibling(self):
        return self.device(self.z, self.y, 1 - self.core, self.x)

    def major(self, s, far=0):
        return (self.y + s * (self.x - self.y) + far) % 2

    def minor(self, s, near=0):
        return (self.x + s * (self.y - self.x) + near) % 2

    def near(self, s):
        return self.device(self.z, (self.y + s) % 2, self.core, (self.x + 1 - s) % 2)

    def far(self, s):
        return self.device(self.z, (self.y + 1 - s) % 2, self.core, (self.x + s) % 2)

    def level(self, z):
        return self.device(z, self.y, self.core, self.x)

    def turned(self, e):
        return (self.y + e // 4) % 2, (self.core + e // 2) % 2, (self.x + e) % 2

    def other(self, e):
        return self.device(self.z, *self.turned(e))

    def rank(self, e=0):
        y, core, x = self.turned(e)
        return 4 * y + 2 * core + x

    def indexed(self, index):
        return (index // 2, index % 2)

    def holder(self, levels):
        index = PLANE * self.z + self.rank()
        return index % levels * PLANE + index // levels

    def held(self, levels):
        return levels * self.rank() + self.z

    def trades(self, levels):
        return self.holder(levels) != PLANE * self.z + self.rank()


def greet(place, levels):
    barrier = pltpu.get_barrier_semaphore()
    others = [place.other(e) for e in range(1, PLANE)]
    others += [place.level((place.z + d) % levels) for d in range(1, levels)]
    for other in others:
        pl.semaphore_signal(barrier, inc=1, device_id=other, device_id_type=MESH)
    trades = place.trades(levels)

    @pl.when(trades)
    def _():
        for index in (place.holder(levels), place.held(levels)):
            pl.semaphore_signal(
                barrier, inc=1, device_id=place.indexed(index), device_id_type=MESH
            )
        pl.semaphore_wait(barrier, len(others) + 2)

    @pl.when(jnp.logical_not(trades))
    def _():
        pl.semaphore_wait(barrier, len(others))


def remote(src, dst, send, recv, device):
    return pltpu.make_async_remote_copy(
        src_ref=src, dst_ref=dst, send_sem=send, recv_sem=recv, device_id=device,
        device_id_type=MESH,
    )


class Exchange:
    def __init__(self, place, phase, buf, scratch):
        (self.part, self.recv_s, self.send_f, self.recv_f, self.send_n, self.recv_n, self.sems) = scratch
        self.place, self.phase, self.buf = place, phase, buf

    def copy(self, s, kind, src, dst, device):
        sems = self.sems
        return remote(
            src, dst, sems.at[self.phase, s, 0, kind], sems.at[self.phase, s, 1, kind], device
        )

    def block(self, s, far, near, core):
        place = self.place
        return self.buf.at[s, place.major(s, far), place.minor(s, near), core]

    def own(self, s):
        return (s, self.place.major(s), self.place.minor(s), self.place.core)

    def to_near(self, s, far=0, near=0):
        rows = self.block(s, far, near, self.place.core)
        return self.copy(s, 0, rows, rows, self.place.near(s))

    def to_far(self, s, far=0, near=0):
        rows = self.block(s, far, near, self.place.core)
        return self.copy(s, 1, rows, rows, self.place.far(s))

    def pass_far(self, s, far=0, near=1):
        rows = self.block(s, far, near, self.place.core)
        return self.copy(s, 2, rows, rows, self.place.far(s))

    def sibling(self, s, kind, core):
        if kind < 2:
            rows = self.block(s, 0, kind, core)
        else:
            rows = self.buf.at[s, self.place.major(s, 1), :, core]
        return self.copy(s, 3 + kind, rows, rows, self.place.sibling())

    def to_sibling(self, s, kind):
        return self.sibling(s, kind, self.place.core)

    def from_sibling(self, s, kind):
        return self.sibling(s, kind, 1 - self.place.core)

    def sum_sibling(self, s, half):
        src = self.part.at[s, half, :, 1 - self.place.core]
        sems = self.sems
        return remote(
            src, self.recv_s.at[s, half], sems.at[self.phase, s, 0, 6 + half],
            sems.at[self.phase, s, 1, 6 + half], self.place.sibling(),
        )

    def sum_far(self, s):
        return self.copy(s, 8, self.send_f.at[s], self.recv_f.at[s], self.place.far(s))

    def sum_near(self, s):
        return self.copy(s, 9, self.send_n.at[s], self.recv_n.at[s], self.place.near(s))

    def start(self, s):
        self.to_near(s).start()
        self.to_far(s).start()
        self.to_sibling(s, 0).start()

    def far_stage(self, s):
        self.sum_sibling(s, 1).wait_recv()
        own = self.part[s, 1, :, self.place.core].astype(F32)
        self.send_f[s] = (own + self.recv_s[s, 1].astype(F32)).astype(BF)
        self.sum_far(s).start()

    def summed(self, s, minor):
        own = self.part[s, 0, minor, self.place.core].astype(F32)
        return own + self.recv_s[s, 0, minor].astype(F32) + self.recv_f[s, minor].astype(F32)

    def near_stage(self, s):
        self.sum_sibling(s, 0).wait_recv()
        self.sum_far(s).wait_recv()
        self.send_n[s] = self.summed(s, self.place.minor(s, 1)).astype(BF)
        self.sum_near(s).start()

    def total(self, s):
        self.sum_near(s).wait_recv()
        total = self.summed(s, self.place.minor(s)) + self.recv_n[s].astype(F32)
        self.to_near(s).wait_send()
        self.to_far(s).wait_send()
        self.pass_far(s).wait_send()
        for kind in range(3):
            self.to_sibling(s, kind).wait_send()
        for half in range(2):
            self.sum_sibling(s, half).wait_send()
        self.sum_far(s).wait_send()
        self.sum_near(s).wait_send()
        return total

    def take_near(self, s):
        self.to_near(s, 0, 1).wait_recv()
        self.pass_far(s).start()
        self.to_sibling(s, 1).start()

    def take_far(self, s):
        self.to_far(s, 1, 0).wait_recv()
        self.pass_far(s, 1, 1).wait_recv()
        self.to_sibling(s, 2).start()

    def take_sibling(self, s):
        for kind in range(3):
            self.from_sibling(s, kind).wait_recv()

    def run(self, compute, hooks, taken=False):
        def body(i, carry):
            s, half = i // 2, i % 2
            if not taken:
                pl.when(half == 0)(lambda: self.take_near(s))

            for at, hook in hooks:
                pl.when(i == at)(hook)

            if not taken:
                @pl.when(half == 0)
                def _():
                    self.from_sibling(s, 0).wait_recv()
                    self.from_sibling(s, 1).wait_recv()

                pl.when(half == 1)(lambda: self.take_far(s))

            @pl.when(i == 2)
            def _():
                self.far_stage(0)

            if not taken:
                pl.when(half == 1)(lambda: self.from_sibling(s, 2).wait_recv())

            major = self.place.major(s, half)
            compute(s * 8 * HALF_BLOCK + major * 4 * HALF_BLOCK, s, half, major)
            self.sum_sibling(s, half).start()
            return carry

        lax.fori_loop(0, 4, body, 0)
        self.near_stage(0)
        self.far_stage(1)


def exchange_scratch(width, phases):
    return [
        pltpu.VMEM((2, 2, 2, 2, HALF_BLOCK, width), BF),
        pltpu.VMEM((2, 2, 2, HALF_BLOCK, width), BF),
        pltpu.VMEM((2, 2, HALF_BLOCK, width), BF),
        pltpu.VMEM((2, 2, HALF_BLOCK, width), BF),
        pltpu.VMEM((2, HALF_BLOCK, width), BF),
        pltpu.VMEM((2, HALF_BLOCK, width), BF),
        pltpu.SemaphoreType.DMA((phases, 2, 2, 10)),
    ]


def flat(ref, columns=slice(None)):
    if len(ref.shape) == 2:
        return ref[:, columns]
    values = ref[(slice(None),) * 5 + (columns,)]
    return values.reshape(-1, values.shape[-1])


def write_part(part, s, half, values, w, contracted):
    width = part.shape[-1]
    step = width // 2
    for n in range(0, width, step):
        columns = slice(n, n + step)
        side = w[:, columns] if contracted == 0 else w[columns, :]
        part[s, half, :, :, :, columns] = blocked(dot(values, side, 1, contracted).astype(BF))


def blocked(values):
    return values.reshape(2, 2, HALF_BLOCK, values.shape[-1])


def root(values):
    return lax.rsqrt(jnp.mean(values * values, axis=-1, keepdims=True) + EPS)


def forward_kernel(levels, *refs):
    (x_in, own_mask, rope, sel_q, sel_o, head_lanes, adjoint, bias_first, bias_last) = refs[:9]
    (gains, w_q, w_in, w_out) = refs[9:13]
    w_down, head_weights = refs[13], refs[14:17]
    (predictions, grad_out, xs, mid) = refs[17:21]
    kept, (slab_q, slab_o, slab_i, slab_d) = refs[21:33], refs[33:37]
    exchange = refs[37:44]
    (nrm, nml, qkv, prb, att, gl, act) = refs[44:51]
    slabs = refs[51:55]
    (wide_q, first, final, pick, first_q, final_q) = refs[55:61]
    (g, g_rows, hidden, gpre, picked, hidden_all) = refs[61:67]
    (mask, cut, pasted, o_cut, o_piece) = refs[67:72]
    (z_sems, own_sems, keep_sems, load_sems, g_sems, trade_sems, mask_sems, o_sems) = refs[72:]
    slab_outs = (slab_q, slab_o, slab_i, slab_d)
    place = Place()
    z = place.z
    heads = sel_o.shape[1] // BLOCK
    lanes = heads * BLOCK
    kept_here, waited = [], []

    def keep(src, dst):
        copy = pltpu.make_async_copy(src, dst, keep_sems.at[len(kept_here)])
        copy.start()
        kept_here.append(copy)
        return copy

    def forget(copy):
        copy.wait()
        waited.append(copy)

    relayed = levels == 4

    def far(delta):
        there = (z + delta) % levels
        return (z + there == 3) & (z * there == 0)

    counts = [slabs[0].shape[1] // levels, o_piece.shape[1], slabs[2].shape[1] // levels,
              w_down.shape[1]]

    def rows_of(m, level):
        return rows_at(level * counts[m], counts[m])

    def piece(layer, m):
        if m == 1:
            return o_piece.at[layer]
        if m == 3:
            return w_down.at[layer]
        return slabs[m].at[layer, rows_of(m, z)]

    def spread(layer, m, delta):
        return remote(
            piece(layer, m), slabs[m].at[layer, rows_of(m, z)],
            z_sems.at[0, layer, m, delta - 1], z_sems.at[1, layer, m, delta - 1],
            place.level((z + delta) % levels),
        )

    def arriving(layer, m, delta):
        rows = slabs[m].at[layer, rows_of(m, (z + levels - delta) % levels)]
        return remote(
            rows, rows, z_sems.at[0, layer, m, delta - 1], z_sems.at[1, layer, m, delta - 1],
            place.level((z + delta) % levels),
        )

    def relay(layer, m):
        rows = slabs[m].at[layer, rows_of(m, (z + 2) % levels)]
        return remote(
            rows, rows, z_sems.at[2, layer, m, 0], z_sems.at[1, layer, m, 2 * (z - 1)],
            place.level(3 * (z - 1)),
        )

    def for_spread(layer, m, act_on):
        for delta in range(1, levels):
            if relayed and delta != 2:
                @pl.when(jnp.logical_not(far(delta)))
                def _(delta=delta):
                    act_on(spread(layer, m, delta))
            else:
                act_on(spread(layer, m, delta))

    def own_piece(layer, m):
        return pltpu.make_async_copy(
            piece(layer, m), slabs[m].at[layer, rows_of(m, z)], own_sems.at[layer, m]
        )

    def send_weights(layer, m):
        if m % 2:
            own_piece(layer, m).start()
        for_spread(layer, m, lambda copy: copy.start())

    rows, q_cols = w_q.shape[1], slabs[0].shape[2]
    span = w_q.shape[2] // 3 // PLANE
    ff_rows = w_in.shape[2] // PLANE // levels
    padded = slabs[2].shape[2] // levels - ff_rows

    def cut_weights(layer):
        scaled_q = w_q[layer].astype(F32) * gains[0, layer]
        scaled_i = w_in[layer].astype(F32) * gains[1, layer]
        for t in range(PLANE):
            parts = []
            for kind in range(3):
                low = (kind * PLANE + t) * span
                parts.append(scaled_q[:, low : low + span])
            if q_cols > 3 * span:
                parts.append(jnp.zeros((rows, q_cols - 3 * span), F32))
            cut[layer, t, :rows, :q_cols] = jnp.concatenate(parts, axis=1).astype(BF)
            parts = []
            for zz in range(levels):
                low = (zz * PLANE + t) * ff_rows
                parts.append(scaled_i[:, low : low + ff_rows])
                if padded:
                    parts.append(jnp.zeros((rows, padded), F32))
            cut[layer, t, :rows, q_cols:] = jnp.concatenate(parts, axis=1).astype(BF)

    def trade(layer, e):
        return remote(
            cut.at[layer, place.rank(e)], pasted.at[layer, place.rank()],
            trade_sems.at[0, layer, e], trade_sems.at[1, layer, e], place.other(e),
        )

    def traded(layer, e):
        there = pasted.at[layer, place.rank(e)]
        return remote(
            there, there, trade_sems.at[0, layer, e], trade_sems.at[1, layer, e], place.other(e)
        )

    def start_trade(layer):
        for e in range(1, PLANE):
            trade(layer, e).start()
        own = place.rank()
        pltpu.make_async_copy(
            cut.at[layer, own], pasted.at[layer, own], trade_sems.at[0, layer, 0]
        ).start()

    def end_trade(layer):
        own = place.rank()
        pltpu.make_async_copy(
            cut.at[layer, own], pasted.at[layer, own], trade_sems.at[0, layer, 0]
        ).wait()
        for e in range(1, PLANE):
            traded(layer, e).wait_recv()
        for e in range(1, PLANE):
            trade(layer, e).wait_send()
        for m, low in ((0, 0), (2, q_cols)):
            width = slabs[m].shape[2]
            whole = [pasted[layer, t, :rows, low : low + width].astype(F32) for t in range(PLANE)]
            slabs[m][layer, rows_of(m, z), :] = jnp.concatenate(whole, axis=0).astype(BF)

    trades = place.trades(levels)
    o_trade = remote(
        o_cut, o_piece, o_sems.at[0], o_sems.at[1], place.indexed(place.holder(levels))
    )
    o_local = pltpu.make_async_copy(o_cut, o_piece, o_sems.at[0])

    def mask_to(e):
        there = mask.at[place.y, place.x, :, place.core]
        return remote(own_mask, there, mask_sems.at[0, e], mask_sems.at[1, e], place.other(e))

    def mask_from(e):
        y, core, x = place.turned(e)
        there = mask.at[y, x, :, core]
        return remote(there, there, mask_sems.at[0, e], mask_sems.at[1, e], place.other(e))

    mask_local = pltpu.make_async_copy(
        own_mask, mask.at[place.y, place.x, :, place.core], mask_sems.at[0, 0]
    )

    middle = (z == 1) | (z == 2)

    def relay_on(layer, m):
        if relayed:
            @pl.when(middle)
            def _():
                arriving(layer, m, 2).wait_recv()
                relay(layer, m).start()

    def weights_here(layer, m):
        for delta in range(1, levels):
            if relayed and delta == 2:
                pl.when(jnp.logical_not(middle))(arriving(layer, m, delta).wait_recv)
            else:
                arriving(layer, m, delta).wait_recv()
        for_spread(layer, m, lambda copy: copy.wait_send())
        if m % 2:
            own_piece(layer, m).wait()
        if relayed:
            pl.when(middle)(relay(layer, m).wait_send)

        return keep(slabs[m].at[layer], slab_outs[m].at[layer])

    skip = slabs[2].at[0, :, : adjoint.shape[3]]
    loads = [
        pltpu.make_async_copy(src, dst, load_sems.at[i])
        for i, (src, dst) in enumerate(zip(head_weights, (first, final, skip)))
    ]
    loads[0].start()
    loads[1].start()
    greet(place, levels)

    g_own = g.at[place.y, :, :, place.core]
    g_far = g.at[1 - place.y, :, :, place.core]
    g_local = pltpu.make_async_copy(adjoint, g_own, g_sems.at[0, 0])
    g_peer = remote(adjoint, g_own, g_sems.at[0, 1], g_sems.at[1, 1], place.far(0))
    g_sibling = remote(adjoint, g_own, g_sems.at[0, 2], g_sems.at[1, 2], place.sibling())
    g_pass = remote(g_far, g_far, g_sems.at[0, 3], g_sems.at[1, 3], place.sibling())
    part = exchange[0]
    lines = nrm.at[0]
    bufs = [nrm.at[0], nml.at[0], nrm.at[1], nml.at[1], lines]
    phases = [Exchange(place, p, buf, exchange) for p, buf in enumerate(bufs)]

    def own_half(s):
        return slice(s * HALF_BLOCK, (s + 1) * HALF_BLOCK)

    def chip_of(s, major, minor):
        return (major + s * (minor - major), minor + s * (major - minor))

    def enter(p, s, values):
        if p < 2 * LAYERS:
            values = values * root(values)
        bufs[p][phases[p].own(s)] = values.astype(BF)
        phases[p].start(s)

    def leave(p, s):
        rows = own_half(s)
        total = phases[p].total(s)
        if p == 2 * LAYERS:
            grad_out[rows, :] = total
            return
        layer = p // 2
        if p % 2 == 0:
            values = xs[layer, rows, :] + total
            mid[layer, rows, :] = values
        else:
            values = mid[layer, rows, :] + total
            if layer + 1 < LAYERS:
                xs[layer + 1, rows, :] = values
        enter(p + 1, s, values)

    def run(p, compute, next_weights, more=()):
        more = list(more)
        hooks = [(1, lambda: leave(p - 1, 1))] if p else []
        hooks += [(2, lambda key=key: relay_on(*key)) for key in next_weights]
        phases[p].run(compute, hooks + more)
        leave(p, 0)
        phases[p].near_stage(1)

    send_weights(0, 3)
    o_cut[...] = jnp.zeros(o_cut.shape, BF)
    for layer in range(LAYERS):
        o_cut[layer, :rows, :] = w_out[layer]
    pl.when(trades)(o_trade.start)
    pl.when(jnp.logical_not(trades))(o_local.start)
    cut_weights(0)
    start_trade(0)
    xs[0] = x_in[...].astype(F32)
    for s in range(2):
        enter(0, s, xs[0, own_half(s), :])
    mask_local.start()
    for e in range(1, PLANE):
        mask_to(e).start()
    cut_weights(1)
    end_trade(0)
    send_weights(0, 0)

    @pl.when(trades)
    def _():
        o_trade.wait_recv()
        o_trade.wait_send()

    pl.when(jnp.logical_not(trades))(o_local.wait)
    send_weights(0, 1)
    start_trade(1)
    for copy in (g_local, g_peer, g_sibling):
        copy.start()
    mask_local.wait()
    for e in range(1, PLANE):
        mask_from(e).wait_recv()
        mask_to(e).wait_send()
    relay_on(0, 0)
    relay_on(0, 1)

    def second_layer():
        end_trade(1)
        send_weights(1, 0)
        send_weights(1, 1)

    slab_keeps = []
    for layer in range(LAYERS):
        wq, wo, wi, wd = [slab.at[layer] for slab in slabs]
        slab_keeps.append(weights_here(layer, 0))
        if layer == 0:
            send_weights(0, 2)
        for n in range(0, wide_q.shape[0], 256):
            wide_q[n : n + 256, :] = dot(wq[n : n + 256, :], sel_q[...]).astype(BF)
        slab_keeps.append(weights_here(layer, 1))
        if layer:
            for copy in attn_saved:
                forget(copy)

        def attend(start, s, half, major, layer=layer, wo=wo):
            both = rows_at(start, 2 * BLOCK, 2 * BLOCK)
            projected = dot(nrm[layer, s, major].reshape(2 * BLOCK, nrm.shape[-1]), wide_q[...])
            cosine, sine = rope[:, :BLOCK], rope[:, BLOCK:]
            allowed = [
                mask[chip_of(s, major, block) + (s,)].reshape(BLOCK, BLOCK) > 0 for block in range(2)
            ]
            units = [(block, h) for block in range(2) for h in range(heads)]
            turned = []
            for low in range(0, 2 * lanes, BLOCK):
                value = projected[:, low : low + BLOCK]
                value = value * cosine + pltpu.roll(value, BLOCK // 2, 1) * sine
                turned.append(value.astype(BF))
            values = projected[:, 2 * lanes :].astype(BF)

            def rows_in(array, block):
                return array[block * BLOCK : (block + 1) * BLOCK]

            scores = [
                dot(rows_in(turned[h], block), rows_in(turned[heads + h], block), 1, 1)
                for block, h in units
            ]
            scores = [
                jnp.where(allowed[block], score * (1.0 / math.sqrt(HDIM)), -1e30)
                for (block, h), score in zip(units, scores)
            ]
            tops = [jnp.max(score, axis=-1, keepdims=True) for score in scores]
            scores = [jnp.exp(score - top) for score, top in zip(scores, tops)]
            sums = [jnp.sum(score, axis=-1, keepdims=True) for score in scores]
            probs = [(score / total).astype(BF) for score, total in zip(scores, sums)]
            outs = [
                dot(prob, rows_in(values, block)[:, h * BLOCK : (h + 1) * BLOCK]).astype(BF)
                for (block, h), prob in zip(units, probs)
            ]

            def joined(parts):
                side = [
                    jnp.concatenate(parts[block * heads : (block + 1) * heads], axis=1)
                    for block in range(2)
                ]
                return jnp.concatenate(side, axis=0)

            attended = dot(joined(outs), sel_o[...], 1, 1).astype(BF)
            write_part(part, s, half, attended, wo, 0)
            att[both, :] = attended
            prb[both, :] = joined(probs)
            qkv[both, :] = jnp.concatenate(turned + [values], axis=1)

        more = [(1, second_layer)] if layer == 0 else []
        run(2 * layer, attend, ((layer, 2), (layer, 3)), more)
        attn_saved = [keep(src, dst.at[layer]) for src, dst in zip((qkv, prb, att), kept[2:5])]
        nrm_saved = keep(nrm.at[layer], kept[0].at[layer])
        if layer == 0:
            g_peer.wait_recv()
            g_pass.start()
        p = 2 * layer + 1
        ending = layer + 1 == LAYERS
        if ending:
            phases[p].take_near(0)
            phases[p].take_far(0)
            leave(p - 1, 1)
            phases[p].take_near(1)
            phases[p].take_far(1)
            for s in range(2):
                phases[p].take_sibling(s)
        slab_keeps.append(weights_here(layer, 2))
        if layer:
            for copy in mlp_saved:
                forget(copy)
        if not ending:
            slab_keeps.append(weights_here(layer, 3))
            for m in (2, 3):
                send_weights(layer + 1, m)

        def lift(start, s, major, layer=layer, wi=wi):
            rows = rows_at(start, 2 * BLOCK, 2 * BLOCK)
            lifted = dot(nml[layer, s, major].reshape(2 * BLOCK, nml.shape[-1]), wi[...])
            root_two = math.sqrt(2.0 / math.pi)
            square = lifted * lifted
            tanh = jnp.tanh(root_two * lifted * (1.0 + 0.044715 * square))
            activated = (0.5 * lifted * (1.0 + tanh)).astype(BF)
            act[rows, :] = activated
            slope = 0.5 * (1.0 + tanh) + 0.5 * lifted * (1.0 - tanh * tanh) * root_two * (
                1.0 + 3.0 * 0.044715 * square
            )
            gl[rows, :] = slope.astype(BF)
            return activated

        def perceptron(start, s, half, major, lift=lift, wd=wd):
            write_part(part, s, half, lift(start, s, major), wd, 0)

        def shrink(start, s, half, major, wd=wd):
            write_part(part, s, half, act[rows_at(start, 2 * BLOCK, 2 * BLOCK), :], wd, 0)

        if ending:
            def lift_step(i, carry, lift=lift):
                lift(i * 4 * HALF_BLOCK, i // 2, i % 2)
                return carry

            lax.fori_loop(0, 4, lift_step, 0)
            slab_keeps.append(weights_here(layer, 3))
            phases[p].run(shrink, [], taken=True)
            leave(p, 0)
            phases[p].near_stage(1)
        else:
            run(p, perceptron, ((layer + 1, 0), (layer + 1, 1)))
        mlp_saved = [keep(src, dst.at[layer]) for src, dst in zip((gl, act), kept[5:7])]
        keep(nml.at[layer], kept[1].at[layer])
        if layer == 0:
            forget(nrm_saved)
            forget(slab_keeps[2])
            loads[2].start()
            loads[0].wait()
            loads[1].wait()
            index = lax.broadcasted_iota(jnp.int32, pick.shape, 0)
            offset = (2 * place.y + place.core) * (pick.shape[0] // (4 * levels))
            pick[...] = jnp.where(index - offset == head_lanes[...], 1.0, 0.0).astype(BF)
            for n in range(0, first.shape[0], 256):
                first_q[n : n + 256, :] = dot(first[n : n + 256, :], pick[...]).astype(BF)
            final_q[...] = dot(pick[...], final[...], 0, 0).astype(BF)

    g_local.wait()
    for copy in (g_sibling, g_pass):
        copy.wait_recv()
    loads[2].wait()
    bias_q = dot(jnp.broadcast_to(bias_first[...], (16, bias_first.shape[1])), pick[...])[:1]
    columns = g.shape[-1]

    def head(start, s, half, major):
        rows = rows_at(start, 2 * BLOCK, 2 * BLOCK)
        pre = dot(lines[s, major].reshape(2 * BLOCK, lines.shape[-1]), first_q[...]) + bias_q
        gate = 1.0 / (1.0 + jnp.exp(-pre))
        hidden[rows, :] = (pre * gate).astype(BF)
        for block in range(2):
            here = rows_at(start + block * BLOCK, BLOCK, BLOCK)
            g_rows[here, :] = g[chip_of(s, major, block) + (s,)].reshape(BLOCK, columns)
        there = g_rows[rows, :]
        grad_hidden = dot(there, final_q[...], 1, 1)
        gpre[rows, :] = (grad_hidden * (gate * (1.0 + pre * (1.0 - gate)))).astype(BF)
        row = lax.broadcasted_iota(jnp.int32, (2 * BLOCK, 1), 0)
        y = major + s * (row // BLOCK - major)
        mine = (row // HALF_BLOCK % 2 == place.core) & (y == place.y)
        mine = jnp.where(mine, there.astype(F32), 0.0).astype(BF)
        whole = dot(gpre[rows, :], first_q[...], 1, 1) + dot(mine, skip[...], 1, 1)
        part[s, half] = blocked(whole.astype(BF))

    p = 2 * LAYERS
    phases[p].run(head, [(1, lambda: leave(p - 1, 1))])

    keep(lines, kept[7])
    keep(hidden, kept[8])
    keep(gpre, kept[9])
    keep(g_rows, kept[11])
    for s in range(2):
        for major in range(2):
            n = (2 * s + major) * 2 * BLOCK
            rows = lines[s, major].reshape(2 * BLOCK, lines.shape[-1])
            picked[n : n + 2 * BLOCK, :] = dot(rows, pick[...]).astype(BF)
    keep(picked, kept[10])
    phases[p].near_stage(1)
    mine = []
    for x in range(2):
        mine += [lines[0, place.y, x, place.core], lines[1, x, place.y, place.core]]
    mine = jnp.concatenate(mine, axis=0)
    pre = dot(mine, first[...]) + bias_first[...].astype(F32)
    hidden_all[...] = (pre / (1.0 + jnp.exp(-pre))).astype(BF)
    out = dot(hidden_all[...], final[...]) + bias_last[...].astype(F32)
    predictions[...] = (out + dot(mine, skip[...])).astype(BF)
    leave(p, 0)
    leave(p, 1)
    for copy in (g_peer, g_sibling, g_pass):
        copy.wait_send()
    for copy in kept_here:
        if not any(copy is other for other in waited):
            copy.wait()


def norm_back(values, q):
    scale = root(values)
    n = values * scale
    return scale * (q - n * jnp.mean(q * n, axis=-1, keepdims=True))


def backward_kernel(levels, *refs):
    (rope, sel_q, sel_o, gains, w_q, w_in) = refs[:6]
    dy_in, stored, head_stored = refs[6], refs[7:20], refs[20:25]
    (dx_out, small_out, q_out, o_out, i_out, d_out, q_gain, i_gain) = refs[25:33]
    (first_out, out_out, skip_out) = refs[33:36]
    exchange, ag = refs[36:43], refs[43]
    loaded, gp = refs[44:57], refs[57]
    stages, arrivals = refs[58:65], refs[65:72]
    own_sums, acc, o_acc = refs[72:76], refs[76], refs[77]
    o_cut, o_pasted = refs[78], refs[79]
    (small_own, small_x, small_z) = refs[80:83]
    row_buf = refs[83]
    z_sems, load_sems, small_sems, trade_sems, o_sems, row_sem = refs[84:]
    (nml, act, gl, wi, wd, mid, nrm, qkv, prb, att, wq, wo, xs) = loaded
    part = exchange[0]
    place = Place()
    z = place.z
    heads = sel_o.shape[1] // BLOCK
    lanes = heads * BLOCK

    def load(layer, i):
        return pltpu.make_async_copy(stored[i].at[layer], loaded[i], load_sems.at[i])

    lines = ag.at[1]
    h_cols, half_width = small_own.shape[2], nrm.shape[-1] // 2
    gpre, hidden = gp.at[:, :h_cols], nrm.at[:, :, :, :, :, :h_cols]
    picked = nrm.at[:, :, :, :, :, half_width : half_width + h_cols]
    g = qkv.at[:, : stages[5].shape[1]]
    head_loads = [
        pltpu.make_async_copy(src, dst, load_sems.at[len(loaded) + i])
        for i, (src, dst) in enumerate(zip(head_stored, (lines, gpre, hidden, picked, g)))
    ]
    mlp_part, attn_part = range(5), range(6, 12)
    norm_loads = [pltpu.make_async_copy(stored[i], loaded[i], load_sems.at[i]) for i in (5, 12)]
    for copy in norm_loads:
        copy.start()
    dy_load = pltpu.make_async_copy(dy_in, dx_out, load_sems.at[len(loaded) + 5])
    dy_load.start()
    for copy in head_loads:
        copy.start()
    for i in mlp_part:
        load(LAYERS - 1, i).start()
    greet(place, levels)

    def count_of(m):
        return arrivals[m].shape[2]

    def slot(m, layer):
        return layer if m < 4 else 0

    relayed = levels == 4
    middle = (z == 1) | (z == 2)

    def send(layer, m, delta):
        there = (z + delta) % levels
        return remote(
            stages[m].at[rows_at(there * count_of(m), count_of(m))],
            arrivals[m].at[slot(m, layer), delta - 1],
            z_sems.at[0, layer, m, delta - 1],
            z_sems.at[1, layer, m, delta - 1],
            place.level(there),
        )

    def far(delta):
        there = (z + delta) % levels
        return (z + there == 3) & (z * there == 0)

    def hand(layer, m, delta):
        there = (z + delta) % levels
        return remote(
            stages[m].at[rows_at(there * count_of(m), count_of(m))],
            arrivals[m].at[slot(m, layer), levels - 1],
            z_sems.at[0, layer, m, delta - 1],
            z_sems.at[1, layer, m, levels - 1],
            place.level(1 + z // 3),
        )

    def send_first(layer, m):
        for delta in range(1, levels):
            if not relayed:
                send(layer, m, delta).start()
            elif delta == 2:
                pl.when(jnp.logical_not(middle))(send(layer, m, delta).start)
            else:
                pl.when(far(delta))(hand(layer, m, delta).start)
                pl.when(jnp.logical_not(far(delta)))(send(layer, m, delta).start)

    def send_rest(layer, m):
        if relayed:
            @pl.when(middle)
            def _():
                hand(layer, m, 1).wait_recv()
                rows = rows_at((z + 2) % levels * count_of(m), count_of(m))
                total = stages[m][rows, :].astype(F32)
                total = total + arrivals[m][slot(m, layer), levels - 1].astype(F32)
                stages[m][rows, :] = total.astype(BF)
                send(layer, m, 2).start()

    def sent(layer, m):
        for delta in range(1, levels):
            send(layer, m, delta).wait_send()

    def result(layer, m):
        if m > 4:
            return (out_out, skip_out)[m - 5]
        if m == 3:
            return d_out.at[layer]
        return own_sums[min(m, 3)].at[slot(m, layer)]

    def weight_grad(layer, m, left, right, tile):
        width = left.shape[-1]
        if m < 4 and layer + 1 < LAYERS:
            sent(layer + 1, m)
        for low in range(0, width, tile):
            here = slice(low, min(low + tile, width))
            stages[m][here, :] = dot(flat(left, here), flat(right), 0, 0).astype(BF)
        send_first(layer, m)
        out = result(layer, m)
        out[...] = stages[m][rows_at(z * count_of(m), count_of(m)), :].astype(out.dtype)

    bufs = [ag.at[p % 2] for p in range(PHASES)]
    phases = [Exchange(place, p, buf, exchange) for p, buf in enumerate(bufs)]

    def own_half(s):
        return slice(s * HALF_BLOCK, (s + 1) * HALF_BLOCK)

    def enter(p, s):
        bufs[p][phases[p].own(s)] = dx_out[own_half(s), :].astype(BF)
        phases[p].start(s)

    def leave(p, s):
        rows = own_half(s)
        values = (mid if p % 2 == 0 else xs)[LAYERS - 1 - p // 2, rows, :]
        dx_out[rows, :] += norm_back(values, phases[p].total(s))
        if p + 1 < PHASES:
            enter(p + 1, s)

    def run(p, compute, relays):
        hooks = [(1, lambda: leave(p - 1, 1))] if p else []
        hooks += [(2, lambda key=key: send_rest(*key)) for key in relays]
        phases[p].run(compute, hooks)

    dy_load.wait()
    for copy in norm_loads:
        copy.wait()
    for s in range(2):
        enter(0, s)

    for copy in head_loads:
        copy.wait()
    last = LAYERS - 1
    bias_sum = jnp.sum(gpre[...].astype(F32), axis=0, keepdims=True)
    small_own[1] = jnp.broadcast_to(bias_sum, small_own.shape[1:])
    to_x = remote(
        small_own.at[1], small_x, small_sems.at[0, 0], small_sems.at[1, 0], place.near(0)
    )
    to_x.start()
    weight_grad(last, 5, hidden, g, 4 * BLOCK)
    weight_grad(last, 6, picked, g, 4 * BLOCK)
    weight_grad(last, 4, lines, gpre, 5 * BLOCK)
    g_sum = jnp.sum(g[...].astype(F32), axis=0, keepdims=True)
    to_x.wait()
    small_z[0, :, : g_sum.shape[1]] = jnp.broadcast_to(g_sum, (8, g_sum.shape[1]))
    small_z[0, :, g_sum.shape[1] :] = small_own[1] + small_x[...]
    to_z = [
        remote(
            small_z.at[0], small_z.at[d], small_sems.at[0, d], small_sems.at[1, d],
            place.level((z + d) % levels),
        )
        for d in range(1, levels)
    ]
    for copy in to_z:
        copy.start()
    for i in attn_part:
        load(last, i).start()

    relays = [(last, 5), (last, 6), (last, 4)]
    for layer in reversed(range(LAYERS)):
        p = 2 * (LAYERS - 1 - layer)
        buf = bufs[p]
        for i in mlp_part:
            load(layer, i).wait()

        def perceptron(start, s, half, major, buf=buf):
            rows = rows_at(start, 2 * BLOCK, 2 * BLOCK)
            grad_act = dot(buf[s, major].reshape(2 * BLOCK, buf.shape[-1]), wd[...], 1, 1)
            grad_lift = (grad_act * gl[rows, :].astype(F32)).astype(BF)
            write_part(part, s, half, grad_lift, wi, 1)
            gl[rows, :] = grad_lift

        run(p, perceptron, relays)
        weight_grad(layer, 3, act, buf, 2 * BLOCK)
        leave(p, 0)
        weight_grad(layer, 2, nml, gl, 5 * BLOCK)
        phases[p].near_stage(1)
        if layer > 0:
            for i in mlp_part:
                load(layer - 1, i).start()
        for i in attn_part:
            load(layer, i).wait()
        buf = bufs[p + 1]

        def attend(start, s, half, major, buf=buf):
            cosine, sine = rope[:, :BLOCK], rope[:, BLOCK:]
            both = rows_at(start, 2 * BLOCK, 2 * BLOCK)
            there = buf[s, major].reshape(2 * BLOCK, buf.shape[-1])
            grad_heads = dot(there, wo[...], 1, 1).astype(BF)
            grad_heads = dot(grad_heads, sel_o[...]).astype(BF)
            kept, probs = qkv[both, :], prb[both, :]
            units = [(block, h) for block in range(2) for h in range(heads)]

            def unit(array, block, h, kind=0):
                low = kind * lanes + h * BLOCK
                return array[block * BLOCK : (block + 1) * BLOCK, low : low + BLOCK]

            queries, keys, values = [[unit(kept, *u, kind) for u in units] for kind in range(3)]
            probs = [unit(probs, *u) for u in units]
            grads = [unit(grad_heads, *u) for u in units]
            grad_probs = [dot(grad, value, 1, 1) for grad, value in zip(grads, values)]
            grad_values = [dot(prob, grad, 0, 0).astype(BF) for prob, grad in zip(probs, grads)]
            wide = [prob.astype(F32) for prob in probs]
            inner = [
                jnp.sum(prob * grad, axis=-1, keepdims=True) for prob, grad in zip(wide, grad_probs)
            ]
            grad_scores = [
                (prob * (grad - total)).astype(BF)
                for prob, grad, total in zip(wide, grad_probs, inner)
            ]
            grad_queries = [dot(grad, key) for grad, key in zip(grad_scores, keys)]
            grad_keys = [dot(grad, query, 0, 0) for grad, query in zip(grad_scores, queries)]
            packed = []
            for parts in (grad_queries, grad_keys):
                for h in range(heads):
                    turned = jnp.concatenate([parts[h], parts[heads + h]], axis=0)
                    turned = turned * (1.0 / math.sqrt(HDIM))
                    turned = turned * cosine - pltpu.roll(turned, BLOCK // 2, 1) * sine
                    packed.append(turned.astype(BF))
            for h in range(heads):
                packed.append(jnp.concatenate([grad_values[h], grad_values[heads + h]], axis=0))
            packed = dot(jnp.concatenate(packed, axis=1), sel_q[...], 1, 1).astype(BF)
            write_part(part, s, half, packed, wq, 1)
            gp[both, :] = packed

        run(p + 1, attend, [(layer, 3), (layer, 2)])
        weight_grad(layer, 0, nrm, gp, 5 * BLOCK)
        leave(p + 1, 0)
        weight_grad(layer, 1, att, buf, 2 * BLOCK)
        phases[p + 1].near_stage(1)
        if layer > 0:
            for i in attn_part:
                load(layer - 1, i).start()
        relays = [(layer, 0), (layer, 1)]
    leave(PHASES - 1, 1)
    for key in relays:
        send_rest(*key)

    total = small_z[0]
    for copy, d in zip(to_z, range(1, levels)):
        copy.wait_recv()
        total = total + small_z[d]
    small_out[...] = total
    for copy in to_z:
        copy.wait_send()
    rows = w_q.shape[1]
    pad_rows = up16(rows)
    kinds = {0: 0, 2: 1, 4: 2}

    def cut_at(m, t):
        start = rows_at((t + PLANE * kinds[m]) * pad_rows, pad_rows)
        return wi.at[start, : stages[m].shape[1]]

    def pasted_at(layer, m, t):
        start = rows_at((slot(m, layer) * PLANE + t) * pad_rows, pad_rows)
        return {0: gl, 2: act, 4: wd}[m].at[start, : stages[m].shape[1]]

    def trade(layer, m, e):
        kind = kinds[m]
        return remote(
            cut_at(m, place.rank(e)), pasted_at(layer, m, place.rank()),
            trade_sems.at[0, layer, kind, e], trade_sems.at[1, layer, kind, e], place.other(e),
        )

    def traded(layer, m, e):
        there = pasted_at(layer, m, place.rank(e))
        return remote(
            there, there, trade_sems.at[0, layer, kinds[m], e],
            trade_sems.at[1, layer, kinds[m], e], place.other(e),
        )

    def own_trade(layer, m):
        own = place.rank()
        return pltpu.make_async_copy(
            cut_at(m, own), pasted_at(layer, m, own), trade_sems.at[0, layer, kinds[m], 0]
        )

    stayed = set()

    def wait_own_trade(layer, m):
        if (layer, m) not in stayed:
            own_trade(layer, m).wait()
            stayed.add((layer, m))

    def pasted(layer, m, t):
        return pasted_at(layer, m, t)[:rows, :].astype(F32)

    trades = place.trades(levels)

    def o_trade(layer):
        return remote(
            o_cut.at[layer], o_pasted.at[layer], o_sems.at[0, layer], o_sems.at[1, layer],
            place.indexed(place.held(levels)),
        )

    def o_local(layer):
        return pltpu.make_async_copy(o_cut.at[layer], o_pasted.at[layer], o_sems.at[0, layer])

    def finalize(layer, m):
        own = result(layer, m)
        if m == 3 or m > 4:
            total = own
        else:
            total = o_acc if m == 1 else acc.at[:, : own.shape[1]]
            total[...] = own[...].astype(F32)
        for delta in range(1, levels):
            def add(delta=delta):
                send(layer, m, delta).wait_recv()
                total[...] += arrivals[m][slot(m, layer), delta - 1].astype(F32)

            if relayed and delta != 2:
                source = (z + levels - delta) % levels
                pl.when(jnp.logical_not((z + source == 3) & (z * source == 0)))(add)
            else:
                add()
        if m > 3 or layer == 0:
            sent(layer, m)
        if m == 1:
            o_cut[layer] = total[...].astype(BF)
            pl.when(trades)(o_trade(layer).start)
            pl.when(jnp.logical_not(trades))(o_local(layer).start)
        elif m in kinds:
            if m < 4 and layer + 1 < LAYERS:
                wait_own_trade(layer + 1, m)
                for e in range(1, PLANE):
                    trade(layer + 1, m, e).wait_send()
            values = total[...].astype(BF).astype(F32)
            for t in range(PLANE):
                cut_at(m, t)[:rows, :] = values[t * rows : (t + 1) * rows].astype(BF)
            own_trade(layer, m).start()
            for e in range(1, PLANE):
                trade(layer, m, e).start()

    def wait_trade(layer, m):
        wait_own_trade(layer, m)
        for e in range(1, PLANE):
            traded(layer, m, e).wait_recv()
        if m > 3 or layer == 0:
            for e in range(1, PLANE):
                trade(layer, m, e).wait_send()

    span = w_q.shape[2] // 3 // PLANE
    ff_rows = w_in.shape[2] // PLANE // levels
    padded_rows = stages[2].shape[1] // levels

    def rows_out(layer, out):
        here = row_buf.at[:, : out.shape[2]]
        return pltpu.make_async_copy(here, out.at[layer], row_sem.at[0])

    on_the_way = []

    def write_rows(layer, parts, out, kind, w, gain_out):
        whole = jnp.concatenate(parts, axis=1)
        gain_out[layer] = jnp.sum(whole * w[layer].astype(F32), axis=1, keepdims=True)
        if on_the_way:
            on_the_way.pop().wait()
        row_buf[:, : out.shape[2]] = whole * gains[kind, layer]
        copy = rows_out(layer, out)
        copy.start()
        on_the_way.append(copy)

    def assemble(layer):
        wait_trade(layer, 0)
        ranks = [pasted(layer, 0, t) for t in range(PLANE)]
        parts = [rank[:, kind * span : (kind + 1) * span] for kind in range(3) for rank in ranks]
        write_rows(layer, parts, q_out, 0, w_q, q_gain)

    def assemble_mlp(layer):
        wait_trade(layer, 2)
        ranks = [pasted(layer, 2, t) for t in range(PLANE)]
        parts = [
            rank[:, zz * padded_rows : zz * padded_rows + ff_rows]
            for zz in range(levels) for rank in ranks
        ]
        write_rows(layer, parts, i_out, 1, w_in, i_gain)

    def assemble_out(layer):
        @pl.when(trades)
        def _():
            o_trade(layer).wait_recv()
            o_trade(layer).wait_send()

        pl.when(jnp.logical_not(trades))(o_local(layer).wait)
        o_out[layer] = o_pasted[layer, :rows, :].astype(F32)

    head_rows, head_share = out_out.shape[0], first_out.shape[1] // 4 // levels

    def assemble_head():
        wait_trade(last, 4)
        sums = []
        for q in range(4):
            sums.append(pasted(last, 4, 2 * q) + pasted(last, 4, 2 * q + 1))
        parts = []
        for zz in range(levels):
            for q in range(4):
                parts.append(sums[q][:, zz * head_rows : zz * head_rows + head_share])
        first_out[...] = jnp.concatenate(parts, axis=1)

    for key in [(last, 5), (last, 6), (last, 4)] + [(last, m) for m in (3, 2, 0, 1)]:
        finalize(*key)
    for layer in reversed(range(LAYERS - 1)):
        finalize(layer, 3)
        finalize(layer, 2)
    assemble_head()
    for layer in reversed(range(LAYERS)):
        if layer == 0:
            finalize(layer, 0)
            finalize(layer, 1)
        assemble_mlp(layer)
        assemble(layer)
        assemble_out(layer)
    on_the_way.pop().wait()


def shape(*dims, dtype=BF):
    return jax.ShapeDtypeStruct(dims, dtype)


def rope_table():
    position = np.arange(2 * BLOCK) % ROW_LEN
    inverse = ROTARY_BASE ** (-np.arange(HALF) / HALF)
    angles = (position[:, None] * inverse[None, :]).astype(np.float32)
    table = np.zeros((2 * BLOCK, 2, 2, BLOCK // 2), np.float32)
    table[:, 0, :, :HALF] = np.cos(angles)[:, None]
    table[:, 1, 0, :HALF] = -np.sin(angles)
    table[:, 1, 1, :HALF] = np.sin(angles)
    return table.reshape(2 * BLOCK, 2 * BLOCK)


def lane_of(index):
    head, inside = divmod(index, HDIM)
    half, place = divmod(inside, HALF)
    return head * BLOCK + half * (BLOCK // 2) + place


def per_device(devices, x, segments, padded, w_qkv, w_out, w_in, w_down, gain_attn, gain_mlp,
               head_first, head_first_bias, head_final, head_bias, head_skip, adjoint):
    levels = devices // PLANE
    width = x.shape[1]
    ff = w_in.shape[2]
    columns = head_final.shape[1]
    tokens = PLANE * BLOCK
    heads = width // HDIM // PLANE
    span = heads * HDIM
    rows = width // devices
    out_rows = up16(rows)
    ff_rows = ff // devices
    down_rows = up16(ff_rows)
    head_share = 2 * width // devices
    head_rows = up16(head_share)
    used_cols, o_rows, f_cols = 3 * span, levels * out_rows, levels * down_rows
    h_cols = -(-levels * head_rows // 128) * 128
    q_cols = -(-used_cols // 128) * 128
    lanes = heads * BLOCK

    sel_q = np.zeros((q_cols, 3 * lanes), np.float32)
    sel_o = np.zeros((o_rows, lanes), np.float32)
    for e in range(span):
        for kind in range(3):
            sel_q[kind * span + e, kind * lanes + lane_of(e)] = 1
        sel_o[e // rows * out_rows + e % rows, lane_of(e)] = 1
    sel_q, sel_o = jnp.asarray(sel_q, BF), jnp.asarray(sel_o, BF)
    rope = jnp.asarray(rope_table())
    head_lanes = np.full((1, h_cols), -width, np.int32)
    for zz in range(levels):
        here = slice(zz * head_rows, zz * head_rows + head_share)
        head_lanes[0, here] = 4 * head_share * zz + np.arange(head_share)
    head_lanes = jnp.asarray(head_lanes)

    seg = segments.reshape(2, HALF_BLOCK)
    open_key = padded.reshape(2, HALF_BLOCK) == 0
    within = jnp.arange(HALF_BLOCK)
    static = within[:, None] // ROW_LEN == within[None, :] // ROW_LEN
    static = static & (within[None, :] <= within[:, None])
    allowed = static[None] & (seg[:, :, None] == seg[:, None, :])
    allowed = allowed & (open_key[:, None, :] | (within[:, None] == within[None, :])[None])
    core = lax.axis_index("wide") % 2
    side = jnp.arange(BLOCK)[None, None, :] // HALF_BLOCK == core
    own_mask = (jnp.concatenate([allowed, allowed], axis=-1) & side).astype(BF)

    gains = jnp.stack([gain_attn, gain_mlp]).astype(F32)[..., None]
    d_piece = w_down
    if down_rows != ff_rows:
        d_piece = jnp.pad(w_down, [(0, 0), (0, down_rows - ff_rows), (0, 0)])
    pad_rows = up16(rows)

    in_blocks = (2, 2, 2, 2, HALF_BLOCK)
    layer_shapes = [
        in_blocks + (width,), in_blocks + (width,), (tokens, 3 * lanes), (tokens, lanes), (tokens, o_rows),
        (tokens, f_cols), (tokens, f_cols),
    ]
    slab_shapes = [(width, q_cols), (o_rows, width), (width, f_cols), (f_cols, width)]
    outs = [
        shape(2 * BLOCK, columns), shape(BLOCK, width, dtype=F32),
        shape(LAYERS, BLOCK, width, dtype=F32), shape(LAYERS, BLOCK, width, dtype=F32),
    ]
    vmem_outs = len(outs)
    outs += [shape(LAYERS, *dims) for dims in layer_shapes]
    outs += [shape(*in_blocks, width)] + [shape(tokens, h_cols)] * 3 + [shape(tokens, columns)]
    outs += [shape(LAYERS, *dims) for dims in slab_shapes]
    (predictions, grad_final, xs, mid, nrm, nml, qkv, prb, att, gl, act, lines, hidden, gpre,
     picked, g, wq, wo, wi, wd) = pl.pallas_call(
        lambda *refs: forward_kernel(levels, *refs),
        out_shape=outs,
        in_specs=[VMEM] * 13 + [ANY] * 4,
        out_specs=[VMEM] * vmem_outs + [ANY] * (len(outs) - vmem_outs),
        scratch_shapes=exchange_scratch(width, PHASES + 1)
        + [pltpu.VMEM((LAYERS,) + dims, BF) for dims in layer_shapes[:2]]
        + [pltpu.VMEM(dims, BF) for dims in layer_shapes[2:]]
        + [pltpu.VMEM((LAYERS,) + dims, BF) for dims in slab_shapes]
        + [
            pltpu.VMEM((width, 3 * lanes), BF), pltpu.VMEM((width, width), BF),
            pltpu.VMEM((width, columns), BF), pltpu.VMEM((width, h_cols), BF),
            pltpu.VMEM((width, h_cols), BF), pltpu.VMEM((h_cols, columns), BF),
            pltpu.VMEM(in_blocks + (columns,), BF), pltpu.VMEM((tokens, columns), BF),
            pltpu.VMEM((tokens, h_cols), BF),
            pltpu.VMEM((tokens, h_cols), BF), pltpu.VMEM((tokens, h_cols), BF),
            pltpu.VMEM((2 * BLOCK, width), BF),
            pltpu.VMEM(in_blocks + (BLOCK,), BF),
            pltpu.VMEM((LAYERS, PLANE, pad_rows, q_cols + f_cols), BF),
            pltpu.VMEM((LAYERS, PLANE, pad_rows, q_cols + f_cols), BF),
            pltpu.VMEM((LAYERS, out_rows, width), BF),
            pltpu.VMEM((LAYERS, out_rows, width), BF),
            pltpu.SemaphoreType.DMA((3, LAYERS, 4, levels - 1)),
            pltpu.SemaphoreType.DMA((LAYERS, 4)),
            pltpu.SemaphoreType.DMA((32,)),
            pltpu.SemaphoreType.DMA((3,)),
            pltpu.SemaphoreType.DMA((2, 4)),
            pltpu.SemaphoreType.DMA((2, LAYERS, PLANE)),
            pltpu.SemaphoreType.DMA((2, PLANE)),
            pltpu.SemaphoreType.DMA((2,)),
        ],
        compiler_params=pltpu.CompilerParams(
            collective_id=1, has_side_effects=True, vmem_limit_bytes=62 * MIB
        ),
        name="decoder_forward",
    )(x, own_mask, rope, sel_q, sel_o, head_lanes,
      adjoint.reshape(2, 2, HALF_BLOCK, columns), head_first_bias[None], head_bias[None], gains,
      w_qkv, w_in, w_out, d_piece, head_first, head_final, head_skip)

    chunk = [PLANE * rows, out_rows, PLANE * rows, down_rows, PLANE * rows, head_rows, head_rows]
    cols = [q_cols, width, f_cols, width, h_cols, columns, columns]
    stage_rows = [levels * n for n in chunk[:5]] + [h_cols] * 2
    kept_shapes = [
        in_blocks + (width,), (tokens, f_cols), (tokens, f_cols), (width, f_cols), (f_cols, width),
        (LAYERS, BLOCK, width), in_blocks + (width,), (tokens, 3 * lanes), (tokens, lanes),
        (tokens, o_rows), (width, q_cols), (o_rows, width), (LAYERS, BLOCK, width),
    ]
    small_cols = columns + h_cols
    outs = [
        shape(BLOCK, width, dtype=F32), shape(8, small_cols, dtype=F32),
        shape(LAYERS, rows, 3 * width, dtype=F32), shape(LAYERS, rows, width, dtype=F32),
        shape(LAYERS, rows, ff, dtype=F32), shape(LAYERS, down_rows, width, dtype=F32),
        shape(LAYERS, rows, 1, dtype=F32), shape(LAYERS, rows, 1, dtype=F32),
        shape(rows, width, dtype=F32), shape(head_rows, columns, dtype=F32),
        shape(head_rows, columns, dtype=F32),
    ]
    (input_grad, small, q_grad, o_grad, i_grad, d_grad, q_gain, i_gain, g_first, g_out,
     g_skip) = pl.pallas_call(
        lambda *refs: backward_kernel(levels, *refs),
        out_shape=outs,
        in_specs=[VMEM] * 6 + [ANY] * 19,
        out_specs=[VMEM, VMEM, ANY, VMEM, ANY] + [VMEM] * (len(outs) - 5),
        scratch_shapes=exchange_scratch(width, PHASES)
        + [pltpu.VMEM((2,) + in_blocks + (width,), BF)]
        + [pltpu.VMEM(dims, F32 if dims[0] == LAYERS and dims[1] == BLOCK else BF) for dims in kept_shapes]
        + [pltpu.VMEM((tokens, q_cols), BF)]
        + [pltpu.VMEM((stage_rows[m], cols[m]), BF) for m in range(7)]
        + [
            pltpu.VMEM((LAYERS if m < 4 else 1, levels, chunk[m], cols[m]), BF)
            for m in range(7)
        ]
        + [
            pltpu.VMEM((LAYERS if m < 4 else 1, chunk[m], cols[m]), BF) for m in (0, 1, 2, 4)
        ]
        + [pltpu.VMEM((chunk[0], max(f_cols, q_cols)), F32), pltpu.VMEM((out_rows, width), F32)]
        + [pltpu.VMEM((LAYERS, out_rows, width), BF)] * 2
        + [
            pltpu.VMEM((2, 8, h_cols), F32), pltpu.VMEM((8, h_cols), F32),
            pltpu.VMEM((levels, 8, small_cols), F32),
            pltpu.VMEM((rows, max(ff, 3 * width)), F32),
            pltpu.SemaphoreType.DMA((2, LAYERS, 7, levels)),
            pltpu.SemaphoreType.DMA((20,)),
            pltpu.SemaphoreType.DMA((2, levels)),
            pltpu.SemaphoreType.DMA((2, LAYERS, 3, PLANE)),
            pltpu.SemaphoreType.DMA((2, LAYERS)),
            pltpu.SemaphoreType.DMA((1,)),
        ],
        compiler_params=pltpu.CompilerParams(
            collective_id=2, has_side_effects=True, vmem_limit_bytes=62 * MIB
        ),
        name="decoder_backward",
    )(rope, sel_q, sel_o, gains, w_qkv, w_in, grad_final, nml, act, gl, wi, wd, mid, nrm, qkv, prb,
      att, wq, wo, xs, lines, gpre, hidden.reshape(in_blocks + (h_cols,)),
      picked.reshape(in_blocks + (h_cols,)), g)

    z, narrow = lax.axis_index("wide") // 4, lax.axis_index("narrow")
    g_first_bias = lax.dynamic_slice(small[0], (columns + z * head_rows + narrow * rows,), (rows,))
    return (
        predictions, input_grad, q_grad, o_grad, i_grad, d_grad[:, :ff_rows], q_gain[..., 0],
        i_gain[..., 0], g_first, g_first_bias, g_out[:head_share], small[0, :columns],
        g_skip[:head_share],
    )


def solution(mesh):
    devices = mesh.shape["wide"] * mesh.shape["narrow"]
    both = ("wide", "narrow")
    weight, gain = P(None, both, None), P(None, both)
    return jax.shard_map(
        lambda *arrays: per_device(devices, *arrays),
        mesh=mesh,
        in_specs=(
            P(both, None), P(both), P(both), weight, weight, weight, weight, gain, gain, P(), P(),
            P(None, "narrow"), P("narrow"), P(None, "narrow"), P("wide", "narrow"),
        ),
        out_specs=(
            P("wide", "narrow"), P(both, None), weight, weight, weight, weight, gain, gain,
            P(both, None), P(both), P("wide", "narrow"), P("narrow"), P("wide", "narrow"),
        ),
        check_vma=False,
    )
```

```python
import math

import jax
import jax.numpy as jnp
import numpy as np
from jax import lax
from jax.experimental import pallas as pl
from jax.experimental.pallas import tpu as pltpu
from jax.sharding import PartitionSpec as P

HDIM = 80
HALF = HDIM // 2
LAYERS = 2
ROW_LEN = 16
BLOCK = 128
HALF_BLOCK = BLOCK // 2
PLANE = 8
PHASES = 2 * LAYERS
MESH = pl.DeviceIdType.MESH
BF = jnp.bfloat16
F32 = jnp.float32
EPS = 1e-06
ROTARY_BASE = 10000.0
MIB = 1024 * 1024
VMEM = pl.BlockSpec(memory_space=pltpu.VMEM)
ANY = pl.BlockSpec(memory_space=pl.ANY)


def up16(rows):
    return -(-rows // 16) * 16


def rows_at(start, count, step=16):
    return pl.ds(pl.multiple_of(start, step), count)


def dot(a, b, ca=1, cb=0):
    return lax.dot_general(a, b, (((ca,), (cb,)), ((), ())), preferred_element_type=F32)


class Place:
    def __init__(self):
        wide = lax.axis_index("wide")
        self.x = lax.axis_index("narrow")
        self.core = wide % 2
        self.y = (wide // 2) % 2
        self.z = wide // 4

    def device(self, z, y, core, x):
        return (z * 4 + y * 2 + core, x)

    def sibling(self):
        return self.device(self.z, self.y, 1 - self.core, self.x)

    def major(self, s, far=0):
        return (self.y + s * (self.x - self.y) + far) % 2

    def minor(self, s, near=0):
        return (self.x + s * (self.y - self.x) + near) % 2

    def near(self, s):
        return self.device(self.z, (self.y + s) % 2, self.core, (self.x + 1 - s) % 2)

    def far(self, s):
        return self.device(self.z, (self.y + 1 - s) % 2, self.core, (self.x + s) % 2)

    def level(self, z):
        return self.device(z, self.y, self.core, self.x)

    def turned(self, e):
        return (self.y + e // 4) % 2, (self.core + e // 2) % 2, (self.x + e) % 2

    def other(self, e):
        return self.device(self.z, *self.turned(e))

    def rank(self, e=0):
        y, core, x = self.turned(e)
        return 4 * y + 2 * core + x

    def indexed(self, index):
        return (index // 2, index % 2)

    def holder(self, levels):
        index = PLANE * self.z + self.rank()
        return index % levels * PLANE + index // levels

    def held(self, levels):
        return levels * self.rank() + self.z

    def trades(self, levels):
        return self.holder(levels) != PLANE * self.z + self.rank()


def greet(place, levels):
    barrier = pltpu.get_barrier_semaphore()
    others = [place.other(e) for e in range(1, PLANE)]
    others += [place.level((place.z + d) % levels) for d in range(1, levels)]
    for other in others:
        pl.semaphore_signal(barrier, inc=1, device_id=other, device_id_type=MESH)
    trades = place.trades(levels)

    @pl.when(trades)
    def _():
        for index in (place.holder(levels), place.held(levels)):
            pl.semaphore_signal(
                barrier, inc=1, device_id=place.indexed(index), device_id_type=MESH
            )
        pl.semaphore_wait(barrier, len(others) + 2)

    @pl.when(jnp.logical_not(trades))
    def _():
        pl.semaphore_wait(barrier, len(others))


def remote(src, dst, send, recv, device):
    return pltpu.make_async_remote_copy(
        src_ref=src, dst_ref=dst, send_sem=send, recv_sem=recv, device_id=device,
        device_id_type=MESH,
    )


class Exchange:
    def __init__(self, place, phase, buf, scratch):
        (self.part, self.recv_s, self.send_f, self.recv_f, self.send_n, self.recv_n, self.sems) = scratch
        self.place, self.phase, self.buf = place, phase, buf

    def copy(self, s, kind, src, dst, device):
        sems = self.sems
        return remote(
            src, dst, sems.at[self.phase, s, 0, kind], sems.at[self.phase, s, 1, kind], device
        )

    def block(self, s, far, near, core):
        place = self.place
        return self.buf.at[s, place.major(s, far), place.minor(s, near), core]

    def own(self, s):
        return (s, self.place.major(s), self.place.minor(s), self.place.core)

    def to_near(self, s, far=0, near=0):
        rows = self.block(s, far, near, self.place.core)
        return self.copy(s, 0, rows, rows, self.place.near(s))

    def to_far(self, s, far=0, near=0):
        rows = self.block(s, far, near, self.place.core)
        return self.copy(s, 1, rows, rows, self.place.far(s))

    def pass_far(self, s, far=0, near=1):
        rows = self.block(s, far, near, self.place.core)
        return self.copy(s, 2, rows, rows, self.place.far(s))

    def sibling(self, s, kind, core):
        if kind < 2:
            rows = self.block(s, 0, kind, core)
        else:
            rows = self.buf.at[s, self.place.major(s, 1), :, core]
        return self.copy(s, 3 + kind, rows, rows, self.place.sibling())

    def to_sibling(self, s, kind):
        return self.sibling(s, kind, self.place.core)

    def from_sibling(self, s, kind):
        return self.sibling(s, kind, 1 - self.place.core)

    def sum_sibling(self, s, half):
        src = self.part.at[s, half, :, 1 - self.place.core]
        sems = self.sems
        return remote(
            src, self.recv_s.at[s, half], sems.at[self.phase, s, 0, 6 + half],
            sems.at[self.phase, s, 1, 6 + half], self.place.sibling(),
        )

    def sum_far(self, s):
        return self.copy(s, 8, self.send_f.at[s], self.recv_f.at[s], self.place.far(s))

    def sum_near(self, s):
        return self.copy(s, 9, self.send_n.at[s], self.recv_n.at[s], self.place.near(s))

    def start(self, s):
        self.to_near(s).start()
        self.to_far(s).start()
        self.to_sibling(s, 0).start()

    def far_stage(self, s):
        self.sum_sibling(s, 1).wait_recv()
        own = self.part[s, 1, :, self.place.core].astype(F32)
        self.send_f[s] = (own + self.recv_s[s, 1].astype(F32)).astype(BF)
        self.sum_far(s).start()

    def summed(self, s, minor):
        own = self.part[s, 0, minor, self.place.core].astype(F32)
        return own + self.recv_s[s, 0, minor].astype(F32) + self.recv_f[s, minor].astype(F32)

    def near_stage(self, s):
        self.sum_sibling(s, 0).wait_recv()
        self.sum_far(s).wait_recv()
        self.send_n[s] = self.summed(s, self.place.minor(s, 1)).astype(BF)
        self.sum_near(s).start()

    def total(self, s):
        self.sum_near(s).wait_recv()
        total = self.summed(s, self.place.minor(s)) + self.recv_n[s].astype(F32)
        self.to_near(s).wait_send()
        self.to_far(s).wait_send()
        self.pass_far(s).wait_send()
        for kind in range(3):
            self.to_sibling(s, kind).wait_send()
        for half in range(2):
            self.sum_sibling(s, half).wait_send()
        self.sum_far(s).wait_send()
        self.sum_near(s).wait_send()
        return total

    def take_near(self, s):
        self.to_near(s, 0, 1).wait_recv()
        self.pass_far(s).start()
        self.to_sibling(s, 1).start()

    def take_far(self, s):
        self.to_far(s, 1, 0).wait_recv()
        self.pass_far(s, 1, 1).wait_recv()
        self.to_sibling(s, 2).start()

    def take_sibling(self, s):
        for kind in range(3):
            self.from_sibling(s, kind).wait_recv()

    def run(self, compute, hooks, taken=False):
        def body(i, carry):
            s, half = i // 2, i % 2
            if not taken:
                pl.when(half == 0)(lambda: self.take_near(s))

            for at, hook in hooks:
                pl.when(i == at)(hook)

            if not taken:
                @pl.when(half == 0)
                def _():
                    self.from_sibling(s, 0).wait_recv()
                    self.from_sibling(s, 1).wait_recv()

                pl.when(half == 1)(lambda: self.take_far(s))

            @pl.when(i == 2)
            def _():
                self.far_stage(0)

            if not taken:
                pl.when(half == 1)(lambda: self.from_sibling(s, 2).wait_recv())

            major = self.place.major(s, half)
            compute(s * 8 * HALF_BLOCK + major * 4 * HALF_BLOCK, s, half, major)
            self.sum_sibling(s, half).start()
            return carry

        lax.fori_loop(0, 4, body, 0)
        self.near_stage(0)
        self.far_stage(1)


def exchange_scratch(width, phases):
    return [
        pltpu.VMEM((2, 2, 2, 2, HALF_BLOCK, width), BF),
        pltpu.VMEM((2, 2, 2, HALF_BLOCK, width), BF),
        pltpu.VMEM((2, 2, HALF_BLOCK, width), BF),
        pltpu.VMEM((2, 2, HALF_BLOCK, width), BF),
        pltpu.VMEM((2, HALF_BLOCK, width), BF),
        pltpu.VMEM((2, HALF_BLOCK, width), BF),
        pltpu.SemaphoreType.DMA((phases, 2, 2, 10)),
    ]


def flat(ref, columns=slice(None)):
    if len(ref.shape) == 2:
        return ref[:, columns]
    values = ref[(slice(None),) * 5 + (columns,)]
    return values.reshape(-1, values.shape[-1])


def write_part(part, s, half, values, w, contracted):
    width = part.shape[-1]
    step = width // 2
    for n in range(0, width, step):
        columns = slice(n, n + step)
        side = w[:, columns] if contracted == 0 else w[columns, :]
        part[s, half, :, :, :, columns] = blocked(dot(values, side, 1, contracted).astype(BF))


def blocked(values):
    return values.reshape(2, 2, HALF_BLOCK, values.shape[-1])


def root(values):
    return lax.rsqrt(jnp.mean(values * values, axis=-1, keepdims=True) + EPS)


def forward_kernel(levels, *refs):
    (x_in, own_mask, rope, sel_q, sel_o, head_lanes, adjoint, bias_first, bias_last) = refs[:9]
    (gains, w_q, w_in, w_out) = refs[9:13]
    w_down, head_weights = refs[13], refs[14:17]
    (predictions, grad_out, xs, mid) = refs[17:21]
    kept, (slab_q, slab_o, slab_i, slab_d) = refs[21:33], refs[33:37]
    exchange = refs[37:44]
    (nrm, nml, qkv, prb, att, gl, act) = refs[44:51]
    slabs = refs[51:55]
    (wide_q, first, final, pick, first_q, final_q) = refs[55:61]
    (g, g_rows, hidden, gpre, picked, hidden_all) = refs[61:67]
    (mask, cut, pasted, o_cut, o_piece) = refs[67:72]
    (z_sems, own_sems, keep_sems, load_sems, g_sems, trade_sems, mask_sems, o_sems) = refs[72:]
    slab_outs = (slab_q, slab_o, slab_i, slab_d)
    place = Place()
    z = place.z
    heads = sel_o.shape[1] // BLOCK
    lanes = heads * BLOCK
    kept_here, waited = [], []

    def keep(src, dst):
        copy = pltpu.make_async_copy(src, dst, keep_sems.at[len(kept_here)])
        copy.start()
        kept_here.append(copy)
        return copy

    def forget(copy):
        copy.wait()
        waited.append(copy)

    relayed = levels == 4

    def far(delta):
        there = (z + delta) % levels
        return (z + there == 3) & (z * there == 0)

    counts = [slabs[0].shape[1] // levels, o_piece.shape[1], slabs[2].shape[1] // levels,
              w_down.shape[1]]

    def rows_of(m, level):
        return rows_at(level * counts[m], counts[m])

    def piece(layer, m):
        if m == 1:
            return o_piece.at[layer]
        if m == 3:
            return w_down.at[layer]
        return slabs[m].at[layer, rows_of(m, z)]

    def spread(layer, m, delta):
        return remote(
            piece(layer, m), slabs[m].at[layer, rows_of(m, z)],
            z_sems.at[0, layer, m, delta - 1], z_sems.at[1, layer, m, delta - 1],
            place.level((z + delta) % levels),
        )

    def arriving(layer, m, delta):
        rows = slabs[m].at[layer, rows_of(m, (z + levels - delta) % levels)]
        return remote(
            rows, rows, z_sems.at[0, layer, m, delta - 1], z_sems.at[1, layer, m, delta - 1],
            place.level((z + delta) % levels),
        )

    def relay(layer, m):
        rows = slabs[m].at[layer, rows_of(m, (z + 2) % levels)]
        return remote(
            rows, rows, z_sems.at[2, layer, m, 0], z_sems.at[1, layer, m, 2 * (z - 1)],
            place.level(3 * (z - 1)),
        )

    def for_spread(layer, m, act_on):
        for delta in range(1, levels):
            if relayed and delta != 2:
                @pl.when(jnp.logical_not(far(delta)))
                def _(delta=delta):
                    act_on(spread(layer, m, delta))
            else:
                act_on(spread(layer, m, delta))

    def own_piece(layer, m):
        return pltpu.make_async_copy(
            piece(layer, m), slabs[m].at[layer, rows_of(m, z)], own_sems.at[layer, m]
        )

    def send_weights(layer, m):
        if m % 2:
            own_piece(layer, m).start()
        for_spread(layer, m, lambda copy: copy.start())

    rows, q_cols = w_q.shape[1], slabs[0].shape[2]
    span = w_q.shape[2] // 3 // PLANE
    ff_rows = w_in.shape[2] // PLANE // levels
    padded = slabs[2].shape[2] // levels - ff_rows

    def cut_weights(layer):
        scaled_q = w_q[layer].astype(F32) * gains[0, layer]
        scaled_i = w_in[layer].astype(F32) * gains[1, layer]
        for t in range(PLANE):
            parts = []
            for kind in range(3):
                low = (kind * PLANE + t) * span
                parts.append(scaled_q[:, low : low + span])
            if q_cols > 3 * span:
                parts.append(jnp.zeros((rows, q_cols - 3 * span), F32))
            cut[layer, t, :rows, :q_cols] = jnp.concatenate(parts, axis=1).astype(BF)
            parts = []
            for zz in range(levels):
                low = (zz * PLANE + t) * ff_rows
                parts.append(scaled_i[:, low : low + ff_rows])
                if padded:
                    parts.append(jnp.zeros((rows, padded), F32))
            cut[layer, t, :rows, q_cols:] = jnp.concatenate(parts, axis=1).astype(BF)

    def trade(layer, e):
        return remote(
            cut.at[layer, place.rank(e)], pasted.at[layer, place.rank()],
            trade_sems.at[0, layer, e], trade_sems.at[1, layer, e], place.other(e),
        )

    def traded(layer, e):
        there = pasted.at[layer, place.rank(e)]
        return remote(
            there, there, trade_sems.at[0, layer, e], trade_sems.at[1, layer, e], place.other(e)
        )

    def start_trade(layer):
        for e in range(1, PLANE):
            trade(layer, e).start()
        own = place.rank()
        pltpu.make_async_copy(
            cut.at[layer, own], pasted.at[layer, own], trade_sems.at[0, layer, 0]
        ).start()

    def end_trade(layer):
        own = place.rank()
        pltpu.make_async_copy(
            cut.at[layer, own], pasted.at[layer, own], trade_sems.at[0, layer, 0]
        ).wait()
        for e in range(1, PLANE):
            traded(layer, e).wait_recv()
        for e in range(1, PLANE):
            trade(layer, e).wait_send()
        for m, low in ((0, 0), (2, q_cols)):
            width = slabs[m].shape[2]
            whole = [pasted[layer, t, :rows, low : low + width].astype(F32) for t in range(PLANE)]
            slabs[m][layer, rows_of(m, z), :] = jnp.concatenate(whole, axis=0).astype(BF)

    trades = place.trades(levels)
    o_trade = remote(
        o_cut, o_piece, o_sems.at[0], o_sems.at[1], place.indexed(place.holder(levels))
    )
    o_local = pltpu.make_async_copy(o_cut, o_piece, o_sems.at[0])

    def mask_to(e):
        there = mask.at[place.y, place.x, :, place.core]
        return remote(own_mask, there, mask_sems.at[0, e], mask_sems.at[1, e], place.other(e))

    def mask_from(e):
        y, core, x = place.turned(e)
        there = mask.at[y, x, :, core]
        return remote(there, there, mask_sems.at[0, e], mask_sems.at[1, e], place.other(e))

    mask_local = pltpu.make_async_copy(
        own_mask, mask.at[place.y, place.x, :, place.core], mask_sems.at[0, 0]
    )

    middle = (z == 1) | (z == 2)

    def relay_on(layer, m):
        if relayed:
            @pl.when(middle)
            def _():
                arriving(layer, m, 2).wait_recv()
                relay(layer, m).start()

    def weights_here(layer, m):
        for delta in range(1, levels):
            if relayed and delta == 2:
                pl.when(jnp.logical_not(middle))(arriving(layer, m, delta).wait_recv)
            else:
                arriving(layer, m, delta).wait_recv()
        for_spread(layer, m, lambda copy: copy.wait_send())
        if m % 2:
            own_piece(layer, m).wait()
        if relayed:
            pl.when(middle)(relay(layer, m).wait_send)

        return keep(slabs[m].at[layer], slab_outs[m].at[layer])

    skip = slabs[2].at[0, :, : adjoint.shape[3]]
    loads = [
        pltpu.make_async_copy(src, dst, load_sems.at[i])
        for i, (src, dst) in enumerate(zip(head_weights, (first, final, skip)))
    ]
    loads[0].start()
    loads[1].start()
    greet(place, levels)

    g_own = g.at[place.y, :, :, place.core]
    g_far = g.at[1 - place.y, :, :, place.core]
    g_local = pltpu.make_async_copy(adjoint, g_own, g_sems.at[0, 0])
    g_peer = remote(adjoint, g_own, g_sems.at[0, 1], g_sems.at[1, 1], place.far(0))
    g_sibling = remote(adjoint, g_own, g_sems.at[0, 2], g_sems.at[1, 2], place.sibling())
    g_pass = remote(g_far, g_far, g_sems.at[0, 3], g_sems.at[1, 3], place.sibling())
    part = exchange[0]
    lines = nrm.at[0]
    bufs = [nrm.at[0], nml.at[0], nrm.at[1], nml.at[1], lines]
    phases = [Exchange(place, p, buf, exchange) for p, buf in enumerate(bufs)]

    def own_half(s):
        return slice(s * HALF_BLOCK, (s + 1) * HALF_BLOCK)

    def chip_of(s, major, minor):
        return (major + s * (minor - major), minor + s * (major - minor))

    def enter(p, s, values):
        if p < 2 * LAYERS:
            values = values * root(values)
        bufs[p][phases[p].own(s)] = values.astype(BF)
        phases[p].start(s)

    def leave(p, s):
        rows = own_half(s)
        total = phases[p].total(s)
        if p == 2 * LAYERS:
            grad_out[rows, :] = total
            return
        layer = p // 2
        if p % 2 == 0:
            values = xs[layer, rows, :] + total
            mid[layer, rows, :] = values
        else:
            values = mid[layer, rows, :] + total
            if layer + 1 < LAYERS:
                xs[layer + 1, rows, :] = values
        enter(p + 1, s, values)

    def run(p, compute, next_weights, more=()):
        more = list(more)
        hooks = [(1, lambda: leave(p - 1, 1))] if p else []
        hooks += [(2, lambda key=key: relay_on(*key)) for key in next_weights]
        phases[p].run(compute, hooks + more)
        leave(p, 0)
        phases[p].near_stage(1)

    o_cut[...] = jnp.zeros(o_cut.shape, BF)
    for layer in range(LAYERS):
        o_cut[layer, :rows, :] = w_out[layer]
    pl.when(trades)(o_trade.start)
    pl.when(jnp.logical_not(trades))(o_local.start)
    cut_weights(0)
    start_trade(0)
    cut_weights(1)
    end_trade(0)
    send_weights(0, 0)
    xs[0] = x_in[...].astype(F32)
    for s in range(2):
        enter(0, s, xs[0, own_half(s), :])
    mask_local.start()
    for e in range(1, PLANE):
        mask_to(e).start()

    @pl.when(trades)
    def _():
        o_trade.wait_recv()
        o_trade.wait_send()

    pl.when(jnp.logical_not(trades))(o_local.wait)
    send_weights(0, 1)
    start_trade(1)
    for copy in (g_local, g_peer, g_sibling):
        copy.start()
    mask_local.wait()
    for e in range(1, PLANE):
        mask_from(e).wait_recv()
        mask_to(e).wait_send()
    relay_on(0, 0)
    relay_on(0, 1)

    def second_layer():
        end_trade(1)
        send_weights(1, 0)
        send_weights(1, 1)

    slab_keeps = []
    for layer in range(LAYERS):
        wq, wo, wi, wd = [slab.at[layer] for slab in slabs]
        slab_keeps.append(weights_here(layer, 0))
        if layer == 0:
            send_weights(0, 2)
            send_weights(0, 3)
        for n in range(0, wide_q.shape[0], 256):
            wide_q[n : n + 256, :] = dot(wq[n : n + 256, :], sel_q[...]).astype(BF)
        slab_keeps.append(weights_here(layer, 1))
        if layer:
            for copy in attn_saved:
                forget(copy)

        def attend(start, s, half, major, layer=layer, wo=wo):
            both = rows_at(start, 2 * BLOCK, 2 * BLOCK)
            projected = dot(nrm[layer, s, major].reshape(2 * BLOCK, nrm.shape[-1]), wide_q[...])
            cosine, sine = rope[:, :BLOCK], rope[:, BLOCK:]
            allowed = [
                mask[chip_of(s, major, block) + (s,)].reshape(BLOCK, BLOCK) > 0 for block in range(2)
            ]
            units = [(block, h) for block in range(2) for h in range(heads)]
            turned = []
            for low in range(0, 2 * lanes, BLOCK):
                value = projected[:, low : low + BLOCK]
                value = value * cosine + pltpu.roll(value, BLOCK // 2, 1) * sine
                turned.append(value.astype(BF))
            values = projected[:, 2 * lanes :].astype(BF)

            def rows_in(array, block):
                return array[block * BLOCK : (block + 1) * BLOCK]

            scores = [
                dot(rows_in(turned[h], block), rows_in(turned[heads + h], block), 1, 1)
                for block, h in units
            ]
            scores = [
                jnp.where(allowed[block], score * (1.0 / math.sqrt(HDIM)), -1e30)
                for (block, h), score in zip(units, scores)
            ]
            tops = [jnp.max(score, axis=-1, keepdims=True) for score in scores]
            scores = [jnp.exp(score - top) for score, top in zip(scores, tops)]
            sums = [jnp.sum(score, axis=-1, keepdims=True) for score in scores]
            probs = [(score / total).astype(BF) for score, total in zip(scores, sums)]
            outs = [
                dot(prob, rows_in(values, block)[:, h * BLOCK : (h + 1) * BLOCK]).astype(BF)
                for (block, h), prob in zip(units, probs)
            ]

            def joined(parts):
                side = [
                    jnp.concatenate(parts[block * heads : (block + 1) * heads], axis=1)
                    for block in range(2)
                ]
                return jnp.concatenate(side, axis=0)

            attended = dot(joined(outs), sel_o[...], 1, 1).astype(BF)
            write_part(part, s, half, attended, wo, 0)
            att[both, :] = attended
            prb[both, :] = joined(probs)
            qkv[both, :] = jnp.concatenate(turned + [values], axis=1)

        more = [(1, second_layer)] if layer == 0 else []
        run(2 * layer, attend, ((layer, 2), (layer, 3)), more)
        attn_saved = [keep(src, dst.at[layer]) for src, dst in zip((qkv, prb, att), kept[2:5])]
        nrm_saved = keep(nrm.at[layer], kept[0].at[layer])
        if layer == 0:
            g_peer.wait_recv()
            g_pass.start()
        ending = layer + 1 == LAYERS
        slab_keeps.append(weights_here(layer, 2))
        if layer:
            for copy in mlp_saved:
                forget(copy)
        slab_keeps.append(weights_here(layer, 3))
        if not ending:
            for m in (2, 3):
                send_weights(layer + 1, m)

        def lift(start, s, major, layer=layer, wi=wi):
            rows = rows_at(start, 2 * BLOCK, 2 * BLOCK)
            lifted = dot(nml[layer, s, major].reshape(2 * BLOCK, nml.shape[-1]), wi[...])
            root_two = math.sqrt(2.0 / math.pi)
            square = lifted * lifted
            tanh = jnp.tanh(root_two * lifted * (1.0 + 0.044715 * square))
            activated = (0.5 * lifted * (1.0 + tanh)).astype(BF)
            act[rows, :] = activated
            slope = 0.5 * (1.0 + tanh) + 0.5 * lifted * (1.0 - tanh * tanh) * root_two * (
                1.0 + 3.0 * 0.044715 * square
            )
            gl[rows, :] = slope.astype(BF)
            return activated

        def perceptron(start, s, half, major, lift=lift, wd=wd):
            write_part(part, s, half, lift(start, s, major), wd, 0)

        following = () if ending else ((layer + 1, 0), (layer + 1, 1))
        run(2 * layer + 1, perceptron, following)
        mlp_saved = [keep(src, dst.at[layer]) for src, dst in zip((gl, act), kept[5:7])]
        keep(nml.at[layer], kept[1].at[layer])
        if layer == 0:
            forget(nrm_saved)
            forget(slab_keeps[2])
            loads[2].start()
            loads[0].wait()
            loads[1].wait()
            index = lax.broadcasted_iota(jnp.int32, pick.shape, 0)
            offset = (2 * place.y + place.core) * (pick.shape[0] // (4 * levels))
            pick[...] = jnp.where(index - offset == head_lanes[...], 1.0, 0.0).astype(BF)
            for n in range(0, first.shape[0], 256):
                first_q[n : n + 256, :] = dot(first[n : n + 256, :], pick[...]).astype(BF)
            final_q[...] = dot(pick[...], final[...], 0, 0).astype(BF)

    g_local.wait()
    for copy in (g_sibling, g_pass):
        copy.wait_recv()
    loads[2].wait()
    bias_q = dot(jnp.broadcast_to(bias_first[...], (16, bias_first.shape[1])), pick[...])[:1]
    columns = g.shape[-1]

    def head(start, s, half, major):
        rows = rows_at(start, 2 * BLOCK, 2 * BLOCK)
        pre = dot(lines[s, major].reshape(2 * BLOCK, lines.shape[-1]), first_q[...]) + bias_q
        gate = 1.0 / (1.0 + jnp.exp(-pre))
        hidden[rows, :] = (pre * gate).astype(BF)
        for block in range(2):
            here = rows_at(start + block * BLOCK, BLOCK, BLOCK)
            g_rows[here, :] = g[chip_of(s, major, block) + (s,)].reshape(BLOCK, columns)
        there = g_rows[rows, :]
        grad_hidden = dot(there, final_q[...], 1, 1)
        gpre[rows, :] = (grad_hidden * (gate * (1.0 + pre * (1.0 - gate)))).astype(BF)
        row = lax.broadcasted_iota(jnp.int32, (2 * BLOCK, 1), 0)
        y = major + s * (row // BLOCK - major)
        mine = (row // HALF_BLOCK % 2 == place.core) & (y == place.y)
        mine = jnp.where(mine, there.astype(F32), 0.0).astype(BF)
        whole = dot(gpre[rows, :], first_q[...], 1, 1) + dot(mine, skip[...], 1, 1)
        part[s, half] = blocked(whole.astype(BF))

    p = 2 * LAYERS
    phases[p].run(head, [(1, lambda: leave(p - 1, 1))])

    keep(lines, kept[7])
    keep(hidden, kept[8])
    keep(gpre, kept[9])
    keep(g_rows, kept[11])
    for s in range(2):
        for major in range(2):
            n = (2 * s + major) * 2 * BLOCK
            rows = lines[s, major].reshape(2 * BLOCK, lines.shape[-1])
            picked[n : n + 2 * BLOCK, :] = dot(rows, pick[...]).astype(BF)
    keep(picked, kept[10])
    phases[p].near_stage(1)
    mine = []
    for x in range(2):
        mine += [lines[0, place.y, x, place.core], lines[1, x, place.y, place.core]]
    mine = jnp.concatenate(mine, axis=0)
    pre = dot(mine, first[...]) + bias_first[...].astype(F32)
    hidden_all[...] = (pre / (1.0 + jnp.exp(-pre))).astype(BF)
    out = dot(hidden_all[...], final[...]) + bias_last[...].astype(F32)
    predictions[...] = (out + dot(mine, skip[...])).astype(BF)
    leave(p, 0)
    leave(p, 1)
    for copy in (g_peer, g_sibling, g_pass):
        copy.wait_send()
    for copy in kept_here:
        if not any(copy is other for other in waited):
            copy.wait()


def norm_back(values, q):
    scale = root(values)
    n = values * scale
    return scale * (q - n * jnp.mean(q * n, axis=-1, keepdims=True))


def backward_kernel(levels, *refs):
    (rope, sel_q, sel_o, gains, w_q, w_in) = refs[:6]
    dy_in, stored, head_stored = refs[6], refs[7:20], refs[20:25]
    (dx_out, small_out, q_out, o_out, i_out, d_out, q_gain, i_gain) = refs[25:33]
    (first_out, out_out, skip_out) = refs[33:36]
    exchange, ag = refs[36:43], refs[43]
    loaded, gp = refs[44:57], refs[57]
    stages, arrivals = refs[58:65], refs[65:72]
    own_sums, acc, o_acc = refs[72:76], refs[76], refs[77]
    o_cut, o_pasted = refs[78], refs[79]
    (small_own, small_x, small_z) = refs[80:83]
    row_buf = refs[83]
    z_sems, load_sems, small_sems, trade_sems, o_sems, row_sem = refs[84:]
    (nml, act, gl, wi, wd, mid, nrm, qkv, prb, att, wq, wo, xs) = loaded
    part = exchange[0]
    place = Place()
    z = place.z
    heads = sel_o.shape[1] // BLOCK
    lanes = heads * BLOCK

    def load(layer, i):
        return pltpu.make_async_copy(stored[i].at[layer], loaded[i], load_sems.at[i])

    lines = ag.at[1]
    h_cols, half_width = small_own.shape[2], nrm.shape[-1] // 2
    gpre, hidden = gp.at[:, :h_cols], nrm.at[:, :, :, :, :, :h_cols]
    picked = nrm.at[:, :, :, :, :, half_width : half_width + h_cols]
    g = qkv.at[:, : stages[5].shape[1]]
    head_loads = [
        pltpu.make_async_copy(src, dst, load_sems.at[len(loaded) + i])
        for i, (src, dst) in enumerate(zip(head_stored, (lines, gpre, hidden, picked, g)))
    ]
    mlp_part, attn_part = range(5), range(6, 12)
    norm_loads = [pltpu.make_async_copy(stored[i], loaded[i], load_sems.at[i]) for i in (5, 12)]
    for copy in norm_loads:
        copy.start()
    dy_load = pltpu.make_async_copy(dy_in, dx_out, load_sems.at[len(loaded) + 5])
    dy_load.start()
    for copy in head_loads:
        copy.start()
    for i in mlp_part:
        load(LAYERS - 1, i).start()
    greet(place, levels)

    def count_of(m):
        return arrivals[m].shape[2]

    def slot(m, layer):
        return layer if m < 4 else 0

    relayed = levels == 4
    middle = (z == 1) | (z == 2)

    def send(layer, m, delta):
        there = (z + delta) % levels
        return remote(
            stages[m].at[rows_at(there * count_of(m), count_of(m))],
            arrivals[m].at[slot(m, layer), delta - 1],
            z_sems.at[0, layer, m, delta - 1],
            z_sems.at[1, layer, m, delta - 1],
            place.level(there),
        )

    def far(delta):
        there = (z + delta) % levels
        return (z + there == 3) & (z * there == 0)

    def hand(layer, m, delta):
        there = (z + delta) % levels
        return remote(
            stages[m].at[rows_at(there * count_of(m), count_of(m))],
            arrivals[m].at[slot(m, layer), levels - 1],
            z_sems.at[0, layer, m, delta - 1],
            z_sems.at[1, layer, m, levels - 1],
            place.level(1 + z // 3),
        )

    def send_first(layer, m):
        for delta in range(1, levels):
            if not relayed:
                send(layer, m, delta).start()
            elif delta == 2:
                pl.when(jnp.logical_not(middle))(send(layer, m, delta).start)
            else:
                pl.when(far(delta))(hand(layer, m, delta).start)
                pl.when(jnp.logical_not(far(delta)))(send(layer, m, delta).start)

    def send_rest(layer, m):
        if relayed:
            @pl.when(middle)
            def _():
                hand(layer, m, 1).wait_recv()
                rows = rows_at((z + 2) % levels * count_of(m), count_of(m))
                total = stages[m][rows, :].astype(F32)
                total = total + arrivals[m][slot(m, layer), levels - 1].astype(F32)
                stages[m][rows, :] = total.astype(BF)
                send(layer, m, 2).start()

    def sent(layer, m):
        for delta in range(1, levels):
            send(layer, m, delta).wait_send()

    def result(layer, m):
        if m > 4:
            return (out_out, skip_out)[m - 5]
        if m == 3:
            return d_out.at[layer]
        return own_sums[min(m, 3)].at[slot(m, layer)]

    def weight_grad(layer, m, left, right, tile):
        width = left.shape[-1]
        if m < 4 and layer + 1 < LAYERS:
            sent(layer + 1, m)
        for low in range(0, width, tile):
            here = slice(low, min(low + tile, width))
            stages[m][here, :] = dot(flat(left, here), flat(right), 0, 0).astype(BF)
        send_first(layer, m)
        out = result(layer, m)
        out[...] = stages[m][rows_at(z * count_of(m), count_of(m)), :].astype(out.dtype)

    bufs = [ag.at[p % 2] for p in range(PHASES)]
    phases = [Exchange(place, p, buf, exchange) for p, buf in enumerate(bufs)]

    def own_half(s):
        return slice(s * HALF_BLOCK, (s + 1) * HALF_BLOCK)

    def enter(p, s):
        bufs[p][phases[p].own(s)] = dx_out[own_half(s), :].astype(BF)
        phases[p].start(s)

    def leave(p, s):
        rows = own_half(s)
        values = (mid if p % 2 == 0 else xs)[LAYERS - 1 - p // 2, rows, :]
        dx_out[rows, :] += norm_back(values, phases[p].total(s))
        if p + 1 < PHASES:
            enter(p + 1, s)

    def run(p, compute, relays):
        hooks = [(1, lambda: leave(p - 1, 1))] if p else []
        hooks += [(2, lambda key=key: send_rest(*key)) for key in relays]
        phases[p].run(compute, hooks)

    dy_load.wait()
    for copy in norm_loads:
        copy.wait()
    for s in range(2):
        enter(0, s)

    for copy in head_loads:
        copy.wait()
    last = LAYERS - 1
    bias_sum = jnp.sum(gpre[...].astype(F32), axis=0, keepdims=True)
    small_own[1] = jnp.broadcast_to(bias_sum, small_own.shape[1:])
    to_x = remote(
        small_own.at[1], small_x, small_sems.at[0, 0], small_sems.at[1, 0], place.near(0)
    )
    to_x.start()
    weight_grad(last, 5, hidden, g, 4 * BLOCK)
    weight_grad(last, 6, picked, g, 4 * BLOCK)
    weight_grad(last, 4, lines, gpre, 5 * BLOCK)
    g_sum = jnp.sum(g[...].astype(F32), axis=0, keepdims=True)
    to_x.wait()
    small_z[0, :, : g_sum.shape[1]] = jnp.broadcast_to(g_sum, (8, g_sum.shape[1]))
    small_z[0, :, g_sum.shape[1] :] = small_own[1] + small_x[...]
    to_z = [
        remote(
            small_z.at[0], small_z.at[d], small_sems.at[0, d], small_sems.at[1, d],
            place.level((z + d) % levels),
        )
        for d in range(1, levels)
    ]
    for copy in to_z:
        copy.start()
    for i in attn_part:
        load(last, i).start()

    relays = [(last, 5), (last, 6), (last, 4)]
    for layer in reversed(range(LAYERS)):
        p = 2 * (LAYERS - 1 - layer)
        buf = bufs[p]
        for i in mlp_part:
            load(layer, i).wait()

        def perceptron(start, s, half, major, buf=buf):
            rows = rows_at(start, 2 * BLOCK, 2 * BLOCK)
            grad_act = dot(buf[s, major].reshape(2 * BLOCK, buf.shape[-1]), wd[...], 1, 1)
            grad_lift = (grad_act * gl[rows, :].astype(F32)).astype(BF)
            write_part(part, s, half, grad_lift, wi, 1)
            gl[rows, :] = grad_lift

        run(p, perceptron, relays)
        weight_grad(layer, 3, act, buf, 2 * BLOCK)
        leave(p, 0)
        weight_grad(layer, 2, nml, gl, 5 * BLOCK)
        phases[p].near_stage(1)
        if layer > 0:
            for i in mlp_part:
                load(layer - 1, i).start()
        for i in attn_part:
            load(layer, i).wait()
        buf = bufs[p + 1]

        def attend(start, s, half, major, buf=buf):
            cosine, sine = rope[:, :BLOCK], rope[:, BLOCK:]
            both = rows_at(start, 2 * BLOCK, 2 * BLOCK)
            there = buf[s, major].reshape(2 * BLOCK, buf.shape[-1])
            grad_heads = dot(there, wo[...], 1, 1).astype(BF)
            grad_heads = dot(grad_heads, sel_o[...]).astype(BF)
            kept, probs = qkv[both, :], prb[both, :]
            units = [(block, h) for block in range(2) for h in range(heads)]

            def unit(array, block, h, kind=0):
                low = kind * lanes + h * BLOCK
                return array[block * BLOCK : (block + 1) * BLOCK, low : low + BLOCK]

            queries, keys, values = [[unit(kept, *u, kind) for u in units] for kind in range(3)]
            probs = [unit(probs, *u) for u in units]
            grads = [unit(grad_heads, *u) for u in units]
            grad_probs = [dot(grad, value, 1, 1) for grad, value in zip(grads, values)]
            grad_values = [dot(prob, grad, 0, 0).astype(BF) for prob, grad in zip(probs, grads)]
            wide = [prob.astype(F32) for prob in probs]
            inner = [
                jnp.sum(prob * grad, axis=-1, keepdims=True) for prob, grad in zip(wide, grad_probs)
            ]
            grad_scores = [
                (prob * (grad - total)).astype(BF)
                for prob, grad, total in zip(wide, grad_probs, inner)
            ]
            grad_queries = [dot(grad, key) for grad, key in zip(grad_scores, keys)]
            grad_keys = [dot(grad, query, 0, 0) for grad, query in zip(grad_scores, queries)]
            packed = []
            for parts in (grad_queries, grad_keys):
                for h in range(heads):
                    turned = jnp.concatenate([parts[h], parts[heads + h]], axis=0)
                    turned = turned * (1.0 / math.sqrt(HDIM))
                    turned = turned * cosine - pltpu.roll(turned, BLOCK // 2, 1) * sine
                    packed.append(turned.astype(BF))
            for h in range(heads):
                packed.append(jnp.concatenate([grad_values[h], grad_values[heads + h]], axis=0))
            packed = dot(jnp.concatenate(packed, axis=1), sel_q[...], 1, 1).astype(BF)
            write_part(part, s, half, packed, wq, 1)
            gp[both, :] = packed

        run(p + 1, attend, [(layer, 3), (layer, 2)])
        weight_grad(layer, 0, nrm, gp, 5 * BLOCK)
        leave(p + 1, 0)
        weight_grad(layer, 1, att, buf, 2 * BLOCK)
        phases[p + 1].near_stage(1)
        if layer > 0:
            for i in attn_part:
                load(layer - 1, i).start()
        relays = [(layer, 0), (layer, 1)]
    leave(PHASES - 1, 1)
    for key in relays:
        send_rest(*key)

    total = small_z[0]
    for copy, d in zip(to_z, range(1, levels)):
        copy.wait_recv()
        total = total + small_z[d]
    small_out[...] = total
    for copy in to_z:
        copy.wait_send()
    rows = w_q.shape[1]
    pad_rows = up16(rows)
    kinds = {0: 0, 2: 1, 4: 2}

    def cut_at(m, t):
        start = rows_at((t + PLANE * kinds[m]) * pad_rows, pad_rows)
        return wi.at[start, : stages[m].shape[1]]

    def pasted_at(layer, m, t):
        start = rows_at((slot(m, layer) * PLANE + t) * pad_rows, pad_rows)
        return {0: gl, 2: act, 4: wd}[m].at[start, : stages[m].shape[1]]

    def trade(layer, m, e):
        kind = kinds[m]
        return remote(
            cut_at(m, place.rank(e)), pasted_at(layer, m, place.rank()),
            trade_sems.at[0, layer, kind, e], trade_sems.at[1, layer, kind, e], place.other(e),
        )

    def traded(layer, m, e):
        there = pasted_at(layer, m, place.rank(e))
        return remote(
            there, there, trade_sems.at[0, layer, kinds[m], e],
            trade_sems.at[1, layer, kinds[m], e], place.other(e),
        )

    def own_trade(layer, m):
        own = place.rank()
        return pltpu.make_async_copy(
            cut_at(m, own), pasted_at(layer, m, own), trade_sems.at[0, layer, kinds[m], 0]
        )

    stayed = set()

    def wait_own_trade(layer, m):
        if (layer, m) not in stayed:
            own_trade(layer, m).wait()
            stayed.add((layer, m))

    def pasted(layer, m, t):
        return pasted_at(layer, m, t)[:rows, :].astype(F32)

    trades = place.trades(levels)

    def o_trade(layer):
        return remote(
            o_cut.at[layer], o_pasted.at[layer], o_sems.at[0, layer], o_sems.at[1, layer],
            place.indexed(place.held(levels)),
        )

    def o_local(layer):
        return pltpu.make_async_copy(o_cut.at[layer], o_pasted.at[layer], o_sems.at[0, layer])

    def finalize(layer, m):
        own = result(layer, m)
        if m == 3 or m > 4:
            total = own
        else:
            total = o_acc if m == 1 else acc.at[:, : own.shape[1]]
            total[...] = own[...].astype(F32)
        for delta in range(1, levels):
            def add(delta=delta):
                send(layer, m, delta).wait_recv()
                total[...] += arrivals[m][slot(m, layer), delta - 1].astype(F32)

            if relayed and delta != 2:
                source = (z + levels - delta) % levels
                pl.when(jnp.logical_not((z + source == 3) & (z * source == 0)))(add)
            else:
                add()
        if m > 3 or layer == 0:
            sent(layer, m)
        if m == 1:
            o_cut[layer] = total[...].astype(BF)
            pl.when(trades)(o_trade(layer).start)
            pl.when(jnp.logical_not(trades))(o_local(layer).start)
        elif m in kinds:
            if m < 4 and layer + 1 < LAYERS:
                wait_own_trade(layer + 1, m)
                for e in range(1, PLANE):
                    trade(layer + 1, m, e).wait_send()
            values = total[...].astype(BF).astype(F32)
            for t in range(PLANE):
                cut_at(m, t)[:rows, :] = values[t * rows : (t + 1) * rows].astype(BF)
            own_trade(layer, m).start()
            for e in range(1, PLANE):
                trade(layer, m, e).start()

    def wait_trade(layer, m):
        wait_own_trade(layer, m)
        for e in range(1, PLANE):
            traded(layer, m, e).wait_recv()
        if m > 3 or layer == 0:
            for e in range(1, PLANE):
                trade(layer, m, e).wait_send()

    span = w_q.shape[2] // 3 // PLANE
    ff_rows = w_in.shape[2] // PLANE // levels
    padded_rows = stages[2].shape[1] // levels

    def rows_out(layer, out):
        here = row_buf.at[:, : out.shape[2]]
        return pltpu.make_async_copy(here, out.at[layer], row_sem.at[0])

    on_the_way = []

    def write_rows(layer, parts, out, kind, w, gain_out):
        whole = jnp.concatenate(parts, axis=1)
        gain_out[layer] = jnp.sum(whole * w[layer].astype(F32), axis=1, keepdims=True)
        if on_the_way:
            on_the_way.pop().wait()
        row_buf[:, : out.shape[2]] = whole * gains[kind, layer]
        copy = rows_out(layer, out)
        copy.start()
        on_the_way.append(copy)

    def assemble(layer):
        wait_trade(layer, 0)
        ranks = [pasted(layer, 0, t) for t in range(PLANE)]
        parts = [rank[:, kind * span : (kind + 1) * span] for kind in range(3) for rank in ranks]
        write_rows(layer, parts, q_out, 0, w_q, q_gain)

    def assemble_mlp(layer):
        wait_trade(layer, 2)
        ranks = [pasted(layer, 2, t) for t in range(PLANE)]
        parts = [
            rank[:, zz * padded_rows : zz * padded_rows + ff_rows]
            for zz in range(levels) for rank in ranks
        ]
        write_rows(layer, parts, i_out, 1, w_in, i_gain)

    def assemble_out(layer):
        @pl.when(trades)
        def _():
            o_trade(layer).wait_recv()
            o_trade(layer).wait_send()

        pl.when(jnp.logical_not(trades))(o_local(layer).wait)
        o_out[layer] = o_pasted[layer, :rows, :].astype(F32)

    head_rows, head_share = out_out.shape[0], first_out.shape[1] // 4 // levels

    def assemble_head():
        wait_trade(last, 4)
        sums = []
        for q in range(4):
            sums.append(pasted(last, 4, 2 * q) + pasted(last, 4, 2 * q + 1))
        parts = []
        for zz in range(levels):
            for q in range(4):
                parts.append(sums[q][:, zz * head_rows : zz * head_rows + head_share])
        first_out[...] = jnp.concatenate(parts, axis=1)

    for key in [(last, 5), (last, 6), (last, 4)] + [(last, m) for m in (3, 2, 0, 1)]:
        finalize(*key)
    for layer in reversed(range(LAYERS - 1)):
        finalize(layer, 3)
        finalize(layer, 2)
    assemble_head()
    for layer in reversed(range(LAYERS - 1)):
        finalize(layer, 0)
        finalize(layer, 1)
    for layer in reversed(range(LAYERS)):
        assemble_mlp(layer)
        assemble(layer)
        assemble_out(layer)
    on_the_way.pop().wait()


def shape(*dims, dtype=BF):
    return jax.ShapeDtypeStruct(dims, dtype)


def rope_table():
    position = np.arange(2 * BLOCK) % ROW_LEN
    inverse = ROTARY_BASE ** (-np.arange(HALF) / HALF)
    angles = (position[:, None] * inverse[None, :]).astype(np.float32)
    table = np.zeros((2 * BLOCK, 2, 2, BLOCK // 2), np.float32)
    table[:, 0, :, :HALF] = np.cos(angles)[:, None]
    table[:, 1, 0, :HALF] = -np.sin(angles)
    table[:, 1, 1, :HALF] = np.sin(angles)
    return table.reshape(2 * BLOCK, 2 * BLOCK)


def lane_of(index):
    head, inside = divmod(index, HDIM)
    half, place = divmod(inside, HALF)
    return head * BLOCK + half * (BLOCK // 2) + place


def per_device(devices, x, segments, padded, w_qkv, w_out, w_in, w_down, gain_attn, gain_mlp,
               head_first, head_first_bias, head_final, head_bias, head_skip, adjoint):
    levels = devices // PLANE
    width = x.shape[1]
    ff = w_in.shape[2]
    columns = head_final.shape[1]
    tokens = PLANE * BLOCK
    heads = width // HDIM // PLANE
    span = heads * HDIM
    rows = width // devices
    out_rows = up16(rows)
    ff_rows = ff // devices
    down_rows = up16(ff_rows)
    head_share = 2 * width // devices
    head_rows = up16(head_share)
    used_cols, o_rows, f_cols = 3 * span, levels * out_rows, levels * down_rows
    h_cols = -(-levels * head_rows // 128) * 128
    q_cols = -(-used_cols // 128) * 128
    lanes = heads * BLOCK

    sel_q = np.zeros((q_cols, 3 * lanes), np.float32)
    sel_o = np.zeros((o_rows, lanes), np.float32)
    for e in range(span):
        for kind in range(3):
            sel_q[kind * span + e, kind * lanes + lane_of(e)] = 1
        sel_o[e // rows * out_rows + e % rows, lane_of(e)] = 1
    sel_q, sel_o = jnp.asarray(sel_q, BF), jnp.asarray(sel_o, BF)
    rope = jnp.asarray(rope_table())
    head_lanes = np.full((1, h_cols), -width, np.int32)
    for zz in range(levels):
        here = slice(zz * head_rows, zz * head_rows + head_share)
        head_lanes[0, here] = 4 * head_share * zz + np.arange(head_share)
    head_lanes = jnp.asarray(head_lanes)

    seg = segments.reshape(2, HALF_BLOCK)
    open_key = padded.reshape(2, HALF_BLOCK) == 0
    within = jnp.arange(HALF_BLOCK)
    static = within[:, None] // ROW_LEN == within[None, :] // ROW_LEN
    static = static & (within[None, :] <= within[:, None])
    allowed = static[None] & (seg[:, :, None] == seg[:, None, :])
    allowed = allowed & (open_key[:, None, :] | (within[:, None] == within[None, :])[None])
    core = lax.axis_index("wide") % 2
    side = jnp.arange(BLOCK)[None, None, :] // HALF_BLOCK == core
    own_mask = (jnp.concatenate([allowed, allowed], axis=-1) & side).astype(BF)

    gains = jnp.stack([gain_attn, gain_mlp]).astype(F32)[..., None]
    d_piece = w_down
    if down_rows != ff_rows:
        d_piece = jnp.pad(w_down, [(0, 0), (0, down_rows - ff_rows), (0, 0)])
    pad_rows = up16(rows)

    in_blocks = (2, 2, 2, 2, HALF_BLOCK)
    layer_shapes = [
        in_blocks + (width,), in_blocks + (width,), (tokens, 3 * lanes), (tokens, lanes), (tokens, o_rows),
        (tokens, f_cols), (tokens, f_cols),
    ]
    slab_shapes = [(width, q_cols), (o_rows, width), (width, f_cols), (f_cols, width)]
    outs = [
        shape(2 * BLOCK, columns), shape(BLOCK, width, dtype=F32),
        shape(LAYERS, BLOCK, width, dtype=F32), shape(LAYERS, BLOCK, width, dtype=F32),
    ]
    vmem_outs = len(outs)
    outs += [shape(LAYERS, *dims) for dims in layer_shapes]
    outs += [shape(*in_blocks, width)] + [shape(tokens, h_cols)] * 3 + [shape(tokens, columns)]
    outs += [shape(LAYERS, *dims) for dims in slab_shapes]
    (predictions, grad_final, xs, mid, nrm, nml, qkv, prb, att, gl, act, lines, hidden, gpre,
     picked, g, wq, wo, wi, wd) = pl.pallas_call(
        lambda *refs: forward_kernel(levels, *refs),
        out_shape=outs,
        in_specs=[VMEM] * 13 + [ANY] * 4,
        out_specs=[VMEM] * vmem_outs + [ANY] * (len(outs) - vmem_outs),
        scratch_shapes=exchange_scratch(width, PHASES + 1)
        + [pltpu.VMEM((LAYERS,) + dims, BF) for dims in layer_shapes[:2]]
        + [pltpu.VMEM(dims, BF) for dims in layer_shapes[2:]]
        + [pltpu.VMEM((LAYERS,) + dims, BF) for dims in slab_shapes]
        + [
            pltpu.VMEM((width, 3 * lanes), BF), pltpu.VMEM((width, width), BF),
            pltpu.VMEM((width, columns), BF), pltpu.VMEM((width, h_cols), BF),
            pltpu.VMEM((width, h_cols), BF), pltpu.VMEM((h_cols, columns), BF),
            pltpu.VMEM(in_blocks + (columns,), BF), pltpu.VMEM((tokens, columns), BF),
            pltpu.VMEM((tokens, h_cols), BF),
            pltpu.VMEM((tokens, h_cols), BF), pltpu.VMEM((tokens, h_cols), BF),
            pltpu.VMEM((2 * BLOCK, width), BF),
            pltpu.VMEM(in_blocks + (BLOCK,), BF),
            pltpu.VMEM((LAYERS, PLANE, pad_rows, q_cols + f_cols), BF),
            pltpu.VMEM((LAYERS, PLANE, pad_rows, q_cols + f_cols), BF),
            pltpu.VMEM((LAYERS, out_rows, width), BF),
            pltpu.VMEM((LAYERS, out_rows, width), BF),
            pltpu.SemaphoreType.DMA((3, LAYERS, 4, levels - 1)),
            pltpu.SemaphoreType.DMA((LAYERS, 4)),
            pltpu.SemaphoreType.DMA((32,)),
            pltpu.SemaphoreType.DMA((3,)),
            pltpu.SemaphoreType.DMA((2, 4)),
            pltpu.SemaphoreType.DMA((2, LAYERS, PLANE)),
            pltpu.SemaphoreType.DMA((2, PLANE)),
            pltpu.SemaphoreType.DMA((2,)),
        ],
        compiler_params=pltpu.CompilerParams(
            collective_id=1, has_side_effects=True, vmem_limit_bytes=62 * MIB
        ),
        name="decoder_forward",
    )(x, own_mask, rope, sel_q, sel_o, head_lanes,
      adjoint.reshape(2, 2, HALF_BLOCK, columns), head_first_bias[None], head_bias[None], gains,
      w_qkv, w_in, w_out, d_piece, head_first, head_final, head_skip)

    chunk = [PLANE * rows, out_rows, PLANE * rows, down_rows, PLANE * rows, head_rows, head_rows]
    cols = [q_cols, width, f_cols, width, h_cols, columns, columns]
    stage_rows = [levels * n for n in chunk[:5]] + [h_cols] * 2
    kept_shapes = [
        in_blocks + (width,), (tokens, f_cols), (tokens, f_cols), (width, f_cols), (f_cols, width),
        (LAYERS, BLOCK, width), in_blocks + (width,), (tokens, 3 * lanes), (tokens, lanes),
        (tokens, o_rows), (width, q_cols), (o_rows, width), (LAYERS, BLOCK, width),
    ]
    small_cols = columns + h_cols
    outs = [
        shape(BLOCK, width, dtype=F32), shape(8, small_cols, dtype=F32),
        shape(LAYERS, rows, 3 * width, dtype=F32), shape(LAYERS, rows, width, dtype=F32),
        shape(LAYERS, rows, ff, dtype=F32), shape(LAYERS, down_rows, width, dtype=F32),
        shape(LAYERS, rows, 1, dtype=F32), shape(LAYERS, rows, 1, dtype=F32),
        shape(rows, width, dtype=F32), shape(head_rows, columns, dtype=F32),
        shape(head_rows, columns, dtype=F32),
    ]
    (input_grad, small, q_grad, o_grad, i_grad, d_grad, q_gain, i_gain, g_first, g_out,
     g_skip) = pl.pallas_call(
        lambda *refs: backward_kernel(levels, *refs),
        out_shape=outs,
        in_specs=[VMEM] * 6 + [ANY] * 19,
        out_specs=[VMEM, VMEM, ANY, VMEM, ANY] + [VMEM] * (len(outs) - 5),
        scratch_shapes=exchange_scratch(width, PHASES)
        + [pltpu.VMEM((2,) + in_blocks + (width,), BF)]
        + [pltpu.VMEM(dims, F32 if dims[0] == LAYERS and dims[1] == BLOCK else BF) for dims in kept_shapes]
        + [pltpu.VMEM((tokens, q_cols), BF)]
        + [pltpu.VMEM((stage_rows[m], cols[m]), BF) for m in range(7)]
        + [
            pltpu.VMEM((LAYERS if m < 4 else 1, levels, chunk[m], cols[m]), BF)
            for m in range(7)
        ]
        + [
            pltpu.VMEM((LAYERS if m < 4 else 1, chunk[m], cols[m]), BF) for m in (0, 1, 2, 4)
        ]
        + [pltpu.VMEM((chunk[0], max(f_cols, q_cols)), F32), pltpu.VMEM((out_rows, width), F32)]
        + [pltpu.VMEM((LAYERS, out_rows, width), BF)] * 2
        + [
            pltpu.VMEM((2, 8, h_cols), F32), pltpu.VMEM((8, h_cols), F32),
            pltpu.VMEM((levels, 8, small_cols), F32),
            pltpu.VMEM((rows, max(ff, 3 * width)), F32),
            pltpu.SemaphoreType.DMA((2, LAYERS, 7, levels)),
            pltpu.SemaphoreType.DMA((20,)),
            pltpu.SemaphoreType.DMA((2, levels)),
            pltpu.SemaphoreType.DMA((2, LAYERS, 3, PLANE)),
            pltpu.SemaphoreType.DMA((2, LAYERS)),
            pltpu.SemaphoreType.DMA((1,)),
        ],
        compiler_params=pltpu.CompilerParams(
            collective_id=2, has_side_effects=True, vmem_limit_bytes=62 * MIB
        ),
        name="decoder_backward",
    )(rope, sel_q, sel_o, gains, w_qkv, w_in, grad_final, nml, act, gl, wi, wd, mid, nrm, qkv, prb,
      att, wq, wo, xs, lines, gpre, hidden.reshape(in_blocks + (h_cols,)),
      picked.reshape(in_blocks + (h_cols,)), g)

    z, narrow = lax.axis_index("wide") // 4, lax.axis_index("narrow")
    g_first_bias = lax.dynamic_slice(small[0], (columns + z * head_rows + narrow * rows,), (rows,))
    return (
        predictions, input_grad, q_grad, o_grad, i_grad, d_grad[:, :ff_rows], q_gain[..., 0],
        i_gain[..., 0], g_first, g_first_bias, g_out[:head_share], small[0, :columns],
        g_skip[:head_share],
    )


def solution(mesh):
    devices = mesh.shape["wide"] * mesh.shape["narrow"]
    both = ("wide", "narrow")
    weight, gain = P(None, both, None), P(None, both)
    return jax.shard_map(
        lambda *arrays: per_device(devices, *arrays),
        mesh=mesh,
        in_specs=(
            P(both, None), P(both), P(both), weight, weight, weight, weight, gain, gain, P(), P(),
            P(None, "narrow"), P("narrow"), P(None, "narrow"), P("wide", "narrow"),
        ),
        out_specs=(
            P("wide", "narrow"), P(both, None), weight, weight, weight, weight, gain, gain,
            P(both, None), P(both), P("wide", "narrow"), P("narrow"), P("wide", "narrow"),
        ),
        check_vma=False,
    )
```

```python
import math

import jax
import jax.numpy as jnp
import numpy as np
from jax import lax
from jax.experimental import pallas as pl
from jax.experimental.pallas import tpu as pltpu
from jax.sharding import PartitionSpec as P

HDIM = 80
HALF = HDIM // 2
LAYERS = 2
ROW_LEN = 16
BLOCK = 128
HALF_BLOCK = BLOCK // 2
PLANE = 8
PHASES = 2 * LAYERS
MESH = pl.DeviceIdType.MESH
BF = jnp.bfloat16
F32 = jnp.float32
EPS = 1e-06
ROTARY_BASE = 10000.0
MIB = 1024 * 1024
VMEM = pl.BlockSpec(memory_space=pltpu.VMEM)
ANY = pl.BlockSpec(memory_space=pl.ANY)


def up16(rows):
    return -(-rows // 16) * 16


def rows_at(start, count, step=16):
    return pl.ds(pl.multiple_of(start, step), count)


def dot(a, b, ca=1, cb=0):
    return lax.dot_general(a, b, (((ca,), (cb,)), ((), ())), preferred_element_type=F32)


class Place:
    def __init__(self):
        wide = lax.axis_index("wide")
        self.x = lax.axis_index("narrow")
        self.core = wide % 2
        self.y = (wide // 2) % 2
        self.z = wide // 4

    def device(self, z, y, core, x):
        return (z * 4 + y * 2 + core, x)

    def sibling(self):
        return self.device(self.z, self.y, 1 - self.core, self.x)

    def major(self, s, far=0):
        return (self.y + s * (self.x - self.y) + far) % 2

    def minor(self, s, near=0):
        return (self.x + s * (self.y - self.x) + near) % 2

    def near(self, s):
        return self.device(self.z, (self.y + s) % 2, self.core, (self.x + 1 - s) % 2)

    def far(self, s):
        return self.device(self.z, (self.y + 1 - s) % 2, self.core, (self.x + s) % 2)

    def level(self, z):
        return self.device(z, self.y, self.core, self.x)

    def turned(self, e):
        return (self.y + e // 4) % 2, (self.core + e // 2) % 2, (self.x + e) % 2

    def other(self, e):
        return self.device(self.z, *self.turned(e))

    def rank(self, e=0):
        y, core, x = self.turned(e)
        return 4 * y + 2 * core + x

    def indexed(self, index):
        return (index // 2, index % 2)

    def holder(self, levels):
        index = PLANE * self.z + self.rank()
        return index % levels * PLANE + index // levels

    def held(self, levels):
        return levels * self.rank() + self.z

    def trades(self, levels):
        return self.holder(levels) != PLANE * self.z + self.rank()


def greet(place, levels):
    barrier = pltpu.get_barrier_semaphore()
    others = [place.other(e) for e in range(1, PLANE)]
    others += [place.level((place.z + d) % levels) for d in range(1, levels)]
    for other in others:
        pl.semaphore_signal(barrier, inc=1, device_id=other, device_id_type=MESH)
    trades = place.trades(levels)

    @pl.when(trades)
    def _():
        for index in (place.holder(levels), place.held(levels)):
            pl.semaphore_signal(
                barrier, inc=1, device_id=place.indexed(index), device_id_type=MESH
            )
        pl.semaphore_wait(barrier, len(others) + 2)

    @pl.when(jnp.logical_not(trades))
    def _():
        pl.semaphore_wait(barrier, len(others))


def remote(src, dst, send, recv, device):
    return pltpu.make_async_remote_copy(
        src_ref=src, dst_ref=dst, send_sem=send, recv_sem=recv, device_id=device,
        device_id_type=MESH,
    )


class Exchange:
    def __init__(self, place, phase, buf, scratch):
        (self.part, self.recv_s, self.send_f, self.recv_f, self.send_n, self.recv_n, self.sems) = scratch
        self.place, self.phase, self.buf = place, phase, buf

    def copy(self, s, kind, src, dst, device):
        sems = self.sems
        return remote(
            src, dst, sems.at[self.phase, s, 0, kind], sems.at[self.phase, s, 1, kind], device
        )

    def block(self, s, far, near, core):
        place = self.place
        return self.buf.at[s, place.major(s, far), place.minor(s, near), core]

    def own(self, s):
        return (s, self.place.major(s), self.place.minor(s), self.place.core)

    def to_near(self, s, far=0, near=0):
        rows = self.block(s, far, near, self.place.core)
        return self.copy(s, 0, rows, rows, self.place.near(s))

    def to_far(self, s, far=0, near=0):
        rows = self.block(s, far, near, self.place.core)
        return self.copy(s, 1, rows, rows, self.place.far(s))

    def pass_far(self, s, far=0, near=1):
        rows = self.block(s, far, near, self.place.core)
        return self.copy(s, 2, rows, rows, self.place.far(s))

    def sibling(self, s, kind, core):
        if kind < 2:
            rows = self.block(s, 0, kind, core)
        else:
            rows = self.buf.at[s, self.place.major(s, 1), :, core]
        return self.copy(s, 3 + kind, rows, rows, self.place.sibling())

    def to_sibling(self, s, kind):
        return self.sibling(s, kind, self.place.core)

    def from_sibling(self, s, kind):
        return self.sibling(s, kind, 1 - self.place.core)

    def sum_sibling(self, s, half):
        src = self.part.at[s, half, :, 1 - self.place.core]
        sems = self.sems
        return remote(
            src, self.recv_s.at[s, half], sems.at[self.phase, s, 0, 6 + half],
            sems.at[self.phase, s, 1, 6 + half], self.place.sibling(),
        )

    def sum_far(self, s):
        return self.copy(s, 8, self.send_f.at[s], self.recv_f.at[s], self.place.far(s))

    def sum_near(self, s):
        return self.copy(s, 9, self.send_n.at[s], self.recv_n.at[s], self.place.near(s))

    def start(self, s):
        self.to_near(s).start()
        self.to_far(s).start()
        self.to_sibling(s, 0).start()

    def far_stage(self, s):
        self.sum_sibling(s, 1).wait_recv()
        own = self.part[s, 1, :, self.place.core].astype(F32)
        self.send_f[s] = (own + self.recv_s[s, 1].astype(F32)).astype(BF)
        self.sum_far(s).start()

    def summed(self, s, minor):
        own = self.part[s, 0, minor, self.place.core].astype(F32)
        return own + self.recv_s[s, 0, minor].astype(F32) + self.recv_f[s, minor].astype(F32)

    def near_stage(self, s):
        self.sum_sibling(s, 0).wait_recv()
        self.sum_far(s).wait_recv()
        self.send_n[s] = self.summed(s, self.place.minor(s, 1)).astype(BF)
        self.sum_near(s).start()

    def total(self, s):
        self.sum_near(s).wait_recv()
        total = self.summed(s, self.place.minor(s)) + self.recv_n[s].astype(F32)
        self.to_near(s).wait_send()
        self.to_far(s).wait_send()
        self.pass_far(s).wait_send()
        for kind in range(3):
            self.to_sibling(s, kind).wait_send()
        for half in range(2):
            self.sum_sibling(s, half).wait_send()
        self.sum_far(s).wait_send()
        self.sum_near(s).wait_send()
        return total

    def take_near(self, s):
        self.to_near(s, 0, 1).wait_recv()
        self.pass_far(s).start()
        self.to_sibling(s, 1).start()

    def take_far(self, s):
        self.to_far(s, 1, 0).wait_recv()
        self.pass_far(s, 1, 1).wait_recv()
        self.to_sibling(s, 2).start()

    def take_sibling(self, s):
        for kind in range(3):
            self.from_sibling(s, kind).wait_recv()

    def run(self, compute, hooks, taken=False):
        def body(i, carry):
            s, half = i // 2, i % 2
            if not taken:
                pl.when(half == 0)(lambda: self.take_near(s))

            for at, hook in hooks:
                pl.when(i == at)(hook)

            if not taken:
                @pl.when(half == 0)
                def _():
                    self.from_sibling(s, 0).wait_recv()
                    self.from_sibling(s, 1).wait_recv()

                pl.when(half == 1)(lambda: self.take_far(s))

            @pl.when(i == 2)
            def _():
                self.far_stage(0)

            @pl.when(i == 3)
            def _():
                self.near_stage(0)

            if not taken:
                pl.when(half == 1)(lambda: self.from_sibling(s, 2).wait_recv())

            major = self.place.major(s, half)
            compute(s * 8 * HALF_BLOCK + major * 4 * HALF_BLOCK, s, half, major)
            self.sum_sibling(s, half).start()
            return carry

        lax.fori_loop(0, 4, body, 0)
        self.far_stage(1)


def exchange_scratch(width, phases):
    return [
        pltpu.VMEM((2, 2, 2, 2, HALF_BLOCK, width), BF),
        pltpu.VMEM((2, 2, 2, HALF_BLOCK, width), BF),
        pltpu.VMEM((2, 2, HALF_BLOCK, width), BF),
        pltpu.VMEM((2, 2, HALF_BLOCK, width), BF),
        pltpu.VMEM((2, HALF_BLOCK, width), BF),
        pltpu.VMEM((2, HALF_BLOCK, width), BF),
        pltpu.SemaphoreType.DMA((phases, 2, 2, 10)),
    ]


def flat(ref, columns=slice(None)):
    if len(ref.shape) == 2:
        return ref[:, columns]
    values = ref[(slice(None),) * 5 + (columns,)]
    return values.reshape(-1, values.shape[-1])


def write_part(part, s, half, values, w, contracted):
    width = part.shape[-1]
    step = width // 2
    for n in range(0, width, step):
        columns = slice(n, n + step)
        side = w[:, columns] if contracted == 0 else w[columns, :]
        part[s, half, :, :, :, columns] = blocked(dot(values, side, 1, contracted).astype(BF))


def blocked(values):
    return values.reshape(2, 2, HALF_BLOCK, values.shape[-1])


def root(values):
    return lax.rsqrt(jnp.mean(values * values, axis=-1, keepdims=True) + EPS)


def forward_kernel(levels, *refs):
    (x_in, own_mask, rope, sel_q, sel_o, head_lanes, adjoint, bias_first, bias_last) = refs[:9]
    (gains, w_q, w_in, w_out) = refs[9:13]
    w_down, head_weights = refs[13], refs[14:17]
    (predictions, grad_out, xs, mid) = refs[17:21]
    kept, (slab_q, slab_o, slab_i, slab_d) = refs[21:33], refs[33:37]
    exchange = refs[37:44]
    (nrm, nml, qkv, prb, att, gl, act) = refs[44:51]
    slabs = refs[51:55]
    (wide_q, first, final, pick, first_q, final_q) = refs[55:61]
    (g, g_rows, hidden, gpre, picked, hidden_all) = refs[61:67]
    (mask, cut, pasted, o_cut, o_piece) = refs[67:72]
    (z_sems, own_sems, keep_sems, load_sems, g_sems, trade_sems, mask_sems, o_sems) = refs[72:]
    slab_outs = (slab_q, slab_o, slab_i, slab_d)
    place = Place()
    z = place.z
    heads = sel_o.shape[1] // BLOCK
    lanes = heads * BLOCK
    kept_here, waited = [], []

    def keep(src, dst):
        copy = pltpu.make_async_copy(src, dst, keep_sems.at[len(kept_here)])
        copy.start()
        kept_here.append(copy)
        return copy

    def forget(copy):
        copy.wait()
        waited.append(copy)

    relayed = levels == 4

    def far(delta):
        there = (z + delta) % levels
        return (z + there == 3) & (z * there == 0)

    counts = [slabs[0].shape[1] // levels, o_piece.shape[1], slabs[2].shape[1] // levels,
              w_down.shape[1]]

    def rows_of(m, level):
        return rows_at(level * counts[m], counts[m])

    def piece(layer, m):
        if m == 1:
            return o_piece.at[layer]
        if m == 3:
            return w_down.at[layer]
        return slabs[m].at[layer, rows_of(m, z)]

    def spread(layer, m, delta):
        return remote(
            piece(layer, m), slabs[m].at[layer, rows_of(m, z)],
            z_sems.at[0, layer, m, delta - 1], z_sems.at[1, layer, m, delta - 1],
            place.level((z + delta) % levels),
        )

    def arriving(layer, m, delta):
        rows = slabs[m].at[layer, rows_of(m, (z + levels - delta) % levels)]
        return remote(
            rows, rows, z_sems.at[0, layer, m, delta - 1], z_sems.at[1, layer, m, delta - 1],
            place.level((z + delta) % levels),
        )

    def relay(layer, m):
        rows = slabs[m].at[layer, rows_of(m, (z + 2) % levels)]
        return remote(
            rows, rows, z_sems.at[2, layer, m, 0], z_sems.at[1, layer, m, 2 * (z - 1)],
            place.level(3 * (z - 1)),
        )

    def for_spread(layer, m, act_on):
        for delta in range(1, levels):
            if relayed and delta != 2:
                @pl.when(jnp.logical_not(far(delta)))
                def _(delta=delta):
                    act_on(spread(layer, m, delta))
            else:
                act_on(spread(layer, m, delta))

    def own_piece(layer, m):
        return pltpu.make_async_copy(
            piece(layer, m), slabs[m].at[layer, rows_of(m, z)], own_sems.at[layer, m]
        )

    def send_weights(layer, m):
        if m % 2:
            own_piece(layer, m).start()
        for_spread(layer, m, lambda copy: copy.start())

    rows, q_cols = w_q.shape[1], slabs[0].shape[2]
    span = w_q.shape[2] // 3 // PLANE
    ff_rows = w_in.shape[2] // PLANE // levels
    padded = slabs[2].shape[2] // levels - ff_rows

    def cut_weights(layer):
        scaled_q = w_q[layer].astype(F32) * gains[0, layer]
        scaled_i = w_in[layer].astype(F32) * gains[1, layer]
        for t in range(PLANE):
            parts = []
            for kind in range(3):
                low = (kind * PLANE + t) * span
                parts.append(scaled_q[:, low : low + span])
            if q_cols > 3 * span:
                parts.append(jnp.zeros((rows, q_cols - 3 * span), F32))
            cut[layer, t, :rows, :q_cols] = jnp.concatenate(parts, axis=1).astype(BF)
            parts = []
            for zz in range(levels):
                low = (zz * PLANE + t) * ff_rows
                parts.append(scaled_i[:, low : low + ff_rows])
                if padded:
                    parts.append(jnp.zeros((rows, padded), F32))
            cut[layer, t, :rows, q_cols:] = jnp.concatenate(parts, axis=1).astype(BF)

    def trade(layer, e):
        return remote(
            cut.at[layer, place.rank(e)], pasted.at[layer, place.rank()],
            trade_sems.at[0, layer, e], trade_sems.at[1, layer, e], place.other(e),
        )

    def traded(layer, e):
        there = pasted.at[layer, place.rank(e)]
        return remote(
            there, there, trade_sems.at[0, layer, e], trade_sems.at[1, layer, e], place.other(e)
        )

    def start_trade(layer):
        for e in range(1, PLANE):
            trade(layer, e).start()
        own = place.rank()
        pltpu.make_async_copy(
            cut.at[layer, own], pasted.at[layer, own], trade_sems.at[0, layer, 0]
        ).start()

    def end_trade(layer):
        own = place.rank()
        pltpu.make_async_copy(
            cut.at[layer, own], pasted.at[layer, own], trade_sems.at[0, layer, 0]
        ).wait()
        for e in range(1, PLANE):
            traded(layer, e).wait_recv()
        for e in range(1, PLANE):
            trade(layer, e).wait_send()
        for m, low in ((0, 0), (2, q_cols)):
            width = slabs[m].shape[2]
            whole = [pasted[layer, t, :rows, low : low + width].astype(F32) for t in range(PLANE)]
            slabs[m][layer, rows_of(m, z), :] = jnp.concatenate(whole, axis=0).astype(BF)

    trades = place.trades(levels)
    o_trade = remote(
        o_cut, o_piece, o_sems.at[0], o_sems.at[1], place.indexed(place.holder(levels))
    )
    o_local = pltpu.make_async_copy(o_cut, o_piece, o_sems.at[0])

    def mask_to(e):
        there = mask.at[place.y, place.x, :, place.core]
        return remote(own_mask, there, mask_sems.at[0, e], mask_sems.at[1, e], place.other(e))

    def mask_from(e):
        y, core, x = place.turned(e)
        there = mask.at[y, x, :, core]
        return remote(there, there, mask_sems.at[0, e], mask_sems.at[1, e], place.other(e))

    mask_local = pltpu.make_async_copy(
        own_mask, mask.at[place.y, place.x, :, place.core], mask_sems.at[0, 0]
    )

    middle = (z == 1) | (z == 2)

    def relay_on(layer, m):
        if relayed:
            @pl.when(middle)
            def _():
                arriving(layer, m, 2).wait_recv()
                relay(layer, m).start()

    def weights_here(layer, m):
        for delta in range(1, levels):
            if relayed and delta == 2:
                pl.when(jnp.logical_not(middle))(arriving(layer, m, delta).wait_recv)
            else:
                arriving(layer, m, delta).wait_recv()
        for_spread(layer, m, lambda copy: copy.wait_send())
        if m % 2:
            own_piece(layer, m).wait()
        if relayed:
            pl.when(middle)(relay(layer, m).wait_send)

        return keep(slabs[m].at[layer], slab_outs[m].at[layer])

    skip = slabs[2].at[0, :, : adjoint.shape[3]]
    loads = [
        pltpu.make_async_copy(src, dst, load_sems.at[i])
        for i, (src, dst) in enumerate(zip(head_weights, (first, final, skip)))
    ]
    loads[0].start()
    loads[1].start()
    greet(place, levels)

    g_own = g.at[place.y, :, :, place.core]
    g_far = g.at[1 - place.y, :, :, place.core]
    g_local = pltpu.make_async_copy(adjoint, g_own, g_sems.at[0, 0])
    g_peer = remote(adjoint, g_own, g_sems.at[0, 1], g_sems.at[1, 1], place.far(0))
    g_sibling = remote(adjoint, g_own, g_sems.at[0, 2], g_sems.at[1, 2], place.sibling())
    g_pass = remote(g_far, g_far, g_sems.at[0, 3], g_sems.at[1, 3], place.sibling())
    part = exchange[0]
    lines = nrm.at[0]
    bufs = [nrm.at[0], nml.at[0], nrm.at[1], nml.at[1], lines]
    phases = [Exchange(place, p, buf, exchange) for p, buf in enumerate(bufs)]

    def own_half(s):
        return slice(s * HALF_BLOCK, (s + 1) * HALF_BLOCK)

    def chip_of(s, major, minor):
        return (major + s * (minor - major), minor + s * (major - minor))

    def enter(p, s, values):
        if p < 2 * LAYERS:
            values = values * root(values)
        bufs[p][phases[p].own(s)] = values.astype(BF)
        phases[p].start(s)

    def leave(p, s):
        rows = own_half(s)
        total = phases[p].total(s)
        if p == 2 * LAYERS:
            grad_out[rows, :] = total
            return
        layer = p // 2
        if p % 2 == 0:
            values = xs[layer, rows, :] + total
            mid[layer, rows, :] = values
        else:
            values = mid[layer, rows, :] + total
            if layer + 1 < LAYERS:
                xs[layer + 1, rows, :] = values
        enter(p + 1, s, values)

    def run(p, compute, next_weights, more=()):
        more = list(more)
        hooks = [(1, lambda: leave(p - 1, 1))] if p else []
        hooks += [(2, lambda key=key: relay_on(*key)) for key in next_weights]
        phases[p].run(compute, hooks + more)
        leave(p, 0)
        phases[p].near_stage(1)

    o_cut[...] = jnp.zeros(o_cut.shape, BF)
    for layer in range(LAYERS):
        o_cut[layer, :rows, :] = w_out[layer]
    pl.when(trades)(o_trade.start)
    pl.when(jnp.logical_not(trades))(o_local.start)
    cut_weights(0)
    start_trade(0)
    cut_weights(1)
    end_trade(0)
    send_weights(0, 0)
    xs[0] = x_in[...].astype(F32)
    for s in range(2):
        enter(0, s, xs[0, own_half(s), :])
    mask_local.start()
    for e in range(1, PLANE):
        mask_to(e).start()

    @pl.when(trades)
    def _():
        o_trade.wait_recv()
        o_trade.wait_send()

    pl.when(jnp.logical_not(trades))(o_local.wait)
    send_weights(0, 1)
    start_trade(1)
    for copy in (g_local, g_peer, g_sibling):
        copy.start()
    mask_local.wait()
    for e in range(1, PLANE):
        mask_from(e).wait_recv()
        mask_to(e).wait_send()
    relay_on(0, 0)
    relay_on(0, 1)

    def second_layer():
        end_trade(1)
        send_weights(1, 0)
        send_weights(1, 1)

    slab_keeps = []
    for layer in range(LAYERS):
        wq, wo, wi, wd = [slab.at[layer] for slab in slabs]
        slab_keeps.append(weights_here(layer, 0))
        if layer == 0:
            send_weights(0, 2)
            send_weights(0, 3)
        for n in range(0, wide_q.shape[0], 256):
            wide_q[n : n + 256, :] = dot(wq[n : n + 256, :], sel_q[...]).astype(BF)
        slab_keeps.append(weights_here(layer, 1))
        if layer:
            for copy in attn_saved:
                forget(copy)

        def attend(start, s, half, major, layer=layer, wo=wo):
            both = rows_at(start, 2 * BLOCK, 2 * BLOCK)
            projected = dot(nrm[layer, s, major].reshape(2 * BLOCK, nrm.shape[-1]), wide_q[...])
            cosine, sine = rope[:, :BLOCK], rope[:, BLOCK:]
            allowed = [
                mask[chip_of(s, major, block) + (s,)].reshape(BLOCK, BLOCK) > 0 for block in range(2)
            ]
            units = [(block, h) for block in range(2) for h in range(heads)]
            turned = []
            for low in range(0, 2 * lanes, BLOCK):
                value = projected[:, low : low + BLOCK]
                value = value * cosine + pltpu.roll(value, BLOCK // 2, 1) * sine
                turned.append(value.astype(BF))
            values = projected[:, 2 * lanes :].astype(BF)

            def rows_in(array, block):
                return array[block * BLOCK : (block + 1) * BLOCK]

            scores = [
                dot(rows_in(turned[h], block), rows_in(turned[heads + h], block), 1, 1)
                for block, h in units
            ]
            scores = [
                jnp.where(allowed[block], score * (1.0 / math.sqrt(HDIM)), -1e30)
                for (block, h), score in zip(units, scores)
            ]
            tops = [jnp.max(score, axis=-1, keepdims=True) for score in scores]
            scores = [jnp.exp(score - top) for score, top in zip(scores, tops)]
            sums = [jnp.sum(score, axis=-1, keepdims=True) for score in scores]
            probs = [(score / total).astype(BF) for score, total in zip(scores, sums)]
            outs = [
                dot(prob, rows_in(values, block)[:, h * BLOCK : (h + 1) * BLOCK]).astype(BF)
                for (block, h), prob in zip(units, probs)
            ]

            def joined(parts):
                side = [
                    jnp.concatenate(parts[block * heads : (block + 1) * heads], axis=1)
                    for block in range(2)
                ]
                return jnp.concatenate(side, axis=0)

            attended = dot(joined(outs), sel_o[...], 1, 1).astype(BF)
            write_part(part, s, half, attended, wo, 0)
            att[both, :] = attended
            prb[both, :] = joined(probs)
            qkv[both, :] = jnp.concatenate(turned + [values], axis=1)

        more = [(1, second_layer)] if layer == 0 else []
        run(2 * layer, attend, ((layer, 2), (layer, 3)), more)
        attn_saved = [keep(src, dst.at[layer]) for src, dst in zip((qkv, prb, att), kept[2:5])]
        nrm_saved = keep(nrm.at[layer], kept[0].at[layer])
        if layer == 0:
            g_peer.wait_recv()
            g_pass.start()
        ending = layer + 1 == LAYERS
        slab_keeps.append(weights_here(layer, 2))
        if layer:
            for copy in mlp_saved:
                forget(copy)
        slab_keeps.append(weights_here(layer, 3))
        if not ending:
            for m in (2, 3):
                send_weights(layer + 1, m)

        def lift(start, s, major, layer=layer, wi=wi):
            rows = rows_at(start, 2 * BLOCK, 2 * BLOCK)
            lifted = dot(nml[layer, s, major].reshape(2 * BLOCK, nml.shape[-1]), wi[...])
            root_two = math.sqrt(2.0 / math.pi)
            square = lifted * lifted
            tanh = jnp.tanh(root_two * lifted * (1.0 + 0.044715 * square))
            activated = (0.5 * lifted * (1.0 + tanh)).astype(BF)
            act[rows, :] = activated
            slope = 0.5 * (1.0 + tanh) + 0.5 * lifted * (1.0 - tanh * tanh) * root_two * (
                1.0 + 3.0 * 0.044715 * square
            )
            gl[rows, :] = slope.astype(BF)
            return activated

        def perceptron(start, s, half, major, lift=lift, wd=wd):
            write_part(part, s, half, lift(start, s, major), wd, 0)

        following = () if ending else ((layer + 1, 0), (layer + 1, 1))
        run(2 * layer + 1, perceptron, following)
        mlp_saved = [keep(src, dst.at[layer]) for src, dst in zip((gl, act), kept[5:7])]
        keep(nml.at[layer], kept[1].at[layer])
        if layer == 0:
            forget(nrm_saved)
            forget(slab_keeps[2])
            loads[2].start()
            loads[0].wait()
            loads[1].wait()
            index = lax.broadcasted_iota(jnp.int32, pick.shape, 0)
            offset = (2 * place.y + place.core) * (pick.shape[0] // (4 * levels))
            pick[...] = jnp.where(index - offset == head_lanes[...], 1.0, 0.0).astype(BF)
            for n in range(0, first.shape[0], 256):
                first_q[n : n + 256, :] = dot(first[n : n + 256, :], pick[...]).astype(BF)
            final_q[...] = dot(pick[...], final[...], 0, 0).astype(BF)

    g_local.wait()
    for copy in (g_sibling, g_pass):
        copy.wait_recv()
    loads[2].wait()
    bias_q = dot(jnp.broadcast_to(bias_first[...], (16, bias_first.shape[1])), pick[...])[:1]
    columns = g.shape[-1]

    def head(start, s, half, major):
        rows = rows_at(start, 2 * BLOCK, 2 * BLOCK)
        pre = dot(lines[s, major].reshape(2 * BLOCK, lines.shape[-1]), first_q[...]) + bias_q
        gate = 1.0 / (1.0 + jnp.exp(-pre))
        hidden[rows, :] = (pre * gate).astype(BF)
        for block in range(2):
            here = rows_at(start + block * BLOCK, BLOCK, BLOCK)
            g_rows[here, :] = g[chip_of(s, major, block) + (s,)].reshape(BLOCK, columns)
        there = g_rows[rows, :]
        grad_hidden = dot(there, final_q[...], 1, 1)
        gpre[rows, :] = (grad_hidden * (gate * (1.0 + pre * (1.0 - gate)))).astype(BF)
        row = lax.broadcasted_iota(jnp.int32, (2 * BLOCK, 1), 0)
        y = major + s * (row // BLOCK - major)
        mine = (row // HALF_BLOCK % 2 == place.core) & (y == place.y)
        mine = jnp.where(mine, there.astype(F32), 0.0).astype(BF)
        whole = dot(gpre[rows, :], first_q[...], 1, 1) + dot(mine, skip[...], 1, 1)
        part[s, half] = blocked(whole.astype(BF))

    p = 2 * LAYERS
    phases[p].run(head, [(1, lambda: leave(p - 1, 1))])

    keep(lines, kept[7])
    keep(hidden, kept[8])
    keep(gpre, kept[9])
    keep(g_rows, kept[11])
    for s in range(2):
        for major in range(2):
            n = (2 * s + major) * 2 * BLOCK
            rows = lines[s, major].reshape(2 * BLOCK, lines.shape[-1])
            picked[n : n + 2 * BLOCK, :] = dot(rows, pick[...]).astype(BF)
    keep(picked, kept[10])
    phases[p].near_stage(1)
    mine = []
    for x in range(2):
        mine += [lines[0, place.y, x, place.core], lines[1, x, place.y, place.core]]
    mine = jnp.concatenate(mine, axis=0)
    pre = dot(mine, first[...]) + bias_first[...].astype(F32)
    hidden_all[...] = (pre / (1.0 + jnp.exp(-pre))).astype(BF)
    out = dot(hidden_all[...], final[...]) + bias_last[...].astype(F32)
    predictions[...] = (out + dot(mine, skip[...])).astype(BF)
    leave(p, 0)
    leave(p, 1)
    for copy in (g_peer, g_sibling, g_pass):
        copy.wait_send()
    for copy in kept_here:
        if not any(copy is other for other in waited):
            copy.wait()


def norm_back(values, q):
    scale = root(values)
    n = values * scale
    return scale * (q - n * jnp.mean(q * n, axis=-1, keepdims=True))


def backward_kernel(levels, *refs):
    (rope, sel_q, sel_o, gains, w_q, w_in) = refs[:6]
    dy_in, stored, head_stored = refs[6], refs[7:20], refs[20:25]
    (dx_out, small_out, q_out, o_out, i_out, d_out, q_gain, i_gain) = refs[25:33]
    (first_out, out_out, skip_out) = refs[33:36]
    exchange, ag = refs[36:43], refs[43]
    loaded, gp = refs[44:57], refs[57]
    stages, arrivals = refs[58:65], refs[65:72]
    own_sums, acc, o_acc = refs[72:76], refs[76], refs[77]
    o_cut, o_pasted = refs[78], refs[79]
    (small_own, small_x, small_z) = refs[80:83]
    row_buf = refs[83]
    z_sems, load_sems, small_sems, trade_sems, o_sems, row_sem = refs[84:]
    (nml, act, gl, wi, wd, mid, nrm, qkv, prb, att, wq, wo, xs) = loaded
    part = exchange[0]
    place = Place()
    z = place.z
    heads = sel_o.shape[1] // BLOCK
    lanes = heads * BLOCK

    def load(layer, i):
        return pltpu.make_async_copy(stored[i].at[layer], loaded[i], load_sems.at[i])

    lines = ag.at[1]
    h_cols, half_width = small_own.shape[2], nrm.shape[-1] // 2
    gpre, hidden = gp.at[:, :h_cols], nrm.at[:, :, :, :, :, :h_cols]
    picked = nrm.at[:, :, :, :, :, half_width : half_width + h_cols]
    g = qkv.at[:, : stages[5].shape[1]]
    head_loads = [
        pltpu.make_async_copy(src, dst, load_sems.at[len(loaded) + i])
        for i, (src, dst) in enumerate(zip(head_stored, (lines, gpre, hidden, picked, g)))
    ]
    mlp_part, attn_part = range(5), range(6, 12)
    norm_loads = [pltpu.make_async_copy(stored[i], loaded[i], load_sems.at[i]) for i in (5, 12)]
    for copy in norm_loads:
        copy.start()
    dy_load = pltpu.make_async_copy(dy_in, dx_out, load_sems.at[len(loaded) + 5])
    dy_load.start()
    for copy in head_loads:
        copy.start()
    for i in mlp_part:
        load(LAYERS - 1, i).start()
    greet(place, levels)

    def count_of(m):
        return arrivals[m].shape[2]

    def slot(m, layer):
        return layer if m < 4 else 0

    relayed = levels == 4
    middle = (z == 1) | (z == 2)

    def send(layer, m, delta):
        there = (z + delta) % levels
        return remote(
            stages[m].at[rows_at(there * count_of(m), count_of(m))],
            arrivals[m].at[slot(m, layer), delta - 1],
            z_sems.at[0, layer, m, delta - 1],
            z_sems.at[1, layer, m, delta - 1],
            place.level(there),
        )

    def far(delta):
        there = (z + delta) % levels
        return (z + there == 3) & (z * there == 0)

    def hand(layer, m, delta):
        there = (z + delta) % levels
        return remote(
            stages[m].at[rows_at(there * count_of(m), count_of(m))],
            arrivals[m].at[slot(m, layer), levels - 1],
            z_sems.at[0, layer, m, delta - 1],
            z_sems.at[1, layer, m, levels - 1],
            place.level(1 + z // 3),
        )

    def send_first(layer, m):
        for delta in range(1, levels):
            if not relayed:
                send(layer, m, delta).start()
            elif delta == 2:
                pl.when(jnp.logical_not(middle))(send(layer, m, delta).start)
            else:
                pl.when(far(delta))(hand(layer, m, delta).start)
                pl.when(jnp.logical_not(far(delta)))(send(layer, m, delta).start)

    def send_rest(layer, m):
        if relayed:
            @pl.when(middle)
            def _():
                hand(layer, m, 1).wait_recv()
                rows = rows_at((z + 2) % levels * count_of(m), count_of(m))
                total = stages[m][rows, :].astype(F32)
                total = total + arrivals[m][slot(m, layer), levels - 1].astype(F32)
                stages[m][rows, :] = total.astype(BF)
                send(layer, m, 2).start()

    def sent(layer, m):
        for delta in range(1, levels):
            send(layer, m, delta).wait_send()

    def result(layer, m):
        if m > 4:
            return (out_out, skip_out)[m - 5]
        if m == 3:
            return d_out.at[layer]
        return own_sums[min(m, 3)].at[slot(m, layer)]

    def weight_grad(layer, m, left, right, tile):
        width = left.shape[-1]
        if m < 4 and layer + 1 < LAYERS:
            sent(layer + 1, m)
        for low in range(0, width, tile):
            here = slice(low, min(low + tile, width))
            stages[m][here, :] = dot(flat(left, here), flat(right), 0, 0).astype(BF)
        send_first(layer, m)
        out = result(layer, m)
        out[...] = stages[m][rows_at(z * count_of(m), count_of(m)), :].astype(out.dtype)

    bufs = [ag.at[p % 2] for p in range(PHASES)]
    phases = [Exchange(place, p, buf, exchange) for p, buf in enumerate(bufs)]

    def own_half(s):
        return slice(s * HALF_BLOCK, (s + 1) * HALF_BLOCK)

    def enter(p, s):
        bufs[p][phases[p].own(s)] = dx_out[own_half(s), :].astype(BF)
        phases[p].start(s)

    def leave(p, s):
        rows = own_half(s)
        values = (mid if p % 2 == 0 else xs)[LAYERS - 1 - p // 2, rows, :]
        dx_out[rows, :] += norm_back(values, phases[p].total(s))
        if p + 1 < PHASES:
            enter(p + 1, s)

    def run(p, compute, relays):
        hooks = [(1, lambda: leave(p - 1, 1))] if p else []
        hooks += [(2, lambda key=key: send_rest(*key)) for key in relays]
        phases[p].run(compute, hooks)

    dy_load.wait()
    for copy in norm_loads:
        copy.wait()
    for s in range(2):
        enter(0, s)

    for copy in head_loads:
        copy.wait()
    last = LAYERS - 1
    bias_sum = jnp.sum(gpre[...].astype(F32), axis=0, keepdims=True)
    small_own[1] = jnp.broadcast_to(bias_sum, small_own.shape[1:])
    to_x = remote(
        small_own.at[1], small_x, small_sems.at[0, 0], small_sems.at[1, 0], place.near(0)
    )
    to_x.start()
    weight_grad(last, 5, hidden, g, 4 * BLOCK)
    weight_grad(last, 6, picked, g, 4 * BLOCK)
    weight_grad(last, 4, lines, gpre, 5 * BLOCK)
    g_sum = jnp.sum(g[...].astype(F32), axis=0, keepdims=True)
    to_x.wait()
    small_z[0, :, : g_sum.shape[1]] = jnp.broadcast_to(g_sum, (8, g_sum.shape[1]))
    small_z[0, :, g_sum.shape[1] :] = small_own[1] + small_x[...]
    to_z = [
        remote(
            small_z.at[0], small_z.at[d], small_sems.at[0, d], small_sems.at[1, d],
            place.level((z + d) % levels),
        )
        for d in range(1, levels)
    ]
    for copy in to_z:
        copy.start()
    for i in attn_part:
        load(last, i).start()

    relays = [(last, 5), (last, 6), (last, 4)]
    for layer in reversed(range(LAYERS)):
        p = 2 * (LAYERS - 1 - layer)
        buf = bufs[p]
        for i in mlp_part:
            load(layer, i).wait()

        def perceptron(start, s, half, major, buf=buf):
            rows = rows_at(start, 2 * BLOCK, 2 * BLOCK)
            grad_act = dot(buf[s, major].reshape(2 * BLOCK, buf.shape[-1]), wd[...], 1, 1)
            grad_lift = (grad_act * gl[rows, :].astype(F32)).astype(BF)
            write_part(part, s, half, grad_lift, wi, 1)
            gl[rows, :] = grad_lift

        run(p, perceptron, relays)
        weight_grad(layer, 3, act, buf, 2 * BLOCK)
        leave(p, 0)
        weight_grad(layer, 2, nml, gl, 5 * BLOCK)
        phases[p].near_stage(1)
        if layer > 0:
            for i in mlp_part:
                load(layer - 1, i).start()
        for i in attn_part:
            load(layer, i).wait()
        buf = bufs[p + 1]

        def attend(start, s, half, major, buf=buf):
            cosine, sine = rope[:, :BLOCK], rope[:, BLOCK:]
            both = rows_at(start, 2 * BLOCK, 2 * BLOCK)
            there = buf[s, major].reshape(2 * BLOCK, buf.shape[-1])
            grad_heads = dot(there, wo[...], 1, 1).astype(BF)
            grad_heads = dot(grad_heads, sel_o[...]).astype(BF)
            kept, probs = qkv[both, :], prb[both, :]
            units = [(block, h) for block in range(2) for h in range(heads)]

            def unit(array, block, h, kind=0):
                low = kind * lanes + h * BLOCK
                return array[block * BLOCK : (block + 1) * BLOCK, low : low + BLOCK]

            queries, keys, values = [[unit(kept, *u, kind) for u in units] for kind in range(3)]
            probs = [unit(probs, *u) for u in units]
            grads = [unit(grad_heads, *u) for u in units]
            grad_probs = [dot(grad, value, 1, 1) for grad, value in zip(grads, values)]
            grad_values = [dot(prob, grad, 0, 0).astype(BF) for prob, grad in zip(probs, grads)]
            wide = [prob.astype(F32) for prob in probs]
            inner = [
                jnp.sum(prob * grad, axis=-1, keepdims=True) for prob, grad in zip(wide, grad_probs)
            ]
            grad_scores = [
                (prob * (grad - total)).astype(BF)
                for prob, grad, total in zip(wide, grad_probs, inner)
            ]
            grad_queries = [dot(grad, key) for grad, key in zip(grad_scores, keys)]
            grad_keys = [dot(grad, query, 0, 0) for grad, query in zip(grad_scores, queries)]
            packed = []
            for parts in (grad_queries, grad_keys):
                for h in range(heads):
                    turned = jnp.concatenate([parts[h], parts[heads + h]], axis=0)
                    turned = turned * (1.0 / math.sqrt(HDIM))
                    turned = turned * cosine - pltpu.roll(turned, BLOCK // 2, 1) * sine
                    packed.append(turned.astype(BF))
            for h in range(heads):
                packed.append(jnp.concatenate([grad_values[h], grad_values[heads + h]], axis=0))
            packed = dot(jnp.concatenate(packed, axis=1), sel_q[...], 1, 1).astype(BF)
            write_part(part, s, half, packed, wq, 1)
            gp[both, :] = packed

        run(p + 1, attend, [(layer, 3), (layer, 2)])
        weight_grad(layer, 0, nrm, gp, 5 * BLOCK)
        leave(p + 1, 0)
        weight_grad(layer, 1, att, buf, 2 * BLOCK)
        phases[p + 1].near_stage(1)
        if layer > 0:
            for i in attn_part:
                load(layer - 1, i).start()
        relays = [(layer, 0), (layer, 1)]
    leave(PHASES - 1, 1)
    for key in relays:
        send_rest(*key)

    total = small_z[0]
    for copy, d in zip(to_z, range(1, levels)):
        copy.wait_recv()
        total = total + small_z[d]
    small_out[...] = total
    for copy in to_z:
        copy.wait_send()
    rows = w_q.shape[1]
    pad_rows = up16(rows)
    kinds = {0: 0, 2: 1, 4: 2}

    def cut_at(m, t):
        start = rows_at((t + PLANE * kinds[m]) * pad_rows, pad_rows)
        return wi.at[start, : stages[m].shape[1]]

    def pasted_at(layer, m, t):
        start = rows_at((slot(m, layer) * PLANE + t) * pad_rows, pad_rows)
        return {0: gl, 2: act, 4: wd}[m].at[start, : stages[m].shape[1]]

    def trade(layer, m, e):
        kind = kinds[m]
        return remote(
            cut_at(m, place.rank(e)), pasted_at(layer, m, place.rank()),
            trade_sems.at[0, layer, kind, e], trade_sems.at[1, layer, kind, e], place.other(e),
        )

    def traded(layer, m, e):
        there = pasted_at(layer, m, place.rank(e))
        return remote(
            there, there, trade_sems.at[0, layer, kinds[m], e],
            trade_sems.at[1, layer, kinds[m], e], place.other(e),
        )

    def own_trade(layer, m):
        own = place.rank()
        return pltpu.make_async_copy(
            cut_at(m, own), pasted_at(layer, m, own), trade_sems.at[0, layer, kinds[m], 0]
        )

    stayed = set()

    def wait_own_trade(layer, m):
        if (layer, m) not in stayed:
            own_trade(layer, m).wait()
            stayed.add((layer, m))

    def pasted(layer, m, t):
        return pasted_at(layer, m, t)[:rows, :].astype(F32)

    trades = place.trades(levels)

    def o_trade(layer):
        return remote(
            o_cut.at[layer], o_pasted.at[layer], o_sems.at[0, layer], o_sems.at[1, layer],
            place.indexed(place.held(levels)),
        )

    def o_local(layer):
        return pltpu.make_async_copy(o_cut.at[layer], o_pasted.at[layer], o_sems.at[0, layer])

    def finalize(layer, m):
        own = result(layer, m)
        if m == 3 or m > 4:
            total = own
        else:
            total = o_acc if m == 1 else acc.at[:, : own.shape[1]]
            total[...] = own[...].astype(F32)
        for delta in range(1, levels):
            def add(delta=delta):
                send(layer, m, delta).wait_recv()
                total[...] += arrivals[m][slot(m, layer), delta - 1].astype(F32)

            if relayed and delta != 2:
                source = (z + levels - delta) % levels
                pl.when(jnp.logical_not((z + source == 3) & (z * source == 0)))(add)
            else:
                add()
        if m > 3 or layer == 0:
            sent(layer, m)
        if m == 1:
            o_cut[layer] = total[...].astype(BF)
            pl.when(trades)(o_trade(layer).start)
            pl.when(jnp.logical_not(trades))(o_local(layer).start)
        elif m in kinds:
            if m < 4 and layer + 1 < LAYERS:
                wait_own_trade(layer + 1, m)
                for e in range(1, PLANE):
                    trade(layer + 1, m, e).wait_send()
            values = total[...].astype(BF).astype(F32)
            for t in range(PLANE):
                cut_at(m, t)[:rows, :] = values[t * rows : (t + 1) * rows].astype(BF)
            own_trade(layer, m).start()
            for e in range(1, PLANE):
                trade(layer, m, e).start()

    def wait_trade(layer, m):
        wait_own_trade(layer, m)
        for e in range(1, PLANE):
            traded(layer, m, e).wait_recv()
        if m > 3 or layer == 0:
            for e in range(1, PLANE):
                trade(layer, m, e).wait_send()

    span = w_q.shape[2] // 3 // PLANE
    ff_rows = w_in.shape[2] // PLANE // levels
    padded_rows = stages[2].shape[1] // levels

    def rows_out(layer, out):
        here = row_buf.at[:, : out.shape[2]]
        return pltpu.make_async_copy(here, out.at[layer], row_sem.at[0])

    on_the_way = []

    def write_rows(layer, parts, out, kind, w, gain_out):
        whole = jnp.concatenate(parts, axis=1)
        gain_out[layer] = jnp.sum(whole * w[layer].astype(F32), axis=1, keepdims=True)
        if on_the_way:
            on_the_way.pop().wait()
        row_buf[:, : out.shape[2]] = whole * gains[kind, layer]
        copy = rows_out(layer, out)
        copy.start()
        on_the_way.append(copy)

    def assemble(layer):
        wait_trade(layer, 0)
        ranks = [pasted(layer, 0, t) for t in range(PLANE)]
        parts = [rank[:, kind * span : (kind + 1) * span] for kind in range(3) for rank in ranks]
        write_rows(layer, parts, q_out, 0, w_q, q_gain)

    def assemble_mlp(layer):
        wait_trade(layer, 2)
        ranks = [pasted(layer, 2, t) for t in range(PLANE)]
        parts = [
            rank[:, zz * padded_rows : zz * padded_rows + ff_rows]
            for zz in range(levels) for rank in ranks
        ]
        write_rows(layer, parts, i_out, 1, w_in, i_gain)

    def assemble_out(layer):
        @pl.when(trades)
        def _():
            o_trade(layer).wait_recv()
            o_trade(layer).wait_send()

        pl.when(jnp.logical_not(trades))(o_local(layer).wait)
        o_out[layer] = o_pasted[layer, :rows, :].astype(F32)

    head_rows, head_share = out_out.shape[0], first_out.shape[1] // 4 // levels

    def assemble_head():
        wait_trade(last, 4)
        sums = []
        for q in range(4):
            sums.append(pasted(last, 4, 2 * q) + pasted(last, 4, 2 * q + 1))
        parts = []
        for zz in range(levels):
            for q in range(4):
                parts.append(sums[q][:, zz * head_rows : zz * head_rows + head_share])
        first_out[...] = jnp.concatenate(parts, axis=1)

    for key in [(last, 5), (last, 6), (last, 4)] + [(last, m) for m in (3, 2, 0, 1)]:
        finalize(*key)
    for layer in reversed(range(LAYERS - 1)):
        finalize(layer, 3)
        finalize(layer, 2)
    assemble_head()
    for layer in reversed(range(LAYERS - 1)):
        finalize(layer, 0)
        finalize(layer, 1)
    for layer in reversed(range(LAYERS)):
        assemble_mlp(layer)
        assemble(layer)
        assemble_out(layer)
    on_the_way.pop().wait()


def shape(*dims, dtype=BF):
    return jax.ShapeDtypeStruct(dims, dtype)


def rope_table():
    position = np.arange(2 * BLOCK) % ROW_LEN
    inverse = ROTARY_BASE ** (-np.arange(HALF) / HALF)
    angles = (position[:, None] * inverse[None, :]).astype(np.float32)
    table = np.zeros((2 * BLOCK, 2, 2, BLOCK // 2), np.float32)
    table[:, 0, :, :HALF] = np.cos(angles)[:, None]
    table[:, 1, 0, :HALF] = -np.sin(angles)
    table[:, 1, 1, :HALF] = np.sin(angles)
    return table.reshape(2 * BLOCK, 2 * BLOCK)


def lane_of(index):
    head, inside = divmod(index, HDIM)
    half, place = divmod(inside, HALF)
    return head * BLOCK + half * (BLOCK // 2) + place


def per_device(devices, x, segments, padded, w_qkv, w_out, w_in, w_down, gain_attn, gain_mlp,
               head_first, head_first_bias, head_final, head_bias, head_skip, adjoint):
    levels = devices // PLANE
    width = x.shape[1]
    ff = w_in.shape[2]
    columns = head_final.shape[1]
    tokens = PLANE * BLOCK
    heads = width // HDIM // PLANE
    span = heads * HDIM
    rows = width // devices
    out_rows = up16(rows)
    ff_rows = ff // devices
    down_rows = up16(ff_rows)
    head_share = 2 * width // devices
    head_rows = up16(head_share)
    used_cols, o_rows, f_cols = 3 * span, levels * out_rows, levels * down_rows
    h_cols = -(-levels * head_rows // 128) * 128
    q_cols = -(-used_cols // 128) * 128
    lanes = heads * BLOCK

    sel_q = np.zeros((q_cols, 3 * lanes), np.float32)
    sel_o = np.zeros((o_rows, lanes), np.float32)
    for e in range(span):
        for kind in range(3):
            sel_q[kind * span + e, kind * lanes + lane_of(e)] = 1
        sel_o[e // rows * out_rows + e % rows, lane_of(e)] = 1
    sel_q, sel_o = jnp.asarray(sel_q, BF), jnp.asarray(sel_o, BF)
    rope = jnp.asarray(rope_table())
    head_lanes = np.full((1, h_cols), -width, np.int32)
    for zz in range(levels):
        here = slice(zz * head_rows, zz * head_rows + head_share)
        head_lanes[0, here] = 4 * head_share * zz + np.arange(head_share)
    head_lanes = jnp.asarray(head_lanes)

    seg = segments.reshape(2, HALF_BLOCK)
    open_key = padded.reshape(2, HALF_BLOCK) == 0
    within = jnp.arange(HALF_BLOCK)
    static = within[:, None] // ROW_LEN == within[None, :] // ROW_LEN
    static = static & (within[None, :] <= within[:, None])
    allowed = static[None] & (seg[:, :, None] == seg[:, None, :])
    allowed = allowed & (open_key[:, None, :] | (within[:, None] == within[None, :])[None])
    core = lax.axis_index("wide") % 2
    side = jnp.arange(BLOCK)[None, None, :] // HALF_BLOCK == core
    own_mask = (jnp.concatenate([allowed, allowed], axis=-1) & side).astype(BF)

    gains = jnp.stack([gain_attn, gain_mlp]).astype(F32)[..., None]
    d_piece = w_down
    if down_rows != ff_rows:
        d_piece = jnp.pad(w_down, [(0, 0), (0, down_rows - ff_rows), (0, 0)])
    pad_rows = up16(rows)

    in_blocks = (2, 2, 2, 2, HALF_BLOCK)
    layer_shapes = [
        in_blocks + (width,), in_blocks + (width,), (tokens, 3 * lanes), (tokens, lanes), (tokens, o_rows),
        (tokens, f_cols), (tokens, f_cols),
    ]
    slab_shapes = [(width, q_cols), (o_rows, width), (width, f_cols), (f_cols, width)]
    outs = [
        shape(2 * BLOCK, columns), shape(BLOCK, width, dtype=F32),
        shape(LAYERS, BLOCK, width, dtype=F32), shape(LAYERS, BLOCK, width, dtype=F32),
    ]
    vmem_outs = len(outs)
    outs += [shape(LAYERS, *dims) for dims in layer_shapes]
    outs += [shape(*in_blocks, width)] + [shape(tokens, h_cols)] * 3 + [shape(tokens, columns)]
    outs += [shape(LAYERS, *dims) for dims in slab_shapes]
    (predictions, grad_final, xs, mid, nrm, nml, qkv, prb, att, gl, act, lines, hidden, gpre,
     picked, g, wq, wo, wi, wd) = pl.pallas_call(
        lambda *refs: forward_kernel(levels, *refs),
        out_shape=outs,
        in_specs=[VMEM] * 13 + [ANY] * 4,
        out_specs=[VMEM] * vmem_outs + [ANY] * (len(outs) - vmem_outs),
        scratch_shapes=exchange_scratch(width, PHASES + 1)
        + [pltpu.VMEM((LAYERS,) + dims, BF) for dims in layer_shapes[:2]]
        + [pltpu.VMEM(dims, BF) for dims in layer_shapes[2:]]
        + [pltpu.VMEM((LAYERS,) + dims, BF) for dims in slab_shapes]
        + [
            pltpu.VMEM((width, 3 * lanes), BF), pltpu.VMEM((width, width), BF),
            pltpu.VMEM((width, columns), BF), pltpu.VMEM((width, h_cols), BF),
            pltpu.VMEM((width, h_cols), BF), pltpu.VMEM((h_cols, columns), BF),
            pltpu.VMEM(in_blocks + (columns,), BF), pltpu.VMEM((tokens, columns), BF),
            pltpu.VMEM((tokens, h_cols), BF),
            pltpu.VMEM((tokens, h_cols), BF), pltpu.VMEM((tokens, h_cols), BF),
            pltpu.VMEM((2 * BLOCK, width), BF),
            pltpu.VMEM(in_blocks + (BLOCK,), BF),
            pltpu.VMEM((LAYERS, PLANE, pad_rows, q_cols + f_cols), BF),
            pltpu.VMEM((LAYERS, PLANE, pad_rows, q_cols + f_cols), BF),
            pltpu.VMEM((LAYERS, out_rows, width), BF),
            pltpu.VMEM((LAYERS, out_rows, width), BF),
            pltpu.SemaphoreType.DMA((3, LAYERS, 4, levels - 1)),
            pltpu.SemaphoreType.DMA((LAYERS, 4)),
            pltpu.SemaphoreType.DMA((32,)),
            pltpu.SemaphoreType.DMA((3,)),
            pltpu.SemaphoreType.DMA((2, 4)),
            pltpu.SemaphoreType.DMA((2, LAYERS, PLANE)),
            pltpu.SemaphoreType.DMA((2, PLANE)),
            pltpu.SemaphoreType.DMA((2,)),
        ],
        compiler_params=pltpu.CompilerParams(
            collective_id=1, has_side_effects=True, vmem_limit_bytes=62 * MIB
        ),
        name="decoder_forward",
    )(x, own_mask, rope, sel_q, sel_o, head_lanes,
      adjoint.reshape(2, 2, HALF_BLOCK, columns), head_first_bias[None], head_bias[None], gains,
      w_qkv, w_in, w_out, d_piece, head_first, head_final, head_skip)

    chunk = [PLANE * rows, out_rows, PLANE * rows, down_rows, PLANE * rows, head_rows, head_rows]
    cols = [q_cols, width, f_cols, width, h_cols, columns, columns]
    stage_rows = [levels * n for n in chunk[:5]] + [h_cols] * 2
    kept_shapes = [
        in_blocks + (width,), (tokens, f_cols), (tokens, f_cols), (width, f_cols), (f_cols, width),
        (LAYERS, BLOCK, width), in_blocks + (width,), (tokens, 3 * lanes), (tokens, lanes),
        (tokens, o_rows), (width, q_cols), (o_rows, width), (LAYERS, BLOCK, width),
    ]
    small_cols = columns + h_cols
    outs = [
        shape(BLOCK, width, dtype=F32), shape(8, small_cols, dtype=F32),
        shape(LAYERS, rows, 3 * width, dtype=F32), shape(LAYERS, rows, width, dtype=F32),
        shape(LAYERS, rows, ff, dtype=F32), shape(LAYERS, down_rows, width, dtype=F32),
        shape(LAYERS, rows, 1, dtype=F32), shape(LAYERS, rows, 1, dtype=F32),
        shape(rows, width, dtype=F32), shape(head_rows, columns, dtype=F32),
        shape(head_rows, columns, dtype=F32),
    ]
    (input_grad, small, q_grad, o_grad, i_grad, d_grad, q_gain, i_gain, g_first, g_out,
     g_skip) = pl.pallas_call(
        lambda *refs: backward_kernel(levels, *refs),
        out_shape=outs,
        in_specs=[VMEM] * 6 + [ANY] * 19,
        out_specs=[VMEM, VMEM, ANY, VMEM, ANY] + [VMEM] * (len(outs) - 5),
        scratch_shapes=exchange_scratch(width, PHASES)
        + [pltpu.VMEM((2,) + in_blocks + (width,), BF)]
        + [pltpu.VMEM(dims, F32 if dims[0] == LAYERS and dims[1] == BLOCK else BF) for dims in kept_shapes]
        + [pltpu.VMEM((tokens, q_cols), BF)]
        + [pltpu.VMEM((stage_rows[m], cols[m]), BF) for m in range(7)]
        + [
            pltpu.VMEM((LAYERS if m < 4 else 1, levels, chunk[m], cols[m]), BF)
            for m in range(7)
        ]
        + [
            pltpu.VMEM((LAYERS if m < 4 else 1, chunk[m], cols[m]), BF) for m in (0, 1, 2, 4)
        ]
        + [pltpu.VMEM((chunk[0], max(f_cols, q_cols)), F32), pltpu.VMEM((out_rows, width), F32)]
        + [pltpu.VMEM((LAYERS, out_rows, width), BF)] * 2
        + [
            pltpu.VMEM((2, 8, h_cols), F32), pltpu.VMEM((8, h_cols), F32),
            pltpu.VMEM((levels, 8, small_cols), F32),
            pltpu.VMEM((rows, max(ff, 3 * width)), F32),
            pltpu.SemaphoreType.DMA((2, LAYERS, 7, levels)),
            pltpu.SemaphoreType.DMA((20,)),
            pltpu.SemaphoreType.DMA((2, levels)),
            pltpu.SemaphoreType.DMA((2, LAYERS, 3, PLANE)),
            pltpu.SemaphoreType.DMA((2, LAYERS)),
            pltpu.SemaphoreType.DMA((1,)),
        ],
        compiler_params=pltpu.CompilerParams(
            collective_id=2, has_side_effects=True, vmem_limit_bytes=62 * MIB
        ),
        name="decoder_backward",
    )(rope, sel_q, sel_o, gains, w_qkv, w_in, grad_final, nml, act, gl, wi, wd, mid, nrm, qkv, prb,
      att, wq, wo, xs, lines, gpre, hidden.reshape(in_blocks + (h_cols,)),
      picked.reshape(in_blocks + (h_cols,)), g)

    z, narrow = lax.axis_index("wide") // 4, lax.axis_index("narrow")
    g_first_bias = lax.dynamic_slice(small[0], (columns + z * head_rows + narrow * rows,), (rows,))
    return (
        predictions, input_grad, q_grad, o_grad, i_grad, d_grad[:, :ff_rows], q_gain[..., 0],
        i_gain[..., 0], g_first, g_first_bias, g_out[:head_share], small[0, :columns],
        g_skip[:head_share],
    )


def solution(mesh):
    devices = mesh.shape["wide"] * mesh.shape["narrow"]
    both = ("wide", "narrow")
    weight, gain = P(None, both, None), P(None, both)
    return jax.shard_map(
        lambda *arrays: per_device(devices, *arrays),
        mesh=mesh,
        in_specs=(
            P(both, None), P(both), P(both), weight, weight, weight, weight, gain, gain, P(), P(),
            P(None, "narrow"), P("narrow"), P(None, "narrow"), P("wide", "narrow"),
        ),
        out_specs=(
            P("wide", "narrow"), P(both, None), weight, weight, weight, weight, gain, gain,
            P(both, None), P(both), P("wide", "narrow"), P("narrow"), P("wide", "narrow"),
        ),
        check_vma=False,
    )
```
